32 devices in a mesh: section: 4 (over z), batch: 8 (over y, x, core).
Axes of the slice: x: 2, y: 2, z: 4, core: 2. Of those that a mesh axis runs over, the one named last changes fastest.
Arguments:
- observations: bfloat16 [4096, 39], P('batch'), may hold values from -6 to 6
- actions: bfloat16 [5, 4096, 6], P(None, 'batch'), may hold values from -1 to 1
- targets: bfloat16 [5, 4096, 512], P(None, 'batch'), may hold values from 0 to 0.25
- task_ids: int32 [4096], P('batch'), may hold values from 0 to 79
- horizons: int32 [4096], P('batch'), may hold values from 3 to 5, as said below
- reward_bins: int32 [5, 4096], P(None, 'batch'), may hold values from 0 to 100
- value_bins: int32 [5, 4096], P(None, 'batch'), may hold values from 0 to 100
- task_table: bfloat16 [80, 96], replicated, may hold values from -3 to 3
- enc_first: bfloat16 [135, 256], replicated, may hold values from -0.5 to 0.5
- enc_gain: float32 [256], replicated, may hold values from 0.5 to 1.5
- enc_shift: float32 [256], replicated, may hold values from -3 to 3
- enc_second: bfloat16 [256, 512], replicated, may hold values from -0.3984375 to 0.3984375
- net_first: bfloat16 [7, 614, 512], replicated, may hold values from -0.25 to 0.25
- net_second: bfloat16 [7, 512, 512], replicated, may hold values from -0.25 to 0.25
- net_gain: float32 [7, 2, 512], replicated, may hold values from 0.5 to 1.5
- net_shift: float32 [7, 2, 512], replicated, may hold values from -3 to 3
- dyn_out: bfloat16 [512, 512], replicated, may hold values from -0.3984375 to 0.3984375
- head_out: bfloat16 [6, 512, 101], replicated, may hold values from -0.3984375 to 0.3984375
Outputs:
- loss: float32 [], replicated
- grad_task_table: float32 [80, 96], replicated
- grad_enc_first: float32 [135, 256], P(None, ('section', 'batch'))
- grad_enc_gain: float32 [256], P(('section', 'batch'))
- grad_enc_shift: float32 [256], P(('section', 'batch'))
- grad_enc_second: float32 [256, 512], P(('section', 'batch'))
- grad_net_first: float32 [7, 614, 512], P(None, None, ('section', 'batch'))
- grad_net_second: float32 [7, 512, 512], P(None, None, ('section', 'batch'))
- grad_net_gain: float32 [7, 2, 512], P(None, None, ('section', 'batch'))
- grad_net_shift: float32 [7, 2, 512], P(None, None, ('section', 'batch'))
- grad_dyn_out: float32 [512, 512], P(('section', 'batch'))
- grad_head_out: float32 [6, 512, 101], P(None, ('section', 'batch'))
The draws below stay inside these ranges and needn't reach their ends.
Inputs may be any that keep to these rules, and one draw needn't show every extreme that they name: `horizons`: each entry is 3 or 5.
All inputs are finite; a program needn't handle non-finite values.
Results may differ from the reference program's by a relative error of at most 0.007.
Values may be sent and summed in bfloat16 or wider, within the bound.
No kernel may reach another device: no remote copies, remote signals or barrier semaphores. Data moves between devices by JAX's collectives and lax.ppermute only.
A program may use at most 192 MiB of HBM per device.

```python
import jax
import jax.numpy as jnp
from jax import lax

LATENT = 512
HID = 512
ENC = 256
OBS = 39
ACT = 6
TASK_DIM = 96
TASKS = 80
BINS = 101
ROWS = 512
HORIZON = 5
NETS = 7
HEADS = 6
TOKENS = 4096


def draw_horizons(key, part):
    key = jax.random.fold_in(key, 11)
    picks = jax.random.randint(key, (TOKENS,), 0, 2)
    values = (HORIZON - 2 + 2 * picks).astype(jnp.int32)
    return values.at[0].set(HORIZON).at[1].set(HORIZON - 2)


def place_ends(drawn, key, low, top_value):
    extent = drawn.shape
    index_at = [jax.random.randint(jax.random.fold_in(key, axis), (), 0, extent[axis]) for axis in range(len(extent))]
    drawn = drawn.at[tuple(index_at)].set(low)
    longest = extent.index(max(extent))
    index_at[longest] = (index_at[longest] + 1) % extent[longest]
    return drawn.at[tuple(index_at)].set(top_value)


def block_levels(rng, extent, pieces, least, top_value):
    gain, own = 1.0, jax.random.fold_in(rng, 6)
    for position, parts in pieces:
        heights = jnp.exp(jax.random.uniform(jax.random.fold_in(own, position), (parts,), jnp.float32, least / len(pieces), top_value / len(pieces)))
        gain = gain * jnp.repeat(heights, extent[position] // parts).reshape([-1 if axis == position else 1 for axis in range(len(extent))])
    return gain


def bell_draw(own_key, dims, scale, bound, cuts=(), held_as=jnp.bfloat16):
    result = scale * jax.random.normal(own_key, dims, jnp.float32)
    if cuts:
        result = result * block_levels(own_key, dims, cuts, -0.22, 0.18)
    return jnp.clip(result, -bound, bound).astype(held_as)


def setup_inputs(seed: int = 0) -> dict:
    keys = jax.random.split(jax.random.key(seed), 19)
    return {
        "observations": bell_draw(keys[0], (TOKENS, OBS), 1.0, 6.0, ((0, 8),)),
        "actions": jnp.clip(jax.random.uniform(keys[1], (HORIZON, TOKENS, ACT), jnp.float32, -1.0, 1.0) * block_levels(keys[1], (HORIZON, TOKENS, ACT), ((1, 8),), -0.4, 0.0), -1.0, 1.0).astype(jnp.bfloat16),
        "targets": jnp.clip(0.25 * jax.random.uniform(keys[2], (HORIZON, TOKENS, LATENT), jnp.float32) ** block_levels(keys[2], (HORIZON, TOKENS, LATENT), ((1, 8),), -0.2, 0.2), 0.0, 0.25).astype(jnp.bfloat16),
        "task_ids": place_ends(jax.random.randint(keys[3], (TOKENS,), 0, TASKS), jax.random.fold_in(keys[3], 1), 0, TASKS - 1).astype(jnp.int32),
        "horizons": draw_horizons(jax.random.fold_in(keys[18], 71), 0),
        "reward_bins": place_ends(jax.random.randint(keys[5], (HORIZON, TOKENS), 0, BINS), jax.random.fold_in(keys[5], 1), 0, BINS - 1).astype(jnp.int32),
        "value_bins": place_ends(jax.random.randint(keys[6], (HORIZON, TOKENS), 0, BINS), jax.random.fold_in(keys[6], 1), 0, BINS - 1).astype(jnp.int32),
        "task_table": bell_draw(keys[7], (TASKS, TASK_DIM), 0.5, 3.0),
        "enc_first": bell_draw(keys[8], (OBS + TASK_DIM, ENC), (OBS + TASK_DIM) ** -0.5, 0.5),
        "enc_gain": jnp.clip(1.0 + 0.1 * jax.random.normal(keys[9], (ENC,), jnp.float32), 0.5, 1.5),
        "enc_shift": bell_draw(keys[10], (ENC,), 0.5, 3.0, (), jnp.float32),
        "enc_second": bell_draw(keys[11], (ENC, LATENT), 0.07, 0.3984375),
        "net_first": bell_draw(keys[12], (NETS, LATENT + ACT + TASK_DIM, HID), (LATENT + ACT + TASK_DIM) ** -0.5, 0.25),
        "net_second": bell_draw(keys[13], (NETS, HID, HID), HID ** -0.5, 0.25),
        "net_gain": jnp.clip(1.0 + 0.1 * jax.random.normal(keys[14], (NETS, 2, HID), jnp.float32), 0.5, 1.5),
        "net_shift": bell_draw(keys[15], (NETS, 2, HID), 0.5, 3.0, (), jnp.float32),
        "dyn_out": bell_draw(keys[16], (HID, LATENT), 0.07, 0.3984375),
        "head_out": bell_draw(keys[17], (HEADS, HID, BINS), 0.07, 0.3984375),
    }


@jax.custom_vjp
def low(v):
    return lax.optimization_barrier(v.astype(jnp.bfloat16)).astype(jnp.float32)

@jax.custom_vjp
def low_back(v):
    return v

def low_keep(v):
    return (low(v), None)

def low_pass(kept, grad):
    return (grad,)

def back_keep(v):
    return (v, None)

def back_low(kept, grad):
    return (low(grad),)
low.defvjp(low_keep, low_pass)
low_back.defvjp(back_keep, back_low)

def layer_mish(pre_act, gain_vec, shift_vec):
    row_mean = lax.optimization_barrier(jnp.mean(pre_act, axis=-1, keepdims=True))
    centred = pre_act - row_mean
    spread = lax.optimization_barrier(jnp.mean(centred * centred, axis=-1, keepdims=True))
    normed = centred * lax.rsqrt(spread + 1e-05) * gain_vec + shift_vec
    return normed * jnp.tanh(jax.nn.softplus(normed))

def simplex_norm(values):
    grouped = values.reshape(values.shape[:-1] + (values.shape[-1] // 8, 8))
    return jax.nn.softmax(grouped, axis=-1).reshape(values.shape)

def head_loss(latent_next, logits, target_rows, reward_rows, value_rows, weight_rows):
    residue = latent_next - target_rows
    consist = lax.optimization_barrier(jnp.mean(residue * residue, axis=-1))
    log_total = jax.nn.logsumexp(logits, axis=-1)
    columns = lax.broadcasted_iota(jnp.int32, logits.shape, 2)
    value_many = jnp.broadcast_to(value_rows[None, :], (logits.shape[0] - 1, value_rows.shape[0]))
    wanted = jnp.concatenate([reward_rows[None, :], value_many], axis=0)
    picked = lax.optimization_barrier(jnp.sum(jnp.where(columns == wanted[:, :, None], logits, 0.0), axis=-1))
    entropy = log_total - picked
    per_row = 20.0 * consist + 0.1 * entropy[0] + 0.1 * lax.optimization_barrier(jnp.mean(entropy[1:], axis=0))
    return jnp.sum(weight_rows * per_row)

def block_loss(params, obs_rows, action_rows, target_rows, task_rows, horizon_rows, reward_rows, value_rows):
    table_w, first_enc, gain_enc, shift_enc, second_enc, first_net, second_net, gain_net, shift_net, dyn_weight, head_weight = params
    highest = lax.Precision.HIGHEST
    embedded = table_w[task_rows]
    enc_input = jnp.concatenate([obs_rows.astype(jnp.float32), embedded], axis=1)
    enc_pre = low_back(jnp.dot(enc_input, first_enc, precision=highest))
    enc_hidden = low(layer_mish(enc_pre, gain_enc, shift_enc))
    enc_out = low_back(jnp.dot(enc_hidden, second_enc, precision=highest))
    latent_now = simplex_norm(enc_out)
    loss_total = jnp.zeros((), jnp.float32)
    for step_no in range(HORIZON):
        latent_in = low_back(low(latent_now))
        step_input = jnp.concatenate([latent_in, action_rows[step_no].astype(jnp.float32), embedded], axis=1)
        pre_one = low_back(jnp.einsum('rk,nkh->nrh', step_input, first_net, precision=highest))
        hid_one = low(layer_mish(pre_one, gain_net[:, 0:1, :], shift_net[:, 0:1, :]))
        pre_two = low_back(jnp.einsum('nrh,nhk->nrk', hid_one, second_net, precision=highest))
        hid_two = low(layer_mish(pre_two, gain_net[:, 1:2, :], shift_net[:, 1:2, :]))
        out_dyn = low_back(jnp.dot(hid_two[0], dyn_weight, precision=highest))
        logits = low_back(jnp.einsum('nrh,nhb->nrb', hid_two[1:], head_weight, precision=highest))
        latent_next = simplex_norm(out_dyn)
        weight_rows = 0.5 ** (step_no / (HORIZON - 1)) * (step_no < horizon_rows).astype(jnp.float32) / (TOKENS * HORIZON)
        loss_total = loss_total + head_loss(latent_next, logits, target_rows[step_no].astype(jnp.float32), reward_rows[step_no], value_rows[step_no], weight_rows)
        latent_now = latent_next
    return loss_total

def reference(observations, actions, targets, task_ids, horizons, reward_bins, value_bins, task_table, enc_first, enc_gain, enc_shift, enc_second, net_first, net_second, net_gain, net_shift, dyn_out, head_out):
    weights = tuple((array_in.astype(jnp.float32) for array_in in (task_table, enc_first, enc_gain, enc_shift, enc_second, net_first, net_second, net_gain, net_shift, dyn_out, head_out)))

    def one_block(carry_in, block_no):
        row_start = block_no * ROWS

        def rows_of(source_arr, axis_no):
            return lax.dynamic_slice_in_dim(source_arr, row_start, ROWS, axis_no)

        def block_fn(params):
            return block_loss(params, rows_of(observations, 0), rows_of(actions, 1), rows_of(targets, 1), rows_of(task_ids, 0), rows_of(horizons, 0), rows_of(reward_bins, 1), rows_of(value_bins, 1))
        loss_value, back_fn = jax.vjp(block_fn, weights)
        grad_terms = back_fn(jnp.ones((), jnp.float32))[0]
        return ((carry_in[0] + loss_value, jax.tree.map(jnp.add, carry_in[1], grad_terms)), None)
    start_sum = (jnp.zeros((), jnp.float32), tuple((jnp.zeros_like(array_in) for array_in in weights)))
    result_sum, ignored = lax.scan(one_block, start_sum, jnp.arange(TOKENS // ROWS, dtype=jnp.int32))
    grad_sum = result_sum[1]
    return (result_sum[0], grad_sum[0], 0.3 * grad_sum[1], 0.3 * grad_sum[2], 0.3 * grad_sum[3], 0.3 * grad_sum[4], grad_sum[5], grad_sum[6], grad_sum[7], grad_sum[8], grad_sum[9], grad_sum[10])
```

```python
import jax
import jax.numpy as jnp
from jax import lax
from jax.sharding import PartitionSpec as P

HORIZON = 5
CORES = 2
BF16 = jnp.bfloat16
F32 = jnp.float32


def layer_mish(pre_act, gain_vec, shift_vec):
    row_mean = jnp.mean(pre_act, axis=-1, keepdims=True)
    centred = pre_act - row_mean
    spread = jnp.mean(centred * centred, axis=-1, keepdims=True)
    normed = centred * lax.rsqrt(spread + 1e-05) * gain_vec + shift_vec
    return normed * jnp.tanh(jax.nn.softplus(normed))


def simplex_norm(values):
    grouped = values.reshape(values.shape[:-1] + (values.shape[-1] // 8, 8))
    return jax.nn.softmax(grouped, axis=-1).reshape(values.shape)


def dot32(spec, left, right):
    return jnp.einsum(spec, left, right, preferred_element_type=F32)


def padded(value, width):
    return jnp.pad(value, [(0, 0)] * (value.ndim - 1) + [(0, width - value.shape[-1])])


def swap(value, axis, distance):
    count = lax.axis_size(axis)
    return lax.ppermute(value, axis, [(place, place ^ distance) for place in range(count)])


def scatter_phases(packed, repeated):
    sections, chips = packed.shape[0], packed.shape[1]
    batch_no = lax.axis_index("batch")
    section_no = lax.axis_index("section")
    places = (
        ("batch", 1, CORES, 2, batch_no % CORES),
        ("batch", CORES, chips, 1, batch_no // CORES),
        ("section", 1, sections, 0, section_no),
    )
    for axis, scale, count, dim, mine in places:
        kept = lax.dynamic_index_in_dim(packed, mine, dim, keepdims=False).astype(F32)
        total = repeated
        for other in range(1, count):
            sent = lax.dynamic_index_in_dim(packed, mine ^ other, dim, keepdims=False)
            kept = kept + swap(sent, axis, other * scale).astype(F32)
            total = total + swap(repeated, axis, other * scale)
        repeated = total
        packed = kept.astype(BF16) if dim else kept
    return packed, repeated


def on_device(
    observations,
    actions,
    targets,
    task_ids,
    horizons,
    reward_bins,
    value_bins,
    task_table,
    enc_first,
    enc_gain,
    enc_shift,
    enc_second,
    net_first,
    net_second,
    net_gain,
    net_shift,
    dyn_out,
    head_out,
):
    sections = lax.axis_size("section")
    section_no = lax.axis_index("section")
    batches = lax.axis_size("batch")
    chips = batches // CORES
    devices = sections * batches
    norm_scale = 1.0 / (observations.shape[0] * batches * HORIZON)
    rows = observations.shape[0] // sections
    latent_width = dyn_out.shape[1]
    hidden = dyn_out.shape[0]
    action_width = actions.shape[2]
    task_count, task_width = task_table.shape
    heads = head_out.shape[0]
    bins = head_out.shape[2]

    def own(source, axis):
        return lax.dynamic_slice_in_dim(source, section_no * rows, rows, axis)

    observations, task_ids, horizons = own(observations, 0), own(task_ids, 0), own(horizons, 0)
    actions, targets = own(actions, 1), own(targets, 1)
    reward_bins, value_bins = own(reward_bins, 1), own(value_bins, 1)

    kind_ids = lax.broadcasted_iota(jnp.int32, (rows, task_count), 1)
    onehot = (kind_ids == task_ids[:, None]).astype(BF16)
    embedded = jnp.dot(onehot, task_table, preferred_element_type=F32).astype(BF16)

    enc_input = jnp.concatenate([observations, embedded], axis=1)
    enc_pre = jnp.dot(enc_input, enc_first, preferred_element_type=F32)
    enc_act, enc_back = jax.vjp(layer_mish, enc_pre, enc_gain, enc_shift)
    enc_hidden = enc_act.astype(BF16)
    enc_out = jnp.dot(enc_hidden, enc_second, preferred_element_type=F32)
    latent_zero, enc_simplex_back = jax.vjp(simplex_norm, enc_out)

    latent_in = latent_zero.astype(BF16)
    inputs, dyn_saved, next_latents = [], [], []
    for step in range(HORIZON):
        step_input = jnp.concatenate([latent_in, actions[step], embedded], axis=1)
        inputs.append(step_input)
        pre_one = jnp.dot(step_input, net_first[0], preferred_element_type=F32)
        act_one, back_one = jax.vjp(layer_mish, pre_one, net_gain[0, 0], net_shift[0, 0])
        hid_one = act_one.astype(BF16)
        pre_two = jnp.dot(hid_one, net_second[0], preferred_element_type=F32)
        act_two, back_two = jax.vjp(layer_mish, pre_two, net_gain[0, 1], net_shift[0, 1])
        hid_two = act_two.astype(BF16)
        out_dyn = jnp.dot(hid_two, dyn_out, preferred_element_type=F32)
        latent_next, simplex_back = jax.vjp(simplex_norm, out_dyn)
        next_latents.append(latent_next)
        latent_in = latent_next.astype(BF16)
        dyn_saved.append((hid_one, back_one, hid_two, back_two, simplex_back))

    x_all = jnp.concatenate(inputs, axis=0)
    decay = jnp.power(F32(0.5), jnp.arange(HORIZON, dtype=F32) / (HORIZON - 1))
    in_use = jnp.arange(HORIZON, dtype=jnp.int32)[:, None] < horizons[None, :]
    weight_rows = (decay[:, None] * norm_scale * in_use.astype(F32)).reshape(-1)

    pre_one = dot32("rk,nkh->nrh", x_all, net_first[1:])
    act_one, back_one = jax.vjp(layer_mish, pre_one, net_gain[1:, 0:1], net_shift[1:, 0:1])
    hid_one = act_one.astype(BF16)
    pre_two = dot32("nrh,nhk->nrk", hid_one, net_second[1:])
    act_two, back_two = jax.vjp(layer_mish, pre_two, net_gain[1:, 1:2], net_shift[1:, 1:2])
    hid_two = act_two.astype(BF16)
    logits = dot32("nrh,nhb->nrb", hid_two, head_out)
    columns = lax.broadcasted_iota(jnp.int32, logits.shape, 2)
    many = jnp.broadcast_to(value_bins.reshape(1, -1), (heads - 1, HORIZON * rows))
    wanted = jnp.concatenate([reward_bins.reshape(1, -1), many], axis=0)
    chosen = columns == wanted[:, :, None]
    share = jnp.full((heads, 1), 0.1 / (heads - 1), F32).at[0].set(0.1)
    row_share = share * weight_rows[None, :]
    top = jnp.max(logits, axis=-1, keepdims=True)
    powers = jnp.exp(logits - top)
    total = jnp.sum(powers, axis=-1, keepdims=True)
    picked = jnp.sum(jnp.where(chosen, logits, 0.0), axis=-1)
    entropy = (jnp.log(total) + top)[..., 0] - picked
    loss = jnp.sum(row_share * entropy)
    d_logits = (row_share[:, :, None] * (powers / total - chosen.astype(F32))).astype(BF16)
    g_head = dot32("nrh,nrb->hnb", hid_two, d_logits)
    d_hid_two = dot32("nrb,nhb->nrh", d_logits, head_out)
    d_pre_two, gain_two, shift_two = back_two(d_hid_two)
    d_two_low = d_pre_two.astype(BF16)
    g_second = dot32("nrk,nrh->knh", d_two_low, hid_one)
    d_hid_one = dot32("nrk,nhk->nrh", d_two_low, net_second[1:])
    d_pre_one, gain_one, shift_one = back_one(d_hid_one)
    d_one_low = d_pre_one.astype(BF16)
    g_first = dot32("nrh,rk->hnk", d_one_low, x_all)
    d_input_all = dot32("nrh,nkh->rk", d_one_low, net_first[1:]).reshape(HORIZON, rows, -1)

    def blocks(value):
        return value.reshape((sections, chips, CORES, value.shape[0] // devices) + value.shape[1:])

    head_small = jnp.stack(
        [gain_one[:, 0], gain_two[:, 0], shift_one[:, 0], shift_two[:, 0]]
    )
    head_pack = jnp.concatenate(
        [padded(g_first, 640), g_second, padded(g_head, 128)], axis=2
    ).astype(BF16)
    head_pack = blocks(head_pack)
    nothing = jnp.zeros((8, 128), F32)
    head_sum, _ = scatter_phases(head_pack, nothing)

    d_embed = jnp.zeros((rows, task_width), F32)
    incoming = jnp.zeros((rows, latent_width), F32)
    d_ones, d_twos, d_outs = [None] * HORIZON, [None] * HORIZON, [None] * HORIZON
    dyn_small = [jnp.zeros((hidden,), F32)] * 4
    for step in reversed(range(HORIZON)):
        hid_one_t, back_one_t, hid_two_t, back_two_t, simplex_back = dyn_saved[step]
        row_weight = weight_rows.reshape(HORIZON, rows)[step][:, None]
        residue = next_latents[step] - targets[step].astype(F32)
        loss = loss + jnp.sum(row_weight * 20.0 * jnp.mean(residue * residue, axis=-1, keepdims=True))
        d_next = (40.0 / latent_width) * row_weight * residue
        d_out = simplex_back(d_next + incoming)[0].astype(BF16)
        d_pre_two_t, gain_two_t, shift_two_t = back_two_t(dot32("rl,hl->rh", d_out, dyn_out))
        d_two_t = d_pre_two_t.astype(BF16)
        d_pre_one_t, gain_one_t, shift_one_t = back_one_t(dot32("rk,hk->rh", d_two_t, net_second[0]))
        d_one_t = d_pre_one_t.astype(BF16)
        d_input = d_input_all[step] + dot32("rh,kh->rk", d_one_t, net_first[0])
        incoming = d_input[:, :latent_width].astype(BF16).astype(F32)
        d_embed = d_embed + d_input[:, latent_width + action_width :]
        d_outs[step], d_twos[step], d_ones[step] = d_out, d_two_t, d_one_t
        terms = (gain_one_t, gain_two_t, shift_one_t, shift_two_t)
        dyn_small = [held + term for held, term in zip(dyn_small, terms)]

    hid_ones = jnp.concatenate([saved[0] for saved in dyn_saved], axis=0)
    hid_twos = jnp.concatenate([saved[2] for saved in dyn_saved], axis=0)
    g_dyn_first = dot32("rh,rk->hk", jnp.concatenate(d_ones, axis=0), x_all)
    g_dyn_second = dot32("rk,rh->kh", jnp.concatenate(d_twos, axis=0), hid_ones)
    g_dyn_out = dot32("rh,rl->hl", hid_twos, jnp.concatenate(d_outs, axis=0))

    d_enc_out = enc_simplex_back(incoming)[0].astype(BF16)
    g_enc_second = dot32("rk,rl->kl", enc_hidden, d_enc_out)
    d_enc_pre, g_enc_gain, g_enc_shift = enc_back(dot32("rl,kl->rk", d_enc_out, enc_second))
    d_enc_low = d_enc_pre.astype(BF16)
    g_enc_first = dot32("rk,ri->ki", d_enc_low, enc_input)
    d_enc_input = dot32("rk,ik->ri", d_enc_low, enc_first)
    d_embed = d_embed + d_enc_input[:, enc_input.shape[1] - task_width :]
    table_sum = jnp.einsum(
        "rt,re->te", onehot.astype(F32), d_embed, precision=lax.Precision.HIGHEST
    )

    small = jnp.concatenate([head_small.reshape(4 * heads, hidden), jnp.stack(dyn_small)], axis=0)
    small = padded(small.T, 128)
    net_pack = jnp.concatenate([padded(g_dyn_first, 640), g_dyn_second, g_dyn_out, small], axis=1)
    enc_small = padded(jnp.stack([g_enc_gain, g_enc_shift], axis=1), 128)
    enc_pack = jnp.concatenate([g_enc_second, padded(g_enc_first, 256), enc_small], axis=1)
    net_pack, enc_pack = blocks(net_pack), blocks(enc_pack)
    net_rows = net_pack.shape[3] * net_pack.shape[4]
    net_flat = net_pack.reshape(sections, chips, CORES, -1, 128)
    enc_flat = enc_pack.reshape(sections, chips, CORES, -1, 128)
    tail_pack = jnp.concatenate([net_flat, enc_flat], axis=3).astype(BF16)
    repeated = jnp.concatenate([padded(table_sum, 128), jnp.full((8, 128), loss, F32)], axis=0)
    tail_sum, repeated = scatter_phases(tail_pack, repeated)
    table_sum = repeated[:task_count, :task_width]
    loss = repeated[task_count, 0]

    mine = hidden // devices
    net_sum = tail_sum[: net_rows // 128].reshape(mine, -1)
    enc_sum = tail_sum[net_rows // 128 :].reshape(enc_first.shape[1] // devices, -1)
    net_in = net_first.shape[1]
    s_first = jnp.concatenate([net_sum[:, None, :net_in], head_sum[:, :, :net_in]], axis=1)
    s_second = jnp.concatenate([net_sum[:, None, 640 : 640 + hidden], head_sum[:, :, 640 : 640 + hidden]], axis=1)
    s_head = head_sum[:, :, 640 + hidden : 640 + hidden + bins]
    s_dyn = net_sum[:, 640 + hidden : 640 + 2 * hidden]
    s_small = net_sum[:, 640 + 2 * hidden :]
    s_pairs = s_small[:, : 4 * heads].reshape(mine, 2, 2, heads)
    s_dyn_pairs = s_small[:, 4 * heads : 4 * heads + 4].reshape(mine, 2, 2, 1)
    s_pairs = jnp.concatenate([s_dyn_pairs, s_pairs], axis=3)
    s_gain = s_pairs[:, 0].transpose(2, 1, 0)
    s_shift = s_pairs[:, 1].transpose(2, 1, 0)
    s_enc_second = enc_sum[:, :latent_width]
    s_enc_first = enc_sum[:, latent_width : latent_width + enc_first.shape[0]].T
    s_enc_gain = enc_sum[:, latent_width + 256]
    s_enc_shift = enc_sum[:, latent_width + 257]
    return (
        loss,
        table_sum,
        0.3 * s_enc_first,
        0.3 * s_enc_gain,
        0.3 * s_enc_shift,
        0.3 * s_enc_second,
        s_first.transpose(1, 2, 0),
        s_second.transpose(1, 2, 0),
        s_gain,
        s_shift,
        s_dyn,
        s_head.transpose(1, 0, 2),
    )


def solution(mesh):
    both = ("section", "batch")
    return jax.shard_map(
        on_device,
        mesh=mesh,
        in_specs=(
            P("batch", None),
            P(None, "batch", None),
            P(None, "batch", None),
            P("batch"),
            P("batch"),
            P(None, "batch"),
            P(None, "batch"),
        )
        + (P(),) * 11,
        out_specs=(
            P(),
            P(),
            P(None, both),
            P(both),
            P(both),
            P(both, None),
            P(None, None, both),
            P(None, None, both),
            P(None, None, both),
            P(None, None, both),
            P(both, None),
            P(None, both, None),
        ),
        check_vma=False,
    )
```

```python
import functools

import jax
import jax.numpy as jnp
from jax import lax
from jax.experimental import pallas as pl
from jax.experimental.pallas import tpu as pltpu
from jax.sharding import PartitionSpec as P

CORES = 2
LANES = 128
GROUP = 16
BF16 = jnp.bfloat16
F32 = jnp.float32
CHUNKS = (2, 2, 2)
VMEM_BYTES = 44 * 1024 * 1024


def nn(left, right):
    return lax.dot_general(left, right, (((1,), (0,)), ((), ())), preferred_element_type=F32)


def nt(left, right):
    return lax.dot_general(left, right, (((1,), (1,)), ((), ())), preferred_element_type=F32)


def tn(left, right):
    return lax.dot_general(left, right, (((0,), (0,)), ((), ())), preferred_element_type=F32)


def column_sum(value):
    grouped = value.reshape(value.shape[0] // 8, 8, value.shape[1])
    return jnp.sum(jnp.sum(grouped, axis=0), axis=0, keepdims=True)


def slabs(features, size=64):
    return [slice(start, start + size) for start in range(0, features, size)]


def lanes_of(step):
    return slice(step * LANES, (step + 1) * LANES)


def spread_columns(gain_rows, shift_rows, rows_ref, spread_ref):
    count = gain_rows.shape[0]
    rows_ref[...] = jnp.zeros_like(rows_ref)
    rows_ref[0:count, :] = gain_rows
    rows_ref[count : 2 * count, :] = shift_rows
    turned = jnp.transpose(rows_ref[...])
    for place in range(2 * count):
        spread_ref[place] = jnp.broadcast_to(turned[:, place : place + 1], spread_ref.shape[1:])


def mish_forward(pre_ref, pre_at, gain_ref, shift_ref, hid_ref, hat_ref, slope_ref, scale_ref, scale_row, at):
    features = pre_ref.shape[0]
    row_mean = column_sum(pre_ref[:, pre_at]) * (1.0 / features)
    centred = pre_ref[:, pre_at] - row_mean
    spread = column_sum(centred * centred) * (1.0 / features)
    scale = lax.rsqrt(spread + 1e-05)
    scale_ref[scale_row : scale_row + 1, at] = scale
    for part in slabs(features):
        hat = (pre_ref[part, pre_at] - row_mean) * scale
        normed = hat * gain_ref[part, :] + shift_ref[part, :]
        power = jnp.exp(normed)
        top = power * (power + 2.0)
        inverse = pl.reciprocal(top + 2.0, approx=True)
        ratio = top * inverse
        hid_ref[part, at] = (normed * ratio).astype(BF16)
        tilt = power * inverse
        slope = ratio + normed * (4.0 * (tilt * (tilt + inverse)))
        slope_ref[part, at] = (slope * gain_ref[part, :]).astype(BF16)
        hat_ref[part, at] = hat.astype(BF16)


def mish_backward(grad_ref, grad_at, hat_ref, slope_ref, scale_ref, scale_row, at, kept_ref, sums_ref, sums_at, first, out_ref):
    features = grad_ref.shape[0]
    total_one = jnp.zeros((8, LANES), F32)
    total_two = jnp.zeros((8, LANES), F32)
    for part in slabs(features):
        term = grad_ref[part, grad_at] * slope_ref[part, at].astype(F32)
        kept_ref[part, :] = term
        crossed = term * hat_ref[part, at].astype(F32)
        groups = (term.shape[0] // 8, 8, LANES)
        total_one = total_one + jnp.sum(term.reshape(groups), axis=0)
        total_two = total_two + jnp.sum(crossed.reshape(groups), axis=0)
        if first:
            sums_ref[sums_at, part, :] = term
            sums_ref[sums_at + 1, part, :] = crossed
        else:
            sums_ref[sums_at, part, :] += term
            sums_ref[sums_at + 1, part, :] += crossed
    mean_one = jnp.sum(total_one, axis=0, keepdims=True) * (1.0 / features)
    mean_two = jnp.sum(total_two, axis=0, keepdims=True) * (1.0 / features)
    scale = scale_ref[scale_row : scale_row + 1, at]
    for part in slabs(features):
        rest = kept_ref[part, :] - mean_one - hat_ref[part, at].astype(F32) * mean_two
        out_ref[part, at] = (rest * scale).astype(BF16)


def simplex(values):
    grouped = values.reshape(values.shape[0] // 8, 8, values.shape[1])
    powers = jnp.exp(grouped - jnp.max(grouped, axis=1, keepdims=True))
    shares = powers / jnp.sum(powers, axis=1, keepdims=True)
    return shares.reshape(values.shape)


def simplex_back(shares, grads):
    grouped = (shares.shape[0] // 8, 8, shares.shape[1])
    crossed = jnp.sum((shares * grads).reshape(grouped), axis=1, keepdims=True)
    return (shares.reshape(grouped) * (grads.reshape(grouped) - crossed)).reshape(shares.shape)


def row_weight(step, steps, scale, horizon_row, place_ref):
    lane = lax.broadcasted_iota(jnp.int32, (1, LANES), 1)
    mine = (lane >= place_ref[2]) & (lane < place_ref[3]) & (horizon_row > step)
    return jnp.where(mine, F32(scale * 0.5 ** (step / (steps - 1))), 0.0)


def put_blocks(place_ref, slots, source_ref, width, targets):
    for relative, (which, slot) in enumerate(slots):
        start = pl.multiple_of((place_ref[0] ^ relative) * GROUP, GROUP)
        targets(which, slot)[:, 0:width] = source_ref[pl.ds(start, GROUP), 0:width].astype(BF16)


def with_vectors(value, vectors, first_lane):
    lane = lax.broadcasted_iota(jnp.int32, value.shape, 1)
    for place, vector in enumerate(vectors):
        value = jnp.where(lane == first_lane + place, vector, value)
    return value


def forward_kernel(
    steps, place_ref, obs_ref, act_ref, ids_ref, table_ref, e1_ref, eg_ref, es_ref, e2_ref,
    w1_ref, w2_ref, g_ref, s_ref, dyn_ref,
    xt_ref, soft_ref, h1_ref, hat1_ref, slope1_ref, h2_ref, hat2_ref, slope2_ref, scale_ref,
    ein_ref, eh_ref, ehat_ref, eslope_ref, escale_ref,
    rows_ref, spread_ref, erows_ref, espread_ref, wide_ref, tall_ref, e1p_ref, w1t_ref, w2t_ref, dynt_ref, pre_ref, epre_ref,
):
    latent = dyn_ref.shape[1]
    tasks, task_width = table_ref.shape
    observed = obs_ref.shape[1]
    acted = act_ref.shape[2]
    spread_columns(eg_ref[...], es_ref[...], erows_ref, espread_ref)
    kinds = lax.broadcasted_iota(jnp.int32, (tasks, LANES), 0)
    onehot = (kinds == ids_ref[...]).astype(F32).astype(BF16)
    wide_ref[...] = jnp.zeros_like(wide_ref)
    wide_ref[:, 0:task_width] = table_ref[...].astype(F32)
    table_tail = pltpu.roll(wide_ref[:, 0:LANES], acted, 1).astype(BF16)
    table_enc = pltpu.roll(wide_ref[...], observed, 1).astype(BF16)
    aux = tn(table_tail, onehot)
    tall_ref[...] = jnp.zeros_like(tall_ref)
    tall_ref[:, 0:observed] = obs_ref[...].astype(F32)
    ein = tn(table_enc, onehot)
    ein_ref[0:LANES, :] = (ein[0:LANES] + jnp.transpose(tall_ref[...])).astype(BF16)
    ein_ref[LANES:, :] = ein[LANES:].astype(BF16)
    e1p_ref[...] = jnp.zeros_like(e1p_ref)
    e1p_ref[0 : e1_ref.shape[0], :] = e1_ref[...]
    epre_ref[...] = tn(e1p_ref[...], ein_ref[...])
    here = slice(0, LANES)
    mish_forward(epre_ref, here, espread_ref.at[0], espread_ref.at[1], eh_ref, ehat_ref, eslope_ref, escale_ref, 0, here)
    shares = simplex(tn(e2_ref[...], eh_ref[...]))
    soft_ref[:, 0:LANES] = shares
    xt_ref[0:latent, 0:LANES] = shares.astype(BF16)

    spread_columns(g_ref[0], s_ref[0], rows_ref, spread_ref)
    tail = w1_ref.shape[1] - latent
    for start in range(0, latent, LANES):
        w1t_ref[:, start : start + LANES] = jnp.transpose(w1_ref[0, start : start + LANES, :])
        w2t_ref[:, start : start + LANES] = jnp.transpose(w2_ref[0, start : start + LANES, :])
        dynt_ref[:, start : start + LANES] = jnp.transpose(dyn_ref[start : start + LANES, :])
    padded_tail = jnp.concatenate(
        [w1_ref[0, latent:, :].astype(F32), jnp.zeros((LANES - tail, w1_ref.shape[2]), F32)], axis=0
    )
    w1t_ref[:, latent:] = jnp.transpose(padded_tail).astype(BF16)
    tall_ref[...] = jnp.zeros_like(tall_ref)
    for step in range(steps):
        tall_ref[:, 0:acted] = act_ref[step].astype(F32)
        xt_ref[latent:, lanes_of(step)] = (aux + jnp.transpose(tall_ref[...])).astype(BF16)

    for step in range(steps):
        at = lanes_of(step)
        pre_ref[...] = nn(w1t_ref[...], xt_ref[:, at])
        mish_forward(pre_ref, here, spread_ref.at[0], spread_ref.at[2], h1_ref, hat1_ref, slope1_ref, scale_ref, 0, at)
        pre_ref[...] = nn(w2t_ref[...], h1_ref[:, at])
        mish_forward(pre_ref, here, spread_ref.at[1], spread_ref.at[3], h2_ref, hat2_ref, slope2_ref, scale_ref, 1, at)
        shares = simplex(nn(dynt_ref[...], h2_ref[:, at]))
        soft_ref[:, lanes_of(step + 1)] = shares
        if step + 1 < steps:
            xt_ref[0:latent, lanes_of(step + 1)] = shares.astype(BF16)


def heads_kernel(
    steps, scale, slots, base, heads, bins,
    place_ref, xt_ref, w1_ref, w2_ref, ho_ref, g_ref, s_ref, rb_ref, vb_ref, hz_ref,
    keep_ref, send_ref, dx_ref, loss_ref,
    rows_ref, spread_ref, w1t_ref, w2t_ref, tail_ref, hop_ref, hot_ref, pre_ref, h1_ref, hat1_ref, slope1_ref,
    h2_ref, hat2_ref, slope2_ref, scale_ref, kept_ref, sums_ref, d_ref, dl_ref, grad_ref,
):
    latent = w2_ref.shape[1]
    count = pl.program_id(0)
    head = base + count
    spread_columns(g_ref[0], s_ref[0], rows_ref, spread_ref)
    tail_rows = w1_ref.shape[1] - latent
    tail_ref[...] = jnp.concatenate(
        [w1_ref[0, latent:, :].astype(F32), jnp.zeros((LANES - tail_rows, w1_ref.shape[2]), F32)], axis=0
    ).astype(BF16)
    for start in range(0, latent, LANES):
        w1t_ref[:, start : start + LANES] = jnp.transpose(w1_ref[0, start : start + LANES, :])
        w2t_ref[:, start : start + LANES] = jnp.transpose(w2_ref[0, start : start + LANES, :])
    w1t_ref[:, latent:] = jnp.transpose(tail_ref[...])
    hop_ref[...] = jnp.zeros_like(hop_ref)
    hop_ref[:, 0:bins] = ho_ref[0]
    hot_ref[...] = jnp.transpose(hop_ref[...])

    pre_ref[...] = nn(w1t_ref[...], xt_ref[...])
    for step in range(steps):
        at = lanes_of(step)
        mish_forward(pre_ref, at, spread_ref.at[0], spread_ref.at[2], h1_ref, hat1_ref, slope1_ref, scale_ref, 0, at)
    pre_ref[...] = nn(w2t_ref[...], h1_ref[...])
    for step in range(steps):
        at = lanes_of(step)
        mish_forward(pre_ref, at, spread_ref.at[1], spread_ref.at[3], h2_ref, hat2_ref, slope2_ref, scale_ref, 1, at)
    pre_ref[0:LANES, :] = nn(hot_ref[...], h2_ref[...])
    share = jnp.where(head == 0, F32(0.1), F32(0.1 / (heads - 1)))
    bin_ids = lax.broadcasted_iota(jnp.int32, (LANES, LANES), 0)
    loss = jnp.zeros((1, LANES), F32)
    for step in range(steps):
        at = lanes_of(step)
        logits = jnp.where(bin_ids < bins, pre_ref[0:LANES, at], F32(-1e30))
        wanted = jnp.where(head == 0, rb_ref[step : step + 1, :], vb_ref[step : step + 1, :])
        chosen = bin_ids == wanted
        top = jnp.max(logits, axis=0, keepdims=True)
        powers = jnp.exp(logits - top)
        total = column_sum(powers)
        picked = column_sum(jnp.where(chosen, logits, 0.0))
        weight = row_weight(step, steps, scale, hz_ref[...], place_ref) * share
        loss = loss + weight * (jnp.log(total) + top - picked)
        dl_ref[:, at] = (powers * (weight / total) - jnp.where(chosen, weight, 0.0)).astype(BF16)

    @pl.when(count == 0)
    def _():
        loss_ref[...] = loss
        dx_ref[...] = jnp.zeros_like(dx_ref)

    @pl.when(count > 0)
    def _():
        loss_ref[...] += loss

    grad_ref[:, latent + latent + LANES :] = nt(h2_ref[...], dl_ref[...])
    pre_ref[...] = nn(hop_ref[...], dl_ref[...])
    for step in range(steps):
        at = lanes_of(step)
        mish_backward(pre_ref, at, hat2_ref, slope2_ref, scale_ref, 1, at, kept_ref, sums_ref, 2, step == 0, d_ref)
    grad_ref[:, latent + LANES : latent + latent + LANES] = nt(d_ref[...], h1_ref[...])
    pre_ref[...] = nn(w2_ref[0], d_ref[...])
    for step in range(steps):
        at = lanes_of(step)
        mish_backward(pre_ref, at, hat1_ref, slope1_ref, scale_ref, 0, at, kept_ref, sums_ref, 0, step == 0, d_ref)
    grad_ref[:, 0 : latent + LANES] = nt(d_ref[...], xt_ref[...])
    dx_ref[0:latent, :] += nn(w1_ref[0, 0:latent, :], d_ref[...])
    dx_ref[latent:, :] += nn(tail_ref[...], d_ref[...])
    vectors = []
    for layer in range(2):
        inverse = 1.0 / spread_ref[layer]
        vectors.append(jnp.sum(sums_ref[2 * layer + 1] * inverse, axis=1, keepdims=True))
        vectors.append(jnp.sum(sums_ref[2 * layer] * inverse, axis=1, keepdims=True))
    grad_ref[:, latent : latent + LANES] = with_vectors(grad_ref[:, latent : latent + LANES], vectors, tail_rows)
    refs = (keep_ref, send_ref)
    put_blocks(place_ref, slots, grad_ref, grad_ref.shape[1], lambda which, slot: refs[which].at[slot, 0])


def backward_kernel(
    steps, scale, slots, chunks, tasks, task_width, acted, observed,
    place_ref, xt_ref, soft_ref, h1_ref, hat1_ref, slope1_ref, h2_ref, hat2_ref, slope2_ref, scale_ref,
    ein_ref, eh_ref, ehat_ref, eslope_ref, escale_ref,
    tgt_ref, hz_ref, ids_ref, e1_ref, eg_ref, e2_ref, w1_ref, w2_ref, g_ref, dyn_ref, *rest,
):
    dx_refs, loss_refs = rest[0:chunks], rest[chunks : 2 * chunks]
    (keep_ref, send_ref, rows_ref, spread_ref, erows_ref, espread_ref, tail_ref, e1p_ref, pre_ref, epre_ref, kept_ref,
     sums_ref, esums_ref, ekept_ref, d1_ref, d2_ref, do_ref, ed_ref, grad_ref, egrad_ref) = rest[2 * chunks :]
    latent = dyn_ref.shape[1]
    here = slice(0, LANES)
    spread_columns(g_ref[0], g_ref[0], rows_ref, spread_ref)
    spread_columns(eg_ref[...], eg_ref[...], erows_ref, espread_ref)
    tail_rows = w1_ref.shape[1] - latent
    tail_ref[...] = jnp.concatenate(
        [w1_ref[0, latent:, :].astype(F32), jnp.zeros((LANES - tail_rows, w1_ref.shape[2]), F32)], axis=0
    ).astype(BF16)
    loss = loss_refs[0][...]
    for loss_ref in loss_refs[1:]:
        loss = loss + loss_ref[...]
    side = jnp.zeros((LANES, LANES), F32)
    incoming = None
    for step in reversed(range(steps)):
        at = lanes_of(step)
        weight = row_weight(step, steps, scale, hz_ref[...], place_ref)
        shares = soft_ref[:, lanes_of(step + 1)]
        residue = shares - jnp.transpose(tgt_ref[step].astype(F32))
        loss = loss + (20.0 / latent) * weight * column_sum(residue * residue)
        grads = residue * ((40.0 / latent) * weight)
        if incoming is not None:
            grads = grads + incoming
        do_ref[:, at] = simplex_back(shares, grads).astype(BF16)
        pre_ref[...] = nn(dyn_ref[...], do_ref[:, at])
        mish_backward(pre_ref, here, hat2_ref, slope2_ref, scale_ref, 1, at, kept_ref, sums_ref, 2, step == steps - 1, d2_ref)
        pre_ref[...] = nn(w2_ref[0], d2_ref[:, at])
        mish_backward(pre_ref, here, hat1_ref, slope1_ref, scale_ref, 0, at, kept_ref, sums_ref, 0, step == steps - 1, d1_ref)
        incoming = nn(w1_ref[0, 0:latent, :], d1_ref[:, at])
        side = side + nn(tail_ref[...], d1_ref[:, at])
        for dx_ref in dx_refs:
            incoming = incoming + dx_ref[0:latent, at]
            side = side + dx_ref[latent:, at]
        incoming = incoming.astype(BF16).astype(F32)

    e1p_ref[...] = jnp.zeros_like(e1p_ref)
    e1p_ref[0 : e1_ref.shape[0], :] = e1_ref[...]
    d_enc = simplex_back(soft_ref[:, 0:LANES], incoming).astype(BF16)
    epre_ref[...] = nn(e2_ref[...], d_enc)
    mish_backward(epre_ref, here, ehat_ref, eslope_ref, escale_ref, 0, here, ekept_ref, esums_ref, 0, True, ed_ref)
    side_enc = nn(e1p_ref[...], ed_ref[...])
    grad_ref[:, 0 : latent + LANES] = nt(d1_ref[...], xt_ref[...])
    grad_ref[:, latent + LANES : 2 * latent + LANES] = nt(d2_ref[...], h1_ref[...])
    grad_ref[:, 2 * latent + LANES :] = nt(h2_ref[...], do_ref[...])
    vectors = []
    for layer in range(2):
        inverse = 1.0 / spread_ref[layer]
        vectors.append(jnp.sum(sums_ref[2 * layer + 1] * inverse, axis=1, keepdims=True))
        vectors.append(jnp.sum(sums_ref[2 * layer] * inverse, axis=1, keepdims=True))
    grad_ref[:, latent : latent + LANES] = with_vectors(grad_ref[:, latent : latent + LANES], vectors, tail_rows)
    refs = (keep_ref, send_ref)
    width = grad_ref.shape[1]
    put_blocks(place_ref, slots, grad_ref, width, lambda which, slot: refs[which].at[slot])

    enc_width = epre_ref.shape[0]
    half = GROUP // 2
    egrad_ref[:, 0:half, :] = nt(eh_ref[...], d_enc).reshape(enc_width // half, half, latent)
    enc_first = nt(ed_ref[...], ein_ref[...])
    inverse = 1.0 / espread_ref[0]
    vectors = [jnp.sum(esums_ref[1] * inverse, axis=1, keepdims=True), jnp.sum(esums_ref[0] * inverse, axis=1, keepdims=True)]
    egrad_ref[:, half:, 0:LANES] = enc_first[:, 0:LANES].reshape(enc_width // half, half, LANES)
    second_lanes = with_vectors(enc_first[:, LANES : 2 * LANES], vectors, LANES - 2)
    egrad_ref[:, half:, LANES : 2 * LANES] = second_lanes.reshape(enc_width // half, half, LANES)
    egrad_ref[:, half:, 2 * LANES :] = jnp.zeros((enc_width // half, half, latent - 2 * LANES), F32)

    kinds = lax.broadcasted_iota(jnp.int32, (tasks, LANES), 0)
    onehot = (kinds == ids_ref[...]).astype(F32)
    over_lanes = (((1,), (1,)), ((), ()))
    highest = lax.Precision.HIGHEST
    side_terms = lax.dot_general(onehot, side, over_lanes, precision=highest, preferred_element_type=F32)
    enc_terms = lax.dot_general(onehot, side_enc, over_lanes, precision=highest, preferred_element_type=F32)
    table = pltpu.roll(side_terms, LANES - acted, 1)
    table = table + pltpu.roll(enc_terms, enc_terms.shape[1] - observed, 1)[:, 0:LANES]
    lane = lax.broadcasted_iota(jnp.int32, table.shape, 1)
    table = jnp.where(lane < task_width, table, 0.0)
    table = jnp.where((lane == LANES - 1) & (kinds == 0), jnp.sum(loss, axis=1, keepdims=True), table)
    table_rows = [table[start : start + GROUP] for start in range(0, tasks, GROUP)]
    table_block = jnp.concatenate(table_rows, axis=1).astype(BF16)
    for relative, (which, slot) in enumerate(slots):
        block = egrad_ref[place_ref[0] ^ relative]
        refs[which][slot, :, width : width + latent] = block.astype(BF16)
        refs[which][slot, :, width + latent :] = table_block


def swap(value, axis, distance):
    count = lax.axis_size(axis)
    return lax.ppermute(value, axis, [(place, place ^ distance) for place in range(count)])


def exchange(parts, axis, scale):
    total = parts[0].astype(F32)
    for distance in range(1, len(parts)):
        total = total + swap(parts[distance], axis, distance * scale).astype(F32)
    return total


def scatter_relative(keep, send, chips, sections):
    held = exchange([keep, send], "batch", 1).astype(BF16)
    held = held.reshape((chips, sections) + held.shape[1:])
    held = exchange([held[place] for place in range(chips)], "batch", CORES).astype(BF16)
    return exchange([held[place] for place in range(sections)], "section", 1)


def scatter_plain(packed, chips, sections):
    held = packed.reshape((sections, chips, CORES) + packed.shape[1:])
    batch_no = lax.axis_index("batch")
    places = (
        ("batch", 1, CORES, 2, batch_no % CORES),
        ("batch", CORES, chips, 1, batch_no // CORES),
        ("section", 1, sections, 0, lax.axis_index("section")),
    )
    for axis, scale, count, dim, mine in places:
        parts = [lax.dynamic_index_in_dim(held, mine ^ other, dim, keepdims=False) for other in range(count)]
        held = exchange(parts, axis, scale)
        held = held.astype(BF16) if dim else held
    return held


def whole(shape):
    return pl.BlockSpec(shape, lambda *_: (0,) * len(shape))


def vmem(shape, dtype):
    return pltpu.VMEM(shape, dtype)


def on_device(
    observations,
    actions,
    targets,
    task_ids,
    horizons,
    reward_bins,
    value_bins,
    task_table,
    enc_first,
    enc_gain,
    enc_shift,
    enc_second,
    net_first,
    net_second,
    net_gain,
    net_shift,
    dyn_out,
    head_out,
):
    sections = lax.axis_size("section")
    batches = lax.axis_size("batch")
    section_no = lax.axis_index("section")
    chips = batches // CORES
    devices = sections * batches
    steps, rows_all, acted = actions.shape
    observed = observations.shape[1]
    rows = rows_all // sections
    latent = dyn_out.shape[1]
    hidden = dyn_out.shape[0]
    tasks, task_width = task_table.shape
    heads, _, bins = head_out.shape
    net_in = net_first.shape[1]
    enc_width = enc_first.shape[1]
    enc_in = enc_first.shape[0]
    wide = steps * LANES
    scale = 1.0 / (rows_all * batches * steps)
    groups = hidden // GROUP
    in_place = hidden // devices == GROUP
    start = section_no * rows
    block_no = start // LANES
    first_lane = start - block_no * LANES
    me = section_no * batches + lax.axis_index("batch") if in_place else jnp.int32(0)
    place = jnp.stack([me, block_no, first_lane, first_lane + rows]).astype(jnp.int32)
    if in_place:
        slots = tuple(
            (relative % CORES, (relative // CORES) % chips * sections + relative // batches) for relative in range(groups)
        )
    else:
        slots = tuple((relative // (groups // 2), relative % (groups // 2)) for relative in range(groups))
    half_slots = groups // 2

    own_rows = lambda width: pl.BlockSpec((LANES, width), lambda i, p: (p[1], 0))
    own_steps = lambda width: pl.BlockSpec((steps, LANES, width), lambda i, p: (0, p[1], 0))
    own_lanes = lambda height: pl.BlockSpec((height, LANES), lambda i, p: (0, p[1]))
    first_net = lambda array: pl.BlockSpec((1,) + array.shape[1:], lambda i, p: (0, 0, 0))
    shape_of = jax.ShapeDtypeStruct
    ids_row = task_ids.reshape(1, rows_all)
    horizon_row = horizons.reshape(1, rows_all)
    eg_row = enc_gain.reshape(1, enc_width)
    es_row = enc_shift.reshape(1, enc_width)

    def params():
        return pltpu.CompilerParams(vmem_limit_bytes=VMEM_BYTES)

    forward_shapes = (
        shape_of((latent + LANES, wide), BF16),
        shape_of((latent, wide + LANES), F32),
        shape_of((hidden, wide), BF16),
        shape_of((hidden, wide), BF16),
        shape_of((hidden, wide), BF16),
        shape_of((hidden, wide), BF16),
        shape_of((hidden, wide), BF16),
        shape_of((hidden, wide), BF16),
        shape_of((8, wide), F32),
        shape_of((2 * LANES, LANES), BF16),
        shape_of((enc_width, LANES), BF16),
        shape_of((enc_width, LANES), BF16),
        shape_of((enc_width, LANES), BF16),
        shape_of((8, LANES), F32),
    )
    saved = pl.pallas_call(
        functools.partial(forward_kernel, steps),
        out_shape=forward_shapes,
        grid_spec=pltpu.PrefetchScalarGridSpec(
            num_scalar_prefetch=1,
            grid=(1,),
            in_specs=[
                own_rows(observed),
                own_steps(acted),
                own_lanes(1),
                whole(task_table.shape),
                whole(enc_first.shape),
                whole(eg_row.shape),
                whole(es_row.shape),
                whole(enc_second.shape),
                first_net(net_first),
                first_net(net_second),
                first_net(net_gain),
                first_net(net_shift),
                whole(dyn_out.shape),
            ],
            out_specs=[whole(each.shape) for each in forward_shapes],
            scratch_shapes=[
                vmem((8, hidden), F32),
                vmem((4, hidden, LANES), F32),
                vmem((8, enc_width), F32),
                vmem((2, enc_width, LANES), F32),
                vmem((tasks, 2 * LANES), F32),
                vmem((LANES, LANES), F32),
                vmem((2 * LANES, enc_width), BF16),
                vmem((hidden, latent + LANES), BF16),
                vmem((hidden, hidden), BF16),
                vmem((latent, hidden), BF16),
                vmem((hidden, LANES), F32),
                vmem((enc_width, LANES), F32),
            ],
        ),
        compiler_params=params(),
        cost_estimate=pl.CostEstimate(flops=10_000_000_000, bytes_accessed=8_000_000, transcendentals=0),
        name="forward_chain",
    )(
        place, observations, actions, ids_row, task_table, enc_first, eg_row, es_row, enc_second,
        net_first, net_second, net_gain, net_shift, dyn_out,
    )
    xt, soft, h1, hat1, slope1, h2, hat2, slope2, scales, ein, eh, ehat, eslope, escale = saved

    head_width = latent + LANES + hidden + LANES

    def run_heads(base, count):
        net_block = lambda array: pl.BlockSpec((1,) + array.shape[1:], lambda i, p: (base + 1 + i, 0, 0))
        head_block = pl.BlockSpec((1,) + head_out.shape[1:], lambda i, p: (base + i, 0, 0))
        pack_shape = (half_slots, count, GROUP, head_width)
        pack_block = pl.BlockSpec((half_slots, 1, GROUP, head_width), lambda i, p: (0, i, 0, 0))
        return pl.pallas_call(
            functools.partial(heads_kernel, steps, scale, slots, base, heads, bins),
            out_shape=(
                shape_of(pack_shape, BF16),
                shape_of(pack_shape, BF16),
                shape_of((latent + LANES, wide), F32),
                shape_of((1, LANES), F32),
            ),
            grid_spec=pltpu.PrefetchScalarGridSpec(
                num_scalar_prefetch=1,
                grid=(count,),
                in_specs=[
                    whole(xt.shape),
                    net_block(net_first),
                    net_block(net_second),
                    head_block,
                    net_block(net_gain),
                    net_block(net_shift),
                    own_lanes(steps),
                    own_lanes(steps),
                    own_lanes(1),
                ],
                out_specs=[pack_block, pack_block, whole((latent + LANES, wide)), whole((1, LANES))],
                scratch_shapes=[
                    vmem((8, hidden), F32),
                    vmem((4, hidden, LANES), F32),
                    vmem((hidden, latent + LANES), BF16),
                    vmem((hidden, hidden), BF16),
                    vmem((LANES, hidden), BF16),
                    vmem((hidden, LANES), BF16),
                    vmem((LANES, hidden), BF16),
                    vmem((hidden, wide), F32),
                    vmem((hidden, wide), BF16),
                    vmem((hidden, wide), BF16),
                    vmem((hidden, wide), BF16),
                    vmem((hidden, wide), BF16),
                    vmem((hidden, wide), BF16),
                    vmem((hidden, wide), BF16),
                    vmem((8, wide), F32),
                    vmem((hidden, LANES), F32),
                    vmem((4, hidden, LANES), F32),
                    vmem((hidden, wide), BF16),
                    vmem((LANES, wide), BF16),
                    vmem((hidden, head_width), F32),
                ],
            ),
            compiler_params=params(),
            cost_estimate=pl.CostEstimate(
                flops=count * 10_000_000_000, bytes_accessed=count * 4_000_000, transcendentals=0
            ),
            name=f"heads_{base}",
        )(place, xt, net_first, net_second, head_out, net_gain, net_shift, reward_bins, value_bins, horizon_row)

    def scattered(keep, send):
        if in_place:
            return scatter_relative(keep, send, chips, sections)
        mine = hidden // devices
        packed = jnp.concatenate([keep, send], axis=0)
        middle = packed.shape[1:-2]
        packed = packed.reshape((groups,) + middle + (GROUP // mine, mine, packed.shape[-1]))
        packed = jnp.moveaxis(packed, -3, 1).reshape((devices,) + middle + (mine, packed.shape[-1]))
        return scatter_plain(packed, chips, sections)

    packs, dx_parts, loss_parts = [], [], []
    base = 0
    for count in CHUNKS:
        keep, send, dx, loss = run_heads(base, count)
        packs.append((keep, send))
        dx_parts.append(dx)
        loss_parts.append(loss)
        base += count

    net_width = latent + LANES + hidden + latent
    tail_width = net_width + latent + tasks // GROUP * LANES
    tail_shape = (half_slots, GROUP, tail_width)
    keep, send = pl.pallas_call(
        functools.partial(
            backward_kernel, steps, scale, slots, len(CHUNKS), tasks, task_width, acted, observed
        ),
        out_shape=(shape_of(tail_shape, BF16), shape_of(tail_shape, BF16)),
        grid_spec=pltpu.PrefetchScalarGridSpec(
            num_scalar_prefetch=1,
            grid=(1,),
            in_specs=[whole(each.shape) for each in saved]
            + [
                own_steps(latent),
                own_lanes(1),
                own_lanes(1),
                whole(enc_first.shape),
                whole(eg_row.shape),
                whole(enc_second.shape),
                first_net(net_first),
                first_net(net_second),
                first_net(net_gain),
                whole(dyn_out.shape),
            ]
            + [whole(each.shape) for each in dx_parts + loss_parts],
            out_specs=[whole(tail_shape), whole(tail_shape)],
            scratch_shapes=[
                vmem((8, hidden), F32),
                vmem((4, hidden, LANES), F32),
                vmem((8, enc_width), F32),
                vmem((2, enc_width, LANES), F32),
                vmem((LANES, hidden), BF16),
                vmem((2 * LANES, enc_width), BF16),
                vmem((hidden, LANES), F32),
                vmem((enc_width, LANES), F32),
                vmem((hidden, LANES), F32),
                vmem((4, hidden, LANES), F32),
                vmem((2, enc_width, LANES), F32),
                vmem((enc_width, LANES), F32),
                vmem((hidden, wide), BF16),
                vmem((hidden, wide), BF16),
                vmem((latent, wide), BF16),
                vmem((enc_width, LANES), BF16),
                vmem((hidden, net_width), F32),
                vmem((groups, GROUP, latent), F32),
            ],
        ),
        compiler_params=params(),
        cost_estimate=pl.CostEstimate(flops=15_000_000_000, bytes_accessed=12_000_000, transcendentals=0),
        name="backward_chain",
    )(
        place, *saved, targets, horizon_row, ids_row, enc_first, eg_row, enc_second,
        net_first, net_second, net_gain, dyn_out, *dx_parts, *loss_parts,
    )

    head_sums = [scattered(*pack) for pack in packs]
    enc_each = enc_width // devices
    if in_place:
        tail = scattered(keep, send)
        net_sum = tail[:, 0:net_width]
        enc_sum = tail[:, net_width : net_width + latent]
        table_sum = tail[:, net_width + latent :]
    else:
        net_sum = scattered(keep[:, :, 0:net_width], send[:, :, 0:net_width])
        rest = jnp.concatenate([keep, send], axis=0)
        enc_all = rest[:, :, net_width : net_width + latent].reshape(groups, 2, enc_width // groups, latent)
        enc_all = enc_all.transpose(0, 2, 1, 3).reshape(devices, enc_each, 2, latent)
        enc_sum = scatter_plain(enc_all, chips, sections)
        enc_sum = enc_sum.transpose(1, 0, 2).reshape(2 * enc_each, latent)
        table_sum = lax.psum(rest[0, :, net_width + latent :].astype(F32), ("section", "batch"))

    head_sum = jnp.concatenate(head_sums, axis=0)
    first_end = latent + LANES
    net_row = jnp.concatenate([net_sum[:, 0 : first_end + hidden], jnp.zeros_like(net_sum[:, 0:LANES])], axis=1)
    sums = jnp.concatenate([net_row[None], head_sum], axis=0)
    s_first = sums[:, :, 0:net_in].transpose(0, 2, 1)
    s_second = sums[:, :, first_end : first_end + hidden].transpose(0, 2, 1)
    vectors = sums[:, :, net_in : net_in + 4].transpose(0, 2, 1)
    s_gain = vectors[:, 0::2]
    s_shift = vectors[:, 1::2]
    s_head = head_sum[:, :, first_end + hidden : first_end + hidden + bins]
    s_dyn = net_sum[:, first_end + hidden :]
    table = table_sum.reshape(GROUP, tasks // GROUP, LANES).transpose(1, 0, 2).reshape(tasks, LANES)
    enc_rows = enc_sum[enc_each:]
    return (
        table[0, LANES - 1],
        table[:, 0:task_width],
        0.3 * enc_rows[:, 0:enc_in].T,
        0.3 * enc_rows[:, 2 * LANES - 2],
        0.3 * enc_rows[:, 2 * LANES - 1],
        0.3 * enc_sum[0:enc_each],
        s_first,
        s_second,
        s_gain,
        s_shift,
        s_dyn,
        s_head,
    )


def solution(mesh):
    both = ("section", "batch")
    return jax.shard_map(
        on_device,
        mesh=mesh,
        in_specs=(
            P("batch", None),
            P(None, "batch", None),
            P(None, "batch", None),
            P("batch"),
            P("batch"),
            P(None, "batch"),
            P(None, "batch"),
        )
        + (P(),) * 11,
        out_specs=(
            P(),
            P(),
            P(None, both),
            P(both),
            P(both),
            P(both, None),
            P(None, None, both),
            P(None, None, both),
            P(None, None, both),
            P(None, None, both),
            P(both, None),
            P(None, both, None),
        ),
        check_vma=False,
    )
```

```python
import functools

import jax
import jax.numpy as jnp
from jax import lax
from jax.experimental import pallas as pl
from jax.experimental.pallas import tpu as pltpu
from jax.sharding import PartitionSpec as P

CORES = 2
LANES = 128
GROUP = 16
BF16 = jnp.bfloat16
F32 = jnp.float32
CHUNKS = (2, 2, 2)
WIDTHS = (2, 2, 1)
VMEM_A = 16
VMEM_B = 28
VMEM_C = 20


def nn(left, right):
    return lax.dot_general(left, right, (((1,), (0,)), ((), ())), preferred_element_type=F32)


def nt(left, right):
    return lax.dot_general(left, right, (((1,), (1,)), ((), ())), preferred_element_type=F32)


def tn(left, right):
    return lax.dot_general(left, right, (((0,), (0,)), ((), ())), preferred_element_type=F32)


def column_sum(value):
    grouped = value.reshape(value.shape[0] // 8, 8, value.shape[1])
    return jnp.sum(jnp.sum(grouped, axis=0), axis=0, keepdims=True)


def slabs(features, size=64):
    return [slice(start, start + size) for start in range(0, features, size)]


def lanes_of(step):
    return slice(step * LANES, (step + 1) * LANES)


def spread_columns(gain_rows, shift_rows, rows_ref, spread_ref):
    count = gain_rows.shape[0]
    rows_ref[...] = jnp.zeros_like(rows_ref)
    rows_ref[0:count, :] = gain_rows
    rows_ref[count : 2 * count, :] = shift_rows
    turned = jnp.transpose(rows_ref[...])
    for place in range(2 * count):
        spread_ref[place] = jnp.broadcast_to(turned[:, place : place + 1], spread_ref.shape[1:])


def mish_forward(pre_ref, pre_at, gain_ref, shift_ref, hid_ref, hat_ref, slope_ref, scale_ref, scale_row, at):
    features = pre_ref.shape[0]
    row_mean = column_sum(pre_ref[:, pre_at]) * (1.0 / features)
    centred = pre_ref[:, pre_at] - row_mean
    spread = column_sum(centred * centred) * (1.0 / features)
    scale = lax.rsqrt(spread + 1e-05)
    scale_ref[scale_row : scale_row + 1, at] = scale
    for part in slabs(features):
        hat = (pre_ref[part, pre_at] - row_mean) * scale
        normed = hat * gain_ref[part, :] + shift_ref[part, :]
        power = jnp.exp(normed)
        top = power * (power + 2.0)
        inverse = pl.reciprocal(top + 2.0, approx=True)
        ratio = top * inverse
        hid_ref[part, at] = (normed * ratio).astype(BF16)
        tilt = power * inverse
        slope = ratio + normed * (4.0 * (tilt * (tilt + inverse)))
        slope_ref[part, at] = (slope * gain_ref[part, :]).astype(BF16)
        hat_ref[part, at] = hat.astype(BF16)


def mish_backward(grad_ref, grad_at, hat_ref, slope_ref, scale_ref, scale_row, at, sums_ref, sums_at, first, out_ref):
    features = grad_ref.shape[0]
    total_one = jnp.zeros((8, LANES), F32)
    total_two = jnp.zeros((8, LANES), F32)
    for part in slabs(features):
        term = grad_ref[part, grad_at] * slope_ref[part, at].astype(F32)
        grad_ref[part, grad_at] = term
        crossed = term * hat_ref[part, at].astype(F32)
        groups = (term.shape[0] // 8, 8, LANES)
        total_one = total_one + jnp.sum(term.reshape(groups), axis=0)
        total_two = total_two + jnp.sum(crossed.reshape(groups), axis=0)
        if first:
            sums_ref[sums_at, part, :] = term
            sums_ref[sums_at + 1, part, :] = crossed
        else:
            sums_ref[sums_at, part, :] += term
            sums_ref[sums_at + 1, part, :] += crossed
    mean_one = jnp.sum(total_one, axis=0, keepdims=True) * (1.0 / features)
    mean_two = jnp.sum(total_two, axis=0, keepdims=True) * (1.0 / features)
    scale = scale_ref[scale_row : scale_row + 1, at]
    for part in slabs(features):
        rest = grad_ref[part, grad_at] - mean_one - hat_ref[part, at].astype(F32) * mean_two
        out_ref[part, at] = (rest * scale).astype(BF16)


def simplex(values):
    grouped = values.reshape(values.shape[0] // 8, 8, values.shape[1])
    powers = jnp.exp(grouped - jnp.max(grouped, axis=1, keepdims=True))
    shares = powers / jnp.sum(powers, axis=1, keepdims=True)
    return shares.reshape(values.shape)


def simplex_back(shares, grads):
    grouped = (shares.shape[0] // 8, 8, shares.shape[1])
    crossed = jnp.sum((shares * grads).reshape(grouped), axis=1, keepdims=True)
    return (shares.reshape(grouped) * (grads.reshape(grouped) - crossed)).reshape(shares.shape)


def row_weight(step, steps, scale, horizon_row, place_ref):
    lane = lax.broadcasted_iota(jnp.int32, (1, LANES), 1)
    mine = (lane >= place_ref[2]) & (lane < place_ref[3]) & (horizon_row > step)
    return jnp.where(mine, F32(scale * 0.5 ** (step / (steps - 1))), 0.0)


def padded_rows(value, rows):
    zeros = jnp.zeros((rows - value.shape[0], value.shape[1]), F32)
    return jnp.concatenate([value.astype(F32), zeros], axis=0).astype(BF16)


def transpose_into(out_ref, source_ref, rows):
    for start in range(0, rows, LANES):
        out_ref[:, start : start + LANES] = jnp.transpose(source_ref[start : start + LANES, :])


def vector_sums(sums_ref, gains_ref, layers):
    vectors = []
    for layer in range(layers):
        inverse = 1.0 / gains_ref[layer]
        vectors.append(jnp.sum(sums_ref[2 * layer + 1] * inverse, axis=1, keepdims=True))
        vectors.append(jnp.sum(sums_ref[2 * layer] * inverse, axis=1, keepdims=True))
    return vectors


def own_lanes(place_ref):
    return pl.ds(pl.multiple_of(place_ref[1] * LANES, LANES), LANES)


def load_all(copies):
    made = [pltpu.make_async_copy(*each) for each in copies]
    for each in made:
        each.start()
    return made


def with_vectors(value, vectors, first_lane):
    lane = lax.broadcasted_iota(jnp.int32, value.shape, 1)
    for place, vector in enumerate(vectors):
        value = jnp.where(lane == first_lane + place, vector, value)
    return value


def forward_kernel(
    steps, ahead,
    place_ref, obs_ref, act_ref, ids_ref, table_ref, e1_ref, eg_ref, es_ref, e2_ref, g_ref, s_ref,
    w1_hbm, w2_hbm, dyn_hbm,
    xt_ref, soft_ref, h1_ref, hat1_ref, slope1_ref, h2_ref, hat2_ref, slope2_ref, scale_ref,
    ein_ref, eh_ref, ehat_ref, eslope_ref, escale_ref,
    w1_ref, w2_ref, dyn_ref, next1_ref, next2_ref,
    rows_ref, spread_ref, erows_ref, espread_ref, wide_ref, tall_ref, e1p_ref, w1t_ref, w2t_ref, dynt_ref, pre_ref, epre_ref,
    sems,
):
    first, second, third, fourth, fifth = load_all([
        (w1_hbm.at[0], w1_ref, sems.at[0]),
        (w2_hbm.at[0], w2_ref, sems.at[1]),
        (dyn_hbm, dyn_ref, sems.at[2]),
        (w1_hbm.at[pl.ds(1, ahead)], next1_ref, sems.at[3]),
        (w2_hbm.at[pl.ds(1, ahead)], next2_ref, sems.at[4]),
    ])
    latent = dyn_ref.shape[1]
    tasks, task_width = table_ref.shape
    observed = obs_ref.shape[0]
    acted = act_ref.shape[1]
    mine = own_lanes(place_ref)
    spread_columns(eg_ref[...], es_ref[...], erows_ref, espread_ref)
    kinds = lax.broadcasted_iota(jnp.int32, (tasks, LANES), 0)
    onehot = (kinds == ids_ref[:, mine]).astype(F32).astype(BF16)
    wide_ref[...] = jnp.zeros_like(wide_ref)
    wide_ref[:, 0:task_width] = table_ref[...].astype(F32)
    table_tail = pltpu.roll(wide_ref[:, 0:LANES], acted, 1).astype(BF16)
    table_enc = pltpu.roll(wide_ref[...], observed, 1).astype(BF16)
    aux = tn(table_tail, onehot)
    tall_ref[...] = jnp.zeros_like(tall_ref)
    tall_ref[0:observed, :] = obs_ref[:, mine].astype(F32)
    ein = tn(table_enc, onehot)
    ein_ref[0:LANES, :] = (ein[0:LANES] + tall_ref[...]).astype(BF16)
    ein_ref[LANES:, :] = ein[LANES:].astype(BF16)
    e1p_ref[...] = padded_rows(e1_ref[...], e1p_ref.shape[0])
    epre_ref[...] = tn(e1p_ref[...], ein_ref[...])
    here = slice(0, LANES)
    mish_forward(epre_ref, here, espread_ref.at[0], espread_ref.at[1], eh_ref, ehat_ref, eslope_ref, escale_ref, 0, here)
    shares = simplex(tn(e2_ref[...], eh_ref[...]))
    soft_ref[:, 0:LANES] = shares
    xt_ref[0:latent, 0:LANES] = shares.astype(BF16)
    spread_columns(g_ref[0], s_ref[0], rows_ref, spread_ref)
    for step in range(steps):
        tall_ref[...] = jnp.zeros_like(tall_ref)
        tall_ref[0:acted, :] = act_ref[step, :, mine].astype(F32)
        xt_ref[latent:, lanes_of(step)] = (aux + tall_ref[...]).astype(BF16)
    first.wait()
    transpose_into(w1t_ref, w1_ref, latent)
    w1t_ref[:, latent:] = jnp.transpose(padded_rows(w1_ref[latent:, :], LANES))
    second.wait()
    transpose_into(w2t_ref, w2_ref, latent)
    third.wait()
    transpose_into(dynt_ref, dyn_ref, latent)
    for step in range(steps):
        at = lanes_of(step)
        pre_ref[...] = nn(w1t_ref[...], xt_ref[:, at])
        mish_forward(pre_ref, here, spread_ref.at[0], spread_ref.at[2], h1_ref, hat1_ref, slope1_ref, scale_ref, 0, at)
        pre_ref[...] = nn(w2t_ref[...], h1_ref[:, at])
        mish_forward(pre_ref, here, spread_ref.at[1], spread_ref.at[3], h2_ref, hat2_ref, slope2_ref, scale_ref, 1, at)
        shares = simplex(nn(dynt_ref[...], h2_ref[:, at]))
        soft_ref[:, lanes_of(step + 1)] = shares
        if step + 1 < steps:
            xt_ref[0:latent, lanes_of(step + 1)] = shares.astype(BF16)
    fourth.wait()
    fifth.wait()


def heads_kernel(steps, scale, slots, base, count, ahead, heads, bins, chained, after, *refs):
    refs = list(refs)
    place_ref, xt_ref, w1_ref, w2_ref, ho_ref, g_ref, s_ref, rb_ref, vb_ref, hz_ref = refs[:10]
    refs = refs[10:]
    before_ref = refs.pop(0) if chained else None
    refs = refs[after:]
    w1_hbm, w2_hbm = refs[:2] if ahead else (None, None)
    refs = refs[2:] if ahead else refs
    keep_ref, send_ref, dx_ref, loss_ref = refs[:4]
    refs = refs[4:]
    copies = []
    if ahead:
        next1_ref, next2_ref, sems = refs[0], refs[1], refs[-1]
        refs = refs[2:-1]
        start = base + 1 + count
        copies = load_all([
            (w1_hbm.at[pl.ds(start, ahead)], next1_ref, sems.at[0]),
            (w2_hbm.at[pl.ds(start, ahead)], next2_ref, sems.at[1]),
        ])
    (rows_ref, spread_ref, w1t_ref, w2t_ref, tail_ref, hop_ref, hot_ref, pre_ref, lg_ref, h1_ref, hat1_ref, slope1_ref,
     h2_ref, hat2_ref, slope2_ref, scale_ref, sums_ref, d2_ref, d1_ref, dl_ref, grad_ref) = refs
    latent = w2_ref.shape[1]
    wide = steps * LANES
    tail_rows = w1_ref.shape[1] - latent
    mine = own_lanes(place_ref)
    horizon_row = hz_ref[:, mine]
    bin_ids = lax.broadcasted_iota(jnp.int32, (LANES, LANES), 0)
    first_end = latent + LANES
    losses = []

    def prepare(one):
        spread_columns(g_ref[base + 1 + one], s_ref[base + 1 + one], rows_ref.at[one], spread_ref.at[one])
        tail_ref[one] = padded_rows(w1_ref[one, latent:, :], LANES)
        transpose_into(w1t_ref.at[one], w1_ref.at[one], latent)
        w1t_ref[one, :, latent:] = jnp.transpose(tail_ref[one])
        transpose_into(w2t_ref.at[one], w2_ref.at[one], latent)
        hot_ref[one] = padded_rows(ho_ref[base + one], LANES)
        hop_ref[one] = jnp.transpose(hot_ref[one])

    def stages(one, first_step, width):
        at_all = slice(first_step * LANES, (first_step + width) * LANES)
        each_step = range(first_step, first_step + width)
        pre, spread, scales, sums = pre_ref.at[one], spread_ref.at[one], scale_ref.at[one], sums_ref.at[one]
        hat1, slope1, hat2, slope2 = hat1_ref.at[one], slope1_ref.at[one], hat2_ref.at[one], slope2_ref.at[one]
        if first_step == 0:
            prepare(one)
        pre[:, at_all] = nn(w1t_ref[one], xt_ref[:, at_all])
        yield
        for step in each_step:
            at = lanes_of(step)
            mish_forward(pre, at, spread.at[0], spread.at[2], h1_ref.at[one], hat1, slope1, scales, 0, at)
        yield
        pre[:, at_all] = nn(w2t_ref[one], h1_ref[one, :, at_all])
        yield
        for step in each_step:
            at = lanes_of(step)
            mish_forward(pre, at, spread.at[1], spread.at[3], h2_ref.at[one], hat2, slope2, scales, 1, at)
        yield
        lg_ref[one, :, at_all] = nn(hot_ref[one], h2_ref[one, :, at_all])
        yield
        share = 0.1 if base + one == 0 else 0.1 / (heads - 1)
        bins_ref = rb_ref if base + one == 0 else vb_ref
        for step in each_step:
            at = lanes_of(step)
            logits = jnp.where(bin_ids < bins, lg_ref[one, :, at], F32(-1e30))
            chosen = bin_ids == bins_ref[step : step + 1, mine]
            top = jnp.max(logits, axis=0, keepdims=True)
            powers = jnp.exp(logits - top)
            total = column_sum(powers)
            picked = column_sum(jnp.where(chosen, logits, 0.0))
            weight = row_weight(step, steps, scale * share, horizon_row, place_ref)
            losses.append(weight * (jnp.log(total) + top - picked))
            dl_ref[one, :, at] = (powers * (weight / total) - jnp.where(chosen, weight, 0.0)).astype(BF16)
        pre[:, at_all] = nn(hop_ref[one], dl_ref[one, :, at_all])
        yield
        if first_step + width == steps:
            grad_ref[one, :, first_end + latent :] = nt(h2_ref[one], dl_ref[one]).astype(BF16)
        for step in each_step:
            at = lanes_of(step)
            mish_backward(pre, at, hat2, slope2, scales, 1, at, sums, 2, step == 0, d2_ref.at[one])
        yield
        pre[:, at_all] = nn(w2_ref[one], d2_ref[one, :, at_all])
        yield
        if first_step + width == steps:
            grad_ref[one, :, first_end : first_end + latent] = nt(d2_ref[one], h1_ref[one]).astype(BF16)
        for step in each_step:
            at = lanes_of(step)
            mish_backward(pre, at, hat1, slope1, scales, 0, at, sums, 0, step == 0, d1_ref.at[one])
        yield
        low_part = nn(w1_ref[one, 0:latent, :], d1_ref[one, :, at_all])
        side_part = nn(tail_ref[one], d1_ref[one, :, at_all])
        if one == 0 and not chained:
            dx_ref[0:latent, at_all] = low_part
            dx_ref[latent:, at_all] = side_part
        else:
            held_ref = before_ref if one == 0 else dx_ref
            dx_ref[0:latent, at_all] = held_ref[0:latent, at_all] + low_part
            dx_ref[latent:, at_all] = held_ref[latent:, at_all] + side_part
        yield
        if first_step + width == steps:
            grad_ref[one, :, 0:latent] = nt(d1_ref[one], xt_ref[0:latent, :]).astype(BF16)
            side_terms = nt(d1_ref[one], xt_ref[latent:, :])
            side_terms = with_vectors(side_terms, vector_sums(sums, spread, 2), tail_rows)
            grad_ref[one, :, latent:first_end] = side_terms.astype(BF16)
            for relative, (which, slot) in enumerate(slots):
                start = pl.multiple_of((place_ref[0] ^ relative) * GROUP, GROUP)
                out_ref = (keep_ref, send_ref)[which]
                out_ref[slot, one] = grad_ref[one, pl.ds(start, GROUP), :]

    waiting = []
    for one in range(count):
        first_step = 0
        for width in WIDTHS:
            waiting.append(stages(one, first_step, width))
            first_step += width
    running = []
    while waiting or running:
        if waiting:
            running.append(waiting.pop(0))
        for each in list(running):
            if next(each, running) is running:
                running.remove(each)
    loss_ref[...] = functools.reduce(jnp.add, losses)
    for each in copies:
        each.wait()


def backward_kernel(
    steps, scale, slots, tasks, task_width, acted, observed, chips, sections, after,
    place_ref, xt_ref, soft_ref, h1_ref, hat1_ref, slope1_ref, h2_ref, hat2_ref, slope2_ref, scale_ref,
    ein_ref, eh_ref, ehat_ref, eslope_ref, escale_ref, w1_ref, w2_ref, dyn_ref,
    hz_ref, ids_ref, e1_ref, eg_ref, e2_ref, g_ref, dx_ref, *rest,
):
    (tgt_hbm, keep_ref, send_ref, tgt_ref, rows_ref, spread_ref, erows_ref, espread_ref, tail_ref, e1p_ref, pre_ref, epre_ref,
     sums_ref, esums_ref, d1_ref, d2_ref, do_ref, ed_ref, grad_ref, egrad_ref, sems) = rest[len(CHUNKS) + after :]
    mine = own_lanes(place_ref)
    order = list(reversed(range(steps)))
    loads = dict(zip(order, load_all([(tgt_hbm.at[step, mine, :], tgt_ref.at[step], sems.at[step]) for step in order])))
    latent = dyn_ref.shape[1]
    here = slice(0, LANES)
    horizon_row = hz_ref[:, mine]
    spread_columns(g_ref[0], g_ref[0], rows_ref, spread_ref)
    spread_columns(eg_ref[...], eg_ref[...], erows_ref, espread_ref)
    tail_rows = w1_ref.shape[0] - latent
    tail_ref[...] = padded_rows(w1_ref[latent:, :], LANES)
    loss = functools.reduce(jnp.add, [each[...] for each in rest[: len(CHUNKS)]])
    side = jnp.zeros((LANES, LANES), F32)
    first_end = latent + LANES
    second_end = first_end + latent
    incoming = None
    pending = []

    def add_terms(at, initial):
        terms = (
            (slice(0, first_end), nt(d1_ref[:, at], xt_ref[:, at])),
            (slice(first_end, second_end), nt(d2_ref[:, at], h1_ref[:, at])),
            (slice(second_end, second_end + latent), nt(h2_ref[:, at], do_ref[:, at])),
        )
        for lanes, term in terms:
            if initial:
                grad_ref[:, lanes] = term
            else:
                grad_ref[:, lanes] += term

    for step in order:
        at = lanes_of(step)
        weight = row_weight(step, steps, scale, horizon_row, place_ref)
        shares = soft_ref[:, lanes_of(step + 1)]
        loads[step].wait()
        residue = shares - jnp.transpose(tgt_ref[step].astype(F32))
        loss = loss + (20.0 / latent) * weight * column_sum(residue * residue)
        grads = residue * ((40.0 / latent) * weight)
        if incoming is not None:
            grads = grads + incoming
        do_ref[:, at] = simplex_back(shares, grads).astype(BF16)
        pre_ref[...] = nn(dyn_ref[...], do_ref[:, at])
        mish_backward(pre_ref, here, hat2_ref, slope2_ref, scale_ref, 1, at, sums_ref, 2, step == order[0], d2_ref)
        pre_ref[...] = nn(w2_ref[...], d2_ref[:, at])
        mish_backward(pre_ref, here, hat1_ref, slope1_ref, scale_ref, 0, at, sums_ref, 0, step == order[0], d1_ref)
        incoming = nn(w1_ref[0:latent, :], d1_ref[:, at]) + dx_ref[0:latent, at]
        side = side + nn(tail_ref[...], d1_ref[:, at]) + dx_ref[latent:, at]
        incoming = incoming.astype(BF16).astype(F32)
        pending.append(step)
        if len(pending) == 2 or step == 0:
            low, high = min(pending), max(pending) + 1
            add_terms(slice(low * LANES, high * LANES), high == steps)
            pending = []

    e1p_ref[...] = padded_rows(e1_ref[...], e1p_ref.shape[0])
    d_enc = simplex_back(soft_ref[:, 0:LANES], incoming).astype(BF16)
    epre_ref[...] = nn(e2_ref[...], d_enc)
    mish_backward(epre_ref, here, ehat_ref, eslope_ref, escale_ref, 0, here, esums_ref, 0, True, ed_ref)
    side_enc = nn(e1p_ref[...], ed_ref[...])
    vectors = vector_sums(sums_ref, spread_ref, 2)
    grad_ref[:, latent:first_end] = with_vectors(grad_ref[:, latent:first_end], vectors, tail_rows)

    enc_width = epre_ref.shape[0]
    half = GROUP // 2
    groups = enc_width // half
    egrad_ref[:, 0:half, :] = nt(eh_ref[...], d_enc).reshape(groups, half, latent)
    enc_first = nt(ed_ref[...], ein_ref[...])
    egrad_ref[:, half:, 0:LANES] = enc_first[:, 0:LANES].reshape(groups, half, LANES)
    second_lanes = with_vectors(enc_first[:, LANES : 2 * LANES], vector_sums(esums_ref, espread_ref, 1), LANES - 2)
    egrad_ref[:, half:, LANES : 2 * LANES] = second_lanes.reshape(groups, half, LANES)
    egrad_ref[:, half:, 2 * LANES :] = jnp.zeros((groups, half, latent - 2 * LANES), F32)

    kinds = lax.broadcasted_iota(jnp.int32, (tasks, LANES), 0)
    onehot = (kinds == ids_ref[:, mine]).astype(F32)
    over_lanes = (((1,), (1,)), ((), ()))
    highest = lax.Precision.HIGHEST
    side_terms = lax.dot_general(onehot, side, over_lanes, precision=highest, preferred_element_type=F32)
    enc_terms = lax.dot_general(onehot, side_enc, over_lanes, precision=highest, preferred_element_type=F32)
    table = pltpu.roll(side_terms, LANES - acted, 1)
    table = table + pltpu.roll(enc_terms, enc_terms.shape[1] - observed, 1)[:, 0:LANES]
    lane = lax.broadcasted_iota(jnp.int32, table.shape, 1)
    table = jnp.where(lane < task_width, table, 0.0)
    table = jnp.where((lane == LANES - 1) & (kinds == 0), jnp.sum(loss, axis=1, keepdims=True), table)
    table_rows = [table[start : start + GROUP] for start in range(0, tasks, GROUP)]
    table_block = jnp.concatenate(table_rows, axis=1).astype(BF16)
    width = grad_ref.shape[1]
    batches = chips * CORES
    for relative, (which, slot) in enumerate(slots):
        dest = place_ref[0] ^ relative
        if chips * sections * CORES == len(slots):
            slot = lax.rem(dest, batches) // CORES * sections + dest // batches
        start = pl.multiple_of(dest * GROUP, GROUP)
        out_ref = (keep_ref, send_ref)[which]
        out_ref[slot, :, 0:width] = grad_ref[pl.ds(start, GROUP), :].astype(BF16)
        out_ref[slot, :, width : width + latent] = egrad_ref[dest].astype(BF16)
        out_ref[slot, :, width + latent :] = table_block


def final_kernel(tasks, task_width, enc_in, bins, net_in, *refs):
    outs = refs[-12:]
    (loss_ref, table_ref, e1_ref, eg_ref, es_ref, e2_ref, first_ref, second_ref, gain_ref, shift_ref, dyn_ref, head_ref) = outs
    refs = refs[:-12]
    tail_ref, refs = refs[0], refs[1:]
    latent = second_ref.shape[2]
    first_end = latent + LANES
    second_end = first_end + latent

    def put_net(net, value):
        first_ref[net] = value[:, 0:net_in]
        second_ref[net] = value[:, first_end:second_end]
        turned = jnp.transpose(value[:, latent:first_end])
        for layer in range(2):
            row = net_in - latent + 2 * layer
            gain_ref[net, layer : layer + 1, :] = turned[row : row + 1, :]
            shift_ref[net, layer : layer + 1, :] = turned[row + 1 : row + 2, :]

    tail = functools.reduce(jnp.add, [tail_ref[place].astype(F32) for place in range(tail_ref.shape[0])])
    put_net(0, tail)
    dyn_ref[...] = tail[:, second_end : second_end + latent]
    enc = tail[:, second_end + latent : second_end + 2 * latent]
    half = GROUP // 2
    e2_ref[...] = 0.3 * enc[0:half, :]
    e1_ref[...] = 0.3 * enc[half:, 0:enc_in]
    turned = 0.3 * jnp.transpose(enc[half:, LANES : 2 * LANES])
    eg_ref[...] = turned[LANES - 2 : LANES - 1, :]
    es_ref[...] = turned[LANES - 1 : LANES, :]
    table = tail[:, second_end + 2 * latent :]
    loss_ref[...] = table[0:1, LANES - 1 : LANES]
    for place in range(tasks // GROUP):
        table_ref[place * GROUP : (place + 1) * GROUP, :] = table[:, place * LANES : place * LANES + task_width]
    net = 1
    parts = len(refs) // len(CHUNKS)
    for chunk, count in enumerate(CHUNKS):
        for one in range(count):
            each = [ref[one].astype(F32) for ref in refs[chunk * parts : (chunk + 1) * parts]]
            value = functools.reduce(jnp.add, each)
            put_net(net, value)
            head_ref[net - 1] = value[:, second_end : second_end + bins]
            net += 1


def swap(value, axis, distance):
    count = lax.axis_size(axis)
    return lax.ppermute(value, axis, [(place, place ^ distance) for place in range(count)])


def exchange(parts, axis, scale):
    total = parts[0].astype(F32)
    for distance in range(1, len(parts)):
        total = total + swap(parts[distance], axis, distance * scale).astype(F32)
    return total


def scatter_plain(packed, chips, sections):
    held = packed.reshape((sections, chips, CORES) + packed.shape[1:])
    batch_no = lax.axis_index("batch")
    places = (
        ("batch", 1, CORES, 2, batch_no % CORES),
        ("batch", CORES, chips, 1, batch_no // CORES),
        ("section", 1, sections, 0, lax.axis_index("section")),
    )
    for axis, scale, count, dim, mine in places:
        parts = [lax.dynamic_index_in_dim(held, mine ^ other, dim, keepdims=False) for other in range(count)]
        held = exchange(parts, axis, scale)
        held = held.astype(BF16) if dim else held
    return held


def on_device(
    observations,
    actions,
    targets,
    task_ids,
    horizons,
    reward_bins,
    value_bins,
    task_table,
    enc_first,
    enc_gain,
    enc_shift,
    enc_second,
    net_first,
    net_second,
    net_gain,
    net_shift,
    dyn_out,
    head_out,
):
    sections = lax.axis_size("section")
    batches = lax.axis_size("batch")
    section_no = lax.axis_index("section")
    chips = batches // CORES
    devices = sections * batches
    steps, rows_all, acted = actions.shape
    observed = observations.shape[1]
    rows = rows_all // sections
    latent = dyn_out.shape[1]
    hidden = dyn_out.shape[0]
    tasks, task_width = task_table.shape
    heads, _, bins = head_out.shape
    nets, net_in, _ = net_first.shape
    enc_in, enc_width = enc_first.shape
    wide = steps * LANES
    scale = 1.0 / (rows_all * batches * steps)
    groups = hidden // GROUP
    in_place = hidden // devices == GROUP
    start = section_no * rows
    block_no = start // LANES
    first_lane = start - block_no * LANES
    me = section_no * batches + lax.axis_index("batch") if in_place else jnp.int32(0)
    place = jnp.stack([me, block_no, first_lane, first_lane + rows]).astype(jnp.int32)
    if in_place:
        slots = tuple(
            (relative % CORES, (relative // CORES) % chips * sections + relative // batches) for relative in range(groups)
        )
    else:
        slots = tuple((relative // (groups // 2), relative % (groups // 2)) for relative in range(groups))
    half_slots = groups // 2
    shape_of = jax.ShapeDtypeStruct
    smem = pl.BlockSpec(memory_space=pltpu.SMEM)
    local = pl.BlockSpec(memory_space=pltpu.VMEM)
    far = pl.BlockSpec(memory_space=pltpu.HBM)
    anywhere = pl.BlockSpec(memory_space=pl.ANY)
    first_far, second_far, dyn_far, targets_far = [
        pltpu.with_memory_space_constraint(array, pltpu.HBM) for array in (net_first, net_second, dyn_out, targets)
    ]
    vmem = pltpu.VMEM
    dmas = pltpu.SemaphoreType.DMA

    def params(mebibytes):
        return pltpu.CompilerParams(vmem_limit_bytes=mebibytes * 1024 * 1024)

    def cost(flops, moved):
        return pl.CostEstimate(flops=flops, bytes_accessed=moved, transcendentals=0)

    ids_row = task_ids.reshape(1, rows_all)
    horizon_row = horizons.reshape(1, rows_all)
    eg_row = enc_gain.reshape(1, enc_width)
    es_row = enc_shift.reshape(1, enc_width)
    head_turned = head_out.transpose(0, 2, 1)
    low = lambda lanes: shape_of((hidden, lanes), BF16)
    forward_shapes = (
        shape_of((latent + LANES, wide), BF16),
        shape_of((latent, wide + LANES), F32),
        low(wide), low(wide), low(wide), low(wide), low(wide), low(wide),
        shape_of((8, wide), F32),
        shape_of((2 * LANES, LANES), BF16),
        shape_of((enc_width, LANES), BF16),
        shape_of((enc_width, LANES), BF16),
        shape_of((enc_width, LANES), BF16),
        shape_of((8, LANES), F32),
        shape_of((net_in, hidden), BF16),
        shape_of((hidden, hidden), BF16),
        shape_of((hidden, latent), BF16),
    )

    def weight_shapes(count):
        return (shape_of((count, net_in, hidden), BF16), shape_of((count, hidden, hidden), BF16))

    made = pl.pallas_call(
        functools.partial(forward_kernel, steps, CHUNKS[0]),
        out_shape=forward_shapes + weight_shapes(CHUNKS[0]),
        in_specs=[smem] + [local] * 10 + [far] * 3,
        out_specs=[local] * (len(forward_shapes) + 2),
        scratch_shapes=[
            vmem((8, hidden), F32),
            vmem((4, hidden, LANES), F32),
            vmem((8, enc_width), F32),
            vmem((2, enc_width, LANES), F32),
            vmem((tasks, 2 * LANES), F32),
            vmem((LANES, LANES), F32),
            vmem((2 * LANES, enc_width), BF16),
            vmem((hidden, latent + LANES), BF16),
            vmem((hidden, hidden), BF16),
            vmem((latent, hidden), BF16),
            vmem((hidden, LANES), F32),
            vmem((enc_width, LANES), F32),
            dmas((5,)),
        ],
        compiler_params=params(VMEM_A),
        cost_estimate=cost(10_000_000_000, 8_000_000),
        name="forward_chain",
    )(
        place, observations.T, actions.transpose(0, 2, 1), ids_row, task_table, enc_first, eg_row, es_row, enc_second,
        net_gain, net_shift, first_far, second_far, dyn_far,
    )
    saved, weights = made[:-2], made[-2:]
    xt = saved[0]
    head_width = latent + LANES + hidden + LANES

    def run_heads(base, count, ahead, weights, before, after):
        pack_shape = shape_of((half_slots, count, GROUP, head_width), BF16)
        dx_shape = shape_of((latent + LANES, wide), F32)
        out_shapes = (pack_shape, pack_shape, dx_shape, shape_of((1, LANES), F32))
        args = [place, xt, *weights, head_turned, net_gain, net_shift, reward_bins, value_bins, horizon_row]
        specs = [smem] + [local] * 9
        aliases = {}
        if before is not None:
            aliases = {len(args): 2}
            args.append(before)
            specs.append(local)
        args += after
        specs += [anywhere] * len(after)
        if ahead:
            args += [first_far, second_far]
            specs += [far, far]
            out_shapes += weight_shapes(ahead)
        scratch = [
            vmem((count, 8, hidden), F32),
            vmem((count, 4, hidden, LANES), F32),
            vmem((count, hidden, latent + LANES), BF16),
            vmem((count, hidden, hidden), BF16),
            vmem((count, LANES, hidden), BF16),
            vmem((count, hidden, LANES), BF16),
            vmem((count, LANES, hidden), BF16),
            vmem((count, hidden, wide), F32),
            vmem((count, LANES, wide), F32),
        ]
        scratch += [vmem((count, hidden, wide), BF16)] * 6
        scratch += [
            vmem((count, 8, wide), F32),
            vmem((count, 4, hidden, LANES), F32),
            vmem((count, hidden, wide), BF16),
            vmem((count, hidden, wide), BF16),
            vmem((count, LANES, wide), BF16),
            vmem((count, hidden, head_width), BF16),
        ]
        if ahead:
            scratch.append(dmas((2,)))
        return pl.pallas_call(
            functools.partial(
                heads_kernel, steps, scale, slots, base, count, ahead, heads, bins, before is not None, len(after)
            ),
            out_shape=out_shapes,
            in_specs=specs,
            out_specs=[local] * len(out_shapes),
            scratch_shapes=scratch,
            input_output_aliases=aliases,
            compiler_params=params(VMEM_B),
            cost_estimate=cost(count * 10_000_000_000, count * 4_000_000),
            name=f"heads_{base}",
        )(*args)

    def core_swap(keep, send):
        return [keep, swap(send, "batch", 1)]

    def core_sum(parts, token):
        return added([each.reshape((chips, sections) + each.shape[1:]) for each in parts], chips, token)

    def chip_swap(held):
        return [held[0]] + [swap(held[place], "batch", CORES * place) for place in range(1, chips)]

    def section_swap(held):
        return [held[0]] + [swap(held[place], "section", place) for place in range(1, sections)]

    def added(parts, pieces, *tokens):
        piece = parts[0].shape[1:]
        out_shapes = [shape_of(piece, BF16)] * pieces

        def add_kernel(*refs):
            refs = refs[len(tokens) :]
            for place in range(pieces):
                each = [ref[place].astype(F32) for ref in refs[: len(parts)]]
                refs[len(parts) + place][...] = functools.reduce(jnp.add, each).astype(BF16)

        return pl.pallas_call(
            add_kernel,
            out_shape=out_shapes,
            in_specs=[anywhere] * len(tokens) + [local] * len(parts),
            out_specs=[local] * pieces,
            cost_estimate=cost(1_000_000, 2_000_000),
            name="added",
        )(*tokens, *parts)

    packs, loss_parts = [], []
    dx = None
    base = 0
    after_core, after_chip, core_parts, chip_parts, ends = {}, {}, {}, {}, {}
    for number, count in enumerate(CHUNKS):
        ahead = CHUNKS[number + 1] if number + 1 < len(CHUNKS) else 0
        after = []
        if in_place and number >= 2:
            after = after_core[number - 2][:1]
        if in_place and number >= 1:
            core_parts[number - 1] = core_swap(*packs[number - 1])
        if in_place and number >= 2:
            chip_parts[number - 2] = chip_swap(after_core[number - 2])
        result = run_heads(base, count, ahead, weights, dx, after)
        if in_place and number >= 1:
            after_core[number - 1] = core_sum(core_parts[number - 1], result[3])
        if in_place and number >= 2:
            after_chip[number - 2] = added(chip_parts[number - 2], sections, result[3])
        keep, send, dx, loss = result[:4]
        weights = result[4:]
        packs.append((keep, send))
        loss_parts.append(loss)
        base += count
    after = []
    last = len(CHUNKS) - 1
    if in_place:
        after = after_core[last - 1][:1] + after_chip[last - 2][:1]
    net_width = latent + LANES + hidden + latent
    tail_width = net_width + latent + tasks // GROUP * LANES
    tail_shape = shape_of((half_slots, GROUP, tail_width), BF16)
    backward = pl.pallas_call(
        functools.partial(
            backward_kernel, steps, scale, slots, tasks, task_width, acted, observed, chips, sections, len(after)
        ),
        out_shape=(tail_shape, tail_shape),
        in_specs=[smem] + [local] * (len(saved) + 7 + len(CHUNKS)) + [anywhere] * len(after) + [far],
        out_specs=[local, local],
        scratch_shapes=[
            vmem((steps, LANES, latent), BF16),
            vmem((8, hidden), F32),
            vmem((4, hidden, LANES), F32),
            vmem((8, enc_width), F32),
            vmem((2, enc_width, LANES), F32),
            vmem((LANES, hidden), BF16),
            vmem((2 * LANES, enc_width), BF16),
            vmem((hidden, LANES), F32),
            vmem((enc_width, LANES), F32),
            vmem((4, hidden, LANES), F32),
            vmem((2, enc_width, LANES), F32),
            vmem((hidden, wide), BF16),
            vmem((hidden, wide), BF16),
            vmem((latent, wide), BF16),
            vmem((enc_width, LANES), BF16),
            vmem((hidden, net_width), F32),
            vmem((groups, GROUP, latent), F32),
            dmas((steps,)),
        ],
        compiler_params=params(VMEM_C),
        cost_estimate=cost(15_000_000_000, 12_000_000),
        name="backward_chain",
    )
    if in_place:
        core_parts[last] = core_swap(*packs[last])
        chip_parts[last - 1] = chip_swap(after_core[last - 1])
        ends[last - 2] = section_swap(after_chip[last - 2])
    keep, send = backward(
        place, *saved, horizon_row, ids_row, enc_first, eg_row, enc_second, net_gain, dx, *loss_parts, *after, targets_far,
    )

    if in_place:
        after_core[last] = core_sum(core_parts[last], keep)
        after_chip[last - 1] = added(chip_parts[last - 1], sections, keep)
        tail_parts = [each[None] for each in core_swap(keep, send)]
        held = added(tail_parts, 1, after_core[last][0], after_chip[last - 1][0])[0]
        held = held.reshape((chips, sections) + held.shape[1:])
        same_core = [[core + CORES * chip for chip in range(chips)] for core in range(CORES)]
        held = lax.all_to_all(held, "batch", 0, 0, axis_index_groups=same_core, tiled=True)
        held = jnp.sum(held.astype(F32), axis=0).astype(BF16)
        tail = lax.all_to_all(held, "section", 0, 0, tiled=True)
        ends[last - 1] = section_swap(after_chip[last - 1])
        after_chip[last] = added(chip_swap(after_core[last]), sections, held)
        ends[last] = section_swap(after_chip[last])
        ends = [part for number in range(len(CHUNKS)) for part in ends[number]]
        each = GROUP // 2
        out_shapes = (
            shape_of((1, 1), F32),
            shape_of((tasks, task_width), F32),
            shape_of((each, enc_in), F32),
            shape_of((1, each), F32),
            shape_of((1, each), F32),
            shape_of((each, latent), F32),
            shape_of((nets, GROUP, net_in), F32),
            shape_of((nets, GROUP, hidden), F32),
            shape_of((nets, 2, GROUP), F32),
            shape_of((nets, 2, GROUP), F32),
            shape_of((GROUP, latent), F32),
            shape_of((heads, GROUP, bins), F32),
        )
        outs = list(pl.pallas_call(
            functools.partial(final_kernel, tasks, task_width, enc_in, bins, net_in),
            out_shape=out_shapes,
            in_specs=[local] * (1 + len(ends)),
            out_specs=[local] * len(out_shapes),
            cost_estimate=cost(1_000_000, 4_000_000),
            name="last_sums",
        )(tail, *ends))
        outs[0] = outs[0].reshape(())
        outs[2] = outs[2].T
        outs[3], outs[4] = outs[3].reshape(each), outs[4].reshape(each)
        outs[6] = outs[6].transpose(0, 2, 1)
        outs[7] = outs[7].transpose(0, 2, 1)
        return tuple(outs)

    def scattered(keep, send):
        mine = hidden // devices
        packed = jnp.concatenate([keep, send], axis=0)
        middle = packed.shape[1:-2]
        packed = packed.reshape((groups,) + middle + (GROUP // mine, mine, packed.shape[-1]))
        packed = jnp.moveaxis(packed, -3, 1).reshape((devices,) + middle + (mine, packed.shape[-1]))
        return scatter_plain(packed, chips, sections)

    head_sum = jnp.concatenate([scattered(*pack) for pack in packs], axis=0)
    enc_each = enc_width // devices
    net_sum = scattered(keep[:, :, 0:net_width], send[:, :, 0:net_width])
    rest = jnp.concatenate([keep, send], axis=0)
    enc_all = rest[:, :, net_width : net_width + latent].reshape(groups, 2, enc_width // groups, latent)
    enc_all = enc_all.transpose(0, 2, 1, 3).reshape(devices, enc_each, 2, latent)
    enc_sum = scatter_plain(enc_all, chips, sections)
    enc_sum = enc_sum.transpose(1, 0, 2).reshape(2 * enc_each, latent)
    table_sum = lax.psum(rest[0, :, net_width + latent :].astype(F32), ("section", "batch"))
    first_end = latent + LANES
    net_row = jnp.concatenate([net_sum[:, 0 : first_end + hidden], jnp.zeros_like(net_sum[:, 0:LANES])], axis=1)
    sums = jnp.concatenate([net_row[None], head_sum], axis=0)
    vectors = sums[:, :, net_in : net_in + 4].transpose(0, 2, 1)
    table = table_sum.reshape(GROUP, tasks // GROUP, LANES).transpose(1, 0, 2).reshape(tasks, LANES)
    enc_rows = enc_sum[enc_each:]
    return (
        table[0, LANES - 1],
        table[:, 0:task_width],
        0.3 * enc_rows[:, 0:enc_in].T,
        0.3 * enc_rows[:, 2 * LANES - 2],
        0.3 * enc_rows[:, 2 * LANES - 1],
        0.3 * enc_sum[0:enc_each],
        sums[:, :, 0:net_in].transpose(0, 2, 1),
        sums[:, :, first_end : first_end + hidden].transpose(0, 2, 1),
        vectors[:, 0::2],
        vectors[:, 1::2],
        net_sum[:, first_end + hidden :],
        head_sum[:, :, first_end + hidden : first_end + hidden + bins],
    )


def solution(mesh):
    both = ("section", "batch")
    return jax.shard_map(
        on_device,
        mesh=mesh,
        in_specs=(
            P("batch", None),
            P(None, "batch", None),
            P(None, "batch", None),
            P("batch"),
            P("batch"),
            P(None, "batch"),
            P(None, "batch"),
        )
        + (P(),) * 11,
        out_specs=(
            P(),
            P(),
            P(None, both),
            P(both),
            P(both),
            P(both, None),
            P(None, None, both),
            P(None, None, both),
            P(None, None, both),
            P(None, None, both),
            P(both, None),
            P(None, both, None),
        ),
        check_vma=False,
    )
```

```python
import functools

import jax
import jax.numpy as jnp
from jax import lax
from jax.experimental import pallas as pl
from jax.experimental.pallas import tpu as pltpu
from jax.sharding import PartitionSpec as P

CORES = 2
LANES = 128
GROUP = 16
BF16 = jnp.bfloat16
F32 = jnp.float32
CHUNKS = (2, 2, 2)
VMEM_A = 16
VMEM_B = 20
VMEM_SUM = 4
VMEM_C = 20


def nn(left, right):
    return lax.dot_general(left, right, (((1,), (0,)), ((), ())), preferred_element_type=F32)


def nt(left, right):
    return lax.dot_general(left, right, (((1,), (1,)), ((), ())), preferred_element_type=F32)


def tn(left, right):
    return lax.dot_general(left, right, (((0,), (0,)), ((), ())), preferred_element_type=F32)


def column_sum(value):
    grouped = value.reshape(value.shape[0] // 8, 8, value.shape[1])
    return jnp.sum(jnp.sum(grouped, axis=0), axis=0, keepdims=True)


def slabs(features, size=64):
    return [slice(start, start + size) for start in range(0, features, size)]


def lanes_of(step):
    return slice(step * LANES, (step + 1) * LANES)


def spread_columns(gain_rows, shift_rows, rows_ref, spread_ref):
    count = gain_rows.shape[0]
    rows_ref[...] = jnp.zeros_like(rows_ref)
    rows_ref[0:count, :] = gain_rows
    rows_ref[count : 2 * count, :] = shift_rows
    turned = jnp.transpose(rows_ref[...])
    for place in range(2 * count):
        spread_ref[place] = jnp.broadcast_to(turned[:, place : place + 1], spread_ref.shape[1:])


def mish_forward(pre_ref, pre_at, gain_ref, shift_ref, hid_ref, hat_ref, slope_ref, scale_ref, scale_row, at):
    features = pre_ref.shape[0]
    row_mean = column_sum(pre_ref[:, pre_at]) * (1.0 / features)
    centred = pre_ref[:, pre_at] - row_mean
    spread = column_sum(centred * centred) * (1.0 / features)
    scale = lax.rsqrt(spread + 1e-05)
    scale_ref[scale_row : scale_row + 1, at] = scale
    for part in slabs(features):
        hat = (pre_ref[part, pre_at] - row_mean) * scale
        normed = hat * gain_ref[part, :] + shift_ref[part, :]
        power = jnp.exp(normed)
        top = power * (power + 2.0)
        inverse = pl.reciprocal(top + 2.0, approx=True)
        ratio = top * inverse
        hid_ref[part, at] = (normed * ratio).astype(BF16)
        tilt = power * inverse
        slope = ratio + normed * (4.0 * (tilt * (tilt + inverse)))
        slope_ref[part, at] = (slope * gain_ref[part, :]).astype(BF16)
        hat_ref[part, at] = hat.astype(BF16)


def mish_backward(grad_ref, grad_at, hat_ref, slope_ref, scale_ref, scale_row, at, sums_ref, sums_at, first, out_ref):
    features = grad_ref.shape[0]
    total_one = jnp.zeros((8, LANES), F32)
    total_two = jnp.zeros((8, LANES), F32)
    for part in slabs(features):
        term = grad_ref[part, grad_at] * slope_ref[part, at].astype(F32)
        grad_ref[part, grad_at] = term
        crossed = term * hat_ref[part, at].astype(F32)
        groups = (term.shape[0] // 8, 8, LANES)
        total_one = total_one + jnp.sum(term.reshape(groups), axis=0)
        total_two = total_two + jnp.sum(crossed.reshape(groups), axis=0)
        if first:
            sums_ref[sums_at, part, :] = term
            sums_ref[sums_at + 1, part, :] = crossed
        else:
            sums_ref[sums_at, part, :] += term
            sums_ref[sums_at + 1, part, :] += crossed
    mean_one = jnp.sum(total_one, axis=0, keepdims=True) * (1.0 / features)
    mean_two = jnp.sum(total_two, axis=0, keepdims=True) * (1.0 / features)
    scale = scale_ref[scale_row : scale_row + 1, at]
    for part in slabs(features):
        rest = grad_ref[part, grad_at] - mean_one - hat_ref[part, at].astype(F32) * mean_two
        out_ref[part, at] = (rest * scale).astype(BF16)


def mish_forward_low(pre_ref, gain_ref, shift_ref, hid_ref, hat_ref, slope_ref, scale_ref, scale_row, at):
    features = pre_ref.shape[0]
    row_mean = column_sum(pre_ref[:, at]) * (1.0 / features)
    centred = pre_ref[:, at] - row_mean
    spread = column_sum(centred * centred) * (1.0 / features)
    scale = lax.rsqrt(spread + 1e-05)
    scale_ref[scale_row : scale_row + 1, at] = scale
    for part in slabs(features):
        hat = (pre_ref[part, at] - row_mean) * scale
        normed = (hat * gain_ref[part, :] + shift_ref[part, :]).astype(BF16)
        hat_ref[part, at] = hat.astype(BF16)
        power = jnp.exp(normed)
        top = power * (power + 2.0)
        inverse = pl.reciprocal(top + 2.0, approx=True)
        ratio = top * inverse
        hid_ref[part, at] = normed * ratio
        tilt = power * inverse
        slope = ratio + (4.0 * normed) * (tilt * (tilt + inverse))
        slope_ref[part, at] = slope * gain_ref[part, :].astype(BF16)


def mish_backward_low(grad_ref, hat_ref, slope_ref, scale_ref, scale_row, steps, sums_ref, sums_at, out_ref):
    features = grad_ref.shape[0]
    rows = []
    for step in range(steps):
        at = lanes_of(step)
        total_one = jnp.zeros((16, LANES), F32)
        total_two = jnp.zeros((16, LANES), F32)
        for part in slabs(features):
            term = grad_ref[part, at] * slope_ref[part, at]
            crossed = term * hat_ref[part, at]
            grad_ref[part, at] = term
            groups = (term.shape[0] // 16, 16, LANES)
            term = term.reshape(groups)
            crossed = crossed.reshape(groups)
            total_one = total_one + functools.reduce(jnp.add, [term[k] for k in range(groups[0])]).astype(F32)
            total_two = total_two + functools.reduce(jnp.add, [crossed[k] for k in range(groups[0])]).astype(F32)
        scale = scale_ref[scale_row : scale_row + 1, at]
        mean_one = jnp.sum(total_one, axis=0, keepdims=True) * (1.0 / features)
        mean_two = jnp.sum(total_two, axis=0, keepdims=True) * (1.0 / features)
        rows.append((mean_one.astype(BF16), mean_two.astype(BF16), scale.astype(BF16)))
    for part in slabs(features):
        sum_one, sum_two = None, None
        for step, (mean_one, mean_two, scale) in enumerate(rows):
            at = lanes_of(step)
            term = grad_ref[part, at]
            hat = hat_ref[part, at]
            out_ref[part, at] = (term - mean_one - hat * mean_two) * scale
            crossed = term * hat
            sum_one = term if sum_one is None else sum_one + term
            sum_two = crossed if sum_two is None else sum_two + crossed
        sums_ref[sums_at, part, :] = sum_one.astype(F32)
        sums_ref[sums_at + 1, part, :] = sum_two.astype(F32)


def simplex(values):
    grouped = values.reshape(values.shape[0] // 8, 8, values.shape[1])
    powers = jnp.exp(grouped - jnp.max(grouped, axis=1, keepdims=True))
    shares = powers / jnp.sum(powers, axis=1, keepdims=True)
    return shares.reshape(values.shape)


def simplex_back(shares, grads):
    grouped = (shares.shape[0] // 8, 8, shares.shape[1])
    crossed = jnp.sum((shares * grads).reshape(grouped), axis=1, keepdims=True)
    return (shares.reshape(grouped) * (grads.reshape(grouped) - crossed)).reshape(shares.shape)


def row_weight(step, steps, scale, horizon_row, place_ref):
    lane = lax.broadcasted_iota(jnp.int32, (1, LANES), 1)
    mine = (lane >= place_ref[2]) & (lane < place_ref[3]) & (horizon_row > step)
    return jnp.where(mine, F32(scale * 0.5 ** (step / (steps - 1))), 0.0)


def padded_rows(value, rows):
    zeros = jnp.zeros((rows - value.shape[0], value.shape[1]), F32)
    return jnp.concatenate([value.astype(F32), zeros], axis=0).astype(BF16)


def transpose_into(out_ref, source_ref, rows):
    for start in range(0, rows, LANES):
        out_ref[:, start : start + LANES] = jnp.transpose(source_ref[start : start + LANES, :])


def vector_sums(sums_ref, gains_ref, layers):
    vectors = []
    for layer in range(layers):
        inverse = 1.0 / gains_ref[layer]
        vectors.append(jnp.sum(sums_ref[2 * layer + 1] * inverse, axis=1, keepdims=True))
        vectors.append(jnp.sum(sums_ref[2 * layer] * inverse, axis=1, keepdims=True))
    return vectors


def own_lanes(place_ref):
    return pl.ds(pl.multiple_of(place_ref[1] * LANES, LANES), LANES)


def load_all(copies):
    made = [pltpu.make_async_copy(*each) for each in copies]
    for each in made:
        each.start()
    return made


def with_vectors(value, vectors, first_lane):
    lane = lax.broadcasted_iota(jnp.int32, value.shape, 1)
    for place, vector in enumerate(vectors):
        value = jnp.where(lane == first_lane + place, vector, value)
    return value


def forward_kernel(
    steps, ahead,
    place_ref, obs_hbm, act_hbm, ids_hbm, table_hbm, e1_hbm, eg_hbm, es_hbm, e2_hbm, g_hbm, s_hbm,
    w1_hbm, w2_hbm, dyn_hbm,
    xt_ref, soft_ref, h1_ref, hat1_ref, slope1_ref, h2_ref, hat2_ref, slope2_ref, scale_ref,
    ein_ref, eh_ref, ehat_ref, eslope_ref, escale_ref,
    w1_ref, w2_ref, dyn_ref, next1_ref, next2_ref,
    rows_ref, spread_ref, erows_ref, espread_ref, wide_ref, tall_ref, e1p_ref, w1t_ref, w2t_ref, dynt_ref, pre_ref, epre_ref,
    obs_ref, act_ref, ids_ref, table_ref, e1_ref, eg_ref, es_ref, e2_ref, g_ref, s_ref,
    sems, early_sems,
):
    early = load_all([
        (table_hbm, table_ref, early_sems.at[0]),
        (ids_hbm, ids_ref, early_sems.at[1]),
        (obs_hbm, obs_ref, early_sems.at[2]),
        (e1_hbm, e1_ref, early_sems.at[3]),
        (eg_hbm, eg_ref, early_sems.at[4]),
        (es_hbm, es_ref, early_sems.at[5]),
        (e2_hbm, e2_ref, early_sems.at[6]),
        (act_hbm, act_ref, early_sems.at[7]),
        (g_hbm, g_ref, early_sems.at[8]),
        (s_hbm, s_ref, early_sems.at[9]),
    ])
    first, second, third, fourth, fifth = load_all([
        (w1_hbm.at[0], w1_ref, sems.at[0]),
        (w2_hbm.at[0], w2_ref, sems.at[1]),
        (dyn_hbm, dyn_ref, sems.at[2]),
        (w1_hbm.at[pl.ds(1, ahead)], next1_ref, sems.at[3]),
        (w2_hbm.at[pl.ds(1, ahead)], next2_ref, sems.at[4]),
    ])
    latent = dyn_ref.shape[1]
    tasks, task_width = table_ref.shape
    observed = obs_ref.shape[0]
    acted = act_ref.shape[1]
    mine = own_lanes(place_ref)
    for each in early:
        each.wait()
    spread_columns(eg_ref[...], es_ref[...], erows_ref, espread_ref)
    kinds = lax.broadcasted_iota(jnp.int32, (tasks, LANES), 0)
    onehot = (kinds == ids_ref[:, mine]).astype(F32).astype(BF16)
    wide_ref[...] = jnp.zeros_like(wide_ref)
    wide_ref[:, 0:task_width] = table_ref[...].astype(F32)
    table_tail = pltpu.roll(wide_ref[:, 0:LANES], acted, 1).astype(BF16)
    table_enc = pltpu.roll(wide_ref[...], observed, 1).astype(BF16)
    aux = tn(table_tail, onehot)
    tall_ref[...] = jnp.zeros_like(tall_ref)
    tall_ref[0:observed, :] = obs_ref[:, mine].astype(F32)
    ein = tn(table_enc, onehot)
    ein_ref[0:LANES, :] = (ein[0:LANES] + tall_ref[...]).astype(BF16)
    ein_ref[LANES:, :] = ein[LANES:].astype(BF16)
    e1p_ref[...] = padded_rows(e1_ref[...], e1p_ref.shape[0])
    epre_ref[...] = tn(e1p_ref[...], ein_ref[...])
    here = slice(0, LANES)
    mish_forward(epre_ref, here, espread_ref.at[0], espread_ref.at[1], eh_ref, ehat_ref, eslope_ref, escale_ref, 0, here)
    shares = simplex(tn(e2_ref[...], eh_ref[...]))
    soft_ref[:, 0:LANES] = shares
    xt_ref[0:latent, 0:LANES] = shares.astype(BF16)
    spread_columns(g_ref[0], s_ref[0], rows_ref, spread_ref)
    for step in range(steps):
        tall_ref[...] = jnp.zeros_like(tall_ref)
        tall_ref[0:acted, :] = act_ref[step, :, mine].astype(F32)
        xt_ref[latent:, lanes_of(step)] = (aux + tall_ref[...]).astype(BF16)
    first.wait()
    transpose_into(w1t_ref, w1_ref, latent)
    w1t_ref[:, latent:] = jnp.transpose(padded_rows(w1_ref[latent:, :], LANES))
    second.wait()
    transpose_into(w2t_ref, w2_ref, latent)
    third.wait()
    transpose_into(dynt_ref, dyn_ref, latent)
    for step in range(steps):
        at = lanes_of(step)
        pre_ref[...] = nn(w1t_ref[...], xt_ref[:, at])
        mish_forward(pre_ref, here, spread_ref.at[0], spread_ref.at[2], h1_ref, hat1_ref, slope1_ref, scale_ref, 0, at)
        pre_ref[...] = nn(w2t_ref[...], h1_ref[:, at])
        mish_forward(pre_ref, here, spread_ref.at[1], spread_ref.at[3], h2_ref, hat2_ref, slope2_ref, scale_ref, 1, at)
        shares = simplex(nn(dynt_ref[...], h2_ref[:, at]))
        soft_ref[:, lanes_of(step + 1)] = shares
        if step + 1 < steps:
            xt_ref[0:latent, lanes_of(step + 1)] = shares.astype(BF16)
    fourth.wait()
    fifth.wait()


def heads_kernel(steps, scale, slots, base, count, ahead, heads, bins, chained, after, *refs):
    refs = list(refs)
    place_ref, xt_ref, w1_ref, w2_ref, ho_ref, g_ref, s_ref, rb_ref, vb_ref, hz_ref = refs[:10]
    refs = refs[10:]
    before_ref = refs.pop(0) if chained else None
    refs = refs[after:]
    w1_hbm, w2_hbm = refs[:2] if ahead else (None, None)
    refs = refs[2:] if ahead else refs
    keep_ref, send_ref, dx_ref, loss_ref = refs[:4]
    refs = refs[4:]
    copies = []
    if ahead:
        next1_ref, next2_ref, sems = refs[0], refs[1], refs[-1]
        refs = refs[2:-1]
        start = base + 1 + count
        copies = load_all([
            (w1_hbm.at[pl.ds(start, ahead)], next1_ref, sems.at[0]),
            (w2_hbm.at[pl.ds(start, ahead)], next2_ref, sems.at[1]),
        ])
    (rows_ref, spread_ref, w1t_ref, w2t_ref, tail_ref, hop_ref, hot_ref, pre_ref, lg_ref, h1_ref, hat1_ref, slope1_ref,
     h2_ref, hat2_ref, slope2_ref, scale_ref, sums_ref, dh_ref, d2_ref, d1_ref, dl_ref, grad_ref) = refs
    latent = w2_ref.shape[1]
    tail_rows = w1_ref.shape[1] - latent
    mine = own_lanes(place_ref)
    horizon_row = hz_ref[:, mine]
    bin_ids = lax.broadcasted_iota(jnp.int32, (LANES, LANES), 0)
    first_end = latent + LANES
    losses = []
    for one in range(count):
        spread_columns(g_ref[base + 1 + one], s_ref[base + 1 + one], rows_ref, spread_ref)
        tail_ref[...] = padded_rows(w1_ref[one, latent:, :], LANES)
        transpose_into(w1t_ref, w1_ref.at[one], latent)
        w1t_ref[:, latent:] = jnp.transpose(tail_ref[...])
        transpose_into(w2t_ref, w2_ref.at[one], latent)
        hot_ref[...] = padded_rows(ho_ref[base + one], LANES)
        hop_ref[...] = jnp.transpose(hot_ref[...])
        gain1, gain2, shift1, shift2 = [spread_ref.at[place] for place in range(4)]
        pre_ref[...] = nn(w1t_ref[...], xt_ref[...])
        for step in range(steps):
            mish_forward_low(pre_ref, gain1, shift1, h1_ref, hat1_ref, slope1_ref, scale_ref, 0, lanes_of(step))
        pre_ref[...] = nn(w2t_ref[...], h1_ref[...])
        for step in range(steps):
            mish_forward_low(pre_ref, gain2, shift2, h2_ref, hat2_ref, slope2_ref, scale_ref, 1, lanes_of(step))
        lg_ref[...] = nn(hot_ref[...], h2_ref[...])
        share = 0.1 if base + one == 0 else 0.1 / (heads - 1)
        bins_ref = rb_ref if base + one == 0 else vb_ref
        for step in range(steps):
            at = lanes_of(step)
            logits = jnp.where(bin_ids < bins, lg_ref[:, at], F32(-1e30))
            chosen = bin_ids == bins_ref[step : step + 1, mine]
            top = jnp.max(logits, axis=0, keepdims=True)
            powers = jnp.exp(logits - top)
            total = column_sum(powers)
            picked = column_sum(jnp.where(chosen, logits, 0.0))
            weight = row_weight(step, steps, scale * share, horizon_row, place_ref)
            losses.append(weight * (jnp.log(total) + top - picked))
            dl_ref[:, at] = (powers * (weight / total) - jnp.where(chosen, weight, 0.0)).astype(BF16)
        dh_ref[...] = nn(hop_ref[...], dl_ref[...]).astype(BF16)
        grad_ref[:, first_end + latent :] = nt(h2_ref[...], dl_ref[...]).astype(BF16)
        mish_backward_low(dh_ref, hat2_ref, slope2_ref, scale_ref, 1, steps, sums_ref, 2, d2_ref)
        dh_ref[...] = nn(w2_ref[one], d2_ref[...]).astype(BF16)
        grad_ref[:, first_end : first_end + latent] = nt(d2_ref[...], h1_ref[...]).astype(BF16)
        mish_backward_low(dh_ref, hat1_ref, slope1_ref, scale_ref, 0, steps, sums_ref, 0, d1_ref)
        low_part = nn(w1_ref[one, 0:latent, :], d1_ref[...])
        side_part = nn(tail_ref[...], d1_ref[...])
        if one == 0 and not chained:
            dx_ref[0:latent, :] = low_part
            dx_ref[latent:, :] = side_part
        else:
            held_ref = before_ref if one == 0 else dx_ref
            dx_ref[0:latent, :] = held_ref[0:latent, :] + low_part
            dx_ref[latent:, :] = held_ref[latent:, :] + side_part
        grad_ref[:, 0:latent] = nt(d1_ref[...], xt_ref[0:latent, :]).astype(BF16)
        side_terms = with_vectors(nt(d1_ref[...], xt_ref[latent:, :]), vector_sums(sums_ref, spread_ref, 2), tail_rows)
        grad_ref[:, latent:first_end] = side_terms.astype(BF16)
        for relative, (which, slot) in enumerate(slots):
            start = pl.multiple_of((place_ref[0] ^ relative) * GROUP, GROUP)
            (keep_ref, send_ref)[which][slot, one] = grad_ref[pl.ds(start, GROUP), :]
    loss_ref[...] = functools.reduce(jnp.add, losses)
    for each in copies:
        each.wait()


def backward_kernel(
    steps, scale, after,
    place_ref, xt_ref, soft_ref, h1_ref, hat1_ref, slope1_ref, h2_ref, hat2_ref, slope2_ref, scale_ref,
    w1_ref, w2_ref, dyn_ref, hz_ref, g_ref, dx_ref, *rest,
):
    (tgt_hbm, low_ref, first_ref, side_ref, loss_ref, tgt_ref, rows_ref, spread_ref, tail_ref, pre_ref,
     sums_ref, d1_ref, d2_ref, do_ref, grad_ref, sems) = rest[len(CHUNKS) + after :]
    mine = own_lanes(place_ref)
    order = list(reversed(range(steps)))
    loads = dict(zip(order, load_all([(tgt_hbm.at[step, mine, :], tgt_ref.at[step], sems.at[step]) for step in order])))
    latent = dyn_ref.shape[1]
    here = slice(0, LANES)
    horizon_row = hz_ref[:, mine]
    spread_columns(g_ref[0], g_ref[0], rows_ref, spread_ref)
    tail_rows = w1_ref.shape[0] - latent
    tail_ref[...] = padded_rows(w1_ref[latent:, :], LANES)
    loss = functools.reduce(jnp.add, [each[...] for each in rest[: len(CHUNKS)]])
    side = jnp.zeros((LANES, LANES), F32)
    first_end = latent + LANES
    second_end = first_end + latent
    incoming = None
    pending = []

    def add_terms(at, initial, final):
        terms = (
            (slice(0, first_end), nt(d1_ref[:, at], xt_ref[:, at])),
            (slice(first_end, second_end), nt(d2_ref[:, at], h1_ref[:, at])),
            (slice(second_end, second_end + latent), nt(h2_ref[:, at], do_ref[:, at])),
        )
        for lanes, term in terms:
            term = term if initial else term + grad_ref[:, lanes]
            if not final:
                grad_ref[:, lanes] = term
            elif lanes.start == 0:
                low_ref[:, 0:latent] = term[:, 0:latent].astype(BF16)
                vectors = vector_sums(sums_ref, spread_ref, 2)
                low_ref[:, latent:first_end] = with_vectors(term[:, latent:], vectors, tail_rows).astype(BF16)
            else:
                low_ref[:, lanes] = term.astype(BF16)

    for step in order:
        at = lanes_of(step)
        weight = row_weight(step, steps, scale, horizon_row, place_ref)
        shares = soft_ref[:, lanes_of(step + 1)]
        loads[step].wait()
        residue = shares - jnp.transpose(tgt_ref[step].astype(F32))
        loss = loss + (20.0 / latent) * weight * column_sum(residue * residue)
        grads = residue * ((40.0 / latent) * weight)
        if incoming is not None:
            grads = grads + incoming
        do_ref[:, at] = simplex_back(shares, grads).astype(BF16)
        pre_ref[...] = nn(dyn_ref[...], do_ref[:, at])
        mish_backward(pre_ref, here, hat2_ref, slope2_ref, scale_ref, 1, at, sums_ref, 2, step == order[0], d2_ref)
        pre_ref[...] = nn(w2_ref[...], d2_ref[:, at])
        mish_backward(pre_ref, here, hat1_ref, slope1_ref, scale_ref, 0, at, sums_ref, 0, step == order[0], d1_ref)
        incoming = nn(w1_ref[0:latent, :], d1_ref[:, at]) + dx_ref[0:latent, at]
        side = side + nn(tail_ref[...], d1_ref[:, at]) + dx_ref[latent:, at]
        incoming = incoming.astype(BF16).astype(F32)
        pending.append(step)
        if len(pending) == 2 or step == 0:
            low, high = min(pending), max(pending) + 1
            add_terms(slice(low * LANES, high * LANES), high == steps, low == 0)
            pending = []

    first_ref[...] = incoming.astype(BF16)
    side_ref[...] = side
    loss_ref[...] = loss


def ending_kernel(
    slots, tasks, task_width, acted, observed, chips, sections, after,
    place_ref, low_ref, first_ref, side_ref, loss_ref, soft_ref, ein_ref, eh_ref, ehat_ref, eslope_ref, escale_ref,
    ids_ref, e1_ref, eg_ref, e2_ref, *rest,
):
    keep_ref, send_ref, erows_ref, espread_ref, e1p_ref, epre_ref, esums_ref, ed_ref, egrad_ref = rest[after:]
    mine = own_lanes(place_ref)
    here = slice(0, LANES)
    latent = first_ref.shape[0]
    spread_columns(eg_ref[...], eg_ref[...], erows_ref, espread_ref)
    e1p_ref[...] = padded_rows(e1_ref[...], e1p_ref.shape[0])
    d_enc = simplex_back(soft_ref[:, 0:LANES], first_ref[...].astype(F32)).astype(BF16)
    epre_ref[...] = nn(e2_ref[...], d_enc)
    mish_backward(epre_ref, here, ehat_ref, eslope_ref, escale_ref, 0, here, esums_ref, 0, True, ed_ref)
    side_enc = nn(e1p_ref[...], ed_ref[...])
    enc_width = epre_ref.shape[0]
    half = GROUP // 2
    groups = enc_width // half
    egrad_ref[:, 0:half, :] = nt(eh_ref[...], d_enc).reshape(groups, half, latent)
    enc_first = nt(ed_ref[...], ein_ref[...])
    egrad_ref[:, half:, 0:LANES] = enc_first[:, 0:LANES].reshape(groups, half, LANES)
    second_lanes = with_vectors(enc_first[:, LANES : 2 * LANES], vector_sums(esums_ref, espread_ref, 1), LANES - 2)
    egrad_ref[:, half:, LANES : 2 * LANES] = second_lanes.reshape(groups, half, LANES)
    egrad_ref[:, half:, 2 * LANES :] = jnp.zeros((groups, half, latent - 2 * LANES), F32)

    kinds = lax.broadcasted_iota(jnp.int32, (tasks, LANES), 0)
    onehot = (kinds == ids_ref[:, mine]).astype(F32)
    over_lanes = (((1,), (1,)), ((), ()))
    highest = lax.Precision.HIGHEST
    side_terms = lax.dot_general(onehot, side_ref[...], over_lanes, precision=highest, preferred_element_type=F32)
    enc_terms = lax.dot_general(onehot, side_enc, over_lanes, precision=highest, preferred_element_type=F32)
    table = pltpu.roll(side_terms, LANES - acted, 1)
    table = table + pltpu.roll(enc_terms, enc_terms.shape[1] - observed, 1)[:, 0:LANES]
    lane = lax.broadcasted_iota(jnp.int32, table.shape, 1)
    table = jnp.where(lane < task_width, table, 0.0)
    table = jnp.where((lane == LANES - 1) & (kinds == 0), jnp.sum(loss_ref[...], axis=1, keepdims=True), table)
    table_rows = [table[start : start + GROUP] for start in range(0, tasks, GROUP)]
    table_block = jnp.concatenate(table_rows, axis=1).astype(BF16)
    width = low_ref.shape[1]
    for relative, (which, slot) in enumerate(slots):
        dest = place_ref[0] ^ relative
        start = pl.multiple_of(dest * GROUP, GROUP)
        out_ref = (keep_ref, send_ref)[which]
        out_ref[slot, :, 0:width] = low_ref[pl.ds(start, GROUP), :]
        out_ref[slot, :, width : width + latent] = egrad_ref[dest].astype(BF16)
        out_ref[slot, :, width + latent :] = table_block


def final_kernel(tasks, task_width, enc_in, bins, net_in, counts, *refs):
    outs = refs[-12:]
    (loss_ref, table_ref, e1_ref, eg_ref, es_ref, e2_ref, first_ref, second_ref, gain_ref, shift_ref, dyn_ref, head_ref) = outs
    refs = refs[:-12]
    tail_refs, refs = refs[: counts[0]], refs[counts[0] :]
    latent = second_ref.shape[2]
    first_end = latent + LANES
    second_end = first_end + latent

    def put_net(net, value):
        first_ref[net] = value[:, 0:net_in]
        second_ref[net] = value[:, first_end:second_end]
        turned = jnp.transpose(value[:, latent:first_end])
        for layer in range(2):
            row = net_in - latent + 2 * layer
            gain_ref[net, layer : layer + 1, :] = turned[row : row + 1, :]
            shift_ref[net, layer : layer + 1, :] = turned[row + 1 : row + 2, :]

    tail = functools.reduce(jnp.add, [ref[...].astype(F32) for ref in tail_refs])
    put_net(0, tail)
    dyn_ref[...] = tail[:, second_end : second_end + latent]
    enc = tail[:, second_end + latent : second_end + 2 * latent]
    half = GROUP // 2
    e2_ref[...] = 0.3 * enc[0:half, :]
    e1_ref[...] = 0.3 * enc[half:, 0:enc_in]
    turned = 0.3 * jnp.transpose(enc[half:, LANES : 2 * LANES])
    eg_ref[...] = turned[LANES - 2 : LANES - 1, :]
    es_ref[...] = turned[LANES - 1 : LANES, :]
    table = tail[:, second_end + 2 * latent :]
    loss_ref[...] = table[0:1, LANES - 1 : LANES]
    for place in range(tasks // GROUP):
        table_ref[place * GROUP : (place + 1) * GROUP, :] = table[:, place * LANES : place * LANES + task_width]
    net = 1
    for count, parts in zip(CHUNKS, counts[1:]):
        chunk_refs, refs = refs[:parts], refs[parts:]
        for one in range(count):
            each = [ref[one].astype(F32) for ref in chunk_refs]
            value = functools.reduce(jnp.add, each)
            put_net(net, value)
            head_ref[net - 1] = value[:, second_end : second_end + bins]
            net += 1


def swap(value, axis, distance):
    count = lax.axis_size(axis)
    return lax.ppermute(value, axis, [(place, place ^ distance) for place in range(count)])


def exchange(parts, axis, scale):
    total = parts[0].astype(F32)
    for distance in range(1, len(parts)):
        total = total + swap(parts[distance], axis, distance * scale).astype(F32)
    return total


def scatter_plain(packed, chips, sections):
    held = packed.reshape((sections, chips, CORES) + packed.shape[1:])
    batch_no = lax.axis_index("batch")
    places = (
        ("batch", 1, CORES, 2, batch_no % CORES),
        ("batch", CORES, chips, 1, batch_no // CORES),
        ("section", 1, sections, 0, lax.axis_index("section")),
    )
    for axis, scale, count, dim, mine in places:
        parts = [lax.dynamic_index_in_dim(held, mine ^ other, dim, keepdims=False) for other in range(count)]
        held = exchange(parts, axis, scale)
        held = held.astype(BF16) if dim else held
    return held


def on_device(
    observations,
    actions,
    targets,
    task_ids,
    horizons,
    reward_bins,
    value_bins,
    task_table,
    enc_first,
    enc_gain,
    enc_shift,
    enc_second,
    net_first,
    net_second,
    net_gain,
    net_shift,
    dyn_out,
    head_out,
):
    sections = lax.axis_size("section")
    batches = lax.axis_size("batch")
    section_no = lax.axis_index("section")
    chips = batches // CORES
    devices = sections * batches
    steps, rows_all, acted = actions.shape
    observed = observations.shape[1]
    rows = rows_all // sections
    latent = dyn_out.shape[1]
    hidden = dyn_out.shape[0]
    tasks, task_width = task_table.shape
    heads, _, bins = head_out.shape
    nets, net_in, _ = net_first.shape
    enc_in, enc_width = enc_first.shape
    wide = steps * LANES
    scale = 1.0 / (rows_all * batches * steps)
    groups = hidden // GROUP
    in_place = hidden // devices == GROUP
    start = section_no * rows
    block_no = start // LANES
    first_lane = start - block_no * LANES
    me = section_no * batches + lax.axis_index("batch") if in_place else jnp.int32(0)
    place = jnp.stack([me, block_no, first_lane, first_lane + rows]).astype(jnp.int32)
    if in_place:
        slots = tuple(
            (relative % CORES, (relative // CORES) % chips * sections + relative // batches) for relative in range(groups)
        )
    else:
        slots = tuple((relative // (groups // 2), relative % (groups // 2)) for relative in range(groups))
    half_slots = groups // 2
    shape_of = jax.ShapeDtypeStruct
    smem = pl.BlockSpec(memory_space=pltpu.SMEM)
    local = pl.BlockSpec(memory_space=pltpu.VMEM)
    far = pl.BlockSpec(memory_space=pltpu.HBM)
    anywhere = pl.BlockSpec(memory_space=pl.ANY)
    first_far, second_far, dyn_far, targets_far = [
        pltpu.with_memory_space_constraint(array, pltpu.HBM) for array in (net_first, net_second, dyn_out, targets)
    ]
    vmem = pltpu.VMEM
    dmas = pltpu.SemaphoreType.DMA

    def params(mebibytes):
        return pltpu.CompilerParams(vmem_limit_bytes=mebibytes * 1024 * 1024)

    def cost(flops, moved):
        return pl.CostEstimate(flops=flops, bytes_accessed=moved, transcendentals=0)

    ids_row = task_ids.reshape(1, rows_all)
    horizon_row = horizons.reshape(1, rows_all)
    eg_row = enc_gain.reshape(1, enc_width)
    es_row = enc_shift.reshape(1, enc_width)
    head_turned = head_out.transpose(0, 2, 1)
    low = lambda lanes: shape_of((hidden, lanes), BF16)
    forward_shapes = (
        shape_of((latent + LANES, wide), BF16),
        shape_of((latent, wide + LANES), F32),
        low(wide), low(wide), low(wide), low(wide), low(wide), low(wide),
        shape_of((8, wide), F32),
        shape_of((2 * LANES, LANES), BF16),
        shape_of((enc_width, LANES), BF16),
        shape_of((enc_width, LANES), BF16),
        shape_of((enc_width, LANES), BF16),
        shape_of((8, LANES), F32),
        shape_of((net_in, hidden), BF16),
        shape_of((hidden, hidden), BF16),
        shape_of((hidden, latent), BF16),
    )

    def weight_shapes(count):
        return (shape_of((count, net_in, hidden), BF16), shape_of((count, hidden, hidden), BF16))

    early = [
        pltpu.with_memory_space_constraint(array, pltpu.HBM)
        for array in (
            observations.T, actions.transpose(0, 2, 1), ids_row, task_table, enc_first, eg_row, es_row, enc_second,
            net_gain, net_shift,
        )
    ]
    made = pl.pallas_call(
        functools.partial(forward_kernel, steps, CHUNKS[0]),
        out_shape=forward_shapes + weight_shapes(CHUNKS[0]),
        in_specs=[smem] + [far] * 13,
        out_specs=[local] * (len(forward_shapes) + 2),
        scratch_shapes=[
            vmem((8, hidden), F32),
            vmem((4, hidden, LANES), F32),
            vmem((8, enc_width), F32),
            vmem((2, enc_width, LANES), F32),
            vmem((tasks, 2 * LANES), F32),
            vmem((LANES, LANES), F32),
            vmem((2 * LANES, enc_width), BF16),
            vmem((hidden, latent + LANES), BF16),
            vmem((hidden, hidden), BF16),
            vmem((latent, hidden), BF16),
            vmem((hidden, LANES), F32),
            vmem((enc_width, LANES), F32),
            *[vmem(each.shape, each.dtype) for each in early],
            dmas((5,)),
            dmas((len(early),)),
        ],
        compiler_params=params(VMEM_A),
        cost_estimate=cost(10_000_000_000, 8_000_000),
        name="forward_chain",
    )(
        place, *early, first_far, second_far, dyn_far,
    )
    saved, weights = made[:-2], made[-2:]
    xt = saved[0]
    head_width = latent + LANES + hidden + LANES

    def run_heads(base, count, ahead, weights, before, after):
        pack_shape = shape_of((half_slots, count, GROUP, head_width), BF16)
        dx_shape = shape_of((latent + LANES, wide), F32)
        out_shapes = (pack_shape, pack_shape, dx_shape, shape_of((1, LANES), F32))
        args = [place, xt, *weights, head_turned, net_gain, net_shift, reward_bins, value_bins, horizon_row]
        specs = [smem] + [local] * 9
        aliases = {}
        if before is not None:
            aliases = {len(args): 2}
            args.append(before)
            specs.append(local)
        args += after
        specs += [anywhere] * len(after)
        if ahead:
            args += [first_far, second_far]
            specs += [far, far]
            out_shapes += weight_shapes(ahead)
        low_wide = vmem((hidden, wide), BF16)
        scratch = [
            vmem((8, hidden), F32),
            vmem((4, hidden, LANES), F32),
            vmem((hidden, latent + LANES), BF16),
            vmem((hidden, hidden), BF16),
            vmem((LANES, hidden), BF16),
            vmem((hidden, LANES), BF16),
            vmem((LANES, hidden), BF16),
            vmem((hidden, wide), F32),
            vmem((LANES, wide), F32),
        ]
        scratch += [low_wide] * 6
        scratch += [vmem((8, wide), F32), vmem((4, hidden, LANES), F32)]
        scratch += [low_wide] * 3
        scratch += [vmem((LANES, wide), BF16), vmem((hidden, head_width), BF16)]
        if ahead:
            scratch.append(dmas((2,)))
        return pl.pallas_call(
            functools.partial(
                heads_kernel, steps, scale, slots, base, count, ahead, heads, bins, before is not None, len(after)
            ),
            out_shape=out_shapes,
            in_specs=specs,
            out_specs=[local] * len(out_shapes),
            scratch_shapes=scratch,
            input_output_aliases=aliases,
            compiler_params=params(VMEM_B),
            cost_estimate=cost(count * 10_000_000_000, count * 4_000_000),
            name=f"heads_{base}",
        )(*args)

    def core_swap(keep, send):
        return [keep, swap(send, "batch", 1)]

    def core_sum(parts, token):
        return added([each.reshape((chips, sections) + each.shape[1:]) for each in parts], chips, token)

    def chip_swap(held):
        return [held[0]] + [swap(held[place], "batch", CORES * place) for place in range(1, chips)]

    def section_swap(held):
        return [held[0]] + [swap(held[place], "section", place) for place in range(1, sections)]

    def added(parts, pieces, *tokens):
        piece = parts[0].shape[1:]
        out_shapes = [shape_of(piece, BF16)] * pieces

        def add_kernel(*refs):
            refs = refs[len(tokens) :]
            for place in range(pieces):
                each = [ref[place].astype(F32) for ref in refs[: len(parts)]]
                refs[len(parts) + place][...] = functools.reduce(jnp.add, each).astype(BF16)

        return pl.pallas_call(
            add_kernel,
            out_shape=out_shapes,
            in_specs=[anywhere] * len(tokens) + [local] * len(parts),
            out_specs=[local] * pieces,
            compiler_params=params(VMEM_SUM),
            cost_estimate=cost(1_000_000, 2_000_000),
            name="added",
        )(*tokens, *parts)

    def total(parts, token):
        def total_kernel(token_ref, *refs):
            refs[-1][...] = functools.reduce(jnp.add, [ref[...].astype(F32) for ref in refs[:-1]])

        return pl.pallas_call(
            total_kernel,
            out_shape=shape_of(parts[0].shape, F32),
            in_specs=[anywhere] + [local] * len(parts),
            out_specs=local,
            compiler_params=params(VMEM_SUM),
            cost_estimate=cost(1_000_000, 2_000_000),
            name="total",
        )(token, *parts)

    packs, loss_parts = [], []
    dx = None
    base = 0
    after_core, after_chip, core_parts, chip_parts, ends = {}, {}, {}, {}, {}
    for number, count in enumerate(CHUNKS):
        ahead = CHUNKS[number + 1] if number + 1 < len(CHUNKS) else 0
        after = []
        if in_place and number >= 2:
            after = after_core[number - 2][:1]
        if in_place and number >= 1:
            core_parts[number - 1] = core_swap(*packs[number - 1])
        if in_place and number >= 2:
            chip_parts[number - 2] = chip_swap(after_core[number - 2])
        result = run_heads(base, count, ahead, weights, dx, after)
        if in_place and number >= 1:
            after_core[number - 1] = core_sum(core_parts[number - 1], result[3])
        if in_place and number >= 2:
            after_chip[number - 2] = added(chip_parts[number - 2], sections, result[3])
        keep, send, dx, loss = result[:4]
        weights = result[4:]
        packs.append((keep, send))
        loss_parts.append(loss)
        base += count
    after = []
    last = len(CHUNKS) - 1
    if in_place:
        after = after_core[last - 1][:1] + after_chip[last - 2][:1]
    net_width = latent + LANES + hidden + latent
    tail_width = net_width + latent + tasks // GROUP * LANES
    tail_shape = shape_of((half_slots, GROUP, tail_width), BF16)
    if in_place:
        core_parts[last] = core_swap(*packs[last])
        chip_parts[last - 1] = chip_swap(after_core[last - 1])
        ends[last - 2] = section_swap(after_chip[last - 2])
    chain_shapes = (
        shape_of((hidden, net_width), BF16),
        shape_of((latent, LANES), BF16),
        shape_of((LANES, LANES), F32),
        shape_of((1, LANES), F32),
    )
    chain_inputs = saved[:9] + saved[14:]
    ending = pl.pallas_call(
        functools.partial(backward_kernel, steps, scale, len(after)),
        out_shape=chain_shapes,
        in_specs=[smem] + [local] * (len(chain_inputs) + 3 + len(CHUNKS)) + [anywhere] * len(after) + [far],
        out_specs=[local] * len(chain_shapes),
        scratch_shapes=[
            vmem((steps, LANES, latent), BF16),
            vmem((8, hidden), F32),
            vmem((4, hidden, LANES), F32),
            vmem((LANES, hidden), BF16),
            vmem((hidden, LANES), F32),
            vmem((4, hidden, LANES), F32),
            vmem((hidden, wide), BF16),
            vmem((hidden, wide), BF16),
            vmem((latent, wide), BF16),
            vmem((hidden, net_width), F32),
            dmas((steps,)),
        ],
        compiler_params=params(VMEM_C),
        cost_estimate=cost(15_000_000_000, 12_000_000),
        name="backward_chain",
    )(place, *chain_inputs, horizon_row, net_gain, dx, *loss_parts, *after, targets_far)
    after = []
    if in_place:
        after_core[last] = core_sum(core_parts[last], ending[3])
        after_chip[last - 1] = added(chip_parts[last - 1], sections, ending[3])
        ends[last - 2] = [total(ends[last - 2], ending[3])]
        after = [after_core[last][0], after_chip[last - 1][0], *ends[last - 2]]
    keep, send = pl.pallas_call(
        functools.partial(ending_kernel, slots, tasks, task_width, acted, observed, chips, sections, len(after)),
        out_shape=(tail_shape, tail_shape),
        in_specs=[smem] + [local] * 14 + [anywhere] * len(after),
        out_specs=[local, local],
        scratch_shapes=[
            vmem((8, enc_width), F32),
            vmem((2, enc_width, LANES), F32),
            vmem((2 * LANES, enc_width), BF16),
            vmem((enc_width, LANES), F32),
            vmem((2, enc_width, LANES), F32),
            vmem((enc_width, LANES), BF16),
            vmem((groups, GROUP, latent), F32),
        ],
        compiler_params=params(VMEM_SUM),
        cost_estimate=cost(1_000_000_000, 4_000_000),
        name="ending",
    )(place, *ending, saved[1], *saved[9:14], ids_row, enc_first, eg_row, enc_second, *after)

    if in_place:
        chip_parts[last] = chip_swap(after_core[last])
        ends[last - 1] = section_swap(after_chip[last - 1])
        tail = chip_swap(core_sum(core_swap(keep, send), keep))
        after_chip[last] = added(chip_parts[last], sections, tail[0])
        ends[last] = section_swap(after_chip[last])
        tail = section_swap(added(tail, sections, after_chip[last][0]))
        counts = [len(tail)] + [len(ends[number]) for number in range(len(CHUNKS))]
        ends = [part for number in range(len(CHUNKS)) for part in ends[number]]
        each = GROUP // 2
        out_shapes = (
            shape_of((1, 1), F32),
            shape_of((tasks, task_width), F32),
            shape_of((each, enc_in), F32),
            shape_of((1, each), F32),
            shape_of((1, each), F32),
            shape_of((each, latent), F32),
            shape_of((nets, GROUP, net_in), F32),
            shape_of((nets, GROUP, hidden), F32),
            shape_of((nets, 2, GROUP), F32),
            shape_of((nets, 2, GROUP), F32),
            shape_of((GROUP, latent), F32),
            shape_of((heads, GROUP, bins), F32),
        )
        outs = list(pl.pallas_call(
            functools.partial(final_kernel, tasks, task_width, enc_in, bins, net_in, counts),
            out_shape=out_shapes,
            in_specs=[local] * sum(counts),
            out_specs=[local] * len(out_shapes),
            compiler_params=params(VMEM_SUM),
            cost_estimate=cost(1_000_000, 4_000_000),
            name="last_sums",
        )(*tail, *ends))
        outs[0] = outs[0].reshape(())
        outs[2] = outs[2].T
        outs[3], outs[4] = outs[3].reshape(each), outs[4].reshape(each)
        outs[6] = outs[6].transpose(0, 2, 1)
        outs[7] = outs[7].transpose(0, 2, 1)
        return tuple(outs)

    def scattered(keep, send):
        mine = hidden // devices
        packed = jnp.concatenate([keep, send], axis=0)
        middle = packed.shape[1:-2]
        packed = packed.reshape((groups,) + middle + (GROUP // mine, mine, packed.shape[-1]))
        packed = jnp.moveaxis(packed, -3, 1).reshape((devices,) + middle + (mine, packed.shape[-1]))
        return scatter_plain(packed, chips, sections)

    head_sum = jnp.concatenate([scattered(*pack) for pack in packs], axis=0)
    enc_each = enc_width // devices
    net_sum = scattered(keep[:, :, 0:net_width], send[:, :, 0:net_width])
    rest = jnp.concatenate([keep, send], axis=0)
    enc_all = rest[:, :, net_width : net_width + latent].reshape(groups, 2, enc_width // groups, latent)
    enc_all = enc_all.transpose(0, 2, 1, 3).reshape(devices, enc_each, 2, latent)
    enc_sum = scatter_plain(enc_all, chips, sections)
    enc_sum = enc_sum.transpose(1, 0, 2).reshape(2 * enc_each, latent)
    table_sum = lax.psum(rest[0, :, net_width + latent :].astype(F32), ("section", "batch"))
    first_end = latent + LANES
    net_row = jnp.concatenate([net_sum[:, 0 : first_end + hidden], jnp.zeros_like(net_sum[:, 0:LANES])], axis=1)
    sums = jnp.concatenate([net_row[None], head_sum], axis=0)
    vectors = sums[:, :, net_in : net_in + 4].transpose(0, 2, 1)
    table = table_sum.reshape(GROUP, tasks // GROUP, LANES).transpose(1, 0, 2).reshape(tasks, LANES)
    enc_rows = enc_sum[enc_each:]
    return (
        table[0, LANES - 1],
        table[:, 0:task_width],
        0.3 * enc_rows[:, 0:enc_in].T,
        0.3 * enc_rows[:, 2 * LANES - 2],
        0.3 * enc_rows[:, 2 * LANES - 1],
        0.3 * enc_sum[0:enc_each],
        sums[:, :, 0:net_in].transpose(0, 2, 1),
        sums[:, :, first_end : first_end + hidden].transpose(0, 2, 1),
        vectors[:, 0::2],
        vectors[:, 1::2],
        net_sum[:, first_end + hidden :],
        head_sum[:, :, first_end + hidden : first_end + hidden + bins],
    )


def solution(mesh):
    both = ("section", "batch")
    return jax.shard_map(
        on_device,
        mesh=mesh,
        in_specs=(
            P("batch", None),
            P(None, "batch", None),
            P(None, "batch", None),
            P("batch"),
            P("batch"),
            P(None, "batch"),
            P(None, "batch"),
        )
        + (P(),) * 11,
        out_specs=(
            P(),
            P(),
            P(None, both),
            P(both),
            P(both),
            P(both, None),
            P(None, None, both),
            P(None, None, both),
            P(None, None, both),
            P(None, None, both),
            P(both, None),
            P(None, both, None),
        ),
        check_vma=False,
    )
```

```python
import functools

import jax
import jax.numpy as jnp
from jax import lax
from jax.experimental import pallas as pl
from jax.experimental.pallas import tpu as pltpu
from jax.sharding import PartitionSpec as P

CORES = 2
LANES = 128
GROUP = 16
BF16 = jnp.bfloat16
F32 = jnp.float32
VMEM_A = 16
VMEM_B = 20
VMEM_SUM = 6
VMEM_C = 20


def nn(left, right):
    return lax.dot_general(left, right, (((1,), (0,)), ((), ())), preferred_element_type=F32)


def nt(left, right):
    return lax.dot_general(left, right, (((1,), (1,)), ((), ())), preferred_element_type=F32)


def tn(left, right):
    return lax.dot_general(left, right, (((0,), (0,)), ((), ())), preferred_element_type=F32)


def column_sum(value):
    grouped = value.reshape(value.shape[0] // 8, 8, value.shape[1])
    return jnp.sum(jnp.sum(grouped, axis=0), axis=0, keepdims=True)


def slabs(features, size=64):
    return [slice(start, start + size) for start in range(0, features, size)]


def lanes_of(step):
    return slice(step * LANES, (step + 1) * LANES)


def spread_columns(gain_rows, shift_rows, rows_ref, spread_ref):
    count = gain_rows.shape[0]
    rows_ref[...] = jnp.zeros_like(rows_ref)
    rows_ref[0:count, :] = gain_rows
    rows_ref[count : 2 * count, :] = shift_rows
    turned = jnp.transpose(rows_ref[...])
    for place in range(2 * count):
        spread_ref[place] = jnp.broadcast_to(turned[:, place : place + 1], spread_ref.shape[1:])


def mish_forward(pre_ref, pre_at, gain_ref, shift_ref, hid_ref, hat_ref, slope_ref, scale_ref, scale_row, at):
    features = pre_ref.shape[0]
    row_mean = column_sum(pre_ref[:, pre_at]) * (1.0 / features)
    centred = pre_ref[:, pre_at] - row_mean
    spread = column_sum(centred * centred) * (1.0 / features)
    scale = lax.rsqrt(spread + 1e-05)
    scale_ref[scale_row : scale_row + 1, at] = scale
    for part in slabs(features):
        hat = (pre_ref[part, pre_at] - row_mean) * scale
        normed = hat * gain_ref[part, :] + shift_ref[part, :]
        power = jnp.exp(normed)
        top = power * (power + 2.0)
        inverse = pl.reciprocal(top + 2.0, approx=True)
        ratio = top * inverse
        hid_ref[part, at] = (normed * ratio).astype(BF16)
        tilt = power * inverse
        slope = ratio + normed * (4.0 * (tilt * (tilt + inverse)))
        slope_ref[part, at] = (slope * gain_ref[part, :]).astype(BF16)
        hat_ref[part, at] = hat.astype(BF16)


def mish_backward(grad_ref, grad_at, hat_ref, slope_ref, scale_ref, scale_row, at, sums_ref, sums_at, first, out_ref):
    features = grad_ref.shape[0]
    total_one = jnp.zeros((8, LANES), F32)
    total_two = jnp.zeros((8, LANES), F32)
    for part in slabs(features):
        term = grad_ref[part, grad_at] * slope_ref[part, at].astype(F32)
        grad_ref[part, grad_at] = term
        crossed = term * hat_ref[part, at].astype(F32)
        groups = (term.shape[0] // 8, 8, LANES)
        total_one = total_one + jnp.sum(term.reshape(groups), axis=0)
        total_two = total_two + jnp.sum(crossed.reshape(groups), axis=0)
        if first:
            sums_ref[sums_at, part, :] = term
            sums_ref[sums_at + 1, part, :] = crossed
        else:
            sums_ref[sums_at, part, :] += term
            sums_ref[sums_at + 1, part, :] += crossed
    mean_one = jnp.sum(total_one, axis=0, keepdims=True) * (1.0 / features)
    mean_two = jnp.sum(total_two, axis=0, keepdims=True) * (1.0 / features)
    scale = scale_ref[scale_row : scale_row + 1, at]
    for part in slabs(features):
        rest = grad_ref[part, grad_at] - mean_one - hat_ref[part, at].astype(F32) * mean_two
        out_ref[part, at] = (rest * scale).astype(BF16)


def mish_forward_low(pre_ref, gain_ref, shift_ref, hid_ref, hat_ref, slope_ref, scale_ref, scale_row, at):
    features = pre_ref.shape[0]
    row_mean = column_sum(pre_ref[:, at]) * (1.0 / features)
    centred = pre_ref[:, at] - row_mean
    spread = column_sum(centred * centred) * (1.0 / features)
    scale = lax.rsqrt(spread + 1e-05)
    scale_ref[scale_row : scale_row + 1, at] = scale
    for part in slabs(features):
        hat = (pre_ref[part, at] - row_mean) * scale
        normed = (hat * gain_ref[part, :] + shift_ref[part, :]).astype(BF16)
        hat_ref[part, at] = hat.astype(BF16)
        power = jnp.exp(normed)
        top = power * (power + 2.0)
        inverse = pl.reciprocal(top + 2.0, approx=True)
        ratio = top * inverse
        hid_ref[part, at] = normed * ratio
        tilt = power * inverse
        slope = ratio + (4.0 * normed) * (tilt * (tilt + inverse))
        slope_ref[part, at] = slope * gain_ref[part, :].astype(BF16)


def mish_backward_low(grad_ref, hat_ref, slope_ref, scale_ref, scale_row, steps, sums_ref, sums_at, out_ref):
    features = grad_ref.shape[0]
    rows = []
    for step in range(steps):
        at = lanes_of(step)
        total_one = jnp.zeros((16, LANES), F32)
        total_two = jnp.zeros((16, LANES), F32)
        for part in slabs(features):
            term = grad_ref[part, at] * slope_ref[part, at]
            crossed = term * hat_ref[part, at]
            grad_ref[part, at] = term
            groups = (term.shape[0] // 16, 16, LANES)
            term = term.reshape(groups)
            crossed = crossed.reshape(groups)
            total_one = total_one + functools.reduce(jnp.add, [term[k] for k in range(groups[0])]).astype(F32)
            total_two = total_two + functools.reduce(jnp.add, [crossed[k] for k in range(groups[0])]).astype(F32)
        scale = scale_ref[scale_row : scale_row + 1, at]
        mean_one = jnp.sum(total_one, axis=0, keepdims=True) * (1.0 / features)
        mean_two = jnp.sum(total_two, axis=0, keepdims=True) * (1.0 / features)
        rows.append((mean_one.astype(BF16), mean_two.astype(BF16), scale.astype(BF16)))
    for part in slabs(features):
        sum_one, sum_two = None, None
        for step, (mean_one, mean_two, scale) in enumerate(rows):
            at = lanes_of(step)
            term = grad_ref[part, at]
            hat = hat_ref[part, at]
            out_ref[part, at] = (term - mean_one - hat * mean_two) * scale
            crossed = term * hat
            sum_one = term if sum_one is None else sum_one + term
            sum_two = crossed if sum_two is None else sum_two + crossed
        sums_ref[sums_at, part, :] = sum_one.astype(F32)
        sums_ref[sums_at + 1, part, :] = sum_two.astype(F32)


def simplex(values):
    grouped = values.reshape(values.shape[0] // 8, 8, values.shape[1])
    powers = jnp.exp(grouped - jnp.max(grouped, axis=1, keepdims=True))
    shares = powers / jnp.sum(powers, axis=1, keepdims=True)
    return shares.reshape(values.shape)


def simplex_back(shares, grads):
    grouped = (shares.shape[0] // 8, 8, shares.shape[1])
    crossed = jnp.sum((shares * grads).reshape(grouped), axis=1, keepdims=True)
    return (shares.reshape(grouped) * (grads.reshape(grouped) - crossed)).reshape(shares.shape)


def row_weight(step, steps, scale, horizon_row, place_ref):
    lane = lax.broadcasted_iota(jnp.int32, (1, LANES), 1)
    mine = (lane >= place_ref[2]) & (lane < place_ref[3]) & (horizon_row > step)
    return jnp.where(mine, F32(scale * 0.5 ** (step / (steps - 1))), 0.0)


def padded_rows(value, rows):
    zeros = jnp.zeros((rows - value.shape[0], value.shape[1]), F32)
    return jnp.concatenate([value.astype(F32), zeros], axis=0).astype(BF16)


def transpose_into(out_ref, source_ref, rows):
    for start in range(0, rows, LANES):
        out_ref[:, start : start + LANES] = jnp.transpose(source_ref[start : start + LANES, :])


def vector_sums(sums_ref, gains_ref, layers):
    vectors = []
    for layer in range(layers):
        inverse = 1.0 / gains_ref[layer]
        vectors.append(jnp.sum(sums_ref[2 * layer + 1] * inverse, axis=1, keepdims=True))
        vectors.append(jnp.sum(sums_ref[2 * layer] * inverse, axis=1, keepdims=True))
    return vectors


def own_lanes(place_ref):
    return pl.ds(pl.multiple_of(place_ref[1] * LANES, LANES), LANES)


def load_all(copies):
    made = [pltpu.make_async_copy(*each) for each in copies]
    for each in made:
        each.start()
    return made


def with_vectors(value, vectors, first_lane):
    lane = lax.broadcasted_iota(jnp.int32, value.shape, 1)
    for place, vector in enumerate(vectors):
        value = jnp.where(lane == first_lane + place, vector, value)
    return value


def forward_kernel(
    steps,
    place_ref, obs_hbm, act_hbm, ids_hbm, table_hbm, e1_hbm, eg_hbm, es_hbm, e2_hbm, g_hbm, s_hbm,
    w1_hbm, w2_hbm, dyn_hbm,
    xt_ref, soft_ref, h1_ref, hat1_ref, slope1_ref, h2_ref, hat2_ref, slope2_ref, scale_ref,
    ein_ref, eh_ref, ehat_ref, eslope_ref, escale_ref,
    w1_ref, w2_ref, dyn_ref, next1_ref, next2_ref,
    rows_ref, spread_ref, erows_ref, espread_ref, wide_ref, tall_ref, e1p_ref, w1t_ref, w2t_ref, dynt_ref, pre_ref, epre_ref,
    obs_ref, act_ref, ids_ref, table_ref, e1_ref, eg_ref, es_ref, e2_ref, g_ref, s_ref,
    sems, early_sems,
):
    early = load_all([
        (table_hbm, table_ref, early_sems.at[0]),
        (ids_hbm, ids_ref, early_sems.at[1]),
        (obs_hbm, obs_ref, early_sems.at[2]),
        (e1_hbm, e1_ref, early_sems.at[3]),
        (eg_hbm, eg_ref, early_sems.at[4]),
        (es_hbm, es_ref, early_sems.at[5]),
        (e2_hbm, e2_ref, early_sems.at[6]),
        (act_hbm, act_ref, early_sems.at[7]),
        (g_hbm, g_ref, early_sems.at[8]),
        (s_hbm, s_ref, early_sems.at[9]),
    ])
    first, second, third, fourth, fifth = load_all([
        (w1_hbm.at[0], w1_ref, sems.at[0]),
        (w2_hbm.at[0], w2_ref, sems.at[1]),
        (dyn_hbm, dyn_ref, sems.at[2]),
        (w1_hbm.at[1], next1_ref, sems.at[3]),
        (w2_hbm.at[1], next2_ref, sems.at[4]),
    ])
    latent = dyn_ref.shape[1]
    tasks, task_width = table_ref.shape
    observed = obs_ref.shape[0]
    acted = act_ref.shape[1]
    mine = own_lanes(place_ref)
    for each in early:
        each.wait()
    spread_columns(eg_ref[...], es_ref[...], erows_ref, espread_ref)
    kinds = lax.broadcasted_iota(jnp.int32, (tasks, LANES), 0)
    onehot = (kinds == ids_ref[:, mine]).astype(F32).astype(BF16)
    wide_ref[...] = jnp.zeros_like(wide_ref)
    wide_ref[:, 0:task_width] = table_ref[...].astype(F32)
    table_tail = pltpu.roll(wide_ref[:, 0:LANES], acted, 1).astype(BF16)
    table_enc = pltpu.roll(wide_ref[...], observed, 1).astype(BF16)
    aux = tn(table_tail, onehot)
    tall_ref[...] = jnp.zeros_like(tall_ref)
    tall_ref[0:observed, :] = obs_ref[:, mine].astype(F32)
    ein = tn(table_enc, onehot)
    ein_ref[0:LANES, :] = (ein[0:LANES] + tall_ref[...]).astype(BF16)
    ein_ref[LANES:, :] = ein[LANES:].astype(BF16)
    e1p_ref[...] = padded_rows(e1_ref[...], e1p_ref.shape[0])
    epre_ref[...] = tn(e1p_ref[...], ein_ref[...])
    here = slice(0, LANES)
    mish_forward(epre_ref, here, espread_ref.at[0], espread_ref.at[1], eh_ref, ehat_ref, eslope_ref, escale_ref, 0, here)
    shares = simplex(tn(e2_ref[...], eh_ref[...]))
    soft_ref[:, 0:LANES] = shares
    xt_ref[0:latent, 0:LANES] = shares.astype(BF16)
    spread_columns(g_ref[0], s_ref[0], rows_ref, spread_ref)
    for step in range(steps):
        tall_ref[...] = jnp.zeros_like(tall_ref)
        tall_ref[0:acted, :] = act_ref[step, :, mine].astype(F32)
        xt_ref[latent:, lanes_of(step)] = (aux + tall_ref[...]).astype(BF16)
    first.wait()
    transpose_into(w1t_ref, w1_ref, latent)
    w1t_ref[:, latent:] = jnp.transpose(padded_rows(w1_ref[latent:, :], LANES))
    second.wait()
    transpose_into(w2t_ref, w2_ref, latent)
    third.wait()
    transpose_into(dynt_ref, dyn_ref, latent)
    for step in range(steps):
        at = lanes_of(step)
        pre_ref[...] = nn(w1t_ref[...], xt_ref[:, at])
        mish_forward(pre_ref, here, spread_ref.at[0], spread_ref.at[2], h1_ref, hat1_ref, slope1_ref, scale_ref, 0, at)
        pre_ref[...] = nn(w2t_ref[...], h1_ref[:, at])
        mish_forward(pre_ref, here, spread_ref.at[1], spread_ref.at[3], h2_ref, hat2_ref, slope2_ref, scale_ref, 1, at)
        shares = simplex(nn(dynt_ref[...], h2_ref[:, at]))
        soft_ref[:, lanes_of(step + 1)] = shares
        if step + 1 < steps:
            xt_ref[0:latent, lanes_of(step + 1)] = shares.astype(BF16)
    fourth.wait()
    fifth.wait()


def heads_kernel(steps, scale, slots, head, ahead, heads, bins, chained, after, *refs):
    refs = list(refs)
    place_ref, xt_ref, w1_ref, w2_ref, ho_ref, g_ref, s_ref, rb_ref, vb_ref, hz_ref = refs[:10]
    refs = refs[10:]
    before_ref = refs.pop(0) if chained else None
    refs = refs[after:]
    w1_hbm, w2_hbm = refs[:2] if ahead else (None, None)
    refs = refs[2:] if ahead else refs
    keep_ref, send_ref, dx_ref, loss_ref = refs[:4]
    refs = refs[4:]
    copies = []
    if ahead:
        next1_ref, next2_ref, sems = refs[0], refs[1], refs[-1]
        refs = refs[2:-1]
        copies = load_all([
            (w1_hbm.at[head + 2], next1_ref, sems.at[0]),
            (w2_hbm.at[head + 2], next2_ref, sems.at[1]),
        ])
    (rows_ref, spread_ref, w1t_ref, w2t_ref, tail_ref, hop_ref, hot_ref, pre_ref, lg_ref, h1_ref, hat1_ref, slope1_ref,
     h2_ref, hat2_ref, slope2_ref, scale_ref, sums_ref, dh_ref, d2_ref, d1_ref, dl_ref, grad_ref) = refs
    latent = w2_ref.shape[0]
    tail_rows = w1_ref.shape[0] - latent
    mine = own_lanes(place_ref)
    horizon_row = hz_ref[:, mine]
    bin_ids = lax.broadcasted_iota(jnp.int32, (LANES, LANES), 0)
    first_end = latent + LANES
    losses = []
    spread_columns(g_ref[head + 1], s_ref[head + 1], rows_ref, spread_ref)
    tail_ref[...] = padded_rows(w1_ref[latent:, :], LANES)
    transpose_into(w1t_ref, w1_ref, latent)
    w1t_ref[:, latent:] = jnp.transpose(tail_ref[...])
    transpose_into(w2t_ref, w2_ref, latent)
    hot_ref[...] = padded_rows(ho_ref[head], LANES)
    hop_ref[...] = jnp.transpose(hot_ref[...])
    gain1, gain2, shift1, shift2 = [spread_ref.at[place] for place in range(4)]
    pre_ref[...] = nn(w1t_ref[...], xt_ref[...])
    for step in range(steps):
        mish_forward_low(pre_ref, gain1, shift1, h1_ref, hat1_ref, slope1_ref, scale_ref, 0, lanes_of(step))
    pre_ref[...] = nn(w2t_ref[...], h1_ref[...])
    for step in range(steps):
        mish_forward_low(pre_ref, gain2, shift2, h2_ref, hat2_ref, slope2_ref, scale_ref, 1, lanes_of(step))
    lg_ref[...] = nn(hot_ref[...], h2_ref[...])
    share = 0.1 if head == 0 else 0.1 / (heads - 1)
    bins_ref = rb_ref if head == 0 else vb_ref
    for step in range(steps):
        at = lanes_of(step)
        logits = jnp.where(bin_ids < bins, lg_ref[:, at], F32(-1e30))
        chosen = bin_ids == bins_ref[step : step + 1, mine]
        top = jnp.max(logits, axis=0, keepdims=True)
        powers = jnp.exp(logits - top)
        total = column_sum(powers)
        picked = column_sum(jnp.where(chosen, logits, 0.0))
        weight = row_weight(step, steps, scale * share, horizon_row, place_ref)
        losses.append(weight * (jnp.log(total) + top - picked))
        dl_ref[:, at] = (powers * (weight / total) - jnp.where(chosen, weight, 0.0)).astype(BF16)
    dh_ref[...] = nn(hop_ref[...], dl_ref[...]).astype(BF16)
    grad_ref[:, first_end + latent :] = nt(h2_ref[...], dl_ref[...]).astype(BF16)
    mish_backward_low(dh_ref, hat2_ref, slope2_ref, scale_ref, 1, steps, sums_ref, 2, d2_ref)
    dh_ref[...] = nn(w2_ref[...], d2_ref[...]).astype(BF16)
    grad_ref[:, first_end : first_end + latent] = nt(d2_ref[...], h1_ref[...]).astype(BF16)
    mish_backward_low(dh_ref, hat1_ref, slope1_ref, scale_ref, 0, steps, sums_ref, 0, d1_ref)
    low_part = nn(w1_ref[0:latent, :], d1_ref[...])
    side_part = nn(tail_ref[...], d1_ref[...])
    if not chained:
        dx_ref[0:latent, :] = low_part
        dx_ref[latent:, :] = side_part
    else:
        dx_ref[0:latent, :] = before_ref[0:latent, :] + low_part
        dx_ref[latent:, :] = before_ref[latent:, :] + side_part
    grad_ref[:, 0:latent] = nt(d1_ref[...], xt_ref[0:latent, :]).astype(BF16)
    side_terms = with_vectors(nt(d1_ref[...], xt_ref[latent:, :]), vector_sums(sums_ref, spread_ref, 2), tail_rows)
    grad_ref[:, latent:first_end] = side_terms.astype(BF16)
    for relative, (which, slot) in enumerate(slots):
        start = pl.multiple_of((place_ref[0] ^ relative) * GROUP, GROUP)
        (keep_ref, send_ref)[which][slot] = grad_ref[pl.ds(start, GROUP), :]
    loss_ref[...] = functools.reduce(jnp.add, losses)
    for each in copies:
        each.wait()


def backward_kernel(
    steps, scale, order, losses, after,
    place_ref, xt_ref, soft_ref, h1_ref, hat1_ref, slope1_ref, h2_ref, hat2_ref, slope2_ref, scale_ref,
    w1_ref, w2_ref, dyn_ref, hz_ref, g_ref, dx_ref, *rest,
):
    initial = order[0] == steps - 1
    final = order[-1] == 0
    loss_refs, rest = rest[:losses], rest[losses:]
    held_refs, rest = ((), rest) if initial else (rest[:4], rest[4:])
    (tgt_hbm, low_ref, first_ref, side_ref, loss_ref, sums_ref, tgt_ref, rows_ref, spread_ref, tail_ref, pre_ref,
     d1_ref, d2_ref, do_ref, grad_ref, sems) = rest[after:]
    mine = own_lanes(place_ref)
    loads = dict(zip(order, load_all([(tgt_hbm.at[step, mine, :], tgt_ref.at[step], sems.at[step]) for step in order])))
    latent = dyn_ref.shape[1]
    here = slice(0, LANES)
    horizon_row = hz_ref[:, mine]
    spread_columns(g_ref[0], g_ref[0], rows_ref, spread_ref)
    tail_rows = w1_ref.shape[0] - latent
    tail_ref[...] = padded_rows(w1_ref[latent:, :], LANES)
    first_end = latent + LANES
    second_end = first_end + latent
    if initial:
        loss = functools.reduce(jnp.add, [each[...] for each in loss_refs])
        side = jnp.zeros((LANES, LANES), F32)
        incoming = None
    else:
        before_ref, given_ref, given_side_ref, given_sums_ref = held_refs
        loss = loss_refs[0][...]
        side = given_side_ref[...]
        incoming = given_ref[...].astype(F32)
        sums_ref[...] = given_sums_ref[...]
    pending = []

    def add_terms(at, fresh, last):
        terms = (
            (slice(0, first_end), nt(d1_ref[:, at], xt_ref[:, at])),
            (slice(first_end, second_end), nt(d2_ref[:, at], h1_ref[:, at])),
            (slice(second_end, second_end + latent), nt(h2_ref[:, at], do_ref[:, at])),
        )
        for lanes, term in terms:
            if not fresh:
                term = term + grad_ref[:, lanes]
            elif not initial:
                term = term + before_ref[:, lanes]
            out_ref = low_ref if last else grad_ref
            if last and final and lanes.start == 0:
                out_ref[:, 0:latent] = term[:, 0:latent].astype(out_ref.dtype)
                vectors = vector_sums(sums_ref, spread_ref, 2)
                out_ref[:, latent:first_end] = with_vectors(term[:, latent:], vectors, tail_rows).astype(out_ref.dtype)
            else:
                out_ref[:, lanes] = term.astype(out_ref.dtype)

    for step in order:
        at = lanes_of(step)
        weight = row_weight(step, steps, scale, horizon_row, place_ref)
        shares = soft_ref[:, lanes_of(step + 1)]
        loads[step].wait()
        residue = shares - jnp.transpose(tgt_ref[step].astype(F32))
        loss = loss + (20.0 / latent) * weight * column_sum(residue * residue)
        grads = residue * ((40.0 / latent) * weight)
        if incoming is not None:
            grads = grads + incoming
        do_ref[:, at] = simplex_back(shares, grads).astype(BF16)
        pre_ref[...] = nn(dyn_ref[...], do_ref[:, at])
        mish_backward(pre_ref, here, hat2_ref, slope2_ref, scale_ref, 1, at, sums_ref, 2, step == steps - 1, d2_ref)
        pre_ref[...] = nn(w2_ref[...], d2_ref[:, at])
        mish_backward(pre_ref, here, hat1_ref, slope1_ref, scale_ref, 0, at, sums_ref, 0, step == steps - 1, d1_ref)
        incoming = nn(w1_ref[0:latent, :], d1_ref[:, at]) + dx_ref[0:latent, at]
        side = side + nn(tail_ref[...], d1_ref[:, at]) + dx_ref[latent:, at]
        incoming = incoming.astype(BF16).astype(F32)
        pending.append(step)
        if len(pending) == 2 or step == order[-1]:
            low, high = min(pending), max(pending) + 1
            add_terms(slice(low * LANES, high * LANES), high == order[0] + 1, low == order[-1])
            pending = []

    first_ref[...] = incoming.astype(BF16)
    side_ref[...] = side
    loss_ref[...] = loss


def ending_kernel(
    slots, tasks, task_width, acted, observed, after,
    place_ref, low_ref, first_ref, side_ref, loss_ref, soft_ref, ein_ref, eh_ref, ehat_ref, eslope_ref, escale_ref,
    ids_ref, e1_ref, eg_ref, e2_ref, *rest,
):
    out_refs, rest = rest[after : after + 4], rest[after + 4 :]
    erows_ref, espread_ref, e1p_ref, epre_ref, esums_ref, ed_ref, egrad_ref = rest
    mine = own_lanes(place_ref)
    here = slice(0, LANES)
    latent = first_ref.shape[0]
    spread_columns(eg_ref[...], eg_ref[...], erows_ref, espread_ref)
    e1p_ref[...] = padded_rows(e1_ref[...], e1p_ref.shape[0])
    d_enc = simplex_back(soft_ref[:, 0:LANES], first_ref[...].astype(F32)).astype(BF16)
    epre_ref[...] = nn(e2_ref[...], d_enc)
    mish_backward(epre_ref, here, ehat_ref, eslope_ref, escale_ref, 0, here, esums_ref, 0, True, ed_ref)
    side_enc = nn(e1p_ref[...], ed_ref[...])
    enc_width = epre_ref.shape[0]
    half = GROUP // 2
    groups = enc_width // half
    egrad_ref[:, 0:half, :] = nt(eh_ref[...], d_enc).reshape(groups, half, latent)
    enc_first = nt(ed_ref[...], ein_ref[...])
    egrad_ref[:, half:, 0:LANES] = enc_first[:, 0:LANES].reshape(groups, half, LANES)
    second_lanes = with_vectors(enc_first[:, LANES : 2 * LANES], vector_sums(esums_ref, espread_ref, 1), LANES - 2)
    egrad_ref[:, half:, LANES : 2 * LANES] = second_lanes.reshape(groups, half, LANES)
    egrad_ref[:, half:, 2 * LANES :] = jnp.zeros((groups, half, latent - 2 * LANES), F32)

    kinds = lax.broadcasted_iota(jnp.int32, (tasks, LANES), 0)
    onehot = (kinds == ids_ref[:, mine]).astype(F32)
    over_lanes = (((1,), (1,)), ((), ()))
    highest = lax.Precision.HIGHEST
    side_terms = lax.dot_general(onehot, side_ref[...], over_lanes, precision=highest, preferred_element_type=F32)
    enc_terms = lax.dot_general(onehot, side_enc, over_lanes, precision=highest, preferred_element_type=F32)
    table = pltpu.roll(side_terms, LANES - acted, 1)
    table = table + pltpu.roll(enc_terms, enc_terms.shape[1] - observed, 1)[:, 0:LANES]
    lane = lax.broadcasted_iota(jnp.int32, table.shape, 1)
    table = jnp.where(lane < task_width, table, 0.0)
    table = jnp.where((lane == LANES - 1) & (kinds == 0), jnp.sum(loss_ref[...], axis=1, keepdims=True), table)
    table_rows = [table[start : start + GROUP] for start in range(0, tasks, GROUP)]
    table_block = jnp.concatenate(table_rows, axis=1).astype(BF16)
    cut = out_refs[0].shape[2]
    width = low_ref.shape[1] - cut
    for half_no in range(2):
        for relative, (which, slot) in enumerate(slots[half_no]):
            dest = place_ref[0] ^ relative
            start = pl.multiple_of(dest * GROUP, GROUP)
            out_ref = out_refs[2 * half_no + which]
            if half_no == 0:
                out_ref[slot] = low_ref[pl.ds(start, GROUP), 0:cut]
            else:
                out_ref[slot, :, 0:width] = low_ref[pl.ds(start, GROUP), cut:]
                out_ref[slot, :, width : width + latent] = egrad_ref[dest].astype(BF16)
                out_ref[slot, :, width + latent :] = table_block


def final_kernel(tasks, task_width, enc_in, bins, net_in, *refs):
    outs = refs[-12:]
    (loss_ref, table_ref, e1_ref, eg_ref, es_ref, e2_ref, first_ref, second_ref, gain_ref, shift_ref, dyn_ref, head_ref) = outs
    refs = refs[:-12]
    tail_refs, refs = refs[:2], refs[2:]
    latent = second_ref.shape[2]
    first_end = latent + LANES
    second_end = first_end + latent

    def put_net(net, value):
        first_ref[net] = value[:, 0:net_in]
        second_ref[net] = value[:, first_end:second_end]
        turned = jnp.transpose(value[:, latent:first_end])
        for layer in range(2):
            row = net_in - latent + 2 * layer
            gain_ref[net, layer : layer + 1, :] = turned[row : row + 1, :]
            shift_ref[net, layer : layer + 1, :] = turned[row + 1 : row + 2, :]

    tail = functools.reduce(jnp.add, [ref[0].astype(F32) for ref in tail_refs])
    put_net(0, tail)
    dyn_ref[...] = tail[:, second_end : second_end + latent]
    enc = tail[:, second_end + latent : second_end + 2 * latent]
    half = GROUP // 2
    e2_ref[...] = 0.3 * enc[0:half, :]
    e1_ref[...] = 0.3 * enc[half:, 0:enc_in]
    turned = 0.3 * jnp.transpose(enc[half:, LANES : 2 * LANES])
    eg_ref[...] = turned[LANES - 2 : LANES - 1, :]
    es_ref[...] = turned[LANES - 1 : LANES, :]
    table = tail[:, second_end + 2 * latent :]
    loss_ref[...] = table[0:1, LANES - 1 : LANES]
    for place in range(tasks // GROUP):
        table_ref[place * GROUP : (place + 1) * GROUP, :] = table[:, place * LANES : place * LANES + task_width]
    net = 1
    for one_ref, other_ref in zip(refs[0::2], refs[1::2]):
        for one in range(one_ref.shape[1]):
            value = one_ref[0, one].astype(F32) + other_ref[0, one].astype(F32)
            put_net(net, value)
            head_ref[net - 1] = value[:, second_end : second_end + bins]
            net += 1


def swap(value, axis, distance):
    count = lax.axis_size(axis)
    return lax.ppermute(value, axis, [(place, place ^ distance) for place in range(count)])


def exchange(parts, axis, scale):
    total = parts[0].astype(F32)
    for distance in range(1, len(parts)):
        total = total + swap(parts[distance], axis, distance * scale).astype(F32)
    return total


def scatter_plain(packed, chips, sections):
    held = packed.reshape((sections, chips, CORES) + packed.shape[1:])
    batch_no = lax.axis_index("batch")
    places = (
        ("batch", 1, CORES, 2, batch_no % CORES),
        ("batch", CORES, chips, 1, batch_no // CORES),
        ("section", 1, sections, 0, lax.axis_index("section")),
    )
    for axis, scale, count, dim, mine in places:
        parts = [lax.dynamic_index_in_dim(held, mine ^ other, dim, keepdims=False) for other in range(count)]
        held = exchange(parts, axis, scale)
        held = held.astype(BF16) if dim else held
    return held


def on_device(
    observations,
    actions,
    targets,
    task_ids,
    horizons,
    reward_bins,
    value_bins,
    task_table,
    enc_first,
    enc_gain,
    enc_shift,
    enc_second,
    net_first,
    net_second,
    net_gain,
    net_shift,
    dyn_out,
    head_out,
):
    sections = lax.axis_size("section")
    batches = lax.axis_size("batch")
    section_no = lax.axis_index("section")
    chips = batches // CORES
    devices = sections * batches
    steps, rows_all, acted = actions.shape
    observed = observations.shape[1]
    rows = rows_all // sections
    latent = dyn_out.shape[1]
    hidden = dyn_out.shape[0]
    tasks, task_width = task_table.shape
    heads, _, bins = head_out.shape
    nets, net_in, _ = net_first.shape
    enc_in, enc_width = enc_first.shape
    wide = steps * LANES
    scale = 1.0 / (rows_all * batches * steps)
    groups = hidden // GROUP
    in_place = hidden // devices == GROUP
    start = section_no * rows
    block_no = start // LANES
    first_lane = start - block_no * LANES
    me = section_no * batches + lax.axis_index("batch") if in_place else jnp.int32(0)
    place = jnp.stack([me, block_no, first_lane, first_lane + rows]).astype(jnp.int32)
    bits = [("batch", 1 << bit) for bit in range(batches.bit_length() - 1)]
    bits += [("section", 1 << bit) for bit in range(sections.bit_length() - 1)]

    def slots_of(order):
        if not in_place:
            return tuple((relative // (groups // 2), relative % (groups // 2)) for relative in range(groups))
        found = []
        for relative in range(groups):
            slot = 0
            for bit in order:
                slot = 2 * slot + (relative >> bit & 1)
            found.append((slot // (groups // 2), slot % (groups // 2)))
        return tuple(found)

    plain = tuple(range(len(bits)))
    y_first = (0, 2, 1) + tuple(range(3, len(bits))) if in_place else plain
    half_slots = groups // 2
    shape_of = jax.ShapeDtypeStruct
    smem = pl.BlockSpec(memory_space=pltpu.SMEM)
    local = pl.BlockSpec(memory_space=pltpu.VMEM)
    far = pl.BlockSpec(memory_space=pltpu.HBM)
    anywhere = pl.BlockSpec(memory_space=pl.ANY)
    first_far, second_far, dyn_far, targets_far = [
        pltpu.with_memory_space_constraint(array, pltpu.HBM) for array in (net_first, net_second, dyn_out, targets)
    ]
    vmem = pltpu.VMEM
    dmas = pltpu.SemaphoreType.DMA

    def params(mebibytes):
        return pltpu.CompilerParams(vmem_limit_bytes=mebibytes * 1024 * 1024)

    def cost(flops, moved):
        return pl.CostEstimate(flops=flops, bytes_accessed=moved, transcendentals=0)

    ids_row = task_ids.reshape(1, rows_all)
    horizon_row = horizons.reshape(1, rows_all)
    eg_row = enc_gain.reshape(1, enc_width)
    es_row = enc_shift.reshape(1, enc_width)
    head_turned = head_out.transpose(0, 2, 1)
    low = lambda lanes: shape_of((hidden, lanes), BF16)
    forward_shapes = (
        shape_of((latent + LANES, wide), BF16),
        shape_of((latent, wide + LANES), F32),
        low(wide), low(wide), low(wide), low(wide), low(wide), low(wide),
        shape_of((8, wide), F32),
        shape_of((2 * LANES, LANES), BF16),
        shape_of((enc_width, LANES), BF16),
        shape_of((enc_width, LANES), BF16),
        shape_of((enc_width, LANES), BF16),
        shape_of((8, LANES), F32),
        shape_of((net_in, hidden), BF16),
        shape_of((hidden, hidden), BF16),
        shape_of((hidden, latent), BF16),
    )

    weight_shapes = (shape_of((net_in, hidden), BF16), shape_of((hidden, hidden), BF16))

    early = [
        pltpu.with_memory_space_constraint(array, pltpu.HBM)
        for array in (
            observations.T, actions.transpose(0, 2, 1), ids_row, task_table, enc_first, eg_row, es_row, enc_second,
            net_gain, net_shift,
        )
    ]
    made = pl.pallas_call(
        functools.partial(forward_kernel, steps),
        out_shape=forward_shapes + weight_shapes,
        in_specs=[smem] + [far] * 13,
        out_specs=[local] * (len(forward_shapes) + 2),
        scratch_shapes=[
            vmem((8, hidden), F32),
            vmem((4, hidden, LANES), F32),
            vmem((8, enc_width), F32),
            vmem((2, enc_width, LANES), F32),
            vmem((tasks, 2 * LANES), F32),
            vmem((LANES, LANES), F32),
            vmem((2 * LANES, enc_width), BF16),
            vmem((hidden, latent + LANES), BF16),
            vmem((hidden, hidden), BF16),
            vmem((latent, hidden), BF16),
            vmem((hidden, LANES), F32),
            vmem((enc_width, LANES), F32),
            *[vmem(each.shape, each.dtype) for each in early],
            dmas((5,)),
            dmas((len(early),)),
        ],
        compiler_params=params(VMEM_A),
        cost_estimate=cost(10_000_000_000, 8_000_000),
        name="forward_chain",
    )(
        place, *early, first_far, second_far, dyn_far,
    )
    saved, weights = made[:-2], made[-2:]
    xt = saved[0]
    head_width = latent + LANES + hidden + LANES

    def run_head(head, ahead, weights, before, after):
        pack_shape = shape_of((half_slots, GROUP, head_width), BF16)
        dx_shape = shape_of((latent + LANES, wide), F32)
        out_shapes = (pack_shape, pack_shape, dx_shape, shape_of((1, LANES), F32))
        args = [place, xt, *weights, head_turned, net_gain, net_shift, reward_bins, value_bins, horizon_row]
        specs = [smem] + [local] * 9
        aliases = {}
        if before is not None:
            aliases = {len(args): 2}
            args.append(before)
            specs.append(local)
        args += after
        specs += [anywhere] * len(after)
        if ahead:
            args += [first_far, second_far]
            specs += [far, far]
            out_shapes += weight_shapes
        low_wide = vmem((hidden, wide), BF16)
        scratch = [
            vmem((8, hidden), F32),
            vmem((4, hidden, LANES), F32),
            vmem((hidden, latent + LANES), BF16),
            vmem((hidden, hidden), BF16),
            vmem((LANES, hidden), BF16),
            vmem((hidden, LANES), BF16),
            vmem((LANES, hidden), BF16),
            vmem((hidden, wide), F32),
            vmem((LANES, wide), F32),
        ]
        scratch += [low_wide] * 6
        scratch += [vmem((8, wide), F32), vmem((4, hidden, LANES), F32)]
        scratch += [low_wide] * 3
        scratch += [vmem((LANES, wide), BF16), vmem((hidden, head_width), BF16)]
        if ahead:
            scratch.append(dmas((2,)))
        return pl.pallas_call(
            functools.partial(
                heads_kernel, steps, scale, slots_of(plain), head, ahead, heads, bins, before is not None, len(after)
            ),
            out_shape=out_shapes,
            in_specs=specs,
            out_specs=[local] * len(out_shapes),
            scratch_shapes=scratch,
            input_output_aliases=aliases,
            compiler_params=params(VMEM_B),
            cost_estimate=cost(9_000_000_000, 4_000_000),
            name=f"head_{head}",
        )(*args)

    def phase(pair, bit):
        return pair[0], swap(pair[1], *bits[bit])

    def fold(members, *tokens, by_lanes=False):
        slots_now = members[0][0].shape[0] // 2
        shape = members[0][0].shape[1:]
        if by_lanes:
            shape = shape[:-1] + (sum(kept.shape[-1] for kept, _ in members),)
        elif len(members) > 1:
            shape = (len(members),) + shape
        out_shape = shape_of((slots_now,) + shape, BF16)
        inputs = [each for member in members for each in member]

        def fold_kernel(*refs):
            refs = refs[len(tokens) :]
            outs = refs[-2:]
            lane = 0
            for place in range(len(members)):
                kept_ref, came_ref = refs[2 * place], refs[2 * place + 1]
                width = kept_ref.shape[-1]
                for half in range(2):
                    part = pl.ds(half * slots_now, slots_now)
                    value = (kept_ref[part].astype(F32) + came_ref[part].astype(F32)).astype(BF16)
                    if by_lanes:
                        outs[half][..., lane : lane + width] = value
                    elif len(members) > 1:
                        outs[half][:, place] = value
                    else:
                        outs[half][...] = value
                lane += width

        return pl.pallas_call(
            fold_kernel,
            out_shape=(out_shape, out_shape),
            in_specs=[anywhere] * len(tokens) + [local] * len(inputs),
            out_specs=(local, local),
            compiler_params=params(VMEM_SUM),
            cost_estimate=cost(1_000_000, 2_000_000),
            name="fold",
        )(*tokens, *inputs)

    net_width = latent + LANES + hidden + latent
    chain_inputs = saved[:9] + saved[14:]

    def run_backward(order, losses, held, after):
        final = order[-1] == 0
        out_shapes = (
            shape_of((hidden, net_width), BF16 if final else F32),
            shape_of((latent, LANES), BF16),
            shape_of((LANES, LANES), F32),
            shape_of((1, LANES), F32),
            shape_of((4, hidden, LANES), F32),
        )
        args = [place, *chain_inputs, horizon_row, net_gain, dx, *losses, *held]
        return pl.pallas_call(
            functools.partial(backward_kernel, steps, scale, order, len(losses), len(after)),
            out_shape=out_shapes,
            in_specs=[smem] + [local] * (len(args) - 1) + [anywhere] * len(after) + [far],
            out_specs=[local] * len(out_shapes),
            scratch_shapes=[
                vmem((steps, LANES, latent), BF16),
                vmem((8, hidden), F32),
                vmem((4, hidden, LANES), F32),
                vmem((LANES, hidden), BF16),
                vmem((hidden, LANES), F32),
                vmem((hidden, wide), BF16),
                vmem((hidden, wide), BF16),
                vmem((latent, wide), BF16),
                vmem((hidden, net_width), F32),
                dmas((steps,)),
            ],
            compiler_params=params(VMEM_C),
            cost_estimate=cost(7_000_000_000, 8_000_000),
            name=f"backward_{order[0]}",
        )(*args, *after, targets_far)

    packs, loss_parts = [], []
    dx = None
    flights = []
    after = []

    def advance(head, bit, token, kept_back):
        if in_place and 0 <= head < heads:
            pair = fold([flights[head]], token)
            kept_back.append(pair[0])
            flights[head] = phase(pair, plain[bit])

    for head in range(heads):
        ahead = head + 1 < heads
        result = run_head(head, ahead, weights, dx, after)
        keep, send, dx, loss = result[:4]
        weights = result[4:]
        packs.append((keep, send))
        loss_parts.append(loss)
        after = []
        advance(head - 1, 1, loss, after)
        advance(head - 2, 2, loss, after)
        if in_place:
            flights.append(phase((keep, send), plain[0]))
    early = heads // 2
    half_way = steps // 2
    if in_place:
        group = fold(flights[0:early], loss_parts[-1])
        after.append(group[0])
        group = phase(group, plain[3])
    chain = run_backward(tuple(range(steps - 1, half_way - 1, -1)), loss_parts, [], after)
    after = []
    advance(heads - 1, 1, chain[3], after)
    advance(heads - 2, 2, chain[3], after)
    if in_place:
        group = fold([group], chain[3])
        after.append(group[0])
        group = phase(group, plain[4])
        after.append(flights[heads - 3][1])
    chain = run_backward(
        tuple(range(half_way - 1, -1, -1)), [chain[3]], [chain[0], chain[1], chain[2], chain[4]], after
    )
    after = []
    advance(heads - 1, 2, chain[3], after)
    if in_place:
        after.append(flights[heads - 2][1])

    tail_width = net_width + latent + tasks // GROUP * LANES
    cut = tail_width // 2 // LANES * LANES
    one_shape = shape_of((half_slots, GROUP, cut), BF16)
    two_shape = shape_of((half_slots, GROUP, tail_width - cut), BF16)
    tail_slots = (slots_of(plain), slots_of(y_first))
    ended = pl.pallas_call(
        functools.partial(ending_kernel, tail_slots, tasks, task_width, acted, observed, len(after)),
        out_shape=(one_shape, one_shape, two_shape, two_shape),
        in_specs=[smem] + [local] * 14 + [anywhere] * len(after),
        out_specs=[local] * 4,
        scratch_shapes=[
            vmem((8, enc_width), F32),
            vmem((2, enc_width, LANES), F32),
            vmem((2 * LANES, enc_width), BF16),
            vmem((enc_width, LANES), F32),
            vmem((2, enc_width, LANES), F32),
            vmem((enc_width, LANES), BF16),
            vmem((groups, GROUP, latent), F32),
        ],
        compiler_params=params(VMEM_SUM),
        cost_estimate=cost(1_000_000_000, 4_000_000),
        name="ending",
    )(place, *chain[:4], saved[1], *saved[9:14], ids_row, enc_first, eg_row, enc_second, *after)

    if in_place:
        one = phase(ended[0:2], plain[0])
        two = phase(ended[2:4], y_first[0])
        one = phase(fold([one], ended[0]), plain[1])
        two = phase(fold([two], ended[0]), y_first[1])
        rest = phase(fold(flights[early:], one[0]), plain[3])
        one = phase(fold([one]), plain[2])
        two = phase(fold([two]), y_first[2])
        rest = phase(fold([rest], one[0]), plain[4])
        tail = phase(fold([one, two], by_lanes=True), plain[3])
        tail = phase(fold([tail]), plain[4])
        each = GROUP // 2
        out_shapes = (
            shape_of((1, 1), F32),
            shape_of((tasks, task_width), F32),
            shape_of((each, enc_in), F32),
            shape_of((1, each), F32),
            shape_of((1, each), F32),
            shape_of((each, latent), F32),
            shape_of((nets, GROUP, net_in), F32),
            shape_of((nets, GROUP, hidden), F32),
            shape_of((nets, 2, GROUP), F32),
            shape_of((nets, 2, GROUP), F32),
            shape_of((GROUP, latent), F32),
            shape_of((heads, GROUP, bins), F32),
        )
        ends = [*tail, *group, *rest]
        outs = list(pl.pallas_call(
            functools.partial(final_kernel, tasks, task_width, enc_in, bins, net_in),
            out_shape=out_shapes,
            in_specs=[local] * len(ends),
            out_specs=[local] * len(out_shapes),
            compiler_params=params(VMEM_SUM),
            cost_estimate=cost(1_000_000, 4_000_000),
            name="last_sums",
        )(*ends))
        outs[0] = outs[0].reshape(())
        outs[2] = outs[2].T
        outs[3], outs[4] = outs[3].reshape(each), outs[4].reshape(each)
        outs[6] = outs[6].transpose(0, 2, 1)
        outs[7] = outs[7].transpose(0, 2, 1)
        return tuple(outs)

    def scattered(keep, send):
        mine = hidden // devices
        packed = jnp.concatenate([keep, send], axis=0)
        middle = packed.shape[1:-2]
        packed = packed.reshape((groups,) + middle + (GROUP // mine, mine, packed.shape[-1]))
        packed = jnp.moveaxis(packed, -3, 1).reshape((devices,) + middle + (mine, packed.shape[-1]))
        return scatter_plain(packed, chips, sections)

    head_sum = jnp.stack([scattered(*pack) for pack in packs], axis=0)
    enc_each = enc_width // devices
    keep, send = [jnp.concatenate([ended[place], ended[2 + place]], axis=2) for place in range(2)]
    net_sum = scattered(keep[:, :, 0:net_width], send[:, :, 0:net_width])
    rest = jnp.concatenate([keep, send], axis=0)
    enc_all = rest[:, :, net_width : net_width + latent].reshape(groups, 2, enc_width // groups, latent)
    enc_all = enc_all.transpose(0, 2, 1, 3).reshape(devices, enc_each, 2, latent)
    enc_sum = scatter_plain(enc_all, chips, sections)
    enc_sum = enc_sum.transpose(1, 0, 2).reshape(2 * enc_each, latent)
    table_sum = lax.psum(rest[0, :, net_width + latent :].astype(F32), ("section", "batch"))
    first_end = latent + LANES
    net_row = jnp.concatenate([net_sum[:, 0 : first_end + hidden], jnp.zeros_like(net_sum[:, 0:LANES])], axis=1)
    sums = jnp.concatenate([net_row[None], head_sum], axis=0)
    vectors = sums[:, :, net_in : net_in + 4].transpose(0, 2, 1)
    table = table_sum.reshape(GROUP, tasks // GROUP, LANES).transpose(1, 0, 2).reshape(tasks, LANES)
    enc_rows = enc_sum[enc_each:]
    return (
        table[0, LANES - 1],
        table[:, 0:task_width],
        0.3 * enc_rows[:, 0:enc_in].T,
        0.3 * enc_rows[:, 2 * LANES - 2],
        0.3 * enc_rows[:, 2 * LANES - 1],
        0.3 * enc_sum[0:enc_each],
        sums[:, :, 0:net_in].transpose(0, 2, 1),
        sums[:, :, first_end : first_end + hidden].transpose(0, 2, 1),
        vectors[:, 0::2],
        vectors[:, 1::2],
        net_sum[:, first_end + hidden :],
        head_sum[:, :, first_end + hidden : first_end + hidden + bins],
    )


def solution(mesh):
    both = ("section", "batch")
    return jax.shard_map(
        on_device,
        mesh=mesh,
        in_specs=(
            P("batch", None),
            P(None, "batch", None),
            P(None, "batch", None),
            P("batch"),
            P("batch"),
            P(None, "batch"),
            P(None, "batch"),
        )
        + (P(),) * 11,
        out_specs=(
            P(),
            P(),
            P(None, both),
            P(both),
            P(both),
            P(both, None),
            P(None, None, both),
            P(None, None, both),
            P(None, None, both),
            P(None, None, both),
            P(both, None),
            P(None, both, None),
        ),
        check_vma=False,
    )
```

```python
import functools

import jax
import jax.numpy as jnp
from jax import lax
from jax.experimental import pallas as pl
from jax.experimental.pallas import tpu as pltpu
from jax.sharding import PartitionSpec as P

CORES = 2
LANES = 128
GROUP = 16
BF16 = jnp.bfloat16
F32 = jnp.float32
VMEM_A = 18
FORMS = ("base", "rows", "plain", "fused", "small", "large")
VMEM_B = 20
VMEM_SUM = 6
VMEM_C = 20


def nn(left, right):
    return lax.dot_general(left, right, (((1,), (0,)), ((), ())), preferred_element_type=F32)


def nt(left, right):
    return lax.dot_general(left, right, (((1,), (1,)), ((), ())), preferred_element_type=F32)


def tn(left, right):
    return lax.dot_general(left, right, (((0,), (0,)), ((), ())), preferred_element_type=F32)


def column_sum(value):
    grouped = value.reshape(value.shape[0] // 8, 8, value.shape[1])
    return jnp.sum(jnp.sum(grouped, axis=0), axis=0, keepdims=True)


def slabs(features, size=64):
    return [slice(start, start + size) for start in range(0, features, size)]


def lanes_of(step):
    return slice(step * LANES, (step + 1) * LANES)


def spread_columns(gain_rows, shift_rows, rows_ref, spread_ref):
    count = gain_rows.shape[0]
    rows_ref[...] = jnp.zeros_like(rows_ref)
    rows_ref[0:count, :] = gain_rows
    rows_ref[count : 2 * count, :] = shift_rows
    turned = jnp.transpose(rows_ref[...])
    for place in range(2 * count):
        spread_ref[place] = jnp.broadcast_to(turned[:, place : place + 1], spread_ref.shape[1:])


def mish_forward(pre_ref, pre_at, gain_ref, shift_ref, hid_ref, hat_ref, slope_ref, scale_ref, scale_row, at):
    features = pre_ref.shape[0]
    row_mean = column_sum(pre_ref[:, pre_at]) * (1.0 / features)
    centred = pre_ref[:, pre_at] - row_mean
    spread = column_sum(centred * centred) * (1.0 / features)
    scale = lax.rsqrt(spread + 1e-05)
    scale_ref[scale_row : scale_row + 1, at] = scale
    for part in slabs(features):
        hat = (pre_ref[part, pre_at] - row_mean) * scale
        normed = hat * gain_ref[part, :] + shift_ref[part, :]
        power = jnp.exp(normed)
        top = power * (power + 2.0)
        inverse = pl.reciprocal(top + 2.0, approx=True)
        ratio = top * inverse
        hid_ref[part, at] = (normed * ratio).astype(BF16)
        tilt = power * inverse
        slope = ratio + normed * (4.0 * (tilt * (tilt + inverse)))
        slope_ref[part, at] = (slope * gain_ref[part, :]).astype(BF16)
        hat_ref[part, at] = hat.astype(BF16)


def mish_backward(grad_ref, grad_at, hat_ref, slope_ref, scale_ref, scale_row, at, sums_ref, sums_at, first, out_ref):
    features = grad_ref.shape[0]
    total_one = jnp.zeros((8, LANES), F32)
    total_two = jnp.zeros((8, LANES), F32)
    for part in slabs(features):
        term = grad_ref[part, grad_at] * slope_ref[part, at].astype(F32)
        grad_ref[part, grad_at] = term
        crossed = term * hat_ref[part, at].astype(F32)
        groups = (term.shape[0] // 8, 8, LANES)
        total_one = total_one + jnp.sum(term.reshape(groups), axis=0)
        total_two = total_two + jnp.sum(crossed.reshape(groups), axis=0)
        if first:
            sums_ref[sums_at, part, :] = term
            sums_ref[sums_at + 1, part, :] = crossed
        else:
            sums_ref[sums_at, part, :] += term
            sums_ref[sums_at + 1, part, :] += crossed
    mean_one = jnp.sum(total_one, axis=0, keepdims=True) * (1.0 / features)
    mean_two = jnp.sum(total_two, axis=0, keepdims=True) * (1.0 / features)
    scale = scale_ref[scale_row : scale_row + 1, at]
    for part in slabs(features):
        rest = grad_ref[part, grad_at] - mean_one - hat_ref[part, at].astype(F32) * mean_two
        out_ref[part, at] = (rest * scale).astype(BF16)


def mish_forward_low(pre_ref, gain_ref, shift_ref, hid_ref, hat_ref, slope_ref, scale_ref, scale_row, at, size):
    features = pre_ref.shape[0]
    row_mean = column_sum(pre_ref[:, at]) * (1.0 / features)
    centred = pre_ref[:, at] - row_mean
    spread = column_sum(centred * centred) * (1.0 / features)
    scale = lax.rsqrt(spread + 1e-05)
    scale_ref[scale_row : scale_row + 1, at] = scale
    for part in slabs(features, size):
        hat = (pre_ref[part, at] - row_mean) * scale
        normed = (hat * gain_ref[part, :] + shift_ref[part, :]).astype(BF16)
        hat_ref[part, at] = hat.astype(BF16)
        power = jnp.exp(normed)
        top = power * (power + 2.0)
        inverse = pl.reciprocal(top + 2.0, approx=True)
        ratio = top * inverse
        hid_ref[part, at] = normed * ratio
        tilt = power * inverse
        slope = ratio + (4.0 * normed) * (tilt * (tilt + inverse))
        slope_ref[part, at] = slope * gain_ref[part, :].astype(BF16)


def mish_backward_low(grad_ref, hat_ref, slope_ref, scale_ref, scale_row, steps, sums_ref, sums_at, out_ref, size):
    features = grad_ref.shape[0]
    rows = []
    for step in range(steps):
        at = lanes_of(step)
        total_one = jnp.zeros((16, LANES), F32)
        total_two = jnp.zeros((16, LANES), F32)
        for part in slabs(features, size):
            term = grad_ref[part, at] * slope_ref[part, at]
            crossed = term * hat_ref[part, at]
            grad_ref[part, at] = term
            groups = (term.shape[0] // 16, 16, LANES)
            term = term.reshape(groups)
            crossed = crossed.reshape(groups)
            total_one = total_one + functools.reduce(jnp.add, [term[k] for k in range(groups[0])]).astype(F32)
            total_two = total_two + functools.reduce(jnp.add, [crossed[k] for k in range(groups[0])]).astype(F32)
        scale = scale_ref[scale_row : scale_row + 1, at]
        mean_one = jnp.sum(total_one, axis=0, keepdims=True) * (1.0 / features)
        mean_two = jnp.sum(total_two, axis=0, keepdims=True) * (1.0 / features)
        rows.append((mean_one.astype(BF16), mean_two.astype(BF16), scale.astype(BF16)))
    for part in slabs(features, size):
        sum_one, sum_two = None, None
        for step, (mean_one, mean_two, scale) in enumerate(rows):
            at = lanes_of(step)
            term = grad_ref[part, at]
            hat = hat_ref[part, at]
            out_ref[part, at] = (term - mean_one - hat * mean_two) * scale
            crossed = term * hat
            sum_one = term if sum_one is None else sum_one + term
            sum_two = crossed if sum_two is None else sum_two + crossed
        sums_ref[sums_at, part, :] = sum_one.astype(F32)
        sums_ref[sums_at + 1, part, :] = sum_two.astype(F32)


def simplex(values):
    grouped = values.reshape(values.shape[0] // 8, 8, values.shape[1])
    powers = jnp.exp(grouped - jnp.max(grouped, axis=1, keepdims=True))
    shares = powers / jnp.sum(powers, axis=1, keepdims=True)
    return shares.reshape(values.shape)


def simplex_back(shares, grads):
    grouped = (shares.shape[0] // 8, 8, shares.shape[1])
    crossed = jnp.sum((shares * grads).reshape(grouped), axis=1, keepdims=True)
    return (shares.reshape(grouped) * (grads.reshape(grouped) - crossed)).reshape(shares.shape)


def row_weight(step, steps, scale, horizon_row, place_ref):
    lane = lax.broadcasted_iota(jnp.int32, (1, LANES), 1)
    mine = (lane >= place_ref[2]) & (lane < place_ref[3]) & (horizon_row > step)
    return jnp.where(mine, F32(scale * 0.5 ** (step / (steps - 1))), 0.0)


def padded_rows(value, rows):
    zeros = jnp.zeros((rows - value.shape[0], value.shape[1]), F32)
    return jnp.concatenate([value.astype(F32), zeros], axis=0).astype(BF16)


def transpose_into(out_ref, source_ref, rows):
    for start in range(0, rows, LANES):
        out_ref[:, start : start + LANES] = jnp.transpose(source_ref[start : start + LANES, :])


def vector_sums(sums_ref, gains_ref, layers):
    vectors = []
    for layer in range(layers):
        inverse = 1.0 / gains_ref[layer]
        vectors.append(jnp.sum(sums_ref[2 * layer + 1] * inverse, axis=1, keepdims=True))
        vectors.append(jnp.sum(sums_ref[2 * layer] * inverse, axis=1, keepdims=True))
    return vectors


def own_lanes(place_ref):
    return pl.ds(pl.multiple_of(place_ref[1] * LANES, LANES), LANES)


def load_all(copies):
    made = [pltpu.make_async_copy(*each) for each in copies]
    for each in made:
        each.start()
    return made


def with_vectors(value, vectors, first_lane):
    lane = lax.broadcasted_iota(jnp.int32, value.shape, 1)
    for place, vector in enumerate(vectors):
        value = jnp.where(lane == first_lane + place, vector, value)
    return value


def forward_kernel(
    steps,
    place_ref, obs_hbm, act_hbm, ids_hbm, table_hbm, e1_hbm, eg_hbm, es_hbm, e2_hbm, g_hbm, s_hbm,
    w1_hbm, w2_hbm, dyn_hbm,
    xt_ref, soft_ref, h1_ref, hat1_ref, slope1_ref, h2_ref, hat2_ref, slope2_ref, scale_ref,
    ein_ref, eh_ref, ehat_ref, eslope_ref, escale_ref,
    w1_ref, w2_ref, dyn_ref, x_ref, next1_ref, next2_ref,
    rows_ref, spread_ref, erows_ref, espread_ref, wide_ref, tall_ref, e1p_ref, w1t_ref, w2t_ref, dynt_ref, pre_ref, epre_ref,
    obs_ref, act_ref, ids_ref, table_ref, e1_ref, eg_ref, es_ref, e2_ref, g_ref, s_ref,
    sems, early_sems,
):
    early = load_all([
        (table_hbm, table_ref, early_sems.at[0]),
        (ids_hbm, ids_ref, early_sems.at[1]),
        (obs_hbm, obs_ref, early_sems.at[2]),
        (e1_hbm, e1_ref, early_sems.at[3]),
        (eg_hbm, eg_ref, early_sems.at[4]),
        (es_hbm, es_ref, early_sems.at[5]),
        (e2_hbm, e2_ref, early_sems.at[6]),
        (act_hbm, act_ref, early_sems.at[7]),
        (g_hbm, g_ref, early_sems.at[8]),
        (s_hbm, s_ref, early_sems.at[9]),
    ])
    first, second, third, fourth, fifth = load_all([
        (w1_hbm.at[0], w1_ref, sems.at[0]),
        (w2_hbm.at[0], w2_ref, sems.at[1]),
        (dyn_hbm, dyn_ref, sems.at[2]),
        (w1_hbm.at[1], next1_ref, sems.at[3]),
        (w2_hbm.at[1], next2_ref, sems.at[4]),
    ])
    latent = dyn_ref.shape[1]
    tasks, task_width = table_ref.shape
    observed = obs_ref.shape[0]
    acted = act_ref.shape[1]
    mine = own_lanes(place_ref)
    for each in early:
        each.wait()
    spread_columns(eg_ref[...], es_ref[...], erows_ref, espread_ref)
    kinds = lax.broadcasted_iota(jnp.int32, (tasks, LANES), 0)
    onehot = (kinds == ids_ref[:, mine]).astype(F32).astype(BF16)
    wide_ref[...] = jnp.zeros_like(wide_ref)
    wide_ref[:, 0:task_width] = table_ref[...].astype(F32)
    table_tail = pltpu.roll(wide_ref[:, 0:LANES], acted, 1).astype(BF16)
    table_enc = pltpu.roll(wide_ref[...], observed, 1).astype(BF16)
    aux = tn(table_tail, onehot)
    tall_ref[...] = jnp.zeros_like(tall_ref)
    tall_ref[0:observed, :] = obs_ref[:, mine].astype(F32)
    ein = tn(table_enc, onehot)
    ein_ref[0:LANES, :] = (ein[0:LANES] + tall_ref[...]).astype(BF16)
    ein_ref[LANES:, :] = ein[LANES:].astype(BF16)
    e1p_ref[...] = padded_rows(e1_ref[...], e1p_ref.shape[0])
    epre_ref[...] = tn(e1p_ref[...], ein_ref[...])
    here = slice(0, LANES)
    mish_forward(epre_ref, here, espread_ref.at[0], espread_ref.at[1], eh_ref, ehat_ref, eslope_ref, escale_ref, 0, here)
    shares = simplex(tn(e2_ref[...], eh_ref[...]))
    soft_ref[:, 0:LANES] = shares
    xt_ref[0:latent, 0:LANES] = shares.astype(BF16)
    spread_columns(g_ref[0], s_ref[0], rows_ref, spread_ref)
    for step in range(steps):
        tall_ref[...] = jnp.zeros_like(tall_ref)
        tall_ref[0:acted, :] = act_ref[step, :, mine].astype(F32)
        xt_ref[latent:, lanes_of(step)] = (aux + tall_ref[...]).astype(BF16)
    first.wait()
    transpose_into(w1t_ref, w1_ref, latent)
    w1t_ref[:, latent:] = jnp.transpose(padded_rows(w1_ref[latent:, :], LANES))
    second.wait()
    transpose_into(w2t_ref, w2_ref, latent)
    third.wait()
    transpose_into(dynt_ref, dyn_ref, latent)
    for step in range(steps):
        at = lanes_of(step)
        pre_ref[...] = nn(w1t_ref[...], xt_ref[:, at])
        mish_forward(pre_ref, here, spread_ref.at[0], spread_ref.at[2], h1_ref, hat1_ref, slope1_ref, scale_ref, 0, at)
        pre_ref[...] = nn(w2t_ref[...], h1_ref[:, at])
        mish_forward(pre_ref, here, spread_ref.at[1], spread_ref.at[3], h2_ref, hat2_ref, slope2_ref, scale_ref, 1, at)
        shares = simplex(nn(dynt_ref[...], h2_ref[:, at]))
        soft_ref[:, lanes_of(step + 1)] = shares
        if step + 1 < steps:
            xt_ref[0:latent, lanes_of(step + 1)] = shares.astype(BF16)
    for step in range(steps):
        for start in range(0, latent + LANES, LANES):
            x_ref[lanes_of(step), start : start + LANES] = jnp.transpose(xt_ref[start : start + LANES, lanes_of(step)])
    fourth.wait()
    fifth.wait()


def heads_kernel(steps, scale, slots, head, ahead, heads, bins, chained, after, form, *refs):
    refs = list(refs)
    place_ref, xt_ref, x_ref, w1_ref, w2_ref, ho_ref, g_ref, s_ref, rb_ref, vb_ref, hz_ref = refs[:11]
    refs = refs[11:]
    size = {"small": 32, "large": 128}.get(form, 64)
    turned = form not in ("plain", "fused")
    before_ref = refs.pop(0) if chained else None
    refs = refs[after:]
    w1_hbm, w2_hbm = refs[:2] if ahead else (None, None)
    refs = refs[2:] if ahead else refs
    keep_ref, send_ref, dx_ref, loss_ref = refs[:4]
    refs = refs[4:]
    copies = []
    if ahead:
        next1_ref, next2_ref, sems = refs[0], refs[1], refs[-1]
        refs = refs[2:-1]
        copies = load_all([
            (w1_hbm.at[head + 2], next1_ref, sems.at[0]),
            (w2_hbm.at[head + 2], next2_ref, sems.at[1]),
        ])
    (rows_ref, spread_ref, w1t_ref, w2t_ref, tail_ref, hop_ref, hot_ref, pre_ref, lg_ref, h1_ref, hat1_ref, slope1_ref,
     h2_ref, hat2_ref, slope2_ref, scale_ref, sums_ref, dh_ref, d2_ref, d1_ref, dl_ref, grad_ref) = refs
    latent = w2_ref.shape[0]
    tail_rows = w1_ref.shape[0] - latent
    mine = own_lanes(place_ref)
    horizon_row = hz_ref[:, mine]
    bin_ids = lax.broadcasted_iota(jnp.int32, (LANES, LANES), 0)
    first_end = latent + LANES
    losses = []
    spread_columns(g_ref[head + 1], s_ref[head + 1], rows_ref, spread_ref)
    tail_ref[...] = padded_rows(w1_ref[latent:, :], LANES)
    if turned:
        transpose_into(w1t_ref, w1_ref, latent)
        w1t_ref[:, latent:] = jnp.transpose(tail_ref[...])
        transpose_into(w2t_ref, w2_ref, latent)
    hot_ref[...] = padded_rows(ho_ref[head], LANES)
    hop_ref[...] = jnp.transpose(hot_ref[...])
    gain1, gain2, shift1, shift2 = [spread_ref.at[place] for place in range(4)]
    if turned:
        pre_ref[...] = nn(w1t_ref[...], xt_ref[...])
    else:
        pre_ref[...] = tn(w1_ref[0:latent, :], xt_ref[0:latent, :]) + tn(tail_ref[...], xt_ref[latent:, :])
    for step in range(steps):
        mish_forward_low(pre_ref, gain1, shift1, h1_ref, hat1_ref, slope1_ref, scale_ref, 0, lanes_of(step), size)
    pre_ref[...] = nn(w2t_ref[...], h1_ref[...]) if turned else tn(w2_ref[...], h1_ref[...])
    for step in range(steps):
        mish_forward_low(pre_ref, gain2, shift2, h2_ref, hat2_ref, slope2_ref, scale_ref, 1, lanes_of(step), size)
    lg_ref[...] = nn(hot_ref[...], h2_ref[...])
    share = 0.1 if head == 0 else 0.1 / (heads - 1)
    bins_ref = rb_ref if head == 0 else vb_ref
    for step in range(steps):
        at = lanes_of(step)
        logits = jnp.where(bin_ids < bins, lg_ref[:, at], F32(-1e30))
        chosen = bin_ids == bins_ref[step : step + 1, mine]
        top = jnp.max(logits, axis=0, keepdims=True)
        powers = jnp.exp(logits - top)
        total = column_sum(powers)
        picked = column_sum(jnp.where(chosen, logits, 0.0))
        weight = row_weight(step, steps, scale * share, horizon_row, place_ref)
        losses.append(weight * (jnp.log(total) + top - picked))
        dl_ref[:, at] = (powers * (weight / total) - jnp.where(chosen, weight, 0.0)).astype(BF16)
    dh_ref[...] = nn(hop_ref[...], dl_ref[...]).astype(BF16)
    grad_ref[:, first_end + latent :] = nt(h2_ref[...], dl_ref[...]).astype(BF16)
    mish_backward_low(dh_ref, hat2_ref, slope2_ref, scale_ref, 1, steps, sums_ref, 2, d2_ref, size)
    dh_ref[...] = nn(w2_ref[...], d2_ref[...]).astype(BF16)
    grad_ref[:, first_end : first_end + latent] = nt(d2_ref[...], h1_ref[...]).astype(BF16)
    mish_backward_low(dh_ref, hat1_ref, slope1_ref, scale_ref, 0, steps, sums_ref, 0, d1_ref, size)
    low_part = nn(w1_ref[0:latent, :], d1_ref[...])
    side_part = nn(tail_ref[...], d1_ref[...])
    if not chained:
        dx_ref[0:latent, :] = low_part
        dx_ref[latent:, :] = side_part
    else:
        dx_ref[0:latent, :] = before_ref[0:latent, :] + low_part
        dx_ref[latent:, :] = before_ref[latent:, :] + side_part
    if form == "rows":
        grad_ref[:, 0:latent] = nn(d1_ref[...], x_ref[:, 0:latent]).astype(BF16)
        side_terms = nn(d1_ref[...], x_ref[:, latent:])
    else:
        grad_ref[:, 0:latent] = nt(d1_ref[...], xt_ref[0:latent, :]).astype(BF16)
        side_terms = nt(d1_ref[...], xt_ref[latent:, :])
    side_terms = with_vectors(side_terms, vector_sums(sums_ref, spread_ref, 2), tail_rows)
    grad_ref[:, latent:first_end] = side_terms.astype(BF16)
    for relative, (which, slot) in enumerate(slots):
        start = pl.multiple_of((place_ref[0] ^ relative) * GROUP, GROUP)
        (keep_ref, send_ref)[which][slot] = grad_ref[pl.ds(start, GROUP), :]
    loss_ref[...] = functools.reduce(jnp.add, losses)
    for each in copies:
        each.wait()


def backward_kernel(
    steps, scale, order, losses, after,
    place_ref, xt_ref, soft_ref, h1_ref, hat1_ref, slope1_ref, h2_ref, hat2_ref, slope2_ref, scale_ref,
    w1_ref, w2_ref, dyn_ref, hz_ref, g_ref, dx_ref, *rest,
):
    initial = order[0] == steps - 1
    final = order[-1] == 0
    loss_refs, rest = rest[:losses], rest[losses:]
    held_refs, rest = ((), rest) if initial else (rest[:4], rest[4:])
    (tgt_hbm, low_ref, first_ref, side_ref, loss_ref, sums_ref, tgt_ref, rows_ref, spread_ref, tail_ref, pre_ref,
     d1_ref, d2_ref, do_ref, grad_ref, sems) = rest[after:]
    mine = own_lanes(place_ref)
    loads = dict(zip(order, load_all([(tgt_hbm.at[step, mine, :], tgt_ref.at[step], sems.at[step]) for step in order])))
    latent = dyn_ref.shape[1]
    here = slice(0, LANES)
    horizon_row = hz_ref[:, mine]
    spread_columns(g_ref[0], g_ref[0], rows_ref, spread_ref)
    tail_rows = w1_ref.shape[0] - latent
    tail_ref[...] = padded_rows(w1_ref[latent:, :], LANES)
    first_end = latent + LANES
    second_end = first_end + latent
    if initial:
        loss = functools.reduce(jnp.add, [each[...] for each in loss_refs])
        side = jnp.zeros((LANES, LANES), F32)
        incoming = None
    else:
        before_ref, given_ref, given_side_ref, given_sums_ref = held_refs
        loss = loss_refs[0][...]
        side = given_side_ref[...]
        incoming = given_ref[...].astype(F32)
        sums_ref[...] = given_sums_ref[...]
    pending = []

    def add_terms(at, fresh, last):
        terms = (
            (slice(0, first_end), nt(d1_ref[:, at], xt_ref[:, at])),
            (slice(first_end, second_end), nt(d2_ref[:, at], h1_ref[:, at])),
            (slice(second_end, second_end + latent), nt(h2_ref[:, at], do_ref[:, at])),
        )
        for lanes, term in terms:
            if not fresh:
                term = term + grad_ref[:, lanes]
            elif not initial:
                term = term + before_ref[:, lanes]
            out_ref = low_ref if last else grad_ref
            if last and final and lanes.start == 0:
                out_ref[:, 0:latent] = term[:, 0:latent].astype(out_ref.dtype)
                vectors = vector_sums(sums_ref, spread_ref, 2)
                out_ref[:, latent:first_end] = with_vectors(term[:, latent:], vectors, tail_rows).astype(out_ref.dtype)
            else:
                out_ref[:, lanes] = term.astype(out_ref.dtype)

    for step in order:
        at = lanes_of(step)
        weight = row_weight(step, steps, scale, horizon_row, place_ref)
        shares = soft_ref[:, lanes_of(step + 1)]
        loads[step].wait()
        residue = shares - jnp.transpose(tgt_ref[step].astype(F32))
        loss = loss + (20.0 / latent) * weight * column_sum(residue * residue)
        grads = residue * ((40.0 / latent) * weight)
        if incoming is not None:
            grads = grads + incoming
        do_ref[:, at] = simplex_back(shares, grads).astype(BF16)
        pre_ref[...] = nn(dyn_ref[...], do_ref[:, at])
        mish_backward(pre_ref, here, hat2_ref, slope2_ref, scale_ref, 1, at, sums_ref, 2, step == steps - 1, d2_ref)
        pre_ref[...] = nn(w2_ref[...], d2_ref[:, at])
        mish_backward(pre_ref, here, hat1_ref, slope1_ref, scale_ref, 0, at, sums_ref, 0, step == steps - 1, d1_ref)
        incoming = nn(w1_ref[0:latent, :], d1_ref[:, at]) + dx_ref[0:latent, at]
        side = side + nn(tail_ref[...], d1_ref[:, at]) + dx_ref[latent:, at]
        incoming = incoming.astype(BF16).astype(F32)
        pending.append(step)
        if len(pending) == 2 or step == order[-1]:
            low, high = min(pending), max(pending) + 1
            add_terms(slice(low * LANES, high * LANES), high == order[0] + 1, low == order[-1])
            pending = []

    first_ref[...] = incoming.astype(BF16)
    side_ref[...] = side
    loss_ref[...] = loss


def ending_kernel(
    slots, tasks, task_width, acted, observed, after,
    place_ref, low_ref, first_ref, side_ref, loss_ref, soft_ref, ein_ref, eh_ref, ehat_ref, eslope_ref, escale_ref,
    ids_ref, e1_ref, eg_ref, e2_ref, *rest,
):
    out_refs, rest = rest[after : after + 4], rest[after + 4 :]
    erows_ref, espread_ref, e1p_ref, epre_ref, esums_ref, ed_ref, egrad_ref = rest
    mine = own_lanes(place_ref)
    here = slice(0, LANES)
    latent = first_ref.shape[0]
    spread_columns(eg_ref[...], eg_ref[...], erows_ref, espread_ref)
    e1p_ref[...] = padded_rows(e1_ref[...], e1p_ref.shape[0])
    d_enc = simplex_back(soft_ref[:, 0:LANES], first_ref[...].astype(F32)).astype(BF16)
    epre_ref[...] = nn(e2_ref[...], d_enc)
    mish_backward(epre_ref, here, ehat_ref, eslope_ref, escale_ref, 0, here, esums_ref, 0, True, ed_ref)
    side_enc = nn(e1p_ref[...], ed_ref[...])
    enc_width = epre_ref.shape[0]
    half = GROUP // 2
    groups = enc_width // half
    egrad_ref[:, 0:half, :] = nt(eh_ref[...], d_enc).reshape(groups, half, latent)
    enc_first = nt(ed_ref[...], ein_ref[...])
    egrad_ref[:, half:, 0:LANES] = enc_first[:, 0:LANES].reshape(groups, half, LANES)
    second_lanes = with_vectors(enc_first[:, LANES : 2 * LANES], vector_sums(esums_ref, espread_ref, 1), LANES - 2)
    egrad_ref[:, half:, LANES : 2 * LANES] = second_lanes.reshape(groups, half, LANES)
    egrad_ref[:, half:, 2 * LANES :] = jnp.zeros((groups, half, latent - 2 * LANES), F32)

    kinds = lax.broadcasted_iota(jnp.int32, (tasks, LANES), 0)
    onehot = (kinds == ids_ref[:, mine]).astype(F32)
    over_lanes = (((1,), (1,)), ((), ()))
    highest = lax.Precision.HIGHEST
    side_terms = lax.dot_general(onehot, side_ref[...], over_lanes, precision=highest, preferred_element_type=F32)
    enc_terms = lax.dot_general(onehot, side_enc, over_lanes, precision=highest, preferred_element_type=F32)
    table = pltpu.roll(side_terms, LANES - acted, 1)
    table = table + pltpu.roll(enc_terms, enc_terms.shape[1] - observed, 1)[:, 0:LANES]
    lane = lax.broadcasted_iota(jnp.int32, table.shape, 1)
    table = jnp.where(lane < task_width, table, 0.0)
    table = jnp.where((lane == LANES - 1) & (kinds == 0), jnp.sum(loss_ref[...], axis=1, keepdims=True), table)
    table_rows = [table[start : start + GROUP] for start in range(0, tasks, GROUP)]
    table_block = jnp.concatenate(table_rows, axis=1).astype(BF16)
    cut = out_refs[0].shape[2]
    width = low_ref.shape[1] - cut
    for half_no in range(2):
        for relative, (which, slot) in enumerate(slots[half_no]):
            dest = place_ref[0] ^ relative
            start = pl.multiple_of(dest * GROUP, GROUP)
            out_ref = out_refs[2 * half_no + which]
            if half_no == 0:
                out_ref[slot] = low_ref[pl.ds(start, GROUP), 0:cut]
            else:
                out_ref[slot, :, 0:width] = low_ref[pl.ds(start, GROUP), cut:]
                out_ref[slot, :, width : width + latent] = egrad_ref[dest].astype(BF16)
                out_ref[slot, :, width + latent :] = table_block


def final_kernel(tasks, task_width, enc_in, bins, net_in, *refs):
    outs = refs[-12:]
    (loss_ref, table_ref, e1_ref, eg_ref, es_ref, e2_ref, first_ref, second_ref, gain_ref, shift_ref, dyn_ref, head_ref) = outs
    refs = refs[:-12]
    tail_refs, refs = refs[:2], refs[2:]
    latent = second_ref.shape[2]
    first_end = latent + LANES
    second_end = first_end + latent

    def put_net(net, value):
        first_ref[net] = value[:, 0:net_in]
        second_ref[net] = value[:, first_end:second_end]
        turned = jnp.transpose(value[:, latent:first_end])
        for layer in range(2):
            row = net_in - latent + 2 * layer
            gain_ref[net, layer : layer + 1, :] = turned[row : row + 1, :]
            shift_ref[net, layer : layer + 1, :] = turned[row + 1 : row + 2, :]

    tail = functools.reduce(jnp.add, [ref[0].astype(F32) for ref in tail_refs])
    put_net(0, tail)
    dyn_ref[...] = tail[:, second_end : second_end + latent]
    enc = tail[:, second_end + latent : second_end + 2 * latent]
    half = GROUP // 2
    e2_ref[...] = 0.3 * enc[0:half, :]
    e1_ref[...] = 0.3 * enc[half:, 0:enc_in]
    turned = 0.3 * jnp.transpose(enc[half:, LANES : 2 * LANES])
    eg_ref[...] = turned[LANES - 2 : LANES - 1, :]
    es_ref[...] = turned[LANES - 1 : LANES, :]
    table = tail[:, second_end + 2 * latent :]
    loss_ref[...] = table[0:1, LANES - 1 : LANES]
    for place in range(tasks // GROUP):
        table_ref[place * GROUP : (place + 1) * GROUP, :] = table[:, place * LANES : place * LANES + task_width]
    net = 1
    for one_ref, other_ref in zip(refs[0::2], refs[1::2]):
        for one in range(one_ref.shape[1]):
            value = one_ref[0, one].astype(F32) + other_ref[0, one].astype(F32)
            put_net(net, value)
            head_ref[net - 1] = value[:, second_end : second_end + bins]
            net += 1


def swap(value, axis, distance):
    count = lax.axis_size(axis)
    return lax.ppermute(value, axis, [(place, place ^ distance) for place in range(count)])


def exchange(parts, axis, scale):
    total = parts[0].astype(F32)
    for distance in range(1, len(parts)):
        total = total + swap(parts[distance], axis, distance * scale).astype(F32)
    return total


def scatter_plain(packed, chips, sections):
    held = packed.reshape((sections, chips, CORES) + packed.shape[1:])
    batch_no = lax.axis_index("batch")
    places = (
        ("batch", 1, CORES, 2, batch_no % CORES),
        ("batch", CORES, chips, 1, batch_no // CORES),
        ("section", 1, sections, 0, lax.axis_index("section")),
    )
    for axis, scale, count, dim, mine in places:
        parts = [lax.dynamic_index_in_dim(held, mine ^ other, dim, keepdims=False) for other in range(count)]
        held = exchange(parts, axis, scale)
        held = held.astype(BF16) if dim else held
    return held


def on_device(
    observations,
    actions,
    targets,
    task_ids,
    horizons,
    reward_bins,
    value_bins,
    task_table,
    enc_first,
    enc_gain,
    enc_shift,
    enc_second,
    net_first,
    net_second,
    net_gain,
    net_shift,
    dyn_out,
    head_out,
):
    sections = lax.axis_size("section")
    batches = lax.axis_size("batch")
    section_no = lax.axis_index("section")
    chips = batches // CORES
    devices = sections * batches
    steps, rows_all, acted = actions.shape
    observed = observations.shape[1]
    rows = rows_all // sections
    latent = dyn_out.shape[1]
    hidden = dyn_out.shape[0]
    tasks, task_width = task_table.shape
    heads, _, bins = head_out.shape
    nets, net_in, _ = net_first.shape
    enc_in, enc_width = enc_first.shape
    wide = steps * LANES
    scale = 1.0 / (rows_all * batches * steps)
    groups = hidden // GROUP
    in_place = hidden // devices == GROUP
    start = section_no * rows
    block_no = start // LANES
    first_lane = start - block_no * LANES
    me = section_no * batches + lax.axis_index("batch") if in_place else jnp.int32(0)
    place = jnp.stack([me, block_no, first_lane, first_lane + rows]).astype(jnp.int32)
    bits = [("batch", 1 << bit) for bit in range(batches.bit_length() - 1)]
    bits += [("section", 1 << bit) for bit in range(sections.bit_length() - 1)]

    def slots_of(order):
        if not in_place:
            return tuple((relative // (groups // 2), relative % (groups // 2)) for relative in range(groups))
        found = []
        for relative in range(groups):
            slot = 0
            for bit in order:
                slot = 2 * slot + (relative >> bit & 1)
            found.append((slot // (groups // 2), slot % (groups // 2)))
        return tuple(found)

    plain = tuple(range(len(bits)))
    y_first = (0, 2, 1) + tuple(range(3, len(bits))) if in_place else plain
    half_slots = groups // 2
    shape_of = jax.ShapeDtypeStruct
    smem = pl.BlockSpec(memory_space=pltpu.SMEM)
    local = pl.BlockSpec(memory_space=pltpu.VMEM)
    far = pl.BlockSpec(memory_space=pltpu.HBM)
    anywhere = pl.BlockSpec(memory_space=pl.ANY)
    first_far, second_far, dyn_far, targets_far = [
        pltpu.with_memory_space_constraint(array, pltpu.HBM) for array in (net_first, net_second, dyn_out, targets)
    ]
    vmem = pltpu.VMEM
    dmas = pltpu.SemaphoreType.DMA

    def params(mebibytes, fused=False):
        return pltpu.CompilerParams(
            vmem_limit_bytes=mebibytes * 1024 * 1024, fuse_transposed_lhs_in_matmul=fused
        )

    def cost(flops, moved):
        return pl.CostEstimate(flops=flops, bytes_accessed=moved, transcendentals=0)

    ids_row = task_ids.reshape(1, rows_all)
    horizon_row = horizons.reshape(1, rows_all)
    eg_row = enc_gain.reshape(1, enc_width)
    es_row = enc_shift.reshape(1, enc_width)
    head_turned = head_out.transpose(0, 2, 1)
    low = lambda lanes: shape_of((hidden, lanes), BF16)
    forward_shapes = (
        shape_of((latent + LANES, wide), BF16),
        shape_of((latent, wide + LANES), F32),
        low(wide), low(wide), low(wide), low(wide), low(wide), low(wide),
        shape_of((8, wide), F32),
        shape_of((2 * LANES, LANES), BF16),
        shape_of((enc_width, LANES), BF16),
        shape_of((enc_width, LANES), BF16),
        shape_of((enc_width, LANES), BF16),
        shape_of((8, LANES), F32),
        shape_of((net_in, hidden), BF16),
        shape_of((hidden, hidden), BF16),
        shape_of((hidden, latent), BF16),
        shape_of((wide, latent + LANES), BF16),
    )

    weight_shapes = (shape_of((net_in, hidden), BF16), shape_of((hidden, hidden), BF16))

    early = [
        pltpu.with_memory_space_constraint(array, pltpu.HBM)
        for array in (
            observations.T, actions.transpose(0, 2, 1), ids_row, task_table, enc_first, eg_row, es_row, enc_second,
            net_gain, net_shift,
        )
    ]
    made = pl.pallas_call(
        functools.partial(forward_kernel, steps),
        out_shape=forward_shapes + weight_shapes,
        in_specs=[smem] + [far] * 13,
        out_specs=[local] * (len(forward_shapes) + 2),
        scratch_shapes=[
            vmem((8, hidden), F32),
            vmem((4, hidden, LANES), F32),
            vmem((8, enc_width), F32),
            vmem((2, enc_width, LANES), F32),
            vmem((tasks, 2 * LANES), F32),
            vmem((LANES, LANES), F32),
            vmem((2 * LANES, enc_width), BF16),
            vmem((hidden, latent + LANES), BF16),
            vmem((hidden, hidden), BF16),
            vmem((latent, hidden), BF16),
            vmem((hidden, LANES), F32),
            vmem((enc_width, LANES), F32),
            *[vmem(each.shape, each.dtype) for each in early],
            dmas((5,)),
            dmas((len(early),)),
        ],
        compiler_params=params(VMEM_A),
        cost_estimate=cost(10_000_000_000, 8_000_000),
        name="forward_chain",
    )(
        place, *early, first_far, second_far, dyn_far,
    )
    saved, x_rows, weights = made[:-3], made[-3], made[-2:]
    xt = saved[0]
    head_width = latent + LANES + hidden + LANES

    def run_head(head, ahead, weights, before, after):
        pack_shape = shape_of((half_slots, GROUP, head_width), BF16)
        dx_shape = shape_of((latent + LANES, wide), F32)
        out_shapes = (pack_shape, pack_shape, dx_shape, shape_of((1, LANES), F32))
        args = [place, xt, x_rows, *weights, head_turned, net_gain, net_shift, reward_bins, value_bins, horizon_row]
        specs = [smem] + [local] * 10
        aliases = {}
        if before is not None:
            aliases = {len(args): 2}
            args.append(before)
            specs.append(local)
        args += after
        specs += [anywhere] * len(after)
        if ahead:
            args += [first_far, second_far]
            specs += [far, far]
            out_shapes += weight_shapes
        low_wide = vmem((hidden, wide), BF16)
        scratch = [
            vmem((8, hidden), F32),
            vmem((4, hidden, LANES), F32),
            vmem((hidden, latent + LANES), BF16),
            vmem((hidden, hidden), BF16),
            vmem((LANES, hidden), BF16),
            vmem((hidden, LANES), BF16),
            vmem((LANES, hidden), BF16),
            vmem((hidden, wide), F32),
            vmem((LANES, wide), F32),
        ]
        scratch += [low_wide] * 6
        scratch += [vmem((8, wide), F32), vmem((4, hidden, LANES), F32)]
        scratch += [low_wide] * 3
        scratch += [vmem((LANES, wide), BF16), vmem((hidden, head_width), BF16)]
        if ahead:
            scratch.append(dmas((2,)))
        return pl.pallas_call(
            functools.partial(
                heads_kernel, steps, scale, slots_of(plain), head, ahead, heads, bins, before is not None, len(after), FORMS[head]
            ),
            out_shape=out_shapes,
            in_specs=specs,
            out_specs=[local] * len(out_shapes),
            scratch_shapes=scratch,
            input_output_aliases=aliases,
            compiler_params=params(VMEM_B, FORMS[head] == "fused"),
            cost_estimate=cost(9_000_000_000, 4_000_000),
            name=f"head_{head}",
        )(*args)

    def phase(pair, bit):
        return pair[0], swap(pair[1], *bits[bit])

    def fold(members, *tokens, by_lanes=False):
        slots_now = members[0][0].shape[0] // 2
        shape = members[0][0].shape[1:]
        if by_lanes:
            shape = shape[:-1] + (sum(kept.shape[-1] for kept, _ in members),)
        elif len(members) > 1:
            shape = (len(members),) + shape
        out_shape = shape_of((slots_now,) + shape, BF16)
        inputs = [each for member in members for each in member]

        def fold_kernel(*refs):
            refs = refs[len(tokens) :]
            outs = refs[-2:]
            lane = 0
            for place in range(len(members)):
                kept_ref, came_ref = refs[2 * place], refs[2 * place + 1]
                width = kept_ref.shape[-1]
                for half in range(2):
                    part = pl.ds(half * slots_now, slots_now)
                    value = (kept_ref[part].astype(F32) + came_ref[part].astype(F32)).astype(BF16)
                    if by_lanes:
                        outs[half][..., lane : lane + width] = value
                    elif len(members) > 1:
                        outs[half][:, place] = value
                    else:
                        outs[half][...] = value
                lane += width

        return pl.pallas_call(
            fold_kernel,
            out_shape=(out_shape, out_shape),
            in_specs=[anywhere] * len(tokens) + [local] * len(inputs),
            out_specs=(local, local),
            compiler_params=params(VMEM_SUM),
            cost_estimate=cost(1_000_000, 2_000_000),
            name="fold",
        )(*tokens, *inputs)

    net_width = latent + LANES + hidden + latent
    chain_inputs = saved[:9] + saved[14:]

    def run_backward(order, losses, held, after):
        final = order[-1] == 0
        out_shapes = (
            shape_of((hidden, net_width), BF16 if final else F32),
            shape_of((latent, LANES), BF16),
            shape_of((LANES, LANES), F32),
            shape_of((1, LANES), F32),
            shape_of((4, hidden, LANES), F32),
        )
        args = [place, *chain_inputs, horizon_row, net_gain, dx, *losses, *held]
        return pl.pallas_call(
            functools.partial(backward_kernel, steps, scale, order, len(losses), len(after)),
            out_shape=out_shapes,
            in_specs=[smem] + [local] * (len(args) - 1) + [anywhere] * len(after) + [far],
            out_specs=[local] * len(out_shapes),
            scratch_shapes=[
                vmem((steps, LANES, latent), BF16),
                vmem((8, hidden), F32),
                vmem((4, hidden, LANES), F32),
                vmem((LANES, hidden), BF16),
                vmem((hidden, LANES), F32),
                vmem((hidden, wide), BF16),
                vmem((hidden, wide), BF16),
                vmem((latent, wide), BF16),
                vmem((hidden, net_width), F32),
                dmas((steps,)),
            ],
            compiler_params=params(VMEM_C),
            cost_estimate=cost(7_000_000_000, 8_000_000),
            name=f"backward_{order[0]}",
        )(*args, *after, targets_far)

    packs, loss_parts = [], []
    dx = None
    flights = []
    after = []

    def advance(head, bit, token, kept_back):
        if in_place and 0 <= head < heads:
            pair = fold([flights[head]], token)
            kept_back.append(pair[0])
            flights[head] = phase(pair, plain[bit])

    for head in range(heads):
        ahead = head + 1 < heads
        result = run_head(head, ahead, weights, dx, after)
        keep, send, dx, loss = result[:4]
        weights = result[4:]
        packs.append((keep, send))
        loss_parts.append(loss)
        after = []
        advance(head - 1, 1, loss, after)
        advance(head - 2, 2, loss, after)
        if in_place:
            flights.append(phase((keep, send), plain[0]))
    early = heads // 2
    half_way = steps // 2
    if in_place:
        group = fold(flights[0:early], loss_parts[-1])
        after.append(group[0])
        group = phase(group, plain[3])
    chain = run_backward(tuple(range(steps - 1, half_way - 1, -1)), loss_parts, [], after)
    after = []
    advance(heads - 1, 1, chain[3], after)
    advance(heads - 2, 2, chain[3], after)
    if in_place:
        group = fold([group], chain[3])
        after.append(group[0])
        group = phase(group, plain[4])
        after.append(flights[heads - 3][1])
    chain = run_backward(
        tuple(range(half_way - 1, -1, -1)), [chain[3]], [chain[0], chain[1], chain[2], chain[4]], after
    )
    after = []
    advance(heads - 1, 2, chain[3], after)
    if in_place:
        after.append(flights[heads - 2][1])

    tail_width = net_width + latent + tasks // GROUP * LANES
    cut = tail_width // 2 // LANES * LANES
    one_shape = shape_of((half_slots, GROUP, cut), BF16)
    two_shape = shape_of((half_slots, GROUP, tail_width - cut), BF16)
    tail_slots = (slots_of(plain), slots_of(y_first))
    ended = pl.pallas_call(
        functools.partial(ending_kernel, tail_slots, tasks, task_width, acted, observed, len(after)),
        out_shape=(one_shape, one_shape, two_shape, two_shape),
        in_specs=[smem] + [local] * 14 + [anywhere] * len(after),
        out_specs=[local] * 4,
        scratch_shapes=[
            vmem((8, enc_width), F32),
            vmem((2, enc_width, LANES), F32),
            vmem((2 * LANES, enc_width), BF16),
            vmem((enc_width, LANES), F32),
            vmem((2, enc_width, LANES), F32),
            vmem((enc_width, LANES), BF16),
            vmem((groups, GROUP, latent), F32),
        ],
        compiler_params=params(VMEM_SUM),
        cost_estimate=cost(1_000_000_000, 4_000_000),
        name="ending",
    )(place, *chain[:4], saved[1], *saved[9:14], ids_row, enc_first, eg_row, enc_second, *after)

    if in_place:
        one = phase(ended[0:2], plain[0])
        two = phase(ended[2:4], y_first[0])
        one = phase(fold([one], ended[0]), plain[1])
        two = phase(fold([two], ended[0]), y_first[1])
        rest = phase(fold(flights[early:], one[0]), plain[3])
        one = phase(fold([one]), plain[2])
        two = phase(fold([two]), y_first[2])
        rest = phase(fold([rest], one[0]), plain[4])
        tail = phase(fold([one, two], by_lanes=True), plain[3])
        tail = phase(fold([tail]), plain[4])
        each = GROUP // 2
        out_shapes = (
            shape_of((1, 1), F32),
            shape_of((tasks, task_width), F32),
            shape_of((each, enc_in), F32),
            shape_of((1, each), F32),
            shape_of((1, each), F32),
            shape_of((each, latent), F32),
            shape_of((nets, GROUP, net_in), F32),
            shape_of((nets, GROUP, hidden), F32),
            shape_of((nets, 2, GROUP), F32),
            shape_of((nets, 2, GROUP), F32),
            shape_of((GROUP, latent), F32),
            shape_of((heads, GROUP, bins), F32),
        )
        ends = [*tail, *group, *rest]
        outs = list(pl.pallas_call(
            functools.partial(final_kernel, tasks, task_width, enc_in, bins, net_in),
            out_shape=out_shapes,
            in_specs=[local] * len(ends),
            out_specs=[local] * len(out_shapes),
            compiler_params=params(VMEM_SUM),
            cost_estimate=cost(1_000_000, 4_000_000),
            name="last_sums",
        )(*ends))
        outs[0] = outs[0].reshape(())
        outs[2] = outs[2].T
        outs[3], outs[4] = outs[3].reshape(each), outs[4].reshape(each)
        outs[6] = outs[6].transpose(0, 2, 1)
        outs[7] = outs[7].transpose(0, 2, 1)
        return tuple(outs)

    def scattered(keep, send):
        mine = hidden // devices
        packed = jnp.concatenate([keep, send], axis=0)
        middle = packed.shape[1:-2]
        packed = packed.reshape((groups,) + middle + (GROUP // mine, mine, packed.shape[-1]))
        packed = jnp.moveaxis(packed, -3, 1).reshape((devices,) + middle + (mine, packed.shape[-1]))
        return scatter_plain(packed, chips, sections)

    head_sum = jnp.stack([scattered(*pack) for pack in packs], axis=0)
    enc_each = enc_width // devices
    keep, send = [jnp.concatenate([ended[place], ended[2 + place]], axis=2) for place in range(2)]
    net_sum = scattered(keep[:, :, 0:net_width], send[:, :, 0:net_width])
    rest = jnp.concatenate([keep, send], axis=0)
    enc_all = rest[:, :, net_width : net_width + latent].reshape(groups, 2, enc_width // groups, latent)
    enc_all = enc_all.transpose(0, 2, 1, 3).reshape(devices, enc_each, 2, latent)
    enc_sum = scatter_plain(enc_all, chips, sections)
    enc_sum = enc_sum.transpose(1, 0, 2).reshape(2 * enc_each, latent)
    table_sum = lax.psum(rest[0, :, net_width + latent :].astype(F32), ("section", "batch"))
    first_end = latent + LANES
    net_row = jnp.concatenate([net_sum[:, 0 : first_end + hidden], jnp.zeros_like(net_sum[:, 0:LANES])], axis=1)
    sums = jnp.concatenate([net_row[None], head_sum], axis=0)
    vectors = sums[:, :, net_in : net_in + 4].transpose(0, 2, 1)
    table = table_sum.reshape(GROUP, tasks // GROUP, LANES).transpose(1, 0, 2).reshape(tasks, LANES)
    enc_rows = enc_sum[enc_each:]
    return (
        table[0, LANES - 1],
        table[:, 0:task_width],
        0.3 * enc_rows[:, 0:enc_in].T,
        0.3 * enc_rows[:, 2 * LANES - 2],
        0.3 * enc_rows[:, 2 * LANES - 1],
        0.3 * enc_sum[0:enc_each],
        sums[:, :, 0:net_in].transpose(0, 2, 1),
        sums[:, :, first_end : first_end + hidden].transpose(0, 2, 1),
        vectors[:, 0::2],
        vectors[:, 1::2],
        net_sum[:, first_end + hidden :],
        head_sum[:, :, first_end + hidden : first_end + hidden + bins],
    )


def solution(mesh):
    both = ("section", "batch")
    return jax.shard_map(
        on_device,
        mesh=mesh,
        in_specs=(
            P("batch", None),
            P(None, "batch", None),
            P(None, "batch", None),
            P("batch"),
            P("batch"),
            P(None, "batch"),
            P(None, "batch"),
        )
        + (P(),) * 11,
        out_specs=(
            P(),
            P(),
            P(None, both),
            P(both),
            P(both),
            P(both, None),
            P(None, None, both),
            P(None, None, both),
            P(None, None, both),
            P(None, None, both),
            P(both, None),
            P(None, both, None),
        ),
        check_vma=False,
    )
```

```python
import functools

import jax
import jax.numpy as jnp
from jax import lax
from jax.experimental import pallas as pl
from jax.experimental.pallas import tpu as pltpu
from jax.sharding import PartitionSpec as P

CORES = 2
LANES = 128
GROUP = 16
BF16 = jnp.bfloat16
F32 = jnp.float32
VMEM_A = 18
VMEM_B = 20
VMEM_SUM = 6
VMEM_C = 20


def nn(left, right):
    return lax.dot_general(left, right, (((1,), (0,)), ((), ())), preferred_element_type=F32)


def nt(left, right):
    return lax.dot_general(left, right, (((1,), (1,)), ((), ())), preferred_element_type=F32)


def tn(left, right):
    return lax.dot_general(left, right, (((0,), (0,)), ((), ())), preferred_element_type=F32)


def column_sum(value):
    grouped = value.reshape(value.shape[0] // 8, 8, value.shape[1])
    return jnp.sum(jnp.sum(grouped, axis=0), axis=0, keepdims=True)


def slabs(features, size=64):
    return [slice(start, start + size) for start in range(0, features, size)]


def lanes_of(step):
    return slice(step * LANES, (step + 1) * LANES)


def spread_columns(gain_rows, shift_rows, rows_ref, spread_ref):
    count = gain_rows.shape[0]
    rows_ref[...] = jnp.zeros_like(rows_ref)
    rows_ref[0:count, :] = gain_rows
    rows_ref[count : 2 * count, :] = shift_rows
    turned = jnp.transpose(rows_ref[...])
    for place in range(2 * count):
        spread_ref[place] = jnp.broadcast_to(turned[:, place : place + 1], spread_ref.shape[1:])


def mish_forward(pre_ref, pre_at, gain_ref, shift_ref, hid_ref, hat_ref, slope_ref, scale_ref, scale_row, at):
    features = pre_ref.shape[0]
    row_mean = column_sum(pre_ref[:, pre_at]) * (1.0 / features)
    centred = pre_ref[:, pre_at] - row_mean
    spread = column_sum(centred * centred) * (1.0 / features)
    scale = lax.rsqrt(spread + 1e-05)
    scale_ref[scale_row : scale_row + 1, at] = scale
    for part in slabs(features):
        hat = (pre_ref[part, pre_at] - row_mean) * scale
        normed = hat * gain_ref[part, :] + shift_ref[part, :]
        power = jnp.exp(normed)
        top = power * (power + 2.0)
        inverse = pl.reciprocal(top + 2.0, approx=True)
        ratio = top * inverse
        hid_ref[part, at] = (normed * ratio).astype(BF16)
        tilt = power * inverse
        slope = ratio + normed * (4.0 * (tilt * (tilt + inverse)))
        slope_ref[part, at] = (slope * gain_ref[part, :]).astype(BF16)
        hat_ref[part, at] = hat.astype(BF16)


def mish_backward(grad_ref, grad_at, hat_ref, slope_ref, scale_ref, scale_row, at, sums_ref, sums_at, first, out_ref):
    features = grad_ref.shape[0]
    total_one = jnp.zeros((8, LANES), F32)
    total_two = jnp.zeros((8, LANES), F32)
    for part in slabs(features):
        term = grad_ref[part, grad_at] * slope_ref[part, at].astype(F32)
        grad_ref[part, grad_at] = term
        crossed = term * hat_ref[part, at].astype(F32)
        groups = (term.shape[0] // 8, 8, LANES)
        total_one = total_one + jnp.sum(term.reshape(groups), axis=0)
        total_two = total_two + jnp.sum(crossed.reshape(groups), axis=0)
        if first:
            sums_ref[sums_at, part, :] = term
            sums_ref[sums_at + 1, part, :] = crossed
        else:
            sums_ref[sums_at, part, :] += term
            sums_ref[sums_at + 1, part, :] += crossed
    mean_one = jnp.sum(total_one, axis=0, keepdims=True) * (1.0 / features)
    mean_two = jnp.sum(total_two, axis=0, keepdims=True) * (1.0 / features)
    scale = scale_ref[scale_row : scale_row + 1, at]
    for part in slabs(features):
        rest = grad_ref[part, grad_at] - mean_one - hat_ref[part, at].astype(F32) * mean_two
        out_ref[part, at] = (rest * scale).astype(BF16)


def mish_forward_low(pre_ref, gain_ref, shift_ref, hid_ref, hat_ref, slope_ref, scale_ref, scale_row, at):
    features = pre_ref.shape[0]
    row_mean = column_sum(pre_ref[:, at]) * (1.0 / features)
    centred = pre_ref[:, at] - row_mean
    spread = column_sum(centred * centred) * (1.0 / features)
    scale = lax.rsqrt(spread + 1e-05)
    scale_ref[scale_row : scale_row + 1, at] = scale
    for part in slabs(features):
        hat = (pre_ref[part, at] - row_mean) * scale
        normed = (hat * gain_ref[part, :] + shift_ref[part, :]).astype(BF16)
        hat_ref[part, at] = hat.astype(BF16)
        power = jnp.exp(normed)
        top = power * (power + 2.0)
        inverse = pl.reciprocal(top + 2.0, approx=True)
        ratio = top * inverse
        hid_ref[part, at] = normed * ratio
        tilt = power * inverse
        slope = ratio + (4.0 * normed) * (tilt * (tilt + inverse))
        slope_ref[part, at] = slope * gain_ref[part, :].astype(BF16)


def mish_backward_low(grad_ref, hat_ref, slope_ref, scale_ref, scale_row, steps, sums_ref, sums_at, out_ref):
    features = grad_ref.shape[0]
    rows = []
    for step in range(steps):
        at = lanes_of(step)
        total_one = jnp.zeros((16, LANES), F32)
        total_two = jnp.zeros((16, LANES), F32)
        for part in slabs(features):
            term = grad_ref[part, at] * slope_ref[part, at]
            crossed = term * hat_ref[part, at]
            grad_ref[part, at] = term
            groups = (term.shape[0] // 16, 16, LANES)
            term = term.reshape(groups)
            crossed = crossed.reshape(groups)
            total_one = total_one + functools.reduce(jnp.add, [term[k] for k in range(groups[0])]).astype(F32)
            total_two = total_two + functools.reduce(jnp.add, [crossed[k] for k in range(groups[0])]).astype(F32)
        scale = scale_ref[scale_row : scale_row + 1, at]
        mean_one = jnp.sum(total_one, axis=0, keepdims=True) * (1.0 / features)
        mean_two = jnp.sum(total_two, axis=0, keepdims=True) * (1.0 / features)
        rows.append((mean_one.astype(BF16), mean_two.astype(BF16), scale.astype(BF16)))
    for part in slabs(features):
        sum_one, sum_two = None, None
        for step, (mean_one, mean_two, scale) in enumerate(rows):
            at = lanes_of(step)
            term = grad_ref[part, at]
            hat = hat_ref[part, at]
            out_ref[part, at] = (term - mean_one - hat * mean_two) * scale
            crossed = term * hat
            sum_one = term if sum_one is None else sum_one + term
            sum_two = crossed if sum_two is None else sum_two + crossed
        sums_ref[sums_at, part, :] = sum_one.astype(F32)
        sums_ref[sums_at + 1, part, :] = sum_two.astype(F32)


def simplex(values):
    grouped = values.reshape(values.shape[0] // 8, 8, values.shape[1])
    powers = jnp.exp(grouped - jnp.max(grouped, axis=1, keepdims=True))
    shares = powers / jnp.sum(powers, axis=1, keepdims=True)
    return shares.reshape(values.shape)


def simplex_back(shares, grads):
    grouped = (shares.shape[0] // 8, 8, shares.shape[1])
    crossed = jnp.sum((shares * grads).reshape(grouped), axis=1, keepdims=True)
    return (shares.reshape(grouped) * (grads.reshape(grouped) - crossed)).reshape(shares.shape)


def row_weight(step, steps, scale, horizon_row, place_ref):
    lane = lax.broadcasted_iota(jnp.int32, (1, LANES), 1)
    mine = (lane >= place_ref[2]) & (lane < place_ref[3]) & (horizon_row > step)
    return jnp.where(mine, F32(scale * 0.5 ** (step / (steps - 1))), 0.0)


def padded_rows(value, rows):
    zeros = jnp.zeros((rows - value.shape[0], value.shape[1]), F32)
    return jnp.concatenate([value.astype(F32), zeros], axis=0).astype(BF16)


def transpose_into(out_ref, source_ref, rows):
    for start in range(0, rows, LANES):
        out_ref[:, start : start + LANES] = jnp.transpose(source_ref[start : start + LANES, :])


def vector_sums(sums_ref, gains_ref, layers):
    vectors = []
    for layer in range(layers):
        inverse = 1.0 / gains_ref[layer]
        vectors.append(jnp.sum(sums_ref[2 * layer + 1] * inverse, axis=1, keepdims=True))
        vectors.append(jnp.sum(sums_ref[2 * layer] * inverse, axis=1, keepdims=True))
    return vectors


def own_lanes(place_ref):
    return pl.ds(pl.multiple_of(place_ref[1] * LANES, LANES), LANES)


def load_all(copies):
    made = [pltpu.make_async_copy(*each) for each in copies]
    for each in made:
        each.start()
    return made


def with_vectors(value, vectors, first_lane):
    lane = lax.broadcasted_iota(jnp.int32, value.shape, 1)
    for place, vector in enumerate(vectors):
        value = jnp.where(lane == first_lane + place, vector, value)
    return value


def forward_kernel(
    steps,
    place_ref, obs_hbm, act_hbm, ids_hbm, table_hbm, e1_hbm, eg_hbm, es_hbm, e2_hbm, g_hbm, s_hbm,
    w1_hbm, w2_hbm, dyn_hbm,
    xt_ref, soft_ref, h1_ref, hat1_ref, slope1_ref, h2_ref, hat2_ref, slope2_ref, scale_ref,
    ein_ref, eh_ref, ehat_ref, eslope_ref, escale_ref,
    w1_ref, w2_ref, dyn_ref, x_ref, next1_ref, next2_ref,
    rows_ref, spread_ref, erows_ref, espread_ref, wide_ref, tall_ref, e1p_ref, w1t_ref, w2t_ref, dynt_ref, pre_ref, epre_ref,
    obs_ref, act_ref, ids_ref, table_ref, e1_ref, eg_ref, es_ref, e2_ref, g_ref, s_ref,
    sems, early_sems,
):
    early = load_all([
        (table_hbm, table_ref, early_sems.at[0]),
        (ids_hbm, ids_ref, early_sems.at[1]),
        (obs_hbm, obs_ref, early_sems.at[2]),
        (e1_hbm, e1_ref, early_sems.at[3]),
        (eg_hbm, eg_ref, early_sems.at[4]),
        (es_hbm, es_ref, early_sems.at[5]),
        (e2_hbm, e2_ref, early_sems.at[6]),
        (act_hbm, act_ref, early_sems.at[7]),
        (g_hbm, g_ref, early_sems.at[8]),
        (s_hbm, s_ref, early_sems.at[9]),
    ])
    first, second, third, fourth, fifth = load_all([
        (w1_hbm.at[0], w1_ref, sems.at[0]),
        (w2_hbm.at[0], w2_ref, sems.at[1]),
        (dyn_hbm, dyn_ref, sems.at[2]),
        (w1_hbm.at[1], next1_ref, sems.at[3]),
        (w2_hbm.at[1], next2_ref, sems.at[4]),
    ])
    latent = dyn_ref.shape[1]
    tasks, task_width = table_ref.shape
    observed = obs_ref.shape[0]
    acted = act_ref.shape[1]
    mine = own_lanes(place_ref)
    for each in early:
        each.wait()
    spread_columns(eg_ref[...], es_ref[...], erows_ref, espread_ref)
    kinds = lax.broadcasted_iota(jnp.int32, (tasks, LANES), 0)
    onehot = (kinds == ids_ref[:, mine]).astype(F32).astype(BF16)
    wide_ref[...] = jnp.zeros_like(wide_ref)
    wide_ref[:, 0:task_width] = table_ref[...].astype(F32)
    table_tail = pltpu.roll(wide_ref[:, 0:LANES], acted, 1).astype(BF16)
    table_enc = pltpu.roll(wide_ref[...], observed, 1).astype(BF16)
    aux = tn(table_tail, onehot)
    tall_ref[...] = jnp.zeros_like(tall_ref)
    tall_ref[0:observed, :] = obs_ref[:, mine].astype(F32)
    ein = tn(table_enc, onehot)
    ein_ref[0:LANES, :] = (ein[0:LANES] + tall_ref[...]).astype(BF16)
    ein_ref[LANES:, :] = ein[LANES:].astype(BF16)
    e1p_ref[...] = padded_rows(e1_ref[...], e1p_ref.shape[0])
    epre_ref[...] = tn(e1p_ref[...], ein_ref[...])
    here = slice(0, LANES)
    mish_forward(epre_ref, here, espread_ref.at[0], espread_ref.at[1], eh_ref, ehat_ref, eslope_ref, escale_ref, 0, here)
    shares = simplex(tn(e2_ref[...], eh_ref[...]))
    soft_ref[:, 0:LANES] = shares
    xt_ref[0:latent, 0:LANES] = shares.astype(BF16)
    spread_columns(g_ref[0], s_ref[0], rows_ref, spread_ref)
    for step in range(steps):
        tall_ref[...] = jnp.zeros_like(tall_ref)
        tall_ref[0:acted, :] = act_ref[step, :, mine].astype(F32)
        xt_ref[latent:, lanes_of(step)] = (aux + tall_ref[...]).astype(BF16)
    first.wait()
    transpose_into(w1t_ref, w1_ref, latent)
    w1t_ref[:, latent:] = jnp.transpose(padded_rows(w1_ref[latent:, :], LANES))
    second.wait()
    transpose_into(w2t_ref, w2_ref, latent)
    third.wait()
    transpose_into(dynt_ref, dyn_ref, latent)
    for step in range(steps):
        at = lanes_of(step)
        pre_ref[...] = nn(w1t_ref[...], xt_ref[:, at])
        mish_forward(pre_ref, here, spread_ref.at[0], spread_ref.at[2], h1_ref, hat1_ref, slope1_ref, scale_ref, 0, at)
        pre_ref[...] = nn(w2t_ref[...], h1_ref[:, at])
        mish_forward(pre_ref, here, spread_ref.at[1], spread_ref.at[3], h2_ref, hat2_ref, slope2_ref, scale_ref, 1, at)
        shares = simplex(nn(dynt_ref[...], h2_ref[:, at]))
        soft_ref[:, lanes_of(step + 1)] = shares
        if step + 1 < steps:
            xt_ref[0:latent, lanes_of(step + 1)] = shares.astype(BF16)
    for step in range(steps):
        for start in range(0, latent + LANES, LANES):
            x_ref[lanes_of(step), start : start + LANES] = jnp.transpose(xt_ref[start : start + LANES, lanes_of(step)])
    fourth.wait()
    fifth.wait()


def heads_kernel(steps, scale, slots, head, ahead, heads, bins, chained, after, *refs):
    refs = list(refs)
    place_ref, xt_ref, x_ref, w1_ref, w2_ref, ho_ref, g_ref, s_ref, rb_ref, vb_ref, hz_ref = refs[:11]
    refs = refs[11:]
    before_ref = refs.pop(0) if chained else None
    refs = refs[after:]
    w1_hbm, w2_hbm = refs[:2] if ahead else (None, None)
    refs = refs[2:] if ahead else refs
    keep_ref, send_ref, dx_ref, loss_ref = refs[:4]
    refs = refs[4:]
    copies = []
    if ahead:
        next1_ref, next2_ref, sems = refs[0], refs[1], refs[-1]
        refs = refs[2:-1]
        copies = load_all([
            (w1_hbm.at[head + 2], next1_ref, sems.at[0]),
            (w2_hbm.at[head + 2], next2_ref, sems.at[1]),
        ])
    (rows_ref, spread_ref, tail_ref, hop_ref, hot_ref, pre_ref, lg_ref, h1_ref, hat1_ref, slope1_ref,
     h2_ref, hat2_ref, slope2_ref, scale_ref, sums_ref, dh_ref, d2_ref, d1_ref, dl_ref, grad_ref) = refs
    latent = w2_ref.shape[0]
    tail_rows = w1_ref.shape[0] - latent
    mine = own_lanes(place_ref)
    horizon_row = hz_ref[:, mine]
    bin_ids = lax.broadcasted_iota(jnp.int32, (LANES, LANES), 0)
    first_end = latent + LANES
    losses = []
    spread_columns(g_ref[head + 1], s_ref[head + 1], rows_ref, spread_ref)
    tail_ref[...] = padded_rows(w1_ref[latent:, :], LANES)
    hot_ref[...] = padded_rows(ho_ref[head], LANES)
    hop_ref[...] = jnp.transpose(hot_ref[...])
    gain1, gain2, shift1, shift2 = [spread_ref.at[place] for place in range(4)]
    pre_ref[...] = tn(w1_ref[0:latent, :], xt_ref[0:latent, :]) + tn(tail_ref[...], xt_ref[latent:, :])
    for step in range(steps):
        mish_forward_low(pre_ref, gain1, shift1, h1_ref, hat1_ref, slope1_ref, scale_ref, 0, lanes_of(step))
    pre_ref[...] = tn(w2_ref[...], h1_ref[...])
    for step in range(steps):
        mish_forward_low(pre_ref, gain2, shift2, h2_ref, hat2_ref, slope2_ref, scale_ref, 1, lanes_of(step))
    lg_ref[...] = nn(hot_ref[...], h2_ref[...])
    share = 0.1 if head == 0 else 0.1 / (heads - 1)
    bins_ref = rb_ref if head == 0 else vb_ref
    for step in range(steps):
        at = lanes_of(step)
        logits = jnp.where(bin_ids < bins, lg_ref[:, at], F32(-1e30))
        chosen = bin_ids == bins_ref[step : step + 1, mine]
        top = jnp.max(logits, axis=0, keepdims=True)
        powers = jnp.exp(logits - top)
        total = column_sum(powers)
        picked = column_sum(jnp.where(chosen, logits, 0.0))
        weight = row_weight(step, steps, scale * share, horizon_row, place_ref)
        losses.append(weight * (jnp.log(total) + top - picked))
        dl_ref[:, at] = (powers * (weight / total) - jnp.where(chosen, weight, 0.0)).astype(BF16)
    dh_ref[...] = nn(hop_ref[...], dl_ref[...]).astype(BF16)
    grad_ref[:, first_end + latent :] = nt(h2_ref[...], dl_ref[...]).astype(BF16)
    mish_backward_low(dh_ref, hat2_ref, slope2_ref, scale_ref, 1, steps, sums_ref, 2, d2_ref)
    dh_ref[...] = nn(w2_ref[...], d2_ref[...]).astype(BF16)
    grad_ref[:, first_end : first_end + latent] = nt(d2_ref[...], h1_ref[...]).astype(BF16)
    mish_backward_low(dh_ref, hat1_ref, slope1_ref, scale_ref, 0, steps, sums_ref, 0, d1_ref)
    low_part = nn(w1_ref[0:latent, :], d1_ref[...])
    side_part = nn(tail_ref[...], d1_ref[...])
    if not chained:
        dx_ref[0:latent, :] = low_part
        dx_ref[latent:, :] = side_part
    else:
        dx_ref[0:latent, :] = before_ref[0:latent, :] + low_part
        dx_ref[latent:, :] = before_ref[latent:, :] + side_part
    grad_ref[:, 0:latent] = nn(d1_ref[...], x_ref[:, 0:latent]).astype(BF16)
    side_terms = nn(d1_ref[...], x_ref[:, latent:])
    side_terms = with_vectors(side_terms, vector_sums(sums_ref, spread_ref, 2), tail_rows)
    grad_ref[:, latent:first_end] = side_terms.astype(BF16)
    for relative, (which, slot) in enumerate(slots):
        start = pl.multiple_of((place_ref[0] ^ relative) * GROUP, GROUP)
        (keep_ref, send_ref)[which][slot] = grad_ref[pl.ds(start, GROUP), :]
    loss_ref[...] = functools.reduce(jnp.add, losses)
    for each in copies:
        each.wait()


def backward_kernel(
    steps, scale, order, losses, after,
    place_ref, xt_ref, soft_ref, h1_ref, hat1_ref, slope1_ref, h2_ref, hat2_ref, slope2_ref, scale_ref,
    w1_ref, w2_ref, dyn_ref, hz_ref, g_ref, dx_ref, *rest,
):
    initial = order[0] == steps - 1
    final = order[-1] == 0
    loss_refs, rest = rest[:losses], rest[losses:]
    held_refs, rest = ((), rest) if initial else (rest[:4], rest[4:])
    (tgt_hbm, low_ref, first_ref, side_ref, loss_ref, sums_ref, tgt_ref, rows_ref, spread_ref, tail_ref, pre_ref,
     d1_ref, d2_ref, do_ref, grad_ref, sems) = rest[after:]
    mine = own_lanes(place_ref)
    loads = dict(zip(order, load_all([(tgt_hbm.at[step, mine, :], tgt_ref.at[step], sems.at[step]) for step in order])))
    latent = dyn_ref.shape[1]
    here = slice(0, LANES)
    horizon_row = hz_ref[:, mine]
    spread_columns(g_ref[0], g_ref[0], rows_ref, spread_ref)
    tail_rows = w1_ref.shape[0] - latent
    tail_ref[...] = padded_rows(w1_ref[latent:, :], LANES)
    first_end = latent + LANES
    second_end = first_end + latent
    if initial:
        loss = functools.reduce(jnp.add, [each[...] for each in loss_refs])
        side = jnp.zeros((LANES, LANES), F32)
        incoming = None
    else:
        before_ref, given_ref, given_side_ref, given_sums_ref = held_refs
        loss = loss_refs[0][...]
        side = given_side_ref[...]
        incoming = given_ref[...].astype(F32)
        sums_ref[...] = given_sums_ref[...]
    pending = []

    def add_terms(at, fresh, last):
        terms = (
            (slice(0, first_end), nt(d1_ref[:, at], xt_ref[:, at])),
            (slice(first_end, second_end), nt(d2_ref[:, at], h1_ref[:, at])),
            (slice(second_end, second_end + latent), nt(h2_ref[:, at], do_ref[:, at])),
        )
        for lanes, term in terms:
            if not fresh:
                term = term + grad_ref[:, lanes]
            elif not initial:
                term = term + before_ref[:, lanes]
            out_ref = low_ref if last else grad_ref
            if last and final and lanes.start == 0:
                out_ref[:, 0:latent] = term[:, 0:latent].astype(out_ref.dtype)
                vectors = vector_sums(sums_ref, spread_ref, 2)
                out_ref[:, latent:first_end] = with_vectors(term[:, latent:], vectors, tail_rows).astype(out_ref.dtype)
            else:
                out_ref[:, lanes] = term.astype(out_ref.dtype)

    for step in order:
        at = lanes_of(step)
        weight = row_weight(step, steps, scale, horizon_row, place_ref)
        shares = soft_ref[:, lanes_of(step + 1)]
        loads[step].wait()
        residue = shares - jnp.transpose(tgt_ref[step].astype(F32))
        loss = loss + (20.0 / latent) * weight * column_sum(residue * residue)
        grads = residue * ((40.0 / latent) * weight)
        if incoming is not None:
            grads = grads + incoming
        do_ref[:, at] = simplex_back(shares, grads).astype(BF16)
        pre_ref[...] = nn(dyn_ref[...], do_ref[:, at])
        mish_backward(pre_ref, here, hat2_ref, slope2_ref, scale_ref, 1, at, sums_ref, 2, step == steps - 1, d2_ref)
        pre_ref[...] = nn(w2_ref[...], d2_ref[:, at])
        mish_backward(pre_ref, here, hat1_ref, slope1_ref, scale_ref, 0, at, sums_ref, 0, step == steps - 1, d1_ref)
        incoming = nn(w1_ref[0:latent, :], d1_ref[:, at]) + dx_ref[0:latent, at]
        side = side + nn(tail_ref[...], d1_ref[:, at]) + dx_ref[latent:, at]
        incoming = incoming.astype(BF16).astype(F32)
        pending.append(step)
        if len(pending) == 2 or step == order[-1]:
            low, high = min(pending), max(pending) + 1
            add_terms(slice(low * LANES, high * LANES), high == order[0] + 1, low == order[-1])
            pending = []

    first_ref[...] = incoming.astype(BF16)
    side_ref[...] = side
    loss_ref[...] = loss


def ending_kernel(
    slots, tasks, task_width, acted, observed, after,
    place_ref, low_ref, first_ref, side_ref, loss_ref, soft_ref, ein_ref, eh_ref, ehat_ref, eslope_ref, escale_ref,
    ids_ref, e1_ref, eg_ref, e2_ref, *rest,
):
    out_refs, rest = rest[after : after + 4], rest[after + 4 :]
    erows_ref, espread_ref, e1p_ref, epre_ref, esums_ref, ed_ref, egrad_ref = rest
    mine = own_lanes(place_ref)
    here = slice(0, LANES)
    latent = first_ref.shape[0]
    spread_columns(eg_ref[...], eg_ref[...], erows_ref, espread_ref)
    e1p_ref[...] = padded_rows(e1_ref[...], e1p_ref.shape[0])
    d_enc = simplex_back(soft_ref[:, 0:LANES], first_ref[...].astype(F32)).astype(BF16)
    epre_ref[...] = nn(e2_ref[...], d_enc)
    mish_backward(epre_ref, here, ehat_ref, eslope_ref, escale_ref, 0, here, esums_ref, 0, True, ed_ref)
    side_enc = nn(e1p_ref[...], ed_ref[...])
    enc_width = epre_ref.shape[0]
    half = GROUP // 2
    groups = enc_width // half
    kept = egrad_ref.shape[2]
    enc_second = nt(eh_ref[...], d_enc)
    egrad_ref[:, 0:half, :] = enc_second[:, 0:kept].reshape(groups, half, kept)
    egrad_ref[:, half:, 0 : latent - kept] = enc_second[:, kept:].reshape(groups, half, latent - kept)
    enc_first = nt(ed_ref[...], ein_ref[...])
    egrad_ref[:, half:, latent - kept : kept - LANES] = enc_first[:, 0:LANES].reshape(groups, half, LANES)
    second_lanes = with_vectors(enc_first[:, LANES : 2 * LANES], vector_sums(esums_ref, espread_ref, 1), LANES - 2)
    egrad_ref[:, half:, kept - LANES :] = second_lanes.reshape(groups, half, LANES)

    kinds = lax.broadcasted_iota(jnp.int32, (tasks, LANES), 0)
    onehot = (kinds == ids_ref[:, mine]).astype(F32)
    over_lanes = (((1,), (1,)), ((), ()))
    highest = lax.Precision.HIGHEST
    side_terms = lax.dot_general(onehot, side_ref[...], over_lanes, precision=highest, preferred_element_type=F32)
    enc_terms = lax.dot_general(onehot, side_enc, over_lanes, precision=highest, preferred_element_type=F32)
    table = pltpu.roll(side_terms, LANES - acted, 1)
    table = table + pltpu.roll(enc_terms, enc_terms.shape[1] - observed, 1)[:, 0:LANES]
    lane = lax.broadcasted_iota(jnp.int32, table.shape, 1)
    table = jnp.where(lane < task_width, table, 0.0)
    table = jnp.where((lane == LANES - 1) & (kinds == 0), jnp.sum(loss_ref[...], axis=1, keepdims=True), table)
    table_rows = [table[start : start + GROUP] for start in range(0, tasks, GROUP)]
    table_block = jnp.concatenate(table_rows, axis=1).astype(BF16)
    cut = out_refs[0].shape[2]
    width = low_ref.shape[1] - cut
    last = len(slots[0]) // 2
    for half_no in range(2):
        for relative, (which, slot) in enumerate(slots[half_no]):
            dest = place_ref[0] ^ relative
            start = pl.multiple_of(dest * GROUP, GROUP)
            out_ref = out_refs[2 * half_no + which]
            if half_no == 0:
                out_ref[slot] = low_ref[pl.ds(start, GROUP), 0:cut]
            else:
                out_ref[slot, :, 0:width] = low_ref[pl.ds(start, GROUP), cut:]
                out_ref[slot, :, width:] = egrad_ref[dest].astype(BF16)
    for place, out_ref in enumerate(out_refs):
        out_ref[last] = jnp.zeros((GROUP, cut), BF16)
        if place < 2:
            out_ref[last, :, 0 : table_block.shape[1]] = table_block


def final_kernel(tasks, task_width, enc_in, bins, net_in, *refs):
    outs = refs[-12:]
    (loss_ref, table_ref, e1_ref, eg_ref, es_ref, e2_ref, first_ref, second_ref, gain_ref, shift_ref, dyn_ref, head_ref) = outs
    refs = refs[:-12]
    tail_refs, refs = refs[:2], refs[2:]
    latent = second_ref.shape[2]
    first_end = latent + LANES
    second_end = first_end + latent

    def put_net(net, value):
        first_ref[net] = value[:, 0:net_in]
        second_ref[net] = value[:, first_end:second_end]
        turned = jnp.transpose(value[:, latent:first_end])
        for layer in range(2):
            row = net_in - latent + 2 * layer
            gain_ref[net, layer : layer + 1, :] = turned[row : row + 1, :]
            shift_ref[net, layer : layer + 1, :] = turned[row + 1 : row + 2, :]

    tail = functools.reduce(jnp.add, [ref[0].astype(F32) for ref in tail_refs])
    put_net(0, tail)
    dyn_ref[...] = tail[:, second_end : second_end + latent]
    enc = tail[:, second_end + latent :]
    half = GROUP // 2
    kept = enc.shape[1]
    e2_ref[:, 0:kept] = 0.3 * enc[0:half, :]
    e2_ref[:, kept:] = 0.3 * enc[half:, 0 : latent - kept]
    e1_ref[...] = 0.3 * enc[half:, latent - kept : latent - kept + enc_in]
    turned = 0.3 * jnp.transpose(enc[half:, kept - LANES :])
    eg_ref[...] = turned[LANES - 2 : LANES - 1, :]
    es_ref[...] = turned[LANES - 1 : LANES, :]
    table = functools.reduce(jnp.add, [ref[1].astype(F32) for ref in tail_refs])
    loss_ref[...] = table[0:1, LANES - 1 : LANES]
    for place in range(tasks // GROUP):
        table_ref[place * GROUP : (place + 1) * GROUP, :] = table[:, place * LANES : place * LANES + task_width]
    net = 1
    for one_ref, other_ref in zip(refs[0::2], refs[1::2]):
        stacked = len(one_ref.shape) == 4
        for one in range(one_ref.shape[1] if stacked else 1):
            at = (0, one) if stacked else (0,)
            value = one_ref[at].astype(F32) + other_ref[at].astype(F32)
            put_net(net, value)
            head_ref[net - 1] = value[:, second_end : second_end + bins]
            net += 1


def swap(value, axis, distance):
    count = lax.axis_size(axis)
    return lax.ppermute(value, axis, [(place, place ^ distance) for place in range(count)])


def exchange(parts, axis, scale):
    total = parts[0].astype(F32)
    for distance in range(1, len(parts)):
        total = total + swap(parts[distance], axis, distance * scale).astype(F32)
    return total


def scatter_plain(packed, chips, sections):
    held = packed.reshape((sections, chips, CORES) + packed.shape[1:])
    batch_no = lax.axis_index("batch")
    places = (
        ("batch", 1, CORES, 2, batch_no % CORES),
        ("batch", CORES, chips, 1, batch_no // CORES),
        ("section", 1, sections, 0, lax.axis_index("section")),
    )
    for axis, scale, count, dim, mine in places:
        parts = [lax.dynamic_index_in_dim(held, mine ^ other, dim, keepdims=False) for other in range(count)]
        held = exchange(parts, axis, scale)
        held = held.astype(BF16) if dim else held
    return held


def on_device(
    observations,
    actions,
    targets,
    task_ids,
    horizons,
    reward_bins,
    value_bins,
    task_table,
    enc_first,
    enc_gain,
    enc_shift,
    enc_second,
    net_first,
    net_second,
    net_gain,
    net_shift,
    dyn_out,
    head_out,
):
    sections = lax.axis_size("section")
    batches = lax.axis_size("batch")
    section_no = lax.axis_index("section")
    chips = batches // CORES
    devices = sections * batches
    steps, rows_all, acted = actions.shape
    observed = observations.shape[1]
    rows = rows_all // sections
    latent = dyn_out.shape[1]
    hidden = dyn_out.shape[0]
    tasks, task_width = task_table.shape
    heads, _, bins = head_out.shape
    nets, net_in, _ = net_first.shape
    enc_in, enc_width = enc_first.shape
    wide = steps * LANES
    scale = 1.0 / (rows_all * batches * steps)
    groups = hidden // GROUP
    in_place = hidden // devices == GROUP
    start = section_no * rows
    block_no = start // LANES
    first_lane = start - block_no * LANES
    me = section_no * batches + lax.axis_index("batch") if in_place else jnp.int32(0)
    place = jnp.stack([me, block_no, first_lane, first_lane + rows]).astype(jnp.int32)
    bits = [("batch", 1 << bit) for bit in range(batches.bit_length() - 1)]
    bits += [("section", 1 << bit) for bit in range(sections.bit_length() - 1)]

    def slots_of(order):
        if not in_place:
            return tuple((relative // (groups // 2), relative % (groups // 2)) for relative in range(groups))
        found = []
        for relative in range(groups):
            slot = 0
            for bit in order:
                slot = 2 * slot + (relative >> bit & 1)
            found.append((slot // (groups // 2), slot % (groups // 2)))
        return tuple(found)

    plain = tuple(range(len(bits)))
    y_first = (0, 2, 1) + tuple(range(3, len(bits))) if in_place else plain
    half_slots = groups // 2
    shape_of = jax.ShapeDtypeStruct
    smem = pl.BlockSpec(memory_space=pltpu.SMEM)
    local = pl.BlockSpec(memory_space=pltpu.VMEM)
    far = pl.BlockSpec(memory_space=pltpu.HBM)
    anywhere = pl.BlockSpec(memory_space=pl.ANY)
    first_far, second_far, dyn_far, targets_far = [
        pltpu.with_memory_space_constraint(array, pltpu.HBM) for array in (net_first, net_second, dyn_out, targets)
    ]
    vmem = pltpu.VMEM
    dmas = pltpu.SemaphoreType.DMA

    def params(mebibytes):
        return pltpu.CompilerParams(vmem_limit_bytes=mebibytes * 1024 * 1024)

    def cost(flops, moved):
        return pl.CostEstimate(flops=flops, bytes_accessed=moved, transcendentals=0)

    ids_row = task_ids.reshape(1, rows_all)
    horizon_row = horizons.reshape(1, rows_all)
    eg_row = enc_gain.reshape(1, enc_width)
    es_row = enc_shift.reshape(1, enc_width)
    head_turned = head_out.transpose(0, 2, 1)
    low = lambda lanes: shape_of((hidden, lanes), BF16)
    forward_shapes = (
        shape_of((latent + LANES, wide), BF16),
        shape_of((latent, wide + LANES), F32),
        low(wide), low(wide), low(wide), low(wide), low(wide), low(wide),
        shape_of((8, wide), F32),
        shape_of((2 * LANES, LANES), BF16),
        shape_of((enc_width, LANES), BF16),
        shape_of((enc_width, LANES), BF16),
        shape_of((enc_width, LANES), BF16),
        shape_of((8, LANES), F32),
        shape_of((net_in, hidden), BF16),
        shape_of((hidden, hidden), BF16),
        shape_of((hidden, latent), BF16),
        shape_of((wide, latent + LANES), BF16),
    )

    weight_shapes = (shape_of((net_in, hidden), BF16), shape_of((hidden, hidden), BF16))

    early = [
        pltpu.with_memory_space_constraint(array, pltpu.HBM)
        for array in (
            observations.T, actions.transpose(0, 2, 1), ids_row, task_table, enc_first, eg_row, es_row, enc_second,
            net_gain, net_shift,
        )
    ]
    made = pl.pallas_call(
        functools.partial(forward_kernel, steps),
        out_shape=forward_shapes + weight_shapes,
        in_specs=[smem] + [far] * 13,
        out_specs=[local] * (len(forward_shapes) + 2),
        scratch_shapes=[
            vmem((8, hidden), F32),
            vmem((4, hidden, LANES), F32),
            vmem((8, enc_width), F32),
            vmem((2, enc_width, LANES), F32),
            vmem((tasks, 2 * LANES), F32),
            vmem((LANES, LANES), F32),
            vmem((2 * LANES, enc_width), BF16),
            vmem((hidden, latent + LANES), BF16),
            vmem((hidden, hidden), BF16),
            vmem((latent, hidden), BF16),
            vmem((hidden, LANES), F32),
            vmem((enc_width, LANES), F32),
            *[vmem(each.shape, each.dtype) for each in early],
            dmas((5,)),
            dmas((len(early),)),
        ],
        compiler_params=params(VMEM_A),
        cost_estimate=cost(10_000_000_000, 8_000_000),
        name="forward_chain",
    )(
        place, *early, first_far, second_far, dyn_far,
    )
    saved, x_rows, weights = made[:-3], made[-3], made[-2:]
    xt = saved[0]
    head_width = latent + LANES + hidden + LANES

    def run_head(head, ahead, weights, before, after):
        pack_shape = shape_of((half_slots, GROUP, head_width), BF16)
        dx_shape = shape_of((latent + LANES, wide), F32)
        out_shapes = (pack_shape, pack_shape, dx_shape, shape_of((1, LANES), F32))
        args = [place, xt, x_rows, *weights, head_turned, net_gain, net_shift, reward_bins, value_bins, horizon_row]
        specs = [smem] + [local] * 10
        aliases = {}
        if before is not None:
            aliases = {len(args): 2}
            args.append(before)
            specs.append(local)
        args += after
        specs += [anywhere] * len(after)
        if ahead:
            args += [first_far, second_far]
            specs += [far, far]
            out_shapes += weight_shapes
        low_wide = vmem((hidden, wide), BF16)
        scratch = [
            vmem((8, hidden), F32),
            vmem((4, hidden, LANES), F32),
            vmem((LANES, hidden), BF16),
            vmem((hidden, LANES), BF16),
            vmem((LANES, hidden), BF16),
            vmem((hidden, wide), F32),
            vmem((LANES, wide), F32),
        ]
        scratch += [low_wide] * 6
        scratch += [vmem((8, wide), F32), vmem((4, hidden, LANES), F32)]
        scratch += [low_wide] * 3
        scratch += [vmem((LANES, wide), BF16), vmem((hidden, head_width), BF16)]
        if ahead:
            scratch.append(dmas((2,)))
        return pl.pallas_call(
            functools.partial(
                heads_kernel, steps, scale, slots_of(plain), head, ahead, heads, bins, before is not None, len(after)
            ),
            out_shape=out_shapes,
            in_specs=specs,
            out_specs=[local] * len(out_shapes),
            scratch_shapes=scratch,
            input_output_aliases=aliases,
            compiler_params=params(VMEM_B),
            cost_estimate=cost(9_000_000_000, 4_000_000),
            name=f"head_{head}",
        )(*args)

    def phase(pair, bit):
        return pair[0], swap(pair[1], *bits[bit])

    def fold(members, *tokens, by_lanes=False, common=0):
        slots_now = (members[0][0].shape[0] - common) // 2
        shape = members[0][0].shape[1:]
        if by_lanes:
            shape = shape[:-1] + (sum(kept.shape[-1] for kept, _ in members),)
        elif len(members) > 1:
            shape = (len(members),) + shape
        out_shape = shape_of((slots_now + common,) + shape, BF16)
        inputs = [each for member in members for each in member]

        def fold_kernel(*refs):
            refs = refs[len(tokens) :]
            outs = refs[-2:]
            lane = 0
            for place in range(len(members)):
                kept_ref, came_ref = refs[2 * place], refs[2 * place + 1]
                width = kept_ref.shape[-1]
                if common:
                    value = (kept_ref[2 * slots_now].astype(F32) + came_ref[2 * slots_now].astype(F32)).astype(BF16)
                    for out in outs:
                        out[slots_now, :, lane : lane + width] = value
                for half in range(2):
                    part = pl.ds(half * slots_now, slots_now)
                    value = (kept_ref[part].astype(F32) + came_ref[part].astype(F32)).astype(BF16)
                    if by_lanes:
                        outs[half][0:slots_now, :, lane : lane + width] = value
                    elif len(members) > 1:
                        outs[half][:, place] = value
                    else:
                        outs[half][...] = value
                lane += width

        return pl.pallas_call(
            fold_kernel,
            out_shape=(out_shape, out_shape),
            in_specs=[anywhere] * len(tokens) + [local] * len(inputs),
            out_specs=(local, local),
            compiler_params=params(VMEM_SUM),
            cost_estimate=cost(1_000_000, 2_000_000),
            name="fold",
        )(*tokens, *inputs)

    net_width = latent + LANES + hidden + latent
    chain_inputs = saved[:9] + saved[14:]

    def run_backward(order, losses, held, after):
        final = order[-1] == 0
        out_shapes = (
            shape_of((hidden, net_width), BF16 if final else F32),
            shape_of((latent, LANES), BF16),
            shape_of((LANES, LANES), F32),
            shape_of((1, LANES), F32),
            shape_of((4, hidden, LANES), F32),
        )
        args = [place, *chain_inputs, horizon_row, net_gain, dx, *losses, *held]
        return pl.pallas_call(
            functools.partial(backward_kernel, steps, scale, order, len(losses), len(after)),
            out_shape=out_shapes,
            in_specs=[smem] + [local] * (len(args) - 1) + [anywhere] * len(after) + [far],
            out_specs=[local] * len(out_shapes),
            scratch_shapes=[
                vmem((steps, LANES, latent), BF16),
                vmem((8, hidden), F32),
                vmem((4, hidden, LANES), F32),
                vmem((LANES, hidden), BF16),
                vmem((hidden, LANES), F32),
                vmem((hidden, wide), BF16),
                vmem((hidden, wide), BF16),
                vmem((latent, wide), BF16),
                vmem((hidden, net_width), F32),
                dmas((steps,)),
            ],
            compiler_params=params(VMEM_C),
            cost_estimate=cost(7_000_000_000, 8_000_000),
            name=f"backward_{order[0]}",
        )(*args, *after, targets_far)

    packs, loss_parts = [], []
    dx = None
    flights = []
    after = []

    def advance(head, bit, token, kept_back):
        if in_place and 0 <= head < heads:
            pair = fold([flights[head]], token)
            kept_back.append(pair[0])
            flights[head] = phase(pair, plain[bit])

    for head in range(heads):
        ahead = head + 1 < heads
        result = run_head(head, ahead, weights, dx, after)
        keep, send, dx, loss = result[:4]
        weights = result[4:]
        packs.append((keep, send))
        loss_parts.append(loss)
        after = []
        advance(head - 1, 1, loss, after)
        advance(head - 2, 2, loss, after)
        if in_place:
            flights.append(phase((keep, send), plain[0]))
    early = heads // 2
    half_way = steps // 2
    if in_place:
        group = fold(flights[0:early], loss_parts[-1])
        after.append(group[0])
        group = phase(group, plain[3])
    chain = run_backward(tuple(range(steps - 1, half_way - 1, -1)), loss_parts, [], after)
    after = []
    advance(heads - 1, 1, chain[3], after)
    advance(heads - 2, 2, chain[3], after)
    if in_place:
        group = fold([group], chain[3])
        after.append(group[0])
        group = phase(group, plain[4])
        after.append(flights[heads - 3][1])
    chain = run_backward(
        tuple(range(half_way - 1, -1, -1)), [chain[3]], [chain[0], chain[1], chain[2], chain[4]], after
    )
    after = []
    advance(heads - 1, 2, chain[3], after)
    if in_place:
        second = fold(flights[early : heads - 1], chain[3])
        after += [group[1], second[0]]
        second = phase(second, plain[3])

    enc_lanes = latent - LANES
    cut = (net_width + enc_lanes) // 2
    one_shape = shape_of((half_slots + 1, GROUP, cut), BF16)
    tail_slots = (slots_of(plain), slots_of(y_first))
    ended = pl.pallas_call(
        functools.partial(ending_kernel, tail_slots, tasks, task_width, acted, observed, len(after)),
        out_shape=(one_shape,) * 4,
        in_specs=[smem] + [local] * 14 + [anywhere] * len(after),
        out_specs=[local] * 4,
        scratch_shapes=[
            vmem((8, enc_width), F32),
            vmem((2, enc_width, LANES), F32),
            vmem((2 * LANES, enc_width), BF16),
            vmem((enc_width, LANES), F32),
            vmem((2, enc_width, LANES), F32),
            vmem((enc_width, LANES), BF16),
            vmem((groups, GROUP, enc_lanes), F32),
        ],
        compiler_params=params(VMEM_SUM),
        cost_estimate=cost(1_000_000_000, 4_000_000),
        name="ending",
    )(place, *chain[:4], saved[1], *saved[9:14], ids_row, enc_first, eg_row, enc_second, *after)

    if in_place:
        one = phase(ended[0:2], plain[0])
        two = phase(ended[2:4], y_first[0])
        one = fold([one], ended[0], flights[heads - 1][1], second[1], by_lanes=True, common=1)
        two = fold([two], ended[0], flights[heads - 1][1], second[1], by_lanes=True, common=1)
        one = phase(one, plain[1])
        two = phase(two, y_first[1])
        second = phase(fold([second], ended[0]), plain[4])
        one = phase(fold([one], second[1], by_lanes=True, common=1), plain[2])
        two = phase(fold([two], second[1], by_lanes=True, common=1), y_first[2])
        rest = phase(fold(flights[heads - 1 :], one[0]), plain[3])
        tail = phase(fold([one, two], rest[1], by_lanes=True, common=1), plain[3])
        rest = phase(fold([rest], tail[0]), plain[4])
        tail = phase(fold([tail], rest[1], by_lanes=True, common=1), plain[4])
        each = GROUP // 2
        out_shapes = (
            shape_of((1, 1), F32),
            shape_of((tasks, task_width), F32),
            shape_of((each, enc_in), F32),
            shape_of((1, each), F32),
            shape_of((1, each), F32),
            shape_of((each, latent), F32),
            shape_of((nets, GROUP, net_in), F32),
            shape_of((nets, GROUP, hidden), F32),
            shape_of((nets, 2, GROUP), F32),
            shape_of((nets, 2, GROUP), F32),
            shape_of((GROUP, latent), F32),
            shape_of((heads, GROUP, bins), F32),
        )
        ends = [*tail, *group, *second, *rest]
        outs = list(pl.pallas_call(
            functools.partial(final_kernel, tasks, task_width, enc_in, bins, net_in),
            out_shape=out_shapes,
            in_specs=[local] * len(ends),
            out_specs=[local] * len(out_shapes),
            compiler_params=params(VMEM_SUM),
            cost_estimate=cost(1_000_000, 4_000_000),
            name="last_sums",
        )(*ends))
        outs[0] = outs[0].reshape(())
        outs[2] = outs[2].T
        outs[3], outs[4] = outs[3].reshape(each), outs[4].reshape(each)
        outs[6] = outs[6].transpose(0, 2, 1)
        outs[7] = outs[7].transpose(0, 2, 1)
        return tuple(outs)

    def scattered(keep, send):
        mine = hidden // devices
        packed = jnp.concatenate([keep, send], axis=0)
        middle = packed.shape[1:-2]
        packed = packed.reshape((groups,) + middle + (GROUP // mine, mine, packed.shape[-1]))
        packed = jnp.moveaxis(packed, -3, 1).reshape((devices,) + middle + (mine, packed.shape[-1]))
        return scatter_plain(packed, chips, sections)

    head_sum = jnp.stack([scattered(*pack) for pack in packs], axis=0)
    enc_each = enc_width // devices
    keep, send = [jnp.concatenate([ended[place], ended[2 + place]], axis=2) for place in range(2)]
    table_sum = lax.psum(ended[0][half_slots, :, 0 : tasks // GROUP * LANES].astype(F32), ("section", "batch"))
    keep, send = keep[:half_slots], send[:half_slots]
    net_sum = scattered(keep[:, :, 0:net_width], send[:, :, 0:net_width])
    enc_all = jnp.concatenate([keep, send], axis=0)[:, :, net_width:]
    enc_all = enc_all.reshape(groups, 2, enc_width // groups, enc_lanes)
    enc_all = enc_all.transpose(0, 2, 1, 3).reshape(devices, enc_each, 2, enc_lanes)
    enc_sum = scatter_plain(enc_all, chips, sections)
    enc_low, enc_high = enc_sum[:, 0], enc_sum[:, 1]
    s_enc_second = jnp.concatenate([enc_low, enc_high[:, 0 : latent - enc_lanes]], axis=1)
    enc_rows = enc_high[:, latent - enc_lanes :]
    first_end = latent + LANES
    net_row = jnp.concatenate([net_sum[:, 0 : first_end + hidden], jnp.zeros_like(net_sum[:, 0:LANES])], axis=1)
    sums = jnp.concatenate([net_row[None], head_sum], axis=0)
    vectors = sums[:, :, net_in : net_in + 4].transpose(0, 2, 1)
    table = table_sum.reshape(GROUP, tasks // GROUP, LANES).transpose(1, 0, 2).reshape(tasks, LANES)
    return (
        table[0, LANES - 1],
        table[:, 0:task_width],
        0.3 * enc_rows[:, 0:enc_in].T,
        0.3 * enc_rows[:, 2 * LANES - 2],
        0.3 * enc_rows[:, 2 * LANES - 1],
        0.3 * s_enc_second,
        sums[:, :, 0:net_in].transpose(0, 2, 1),
        sums[:, :, first_end : first_end + hidden].transpose(0, 2, 1),
        vectors[:, 0::2],
        vectors[:, 1::2],
        net_sum[:, first_end + hidden :],
        head_sum[:, :, first_end + hidden : first_end + hidden + bins],
    )


def solution(mesh):
    both = ("section", "batch")
    return jax.shard_map(
        on_device,
        mesh=mesh,
        in_specs=(
            P("batch", None),
            P(None, "batch", None),
            P(None, "batch", None),
            P("batch"),
            P("batch"),
            P(None, "batch"),
            P(None, "batch"),
        )
        + (P(),) * 11,
        out_specs=(
            P(),
            P(),
            P(None, both),
            P(both),
            P(both),
            P(both, None),
            P(None, None, both),
            P(None, None, both),
            P(None, None, both),
            P(None, None, both),
            P(both, None),
            P(None, both, None),
        ),
        check_vma=False,
    )
```

```python
import functools

import jax
import jax.numpy as jnp
from jax import lax
from jax.experimental import pallas as pl
from jax.experimental.pallas import tpu as pltpu
from jax.sharding import PartitionSpec as P

CORES = 2
LANES = 128
GROUP = 16
BF16 = jnp.bfloat16
F32 = jnp.float32
VMEM_A = 18
VMEM_B = 20
VMEM_SUM = 6
VMEM_C = 20


def nn(left, right):
    return lax.dot_general(left, right, (((1,), (0,)), ((), ())), preferred_element_type=F32)


def nt(left, right):
    return lax.dot_general(left, right, (((1,), (1,)), ((), ())), preferred_element_type=F32)


def tn(left, right):
    return lax.dot_general(left, right, (((0,), (0,)), ((), ())), preferred_element_type=F32)


def column_sum(value):
    grouped = value.reshape(value.shape[0] // 8, 8, value.shape[1])
    return jnp.sum(jnp.sum(grouped, axis=0), axis=0, keepdims=True)


def slabs(features, size=64):
    return [slice(start, start + size) for start in range(0, features, size)]


def lanes_of(step):
    return slice(step * LANES, (step + 1) * LANES)


def spread_columns(gain_rows, shift_rows, rows_ref, spread_ref):
    count = gain_rows.shape[0]
    rows_ref[...] = jnp.zeros_like(rows_ref)
    rows_ref[0:count, :] = gain_rows
    rows_ref[count : 2 * count, :] = shift_rows
    turned = jnp.transpose(rows_ref[...])
    for place in range(2 * count):
        spread_ref[place] = jnp.broadcast_to(turned[:, place : place + 1], spread_ref.shape[1:])


def mish_forward(pre_ref, pre_at, gain_ref, shift_ref, hid_ref, hat_ref, slope_ref, scale_ref, scale_row, at):
    features = pre_ref.shape[0]
    row_mean = column_sum(pre_ref[:, pre_at]) * (1.0 / features)
    centred = pre_ref[:, pre_at] - row_mean
    spread = column_sum(centred * centred) * (1.0 / features)
    scale = lax.rsqrt(spread + 1e-05)
    scale_ref[scale_row : scale_row + 1, at] = scale
    for part in slabs(features):
        hat = (pre_ref[part, pre_at] - row_mean) * scale
        normed = hat * gain_ref[part, :] + shift_ref[part, :]
        power = jnp.exp(normed)
        top = power * (power + 2.0)
        inverse = pl.reciprocal(top + 2.0, approx=True)
        ratio = top * inverse
        hid_ref[part, at] = (normed * ratio).astype(BF16)
        tilt = power * inverse
        slope = ratio + normed * (4.0 * (tilt * (tilt + inverse)))
        slope_ref[part, at] = (slope * gain_ref[part, :]).astype(BF16)
        hat_ref[part, at] = hat.astype(BF16)


def mish_backward(grad_ref, grad_at, hat_ref, slope_ref, scale_ref, scale_row, at, sums_ref, sums_at, first, out_ref):
    features = grad_ref.shape[0]
    total_one = jnp.zeros((8, LANES), F32)
    total_two = jnp.zeros((8, LANES), F32)
    for part in slabs(features):
        term = grad_ref[part, grad_at] * slope_ref[part, at].astype(F32)
        grad_ref[part, grad_at] = term
        crossed = term * hat_ref[part, at].astype(F32)
        groups = (term.shape[0] // 8, 8, LANES)
        total_one = total_one + jnp.sum(term.reshape(groups), axis=0)
        total_two = total_two + jnp.sum(crossed.reshape(groups), axis=0)
        if first:
            sums_ref[sums_at, part, :] = term
            sums_ref[sums_at + 1, part, :] = crossed
        else:
            sums_ref[sums_at, part, :] += term
            sums_ref[sums_at + 1, part, :] += crossed
    mean_one = jnp.sum(total_one, axis=0, keepdims=True) * (1.0 / features)
    mean_two = jnp.sum(total_two, axis=0, keepdims=True) * (1.0 / features)
    scale = scale_ref[scale_row : scale_row + 1, at]
    for part in slabs(features):
        rest = grad_ref[part, grad_at] - mean_one - hat_ref[part, at].astype(F32) * mean_two
        out_ref[part, at] = (rest * scale).astype(BF16)


def mish_forward_low(pre_ref, gain_ref, shift_ref, hid_ref, hat_ref, slope_ref, scale_ref, scale_row, at):
    features = pre_ref.shape[0]
    row_mean = column_sum(pre_ref[:, at]) * (1.0 / features)
    centred = pre_ref[:, at] - row_mean
    spread = column_sum(centred * centred) * (1.0 / features)
    scale = lax.rsqrt(spread + 1e-05)
    scale_ref[scale_row : scale_row + 1, at] = scale
    for part in slabs(features):
        hat = (pre_ref[part, at] - row_mean) * scale
        normed = (hat * gain_ref[part, :] + shift_ref[part, :]).astype(BF16)
        hat_ref[part, at] = hat.astype(BF16)
        power = jnp.exp(normed)
        top = power * (power + 2.0)
        inverse = pl.reciprocal(top + 2.0, approx=True)
        ratio = top * inverse
        hid_ref[part, at] = normed * ratio
        tilt = power * inverse
        slope = ratio + (4.0 * normed) * (tilt * (tilt + inverse))
        slope_ref[part, at] = slope * gain_ref[part, :].astype(BF16)


def mish_backward_low(grad_ref, hat_ref, slope_ref, scale_ref, scale_row, steps, sums_ref, sums_at, out_ref):
    features = grad_ref.shape[0]
    rows = []
    for step in range(steps):
        at = lanes_of(step)
        total_one = jnp.zeros((16, LANES), F32)
        total_two = jnp.zeros((16, LANES), F32)
        for part in slabs(features):
            term = grad_ref[part, at] * slope_ref[part, at]
            crossed = term * hat_ref[part, at]
            grad_ref[part, at] = term
            groups = (term.shape[0] // 16, 16, LANES)
            term = term.reshape(groups)
            crossed = crossed.reshape(groups)
            total_one = total_one + functools.reduce(jnp.add, [term[k] for k in range(groups[0])]).astype(F32)
            total_two = total_two + functools.reduce(jnp.add, [crossed[k] for k in range(groups[0])]).astype(F32)
        scale = scale_ref[scale_row : scale_row + 1, at]
        mean_one = jnp.sum(total_one, axis=0, keepdims=True) * (1.0 / features)
        mean_two = jnp.sum(total_two, axis=0, keepdims=True) * (1.0 / features)
        rows.append((mean_one.astype(BF16), mean_two.astype(BF16), scale.astype(BF16)))
    for part in slabs(features):
        sum_one, sum_two = None, None
        for step, (mean_one, mean_two, scale) in enumerate(rows):
            at = lanes_of(step)
            term = grad_ref[part, at]
            hat = hat_ref[part, at]
            out_ref[part, at] = (term - mean_one - hat * mean_two) * scale
            crossed = term * hat
            sum_one = term if sum_one is None else sum_one + term
            sum_two = crossed if sum_two is None else sum_two + crossed
        sums_ref[sums_at, part, :] = sum_one.astype(F32)
        sums_ref[sums_at + 1, part, :] = sum_two.astype(F32)


def simplex(values):
    grouped = values.reshape(values.shape[0] // 8, 8, values.shape[1])
    powers = jnp.exp(grouped - jnp.max(grouped, axis=1, keepdims=True))
    shares = powers / jnp.sum(powers, axis=1, keepdims=True)
    return shares.reshape(values.shape)


def simplex_back(shares, grads):
    grouped = (shares.shape[0] // 8, 8, shares.shape[1])
    crossed = jnp.sum((shares * grads).reshape(grouped), axis=1, keepdims=True)
    return (shares.reshape(grouped) * (grads.reshape(grouped) - crossed)).reshape(shares.shape)


def row_weight(step, steps, scale, horizon_row, place_ref):
    lane = lax.broadcasted_iota(jnp.int32, (1, LANES), 1)
    mine = (lane >= place_ref[2]) & (lane < place_ref[3]) & (horizon_row > step)
    return jnp.where(mine, F32(scale * 0.5 ** (step / (steps - 1))), 0.0)


def padded_rows(value, rows):
    zeros = jnp.zeros((rows - value.shape[0], value.shape[1]), F32)
    return jnp.concatenate([value.astype(F32), zeros], axis=0).astype(BF16)


def transpose_into(out_ref, source_ref, rows):
    for start in range(0, rows, LANES):
        out_ref[:, start : start + LANES] = jnp.transpose(source_ref[start : start + LANES, :])


def vector_sums(sums_ref, gains_ref, layers):
    vectors = []
    for layer in range(layers):
        inverse = 1.0 / gains_ref[layer]
        vectors.append(jnp.sum(sums_ref[2 * layer + 1] * inverse, axis=1, keepdims=True))
        vectors.append(jnp.sum(sums_ref[2 * layer] * inverse, axis=1, keepdims=True))
    return vectors


def own_lanes(place_ref):
    return pl.ds(pl.multiple_of(place_ref[1] * LANES, LANES), LANES)


def load_all(copies):
    made = [pltpu.make_async_copy(*each) for each in copies]
    for each in made:
        each.start()
    return made


def with_vectors(value, vectors, first_lane):
    lane = lax.broadcasted_iota(jnp.int32, value.shape, 1)
    for place, vector in enumerate(vectors):
        value = jnp.where(lane == first_lane + place, vector, value)
    return value


def forward_kernel(
    steps,
    place_ref, obs_hbm, act_hbm, ids_hbm, table_hbm, e1_hbm, eg_hbm, es_hbm, e2_hbm, g_hbm, s_hbm,
    w1_hbm, w2_hbm, dyn_hbm,
    xt_ref, soft_ref, h1_ref, hat1_ref, slope1_ref, h2_ref, hat2_ref, slope2_ref, scale_ref,
    ein_ref, eh_ref, ehat_ref, eslope_ref, escale_ref,
    w1_ref, w2_ref, dyn_ref, x_ref, next1_ref, next2_ref,
    rows_ref, spread_ref, erows_ref, espread_ref, wide_ref, tall_ref, e1p_ref, w1t_ref, w2t_ref, dynt_ref, pre_ref, epre_ref,
    obs_ref, act_ref, ids_ref, table_ref, e1_ref, eg_ref, es_ref, e2_ref, g_ref, s_ref,
    sems, early_sems,
):
    early = load_all([
        (table_hbm, table_ref, early_sems.at[0]),
        (ids_hbm, ids_ref, early_sems.at[1]),
        (obs_hbm, obs_ref, early_sems.at[2]),
        (e1_hbm, e1_ref, early_sems.at[3]),
        (eg_hbm, eg_ref, early_sems.at[4]),
        (es_hbm, es_ref, early_sems.at[5]),
        (e2_hbm, e2_ref, early_sems.at[6]),
        (act_hbm, act_ref, early_sems.at[7]),
        (g_hbm, g_ref, early_sems.at[8]),
        (s_hbm, s_ref, early_sems.at[9]),
    ])
    first, second, third, fourth, fifth = load_all([
        (w1_hbm.at[0], w1_ref, sems.at[0]),
        (w2_hbm.at[0], w2_ref, sems.at[1]),
        (dyn_hbm, dyn_ref, sems.at[2]),
        (w1_hbm.at[1], next1_ref, sems.at[3]),
        (w2_hbm.at[1], next2_ref, sems.at[4]),
    ])
    latent = dyn_ref.shape[1]
    tasks, task_width = table_ref.shape
    observed = obs_ref.shape[0]
    acted = act_ref.shape[1]
    mine = own_lanes(place_ref)
    for each in early:
        each.wait()
    spread_columns(eg_ref[...], es_ref[...], erows_ref, espread_ref)
    kinds = lax.broadcasted_iota(jnp.int32, (tasks, LANES), 0)
    onehot = (kinds == ids_ref[:, mine]).astype(F32).astype(BF16)
    wide_ref[...] = jnp.zeros_like(wide_ref)
    wide_ref[:, 0:task_width] = table_ref[...].astype(F32)
    table_tail = pltpu.roll(wide_ref[:, 0:LANES], acted, 1).astype(BF16)
    table_enc = pltpu.roll(wide_ref[...], observed, 1).astype(BF16)
    aux = tn(table_tail, onehot)
    tall_ref[...] = jnp.zeros_like(tall_ref)
    tall_ref[0:observed, :] = obs_ref[:, mine].astype(F32)
    ein = tn(table_enc, onehot)
    ein_ref[0:LANES, :] = (ein[0:LANES] + tall_ref[...]).astype(BF16)
    ein_ref[LANES:, :] = ein[LANES:].astype(BF16)
    e1p_ref[...] = padded_rows(e1_ref[...], e1p_ref.shape[0])
    epre_ref[...] = tn(e1p_ref[...], ein_ref[...])
    here = slice(0, LANES)
    mish_forward(epre_ref, here, espread_ref.at[0], espread_ref.at[1], eh_ref, ehat_ref, eslope_ref, escale_ref, 0, here)
    shares = simplex(tn(e2_ref[...], eh_ref[...]))
    soft_ref[:, 0:LANES] = shares
    xt_ref[0:latent, 0:LANES] = shares.astype(BF16)
    spread_columns(g_ref[0], s_ref[0], rows_ref, spread_ref)
    for step in range(steps):
        tall_ref[...] = jnp.zeros_like(tall_ref)
        tall_ref[0:acted, :] = act_ref[step, :, mine].astype(F32)
        xt_ref[latent:, lanes_of(step)] = (aux + tall_ref[...]).astype(BF16)
    first.wait()
    transpose_into(w1t_ref, w1_ref, latent)
    w1t_ref[:, latent:] = jnp.transpose(padded_rows(w1_ref[latent:, :], LANES))
    second.wait()
    transpose_into(w2t_ref, w2_ref, latent)
    third.wait()
    transpose_into(dynt_ref, dyn_ref, latent)
    for step in range(steps):
        at = lanes_of(step)
        pre_ref[...] = nn(w1t_ref[...], xt_ref[:, at])
        mish_forward(pre_ref, here, spread_ref.at[0], spread_ref.at[2], h1_ref, hat1_ref, slope1_ref, scale_ref, 0, at)
        pre_ref[...] = nn(w2t_ref[...], h1_ref[:, at])
        mish_forward(pre_ref, here, spread_ref.at[1], spread_ref.at[3], h2_ref, hat2_ref, slope2_ref, scale_ref, 1, at)
        shares = simplex(nn(dynt_ref[...], h2_ref[:, at]))
        soft_ref[:, lanes_of(step + 1)] = shares
        if step + 1 < steps:
            xt_ref[0:latent, lanes_of(step + 1)] = shares.astype(BF16)
    for step in range(steps):
        for start in range(0, latent + LANES, LANES):
            x_ref[lanes_of(step), start : start + LANES] = jnp.transpose(xt_ref[start : start + LANES, lanes_of(step)])
    fourth.wait()
    fifth.wait()


def heads_kernel(steps, scale, slots, head, ahead, heads, bins, chained, after, *refs):
    refs = list(refs)
    place_ref, xt_ref, x_ref, w1_ref, w2_ref, ho_ref, g_ref, s_ref, rb_ref, vb_ref, hz_ref = refs[:11]
    refs = refs[11:]
    before_ref = refs.pop(0) if chained else None
    refs = refs[after:]
    w1_hbm, w2_hbm = refs[:2] if ahead else (None, None)
    refs = refs[2:] if ahead else refs
    keep_ref, send_ref, dx_ref, loss_ref = refs[:4]
    refs = refs[4:]
    copies = []
    if ahead:
        next1_ref, next2_ref, sems = refs[0], refs[1], refs[-1]
        refs = refs[2:-1]
        copies = load_all([
            (w1_hbm.at[head + 2], next1_ref, sems.at[0]),
            (w2_hbm.at[head + 2], next2_ref, sems.at[1]),
        ])
    (rows_ref, spread_ref, tail_ref, hop_ref, hot_ref, pre_ref, lg_ref, h1_ref, hat1_ref, slope1_ref,
     h2_ref, hat2_ref, slope2_ref, scale_ref, sums_ref, dh_ref, d2_ref, d1_ref, dl_ref, grad_ref) = refs
    latent = w2_ref.shape[0]
    tail_rows = w1_ref.shape[0] - latent
    mine = own_lanes(place_ref)
    horizon_row = hz_ref[:, mine]
    bin_ids = lax.broadcasted_iota(jnp.int32, (LANES, LANES), 0)
    first_end = latent + LANES
    losses = []
    spread_columns(g_ref[head + 1], s_ref[head + 1], rows_ref, spread_ref)
    tail_ref[...] = padded_rows(w1_ref[latent:, :], LANES)
    hot_ref[...] = padded_rows(ho_ref[head], LANES)
    hop_ref[...] = jnp.transpose(hot_ref[...])
    gain1, gain2, shift1, shift2 = [spread_ref.at[place] for place in range(4)]
    pre_ref[...] = tn(w1_ref[0:latent, :], xt_ref[0:latent, :]) + tn(tail_ref[...], xt_ref[latent:, :])
    for step in range(steps):
        mish_forward_low(pre_ref, gain1, shift1, h1_ref, hat1_ref, slope1_ref, scale_ref, 0, lanes_of(step))
    pre_ref[...] = tn(w2_ref[...], h1_ref[...])
    for step in range(steps):
        mish_forward_low(pre_ref, gain2, shift2, h2_ref, hat2_ref, slope2_ref, scale_ref, 1, lanes_of(step))
    lg_ref[...] = nn(hot_ref[...], h2_ref[...])
    share = 0.1 if head == 0 else 0.1 / (heads - 1)
    bins_ref = rb_ref if head == 0 else vb_ref
    for step in range(steps):
        at = lanes_of(step)
        logits = jnp.where(bin_ids < bins, lg_ref[:, at], F32(-1e30))
        chosen = bin_ids == bins_ref[step : step + 1, mine]
        top = jnp.max(logits, axis=0, keepdims=True)
        powers = jnp.exp(logits - top)
        total = column_sum(powers)
        picked = column_sum(jnp.where(chosen, logits, 0.0))
        weight = row_weight(step, steps, scale * share, horizon_row, place_ref)
        losses.append(weight * (jnp.log(total) + top - picked))
        dl_ref[:, at] = (powers * (weight / total) - jnp.where(chosen, weight, 0.0)).astype(BF16)
    dh_ref[...] = nn(hop_ref[...], dl_ref[...]).astype(BF16)
    grad_ref[:, first_end + latent :] = nt(h2_ref[...], dl_ref[...]).astype(BF16)
    mish_backward_low(dh_ref, hat2_ref, slope2_ref, scale_ref, 1, steps, sums_ref, 2, d2_ref)
    dh_ref[...] = nn(w2_ref[...], d2_ref[...]).astype(BF16)
    grad_ref[:, first_end : first_end + latent] = nt(d2_ref[...], h1_ref[...]).astype(BF16)
    mish_backward_low(dh_ref, hat1_ref, slope1_ref, scale_ref, 0, steps, sums_ref, 0, d1_ref)
    low_part = nn(w1_ref[0:latent, :], d1_ref[...])
    side_part = nn(tail_ref[...], d1_ref[...])
    if not chained:
        dx_ref[0:latent, :] = low_part
        dx_ref[latent:, :] = side_part
    else:
        dx_ref[0:latent, :] = before_ref[0:latent, :] + low_part
        dx_ref[latent:, :] = before_ref[latent:, :] + side_part
    grad_ref[:, 0:latent] = nn(d1_ref[...], x_ref[:, 0:latent]).astype(BF16)
    side_terms = nn(d1_ref[...], x_ref[:, latent:])
    side_terms = with_vectors(side_terms, vector_sums(sums_ref, spread_ref, 2), tail_rows)
    grad_ref[:, latent:first_end] = side_terms.astype(BF16)
    for relative, (which, slot) in enumerate(slots):
        start = pl.multiple_of((place_ref[0] ^ relative) * GROUP, GROUP)
        (keep_ref, send_ref)[which][slot] = grad_ref[pl.ds(start, GROUP), :]
    loss_ref[...] = functools.reduce(jnp.add, losses)
    for each in copies:
        each.wait()


def backward_kernel(
    steps, scale, order, losses, after,
    place_ref, xt_ref, soft_ref, h1_ref, hat1_ref, slope1_ref, h2_ref, hat2_ref, slope2_ref, scale_ref,
    w1_ref, w2_ref, dyn_ref, hz_ref, g_ref, dx_ref, *rest,
):
    initial = order[0] == steps - 1
    final = order[-1] == 0
    loss_refs, rest = rest[:losses], rest[losses:]
    held_refs, rest = ((), rest) if initial else (rest[:4], rest[4:])
    (tgt_hbm, low_ref, first_ref, side_ref, loss_ref, sums_ref, tgt_ref, rows_ref, spread_ref, tail_ref, pre_ref,
     d1_ref, d2_ref, do_ref, grad_ref, sems) = rest[after:]
    mine = own_lanes(place_ref)
    loads = dict(zip(order, load_all([(tgt_hbm.at[step, mine, :], tgt_ref.at[step], sems.at[step]) for step in order])))
    latent = dyn_ref.shape[1]
    here = slice(0, LANES)
    horizon_row = hz_ref[:, mine]
    spread_columns(g_ref[0], g_ref[0], rows_ref, spread_ref)
    tail_rows = w1_ref.shape[0] - latent
    tail_ref[...] = padded_rows(w1_ref[latent:, :], LANES)
    first_end = latent + LANES
    second_end = first_end + latent
    if initial:
        loss = functools.reduce(jnp.add, [each[...] for each in loss_refs])
        side = jnp.zeros((LANES, LANES), F32)
        incoming = None
    else:
        before_ref, given_ref, given_side_ref, given_sums_ref = held_refs
        loss = loss_refs[0][...]
        side = given_side_ref[...]
        incoming = given_ref[...].astype(F32)
        sums_ref[...] = given_sums_ref[...]
    pending = []

    def add_terms(at, fresh, last):
        terms = (
            (slice(0, first_end), nt(d1_ref[:, at], xt_ref[:, at])),
            (slice(first_end, second_end), nt(d2_ref[:, at], h1_ref[:, at])),
            (slice(second_end, second_end + latent), nt(h2_ref[:, at], do_ref[:, at])),
        )
        for lanes, term in terms:
            if not fresh:
                term = term + grad_ref[:, lanes]
            elif not initial:
                term = term + before_ref[:, lanes]
            out_ref = low_ref if last else grad_ref
            if last and final and lanes.start == 0:
                out_ref[:, 0:latent] = term[:, 0:latent].astype(out_ref.dtype)
                vectors = vector_sums(sums_ref, spread_ref, 2)
                out_ref[:, latent:first_end] = with_vectors(term[:, latent:], vectors, tail_rows).astype(out_ref.dtype)
            else:
                out_ref[:, lanes] = term.astype(out_ref.dtype)

    for step in order:
        at = lanes_of(step)
        weight = row_weight(step, steps, scale, horizon_row, place_ref)
        shares = soft_ref[:, lanes_of(step + 1)]
        loads[step].wait()
        residue = shares - jnp.transpose(tgt_ref[step].astype(F32))
        loss = loss + (20.0 / latent) * weight * column_sum(residue * residue)
        grads = residue * ((40.0 / latent) * weight)
        if incoming is not None:
            grads = grads + incoming
        do_ref[:, at] = simplex_back(shares, grads).astype(BF16)
        pre_ref[...] = nn(dyn_ref[...], do_ref[:, at])
        mish_backward(pre_ref, here, hat2_ref, slope2_ref, scale_ref, 1, at, sums_ref, 2, step == steps - 1, d2_ref)
        pre_ref[...] = nn(w2_ref[...], d2_ref[:, at])
        mish_backward(pre_ref, here, hat1_ref, slope1_ref, scale_ref, 0, at, sums_ref, 0, step == steps - 1, d1_ref)
        incoming = nn(w1_ref[0:latent, :], d1_ref[:, at]) + dx_ref[0:latent, at]
        side = side + nn(tail_ref[...], d1_ref[:, at]) + dx_ref[latent:, at]
        incoming = incoming.astype(BF16).astype(F32)
        pending.append(step)
        if len(pending) == 2 or step == order[-1]:
            low, high = min(pending), max(pending) + 1
            add_terms(slice(low * LANES, high * LANES), high == order[0] + 1, low == order[-1])
            pending = []

    first_ref[...] = incoming.astype(BF16)
    side_ref[...] = side
    loss_ref[...] = loss


def ending_kernel(
    slots, tasks, task_width, acted, observed, after,
    place_ref, low_ref, first_ref, side_ref, loss_ref, soft_ref, ein_ref, eh_ref, ehat_ref, eslope_ref, escale_ref,
    ids_ref, e1_ref, eg_ref, e2_ref, *rest,
):
    out_refs, rest = rest[after : after + 4], rest[after + 4 :]
    erows_ref, espread_ref, e1p_ref, epre_ref, esums_ref, ed_ref, egrad_ref = rest
    mine = own_lanes(place_ref)
    here = slice(0, LANES)
    latent = first_ref.shape[0]
    spread_columns(eg_ref[...], eg_ref[...], erows_ref, espread_ref)
    e1p_ref[...] = padded_rows(e1_ref[...], e1p_ref.shape[0])
    d_enc = simplex_back(soft_ref[:, 0:LANES], first_ref[...].astype(F32)).astype(BF16)
    epre_ref[...] = nn(e2_ref[...], d_enc)
    mish_backward(epre_ref, here, ehat_ref, eslope_ref, escale_ref, 0, here, esums_ref, 0, True, ed_ref)
    side_enc = nn(e1p_ref[...], ed_ref[...])
    enc_width = epre_ref.shape[0]
    half = GROUP // 2
    groups = enc_width // half
    kept = egrad_ref.shape[2]
    enc_second = nt(eh_ref[...], d_enc)
    egrad_ref[:, 0:half, :] = enc_second[:, 0:kept].reshape(groups, half, kept)
    egrad_ref[:, half:, 0 : latent - kept] = enc_second[:, kept:].reshape(groups, half, latent - kept)
    enc_first = nt(ed_ref[...], ein_ref[...])
    egrad_ref[:, half:, latent - kept : kept - LANES] = enc_first[:, 0:LANES].reshape(groups, half, LANES)
    second_lanes = with_vectors(enc_first[:, LANES : 2 * LANES], vector_sums(esums_ref, espread_ref, 1), LANES - 2)
    egrad_ref[:, half:, kept - LANES :] = second_lanes.reshape(groups, half, LANES)

    kinds = lax.broadcasted_iota(jnp.int32, (tasks, LANES), 0)
    onehot = (kinds == ids_ref[:, mine]).astype(F32)
    over_lanes = (((1,), (1,)), ((), ()))
    highest = lax.Precision.HIGHEST
    side_terms = lax.dot_general(onehot, side_ref[...], over_lanes, precision=highest, preferred_element_type=F32)
    enc_terms = lax.dot_general(onehot, side_enc, over_lanes, precision=highest, preferred_element_type=F32)
    table = pltpu.roll(side_terms, LANES - acted, 1)
    table = table + pltpu.roll(enc_terms, enc_terms.shape[1] - observed, 1)[:, 0:LANES]
    lane = lax.broadcasted_iota(jnp.int32, table.shape, 1)
    table = jnp.where(lane < task_width, table, 0.0)
    table = jnp.where((lane == LANES - 1) & (kinds == 0), jnp.sum(loss_ref[...], axis=1, keepdims=True), table)
    table_rows = [table[start : start + GROUP] for start in range(0, tasks, GROUP)]
    table_block = jnp.concatenate(table_rows, axis=1).astype(BF16)
    count = low_ref.shape[1] // LANES
    units = (count + kept // LANES) // 2
    for half_no in range(2):
        for relative, (which, slot) in enumerate(slots[half_no]):
            dest = place_ref[0] ^ relative
            start = pl.multiple_of(dest * GROUP, GROUP)
            out_ref = out_refs[2 * half_no + which]
            block = egrad_ref[dest].astype(BF16) if half_no else None
            for unit in range(units):
                column = half_no * units + unit
                if column < count:
                    piece = low_ref[pl.ds(start, GROUP), column * LANES : (column + 1) * LANES]
                else:
                    piece = block[:, (column - count) * LANES : (column - count + 1) * LANES]
                out_ref[slot * units + unit] = piece
    last = len(slots[0]) // 2 * units
    for unit in range(tasks // GROUP):
        for out_ref in out_refs[0:2]:
            out_ref[last + unit] = table_block[:, unit * LANES : (unit + 1) * LANES]


def final_kernel(tasks, task_width, enc_in, bins, net_in, *refs):
    outs = refs[-12:]
    (loss_ref, table_ref, e1_ref, eg_ref, es_ref, e2_ref, first_ref, second_ref, gain_ref, shift_ref, dyn_ref, head_ref) = outs
    refs = refs[:-12]
    tail_refs, refs = refs[:2], refs[2:]
    latent = second_ref.shape[2]
    first_end = latent + LANES
    second_end = first_end + latent

    def put_net(net, value):
        first_ref[net] = value[:, 0:net_in]
        second_ref[net] = value[:, first_end:second_end]
        turned = jnp.transpose(value[:, latent:first_end])
        for layer in range(2):
            row = net_in - latent + 2 * layer
            gain_ref[net, layer : layer + 1, :] = turned[row : row + 1, :]
            shift_ref[net, layer : layer + 1, :] = turned[row + 1 : row + 2, :]

    sums = functools.reduce(jnp.add, [ref[...].astype(F32) for ref in tail_refs])
    units = sums.shape[0] - tasks // GROUP
    tail = jnp.concatenate([sums[unit] for unit in range(units)], axis=1)
    put_net(0, tail)
    dyn_ref[...] = tail[:, second_end : second_end + latent]
    enc = tail[:, second_end + latent :]
    half = GROUP // 2
    kept = enc.shape[1]
    e2_ref[:, 0:kept] = 0.3 * enc[0:half, :]
    e2_ref[:, kept:] = 0.3 * enc[half:, 0 : latent - kept]
    e1_ref[...] = 0.3 * enc[half:, latent - kept : latent - kept + enc_in]
    turned = 0.3 * jnp.transpose(enc[half:, kept - LANES :])
    eg_ref[...] = turned[LANES - 2 : LANES - 1, :]
    es_ref[...] = turned[LANES - 1 : LANES, :]
    loss_ref[...] = sums[units, 0:1, LANES - 1 : LANES]
    for place in range(tasks // GROUP):
        table_ref[place * GROUP : (place + 1) * GROUP, :] = sums[units + place, :, 0:task_width]
    net = 1
    for one_ref, other_ref in zip(refs[0::2], refs[1::2]):
        stacked = len(one_ref.shape) == 4
        for one in range(one_ref.shape[1] if stacked else 1):
            at = (0, one) if stacked else (0,)
            value = one_ref[at].astype(F32) + other_ref[at].astype(F32)
            put_net(net, value)
            head_ref[net - 1] = value[:, second_end : second_end + bins]
            net += 1


def swap(value, axis, distance):
    count = lax.axis_size(axis)
    return lax.ppermute(value, axis, [(place, place ^ distance) for place in range(count)])


def exchange(parts, axis, scale):
    total = parts[0].astype(F32)
    for distance in range(1, len(parts)):
        total = total + swap(parts[distance], axis, distance * scale).astype(F32)
    return total


def scatter_plain(packed, chips, sections):
    held = packed.reshape((sections, chips, CORES) + packed.shape[1:])
    batch_no = lax.axis_index("batch")
    places = (
        ("batch", 1, CORES, 2, batch_no % CORES),
        ("batch", CORES, chips, 1, batch_no // CORES),
        ("section", 1, sections, 0, lax.axis_index("section")),
    )
    for axis, scale, count, dim, mine in places:
        parts = [lax.dynamic_index_in_dim(held, mine ^ other, dim, keepdims=False) for other in range(count)]
        held = exchange(parts, axis, scale)
        held = held.astype(BF16) if dim else held
    return held


def on_device(
    observations,
    actions,
    targets,
    task_ids,
    horizons,
    reward_bins,
    value_bins,
    task_table,
    enc_first,
    enc_gain,
    enc_shift,
    enc_second,
    net_first,
    net_second,
    net_gain,
    net_shift,
    dyn_out,
    head_out,
):
    sections = lax.axis_size("section")
    batches = lax.axis_size("batch")
    section_no = lax.axis_index("section")
    chips = batches // CORES
    devices = sections * batches
    steps, rows_all, acted = actions.shape
    observed = observations.shape[1]
    rows = rows_all // sections
    latent = dyn_out.shape[1]
    hidden = dyn_out.shape[0]
    tasks, task_width = task_table.shape
    heads, _, bins = head_out.shape
    nets, net_in, _ = net_first.shape
    enc_in, enc_width = enc_first.shape
    wide = steps * LANES
    scale = 1.0 / (rows_all * batches * steps)
    groups = hidden // GROUP
    in_place = hidden // devices == GROUP
    start = section_no * rows
    block_no = start // LANES
    first_lane = start - block_no * LANES
    me = section_no * batches + lax.axis_index("batch") if in_place else jnp.int32(0)
    place = jnp.stack([me, block_no, first_lane, first_lane + rows]).astype(jnp.int32)
    bits = [("batch", 1 << bit) for bit in range(batches.bit_length() - 1)]
    bits += [("section", 1 << bit) for bit in range(sections.bit_length() - 1)]

    def slots_of(order):
        if not in_place:
            return tuple((relative // (groups // 2), relative % (groups // 2)) for relative in range(groups))
        found = []
        for relative in range(groups):
            slot = 0
            for bit in order:
                slot = 2 * slot + (relative >> bit & 1)
            found.append((slot // (groups // 2), slot % (groups // 2)))
        return tuple(found)

    plain = tuple(range(len(bits)))
    y_first = (0, 2, 1) + tuple(range(3, len(bits))) if in_place else plain
    half_slots = groups // 2
    shape_of = jax.ShapeDtypeStruct
    smem = pl.BlockSpec(memory_space=pltpu.SMEM)
    local = pl.BlockSpec(memory_space=pltpu.VMEM)
    far = pl.BlockSpec(memory_space=pltpu.HBM)
    anywhere = pl.BlockSpec(memory_space=pl.ANY)
    first_far, second_far, dyn_far, targets_far = [
        pltpu.with_memory_space_constraint(array, pltpu.HBM) for array in (net_first, net_second, dyn_out, targets)
    ]
    vmem = pltpu.VMEM
    dmas = pltpu.SemaphoreType.DMA

    def params(mebibytes):
        return pltpu.CompilerParams(vmem_limit_bytes=mebibytes * 1024 * 1024)

    def cost(flops, moved):
        return pl.CostEstimate(flops=flops, bytes_accessed=moved, transcendentals=0)

    ids_row = task_ids.reshape(1, rows_all)
    horizon_row = horizons.reshape(1, rows_all)
    eg_row = enc_gain.reshape(1, enc_width)
    es_row = enc_shift.reshape(1, enc_width)
    head_turned = head_out.transpose(0, 2, 1)
    low = lambda lanes: shape_of((hidden, lanes), BF16)
    forward_shapes = (
        shape_of((latent + LANES, wide), BF16),
        shape_of((latent, wide + LANES), F32),
        low(wide), low(wide), low(wide), low(wide), low(wide), low(wide),
        shape_of((8, wide), F32),
        shape_of((2 * LANES, LANES), BF16),
        shape_of((enc_width, LANES), BF16),
        shape_of((enc_width, LANES), BF16),
        shape_of((enc_width, LANES), BF16),
        shape_of((8, LANES), F32),
        shape_of((net_in, hidden), BF16),
        shape_of((hidden, hidden), BF16),
        shape_of((hidden, latent), BF16),
        shape_of((wide, latent + LANES), BF16),
    )

    weight_shapes = (shape_of((net_in, hidden), BF16), shape_of((hidden, hidden), BF16))

    early = [
        pltpu.with_memory_space_constraint(array, pltpu.HBM)
        for array in (
            observations.T, actions.transpose(0, 2, 1), ids_row, task_table, enc_first, eg_row, es_row, enc_second,
            net_gain, net_shift,
        )
    ]
    made = pl.pallas_call(
        functools.partial(forward_kernel, steps),
        out_shape=forward_shapes + weight_shapes,
        in_specs=[smem] + [far] * 13,
        out_specs=[local] * (len(forward_shapes) + 2),
        scratch_shapes=[
            vmem((8, hidden), F32),
            vmem((4, hidden, LANES), F32),
            vmem((8, enc_width), F32),
            vmem((2, enc_width, LANES), F32),
            vmem((tasks, 2 * LANES), F32),
            vmem((LANES, LANES), F32),
            vmem((2 * LANES, enc_width), BF16),
            vmem((hidden, latent + LANES), BF16),
            vmem((hidden, hidden), BF16),
            vmem((latent, hidden), BF16),
            vmem((hidden, LANES), F32),
            vmem((enc_width, LANES), F32),
            *[vmem(each.shape, each.dtype) for each in early],
            dmas((5,)),
            dmas((len(early),)),
        ],
        compiler_params=params(VMEM_A),
        cost_estimate=cost(10_000_000_000, 8_000_000),
        name="forward_chain",
    )(
        place, *early, first_far, second_far, dyn_far,
    )
    saved, x_rows, weights = made[:-3], made[-3], made[-2:]
    xt = saved[0]
    head_width = latent + LANES + hidden + LANES

    def run_head(head, ahead, weights, before, after):
        pack_shape = shape_of((half_slots, GROUP, head_width), BF16)
        dx_shape = shape_of((latent + LANES, wide), F32)
        out_shapes = (pack_shape, pack_shape, dx_shape, shape_of((1, LANES), F32))
        args = [place, xt, x_rows, *weights, head_turned, net_gain, net_shift, reward_bins, value_bins, horizon_row]
        specs = [smem] + [local] * 10
        aliases = {}
        if before is not None:
            aliases = {len(args): 2}
            args.append(before)
            specs.append(local)
        args += after
        specs += [anywhere] * len(after)
        if ahead:
            args += [first_far, second_far]
            specs += [far, far]
            out_shapes += weight_shapes
        low_wide = vmem((hidden, wide), BF16)
        scratch = [
            vmem((8, hidden), F32),
            vmem((4, hidden, LANES), F32),
            vmem((LANES, hidden), BF16),
            vmem((hidden, LANES), BF16),
            vmem((LANES, hidden), BF16),
            vmem((hidden, wide), F32),
            vmem((LANES, wide), F32),
        ]
        scratch += [low_wide] * 6
        scratch += [vmem((8, wide), F32), vmem((4, hidden, LANES), F32)]
        scratch += [low_wide] * 3
        scratch += [vmem((LANES, wide), BF16), vmem((hidden, head_width), BF16)]
        if ahead:
            scratch.append(dmas((2,)))
        return pl.pallas_call(
            functools.partial(
                heads_kernel, steps, scale, slots_of(plain), head, ahead, heads, bins, before is not None, len(after)
            ),
            out_shape=out_shapes,
            in_specs=specs,
            out_specs=[local] * len(out_shapes),
            scratch_shapes=scratch,
            input_output_aliases=aliases,
            compiler_params=params(VMEM_B),
            cost_estimate=cost(9_000_000_000, 4_000_000),
            name=f"head_{head}",
        )(*args)

    def phase(pair, bit):
        return pair[0], swap(pair[1], *bits[bit])

    def fold(members, *tokens):
        slots_now = members[0][0].shape[0] // 2
        shape = members[0][0].shape[1:]
        if len(members) > 1:
            shape = (len(members),) + shape
        out_shape = shape_of((slots_now,) + shape, BF16)

        def fold_kernel(*refs):
            refs = refs[len(tokens) :]
            outs = refs[-2:]
            for place in range(len(members)):
                kept_ref, came_ref = refs[2 * place], refs[2 * place + 1]
                for half in range(2):
                    part = pl.ds(half * slots_now, slots_now)
                    value = (kept_ref[part].astype(F32) + came_ref[part].astype(F32)).astype(BF16)
                    if len(members) > 1:
                        outs[half][:, place] = value
                    else:
                        outs[half][...] = value

        return run_fold(fold_kernel, out_shape, members, tokens)

    def fold_units(members, slots_now, common, *tokens):
        counts = [(kept.shape[0] - (0 if place else common)) // slots_now for place, (kept, _) in enumerate(members)]
        half_now = slots_now // 2
        width = sum(counts)
        out_shape = shape_of((half_now * width + common,) + members[0][0].shape[1:], BF16)

        def fold_kernel(*refs):
            refs = refs[len(tokens) :]
            outs = refs[-2:]
            before = 0
            for place, count in enumerate(counts):
                kept_ref, came_ref = refs[2 * place], refs[2 * place + 1]

                def added(start, size):
                    part = pl.ds(start, size)
                    return (kept_ref[part].astype(F32) + came_ref[part].astype(F32)).astype(BF16)

                for half in range(2):
                    if len(counts) == 1:
                        outs[half][0 : half_now * count] = added(half * half_now * count, half_now * count)
                    else:
                        for slot in range(half_now):
                            at = slot * width + before
                            outs[half][at : at + count] = added((half * half_now + slot) * count, count)
                if place == 0 and common:
                    value = added(slots_now * count, common)
                    for out in outs:
                        out[half_now * width :] = value
                before += count

        return run_fold(fold_kernel, out_shape, members, tokens)

    def run_fold(kernel, out_shape, members, tokens):
        inputs = [each for member in members for each in member]
        return pl.pallas_call(
            kernel,
            out_shape=(out_shape, out_shape),
            in_specs=[anywhere] * len(tokens) + [local] * len(inputs),
            out_specs=(local, local),
            compiler_params=params(VMEM_SUM),
            cost_estimate=cost(1_000_000, 2_000_000),
            name="fold",
        )(*tokens, *inputs)

    net_width = latent + LANES + hidden + latent
    chain_inputs = saved[:9] + saved[14:]

    def run_backward(order, losses, held, after):
        final = order[-1] == 0
        out_shapes = (
            shape_of((hidden, net_width), BF16 if final else F32),
            shape_of((latent, LANES), BF16),
            shape_of((LANES, LANES), F32),
            shape_of((1, LANES), F32),
            shape_of((4, hidden, LANES), F32),
        )
        args = [place, *chain_inputs, horizon_row, net_gain, dx, *losses, *held]
        return pl.pallas_call(
            functools.partial(backward_kernel, steps, scale, order, len(losses), len(after)),
            out_shape=out_shapes,
            in_specs=[smem] + [local] * (len(args) - 1) + [anywhere] * len(after) + [far],
            out_specs=[local] * len(out_shapes),
            scratch_shapes=[
                vmem((steps, LANES, latent), BF16),
                vmem((8, hidden), F32),
                vmem((4, hidden, LANES), F32),
                vmem((LANES, hidden), BF16),
                vmem((hidden, LANES), F32),
                vmem((hidden, wide), BF16),
                vmem((hidden, wide), BF16),
                vmem((latent, wide), BF16),
                vmem((hidden, net_width), F32),
                dmas((steps,)),
            ],
            compiler_params=params(VMEM_C),
            cost_estimate=cost(7_000_000_000, 8_000_000),
            name=f"backward_{order[0]}",
        )(*args, *after, targets_far)

    packs, loss_parts = [], []
    dx = None
    flights = []
    after = []

    def advance(head, bit, token, kept_back):
        if in_place and 0 <= head < heads:
            pair = fold([flights[head]], token)
            kept_back.append(pair[0])
            flights[head] = phase(pair, plain[bit])

    for head in range(heads):
        ahead = head + 1 < heads
        result = run_head(head, ahead, weights, dx, after)
        keep, send, dx, loss = result[:4]
        weights = result[4:]
        packs.append((keep, send))
        loss_parts.append(loss)
        after = []
        advance(head - 1, 1, loss, after)
        advance(head - 2, 2, loss, after)
        if in_place:
            flights.append(phase((keep, send), plain[0]))
    early = heads // 2
    half_way = steps // 2
    if in_place:
        group = fold(flights[0:early], loss_parts[-1])
        after.append(group[0])
        group = phase(group, plain[3])
    chain = run_backward(tuple(range(steps - 1, half_way - 1, -1)), loss_parts, [], after)
    after = []
    advance(heads - 1, 1, chain[3], after)
    advance(heads - 2, 2, chain[3], after)
    if in_place:
        group = fold([group], chain[3])
        after.append(group[0])
        group = phase(group, plain[4])
        after.append(flights[heads - 3][1])
    chain = run_backward(
        tuple(range(half_way - 1, -1, -1)), [chain[3]], [chain[0], chain[1], chain[2], chain[4]], after
    )
    after = []
    advance(heads - 1, 2, chain[3], after)
    if in_place:
        second = fold(flights[early : heads - 1], chain[3])
        after += [group[1], second[0]]
        second = phase(second, plain[3])

    enc_lanes = latent - LANES
    units = (net_width + enc_lanes) // 2 // LANES
    common = tasks // GROUP
    one_shape = shape_of((half_slots * units + common, GROUP, LANES), BF16)
    two_shape = shape_of((half_slots * units, GROUP, LANES), BF16)
    tail_slots = (slots_of(plain), slots_of(y_first))
    ended = pl.pallas_call(
        functools.partial(ending_kernel, tail_slots, tasks, task_width, acted, observed, len(after)),
        out_shape=(one_shape, one_shape, two_shape, two_shape),
        in_specs=[smem] + [local] * 14 + [anywhere] * len(after),
        out_specs=[local] * 4,
        scratch_shapes=[
            vmem((8, enc_width), F32),
            vmem((2, enc_width, LANES), F32),
            vmem((2 * LANES, enc_width), BF16),
            vmem((enc_width, LANES), F32),
            vmem((2, enc_width, LANES), F32),
            vmem((enc_width, LANES), BF16),
            vmem((groups, GROUP, enc_lanes), F32),
        ],
        compiler_params=params(VMEM_SUM),
        cost_estimate=cost(1_000_000_000, 4_000_000),
        name="ending",
    )(place, *chain[:4], saved[1], *saved[9:14], ids_row, enc_first, eg_row, enc_second, *after)

    if in_place:
        one = phase(ended[0:2], plain[0])
        two = phase(ended[2:4], y_first[0])
        one = phase(fold_units([one], half_slots, common, ended[0]), plain[1])
        two = phase(fold_units([two], half_slots, 0, ended[0]), y_first[1])
        rest = phase(fold(flights[heads - 1 :], ended[0]), plain[3])
        one = fold_units([one], half_slots // 2, common, second[1], rest[1])
        two = fold_units([two], half_slots // 2, 0, second[1], rest[1])
        second = phase(fold([second], ended[0]), plain[4])
        one = phase(one, plain[2])
        two = phase(two, y_first[2])
        rest = phase(fold([rest], ended[0]), plain[4])
        tail = phase(fold_units([one, two], half_slots // 4, common, second[1], rest[1]), plain[3])
        tail = phase(fold_units([tail], half_slots // 8, common), plain[4])
        each = GROUP // 2
        out_shapes = (
            shape_of((1, 1), F32),
            shape_of((tasks, task_width), F32),
            shape_of((each, enc_in), F32),
            shape_of((1, each), F32),
            shape_of((1, each), F32),
            shape_of((each, latent), F32),
            shape_of((nets, GROUP, net_in), F32),
            shape_of((nets, GROUP, hidden), F32),
            shape_of((nets, 2, GROUP), F32),
            shape_of((nets, 2, GROUP), F32),
            shape_of((GROUP, latent), F32),
            shape_of((heads, GROUP, bins), F32),
        )
        ends = [*tail, *group, *second, *rest]
        outs = list(pl.pallas_call(
            functools.partial(final_kernel, tasks, task_width, enc_in, bins, net_in),
            out_shape=out_shapes,
            in_specs=[local] * len(ends),
            out_specs=[local] * len(out_shapes),
            compiler_params=params(VMEM_SUM),
            cost_estimate=cost(1_000_000, 4_000_000),
            name="last_sums",
        )(*ends))
        outs[0] = outs[0].reshape(())
        outs[2] = outs[2].T
        outs[3], outs[4] = outs[3].reshape(each), outs[4].reshape(each)
        outs[6] = outs[6].transpose(0, 2, 1)
        outs[7] = outs[7].transpose(0, 2, 1)
        return tuple(outs)

    def scattered(keep, send):
        mine = hidden // devices
        packed = jnp.concatenate([keep, send], axis=0)
        middle = packed.shape[1:-2]
        packed = packed.reshape((groups,) + middle + (GROUP // mine, mine, packed.shape[-1]))
        packed = jnp.moveaxis(packed, -3, 1).reshape((devices,) + middle + (mine, packed.shape[-1]))
        return scatter_plain(packed, chips, sections)

    head_sum = jnp.stack([scattered(*pack) for pack in packs], axis=0)
    enc_each = enc_width // devices
    def by_rows(place):
        parts = [each[: half_slots * units].reshape(half_slots, units, GROUP, LANES) for each in (ended[place], ended[2 + place])]
        joined = jnp.concatenate(parts, axis=1).transpose(0, 2, 1, 3)
        return joined.reshape(half_slots, GROUP, 2 * units * LANES)

    keep, send = by_rows(0), by_rows(1)
    table_sum = lax.psum(ended[0][half_slots * units :].astype(F32), ("section", "batch"))
    table_sum = table_sum.transpose(1, 0, 2).reshape(GROUP, common * LANES)
    net_sum = scattered(keep[:, :, 0:net_width], send[:, :, 0:net_width])
    enc_all = jnp.concatenate([keep, send], axis=0)[:, :, net_width:]
    enc_all = enc_all.reshape(groups, 2, enc_width // groups, enc_lanes)
    enc_all = enc_all.transpose(0, 2, 1, 3).reshape(devices, enc_each, 2, enc_lanes)
    enc_sum = scatter_plain(enc_all, chips, sections)
    enc_low, enc_high = enc_sum[:, 0], enc_sum[:, 1]
    s_enc_second = jnp.concatenate([enc_low, enc_high[:, 0 : latent - enc_lanes]], axis=1)
    enc_rows = enc_high[:, latent - enc_lanes :]
    first_end = latent + LANES
    net_row = jnp.concatenate([net_sum[:, 0 : first_end + hidden], jnp.zeros_like(net_sum[:, 0:LANES])], axis=1)
    sums = jnp.concatenate([net_row[None], head_sum], axis=0)
    vectors = sums[:, :, net_in : net_in + 4].transpose(0, 2, 1)
    table = table_sum.reshape(GROUP, tasks // GROUP, LANES).transpose(1, 0, 2).reshape(tasks, LANES)
    return (
        table[0, LANES - 1],
        table[:, 0:task_width],
        0.3 * enc_rows[:, 0:enc_in].T,
        0.3 * enc_rows[:, 2 * LANES - 2],
        0.3 * enc_rows[:, 2 * LANES - 1],
        0.3 * s_enc_second,
        sums[:, :, 0:net_in].transpose(0, 2, 1),
        sums[:, :, first_end : first_end + hidden].transpose(0, 2, 1),
        vectors[:, 0::2],
        vectors[:, 1::2],
        net_sum[:, first_end + hidden :],
        head_sum[:, :, first_end + hidden : first_end + hidden + bins],
    )


def solution(mesh):
    both = ("section", "batch")
    return jax.shard_map(
        on_device,
        mesh=mesh,
        in_specs=(
            P("batch", None),
            P(None, "batch", None),
            P(None, "batch", None),
            P("batch"),
            P("batch"),
            P(None, "batch"),
            P(None, "batch"),
        )
        + (P(),) * 11,
        out_specs=(
            P(),
            P(),
            P(None, both),
            P(both),
            P(both),
            P(both, None),
            P(None, None, both),
            P(None, None, both),
            P(None, None, both),
            P(None, None, both),
            P(both, None),
            P(None, both, None),
        ),
        check_vma=False,
    )
```

```python
import functools

import jax
import jax.numpy as jnp
from jax import lax
from jax.experimental import pallas as pl
from jax.experimental.pallas import tpu as pltpu
from jax.sharding import PartitionSpec as P

CORES = 2
LANES = 128
GROUP = 16
BF16 = jnp.bfloat16
F32 = jnp.float32
VMEM_A = 18
VMEM_B = 20
VMEM_SUM = 6
VMEM_C = 20


def nn(left, right):
    return lax.dot_general(left, right, (((1,), (0,)), ((), ())), preferred_element_type=F32)


def nt(left, right):
    return lax.dot_general(left, right, (((1,), (1,)), ((), ())), preferred_element_type=F32)


def tn(left, right):
    return lax.dot_general(left, right, (((0,), (0,)), ((), ())), preferred_element_type=F32)


def column_sum(value):
    grouped = value.reshape(value.shape[0] // 8, 8, value.shape[1])
    return jnp.sum(jnp.sum(grouped, axis=0), axis=0, keepdims=True)


def slabs(features, size=64):
    return [slice(start, start + size) for start in range(0, features, size)]


def lanes_of(step):
    return slice(step * LANES, (step + 1) * LANES)


def spread_columns(gain_rows, shift_rows, rows_ref, spread_ref):
    count = gain_rows.shape[0]
    rows_ref[...] = jnp.zeros_like(rows_ref)
    rows_ref[0:count, :] = gain_rows
    rows_ref[count : 2 * count, :] = shift_rows
    turned = jnp.transpose(rows_ref[...])
    for place in range(2 * count):
        spread_ref[place] = jnp.broadcast_to(turned[:, place : place + 1], spread_ref.shape[1:])


def mish_forward(pre_ref, pre_at, gain_ref, shift_ref, hid_ref, hat_ref, slope_ref, scale_ref, scale_row, at):
    features = pre_ref.shape[0]
    row_mean = column_sum(pre_ref[:, pre_at]) * (1.0 / features)
    centred = pre_ref[:, pre_at] - row_mean
    spread = column_sum(centred * centred) * (1.0 / features)
    scale = lax.rsqrt(spread + 1e-05)
    scale_ref[scale_row : scale_row + 1, at] = scale
    for part in slabs(features):
        hat = (pre_ref[part, pre_at] - row_mean) * scale
        normed = hat * gain_ref[part, :] + shift_ref[part, :]
        power = jnp.exp(normed)
        top = power * (power + 2.0)
        inverse = pl.reciprocal(top + 2.0, approx=True)
        ratio = top * inverse
        hid_ref[part, at] = (normed * ratio).astype(BF16)
        tilt = power * inverse
        slope = ratio + normed * (4.0 * (tilt * (tilt + inverse)))
        slope_ref[part, at] = (slope * gain_ref[part, :]).astype(BF16)
        hat_ref[part, at] = hat.astype(BF16)


def mish_backward(grad_ref, grad_at, hat_ref, slope_ref, scale_ref, scale_row, at, sums_ref, sums_at, first, out_ref):
    features = grad_ref.shape[0]
    total_one = jnp.zeros((8, LANES), F32)
    total_two = jnp.zeros((8, LANES), F32)
    for part in slabs(features):
        term = grad_ref[part, grad_at] * slope_ref[part, at].astype(F32)
        grad_ref[part, grad_at] = term
        crossed = term * hat_ref[part, at].astype(F32)
        groups = (term.shape[0] // 8, 8, LANES)
        total_one = total_one + jnp.sum(term.reshape(groups), axis=0)
        total_two = total_two + jnp.sum(crossed.reshape(groups), axis=0)
        if first:
            sums_ref[sums_at, part, :] = term
            sums_ref[sums_at + 1, part, :] = crossed
        else:
            sums_ref[sums_at, part, :] += term
            sums_ref[sums_at + 1, part, :] += crossed
    mean_one = jnp.sum(total_one, axis=0, keepdims=True) * (1.0 / features)
    mean_two = jnp.sum(total_two, axis=0, keepdims=True) * (1.0 / features)
    scale = scale_ref[scale_row : scale_row + 1, at]
    for part in slabs(features):
        rest = grad_ref[part, grad_at] - mean_one - hat_ref[part, at].astype(F32) * mean_two
        out_ref[part, at] = (rest * scale).astype(BF16)


def mish_forward_low(pre_ref, gain_ref, shift_ref, hid_ref, hat_ref, slope_ref, scale_ref, scale_row, at):
    features = pre_ref.shape[0]
    row_mean = column_sum(pre_ref[:, at]) * (1.0 / features)
    centred = pre_ref[:, at] - row_mean
    spread = column_sum(centred * centred) * (1.0 / features)
    scale = lax.rsqrt(spread + 1e-05)
    scale_ref[scale_row : scale_row + 1, at] = scale
    for part in slabs(features):
        hat = (pre_ref[part, at] - row_mean) * scale
        normed = (hat * gain_ref[part, :] + shift_ref[part, :]).astype(BF16)
        hat_ref[part, at] = hat.astype(BF16)
        power = jnp.exp(normed)
        top = power * (power + 2.0)
        inverse = pl.reciprocal(top + 2.0, approx=True)
        ratio = top * inverse
        hid_ref[part, at] = normed * ratio
        tilt = power * inverse
        slope = ratio + (4.0 * normed) * (tilt * (tilt + inverse))
        slope_ref[part, at] = slope * gain_ref[part, :].astype(BF16)


def mish_backward_low(grad_ref, hat_ref, slope_ref, scale_ref, scale_row, steps, sums_ref, sums_at, out_ref):
    features = grad_ref.shape[0]
    rows = []
    for step in range(steps):
        at = lanes_of(step)
        total_one = jnp.zeros((16, LANES), F32)
        total_two = jnp.zeros((16, LANES), F32)
        for part in slabs(features):
            term = grad_ref[part, at] * slope_ref[part, at]
            crossed = term * hat_ref[part, at]
            grad_ref[part, at] = term
            groups = (term.shape[0] // 16, 16, LANES)
            term = term.reshape(groups)
            crossed = crossed.reshape(groups)
            total_one = total_one + functools.reduce(jnp.add, [term[k] for k in range(groups[0])]).astype(F32)
            total_two = total_two + functools.reduce(jnp.add, [crossed[k] for k in range(groups[0])]).astype(F32)
        scale = scale_ref[scale_row : scale_row + 1, at]
        mean_one = jnp.sum(total_one, axis=0, keepdims=True) * (1.0 / features)
        mean_two = jnp.sum(total_two, axis=0, keepdims=True) * (1.0 / features)
        rows.append((mean_one.astype(BF16), mean_two.astype(BF16), scale.astype(BF16)))
    for part in slabs(features):
        sum_one, sum_two = None, None
        for step, (mean_one, mean_two, scale) in enumerate(rows):
            at = lanes_of(step)
            term = grad_ref[part, at]
            hat = hat_ref[part, at]
            out_ref[part, at] = (term - mean_one - hat * mean_two) * scale
            crossed = term * hat
            sum_one = term if sum_one is None else sum_one + term
            sum_two = crossed if sum_two is None else sum_two + crossed
        sums_ref[sums_at, part, :] = sum_one.astype(F32)
        sums_ref[sums_at + 1, part, :] = sum_two.astype(F32)


def simplex(values):
    grouped = values.reshape(values.shape[0] // 8, 8, values.shape[1])
    powers = jnp.exp(grouped - jnp.max(grouped, axis=1, keepdims=True))
    shares = powers / jnp.sum(powers, axis=1, keepdims=True)
    return shares.reshape(values.shape)


def simplex_back(shares, grads):
    grouped = (shares.shape[0] // 8, 8, shares.shape[1])
    crossed = jnp.sum((shares * grads).reshape(grouped), axis=1, keepdims=True)
    return (shares.reshape(grouped) * (grads.reshape(grouped) - crossed)).reshape(shares.shape)


def row_weight(step, steps, scale, horizon_row, place_ref):
    lane = lax.broadcasted_iota(jnp.int32, (1, LANES), 1)
    mine = (lane >= place_ref[2]) & (lane < place_ref[3]) & (horizon_row > step)
    return jnp.where(mine, F32(scale * 0.5 ** (step / (steps - 1))), 0.0)


def padded_rows(value, rows):
    zeros = jnp.zeros((rows - value.shape[0], value.shape[1]), F32)
    return jnp.concatenate([value.astype(F32), zeros], axis=0).astype(BF16)


def transpose_into(out_ref, source_ref, rows):
    for start in range(0, rows, LANES):
        out_ref[:, start : start + LANES] = jnp.transpose(source_ref[start : start + LANES, :])


def vector_sums(sums_ref, gains_ref, layers):
    vectors = []
    for layer in range(layers):
        inverse = 1.0 / gains_ref[layer]
        vectors.append(jnp.sum(sums_ref[2 * layer + 1] * inverse, axis=1, keepdims=True))
        vectors.append(jnp.sum(sums_ref[2 * layer] * inverse, axis=1, keepdims=True))
    return vectors


def own_lanes(place_ref):
    return pl.ds(pl.multiple_of(place_ref[1] * LANES, LANES), LANES)


def load_all(copies):
    made = [pltpu.make_async_copy(*each) for each in copies]
    for each in made:
        each.start()
    return made


def with_vectors(value, vectors, first_lane):
    lane = lax.broadcasted_iota(jnp.int32, value.shape, 1)
    for place, vector in enumerate(vectors):
        value = jnp.where(lane == first_lane + place, vector, value)
    return value


def forward_kernel(
    steps,
    place_ref, obs_hbm, act_hbm, ids_hbm, table_hbm, e1_hbm, eg_hbm, es_hbm, e2_hbm, g_hbm, s_hbm,
    w1_hbm, w2_hbm, dyn_hbm,
    xt_ref, soft_ref, h1_ref, hat1_ref, slope1_ref, h2_ref, hat2_ref, slope2_ref, scale_ref,
    ein_ref, eh_ref, ehat_ref, eslope_ref, escale_ref,
    w1_ref, w2_ref, dyn_ref, x_ref, next1_ref, next2_ref,
    rows_ref, spread_ref, erows_ref, espread_ref, wide_ref, tall_ref, e1p_ref, w1t_ref, w2t_ref, dynt_ref, pre_ref, epre_ref,
    obs_ref, act_ref, ids_ref, table_ref, e1_ref, eg_ref, es_ref, e2_ref, g_ref, s_ref,
    sems, early_sems,
):
    early = load_all([
        (table_hbm, table_ref, early_sems.at[0]),
        (ids_hbm, ids_ref, early_sems.at[1]),
        (obs_hbm, obs_ref, early_sems.at[2]),
        (e1_hbm, e1_ref, early_sems.at[3]),
        (eg_hbm, eg_ref, early_sems.at[4]),
        (es_hbm, es_ref, early_sems.at[5]),
        (e2_hbm, e2_ref, early_sems.at[6]),
        (act_hbm, act_ref, early_sems.at[7]),
        (g_hbm, g_ref, early_sems.at[8]),
        (s_hbm, s_ref, early_sems.at[9]),
    ])
    first, second, third, fourth, fifth = load_all([
        (w1_hbm.at[0], w1_ref, sems.at[0]),
        (w2_hbm.at[0], w2_ref, sems.at[1]),
        (dyn_hbm, dyn_ref, sems.at[2]),
        (w1_hbm.at[1], next1_ref, sems.at[3]),
        (w2_hbm.at[1], next2_ref, sems.at[4]),
    ])
    latent = dyn_ref.shape[1]
    tasks, task_width = table_ref.shape
    observed = obs_ref.shape[0]
    acted = act_ref.shape[1]
    mine = own_lanes(place_ref)
    for each in early:
        each.wait()
    spread_columns(eg_ref[...], es_ref[...], erows_ref, espread_ref)
    kinds = lax.broadcasted_iota(jnp.int32, (tasks, LANES), 0)
    onehot = (kinds == ids_ref[:, mine]).astype(F32).astype(BF16)
    wide_ref[...] = jnp.zeros_like(wide_ref)
    wide_ref[:, 0:task_width] = table_ref[...].astype(F32)
    table_tail = pltpu.roll(wide_ref[:, 0:LANES], acted, 1).astype(BF16)
    table_enc = pltpu.roll(wide_ref[...], observed, 1).astype(BF16)
    aux = tn(table_tail, onehot)
    tall_ref[...] = jnp.zeros_like(tall_ref)
    tall_ref[0:observed, :] = obs_ref[:, mine].astype(F32)
    ein = tn(table_enc, onehot)
    ein_ref[0:LANES, :] = (ein[0:LANES] + tall_ref[...]).astype(BF16)
    ein_ref[LANES:, :] = ein[LANES:].astype(BF16)
    e1p_ref[...] = padded_rows(e1_ref[...], e1p_ref.shape[0])
    epre_ref[...] = tn(e1p_ref[...], ein_ref[...])
    here = slice(0, LANES)
    mish_forward(epre_ref, here, espread_ref.at[0], espread_ref.at[1], eh_ref, ehat_ref, eslope_ref, escale_ref, 0, here)
    shares = simplex(tn(e2_ref[...], eh_ref[...]))
    soft_ref[:, 0:LANES] = shares
    xt_ref[0:latent, 0:LANES] = shares.astype(BF16)
    spread_columns(g_ref[0], s_ref[0], rows_ref, spread_ref)
    for step in range(steps):
        tall_ref[...] = jnp.zeros_like(tall_ref)
        tall_ref[0:acted, :] = act_ref[step, :, mine].astype(F32)
        xt_ref[latent:, lanes_of(step)] = (aux + tall_ref[...]).astype(BF16)
    first.wait()
    transpose_into(w1t_ref, w1_ref, latent)
    w1t_ref[:, latent:] = jnp.transpose(padded_rows(w1_ref[latent:, :], LANES))
    second.wait()
    transpose_into(w2t_ref, w2_ref, latent)
    third.wait()
    transpose_into(dynt_ref, dyn_ref, latent)
    for step in range(steps):
        at = lanes_of(step)
        pre_ref[...] = nn(w1t_ref[...], xt_ref[:, at])
        mish_forward(pre_ref, here, spread_ref.at[0], spread_ref.at[2], h1_ref, hat1_ref, slope1_ref, scale_ref, 0, at)
        pre_ref[...] = nn(w2t_ref[...], h1_ref[:, at])
        mish_forward(pre_ref, here, spread_ref.at[1], spread_ref.at[3], h2_ref, hat2_ref, slope2_ref, scale_ref, 1, at)
        shares = simplex(nn(dynt_ref[...], h2_ref[:, at]))
        soft_ref[:, lanes_of(step + 1)] = shares
        if step + 1 < steps:
            xt_ref[0:latent, lanes_of(step + 1)] = shares.astype(BF16)
    for step in range(steps):
        for start in range(0, latent + LANES, LANES):
            x_ref[lanes_of(step), start : start + LANES] = jnp.transpose(xt_ref[start : start + LANES, lanes_of(step)])
    fourth.wait()
    fifth.wait()


def heads_kernel(steps, scale, packs, head, ahead, heads, bins, chained, after, *refs):
    refs = list(refs)
    place_ref, xt_ref, x_ref, w1_ref, w2_ref, ho_ref, g_ref, s_ref, rb_ref, vb_ref, hz_ref = refs[:11]
    refs = refs[11:]
    before_ref = refs.pop(0) if chained else None
    refs = refs[after:]
    w1_hbm, w2_hbm = refs[:2] if ahead else (None, None)
    refs = refs[2:] if ahead else refs
    pack_refs, refs = refs[: 2 * len(packs)], refs[2 * len(packs) :]
    dx_ref, loss_ref = refs[:2]
    refs = refs[2:]
    copies = []
    if ahead:
        next1_ref, next2_ref, sems = refs[0], refs[1], refs[-1]
        refs = refs[2:-1]
        copies = load_all([
            (w1_hbm.at[head + 2], next1_ref, sems.at[0]),
            (w2_hbm.at[head + 2], next2_ref, sems.at[1]),
        ])
    (rows_ref, spread_ref, tail_ref, hop_ref, hot_ref, pre_ref, lg_ref, h1_ref, hat1_ref, slope1_ref,
     h2_ref, hat2_ref, slope2_ref, scale_ref, sums_ref, dh_ref, d2_ref, d1_ref, dl_ref, grad_ref) = refs
    latent = w2_ref.shape[0]
    tail_rows = w1_ref.shape[0] - latent
    mine = own_lanes(place_ref)
    horizon_row = hz_ref[:, mine]
    bin_ids = lax.broadcasted_iota(jnp.int32, (LANES, LANES), 0)
    first_end = latent + LANES
    losses = []
    spread_columns(g_ref[head + 1], s_ref[head + 1], rows_ref, spread_ref)
    tail_ref[...] = padded_rows(w1_ref[latent:, :], LANES)
    hot_ref[...] = padded_rows(ho_ref[head], LANES)
    hop_ref[...] = jnp.transpose(hot_ref[...])
    gain1, gain2, shift1, shift2 = [spread_ref.at[place] for place in range(4)]
    pre_ref[...] = tn(w1_ref[0:latent, :], xt_ref[0:latent, :]) + tn(tail_ref[...], xt_ref[latent:, :])
    for step in range(steps):
        mish_forward_low(pre_ref, gain1, shift1, h1_ref, hat1_ref, slope1_ref, scale_ref, 0, lanes_of(step))
    pre_ref[...] = tn(w2_ref[...], h1_ref[...])
    for step in range(steps):
        mish_forward_low(pre_ref, gain2, shift2, h2_ref, hat2_ref, slope2_ref, scale_ref, 1, lanes_of(step))
    lg_ref[...] = nn(hot_ref[...], h2_ref[...])
    share = 0.1 if head == 0 else 0.1 / (heads - 1)
    bins_ref = rb_ref if head == 0 else vb_ref
    for step in range(steps):
        at = lanes_of(step)
        logits = jnp.where(bin_ids < bins, lg_ref[:, at], F32(-1e30))
        chosen = bin_ids == bins_ref[step : step + 1, mine]
        top = jnp.max(logits, axis=0, keepdims=True)
        powers = jnp.exp(logits - top)
        total = column_sum(powers)
        picked = column_sum(jnp.where(chosen, logits, 0.0))
        weight = row_weight(step, steps, scale * share, horizon_row, place_ref)
        losses.append(weight * (jnp.log(total) + top - picked))
        dl_ref[:, at] = (powers * (weight / total) - jnp.where(chosen, weight, 0.0)).astype(BF16)
    dh_ref[...] = nn(hop_ref[...], dl_ref[...]).astype(BF16)
    grad_ref[:, first_end + latent :] = nt(h2_ref[...], dl_ref[...]).astype(BF16)
    mish_backward_low(dh_ref, hat2_ref, slope2_ref, scale_ref, 1, steps, sums_ref, 2, d2_ref)
    dh_ref[...] = nn(w2_ref[...], d2_ref[...]).astype(BF16)
    grad_ref[:, first_end : first_end + latent] = nt(d2_ref[...], h1_ref[...]).astype(BF16)
    mish_backward_low(dh_ref, hat1_ref, slope1_ref, scale_ref, 0, steps, sums_ref, 0, d1_ref)
    low_part = nn(w1_ref[0:latent, :], d1_ref[...])
    side_part = nn(tail_ref[...], d1_ref[...])
    if not chained:
        dx_ref[0:latent, :] = low_part
        dx_ref[latent:, :] = side_part
    else:
        dx_ref[0:latent, :] = before_ref[0:latent, :] + low_part
        dx_ref[latent:, :] = before_ref[latent:, :] + side_part
    grad_ref[:, 0:latent] = nn(d1_ref[...], x_ref[:, 0:latent]).astype(BF16)
    side_terms = nn(d1_ref[...], x_ref[:, latent:])
    side_terms = with_vectors(side_terms, vector_sums(sums_ref, spread_ref, 2), tail_rows)
    grad_ref[:, latent:first_end] = side_terms.astype(BF16)
    for place, (slots, first, units) in enumerate(packs):
        for relative, (which, slot) in enumerate(slots):
            start = pl.multiple_of((place_ref[0] ^ relative) * GROUP, GROUP)
            out_ref = pack_refs[2 * place + which]
            if not units:
                out_ref[slot] = grad_ref[pl.ds(start, GROUP), :]
            for unit in range(units):
                at = slice((first + unit) * LANES, (first + unit + 1) * LANES)
                out_ref[slot * units + unit] = grad_ref[pl.ds(start, GROUP), at]
    loss_ref[...] = functools.reduce(jnp.add, losses)
    for each in copies:
        each.wait()


def backward_kernel(
    steps, scale, order, losses, after,
    place_ref, xt_ref, soft_ref, h1_ref, hat1_ref, slope1_ref, h2_ref, hat2_ref, slope2_ref, scale_ref,
    w1_ref, w2_ref, dyn_ref, hz_ref, g_ref, dx_ref, *rest,
):
    initial = order[0] == steps - 1
    final = order[-1] == 0
    loss_refs, rest = rest[:losses], rest[losses:]
    held_refs, rest = ((), rest) if initial else (rest[:4], rest[4:])
    (tgt_hbm, low_ref, first_ref, side_ref, loss_ref, sums_ref, tgt_ref, rows_ref, spread_ref, tail_ref, pre_ref,
     d1_ref, d2_ref, do_ref, grad_ref, sems) = rest[after:]
    mine = own_lanes(place_ref)
    loads = dict(zip(order, load_all([(tgt_hbm.at[step, mine, :], tgt_ref.at[step], sems.at[step]) for step in order])))
    latent = dyn_ref.shape[1]
    here = slice(0, LANES)
    horizon_row = hz_ref[:, mine]
    spread_columns(g_ref[0], g_ref[0], rows_ref, spread_ref)
    tail_rows = w1_ref.shape[0] - latent
    tail_ref[...] = padded_rows(w1_ref[latent:, :], LANES)
    first_end = latent + LANES
    second_end = first_end + latent
    if initial:
        loss = functools.reduce(jnp.add, [each[...] for each in loss_refs])
        side = jnp.zeros((LANES, LANES), F32)
        incoming = None
    else:
        before_ref, given_ref, given_side_ref, given_sums_ref = held_refs
        loss = loss_refs[0][...]
        side = given_side_ref[...]
        incoming = given_ref[...].astype(F32)
        sums_ref[...] = given_sums_ref[...]
    pending = []

    def add_terms(at, fresh, last):
        terms = (
            (slice(0, first_end), nt(d1_ref[:, at], xt_ref[:, at])),
            (slice(first_end, second_end), nt(d2_ref[:, at], h1_ref[:, at])),
            (slice(second_end, second_end + latent), nt(h2_ref[:, at], do_ref[:, at])),
        )
        for lanes, term in terms:
            if not fresh:
                term = term + grad_ref[:, lanes]
            elif not initial:
                term = term + before_ref[:, lanes]
            out_ref = low_ref if last else grad_ref
            if last and final and lanes.start == 0:
                out_ref[:, 0:latent] = term[:, 0:latent].astype(out_ref.dtype)
                vectors = vector_sums(sums_ref, spread_ref, 2)
                out_ref[:, latent:first_end] = with_vectors(term[:, latent:], vectors, tail_rows).astype(out_ref.dtype)
            else:
                out_ref[:, lanes] = term.astype(out_ref.dtype)

    for step in order:
        at = lanes_of(step)
        weight = row_weight(step, steps, scale, horizon_row, place_ref)
        shares = soft_ref[:, lanes_of(step + 1)]
        loads[step].wait()
        residue = shares - jnp.transpose(tgt_ref[step].astype(F32))
        loss = loss + (20.0 / latent) * weight * column_sum(residue * residue)
        grads = residue * ((40.0 / latent) * weight)
        if incoming is not None:
            grads = grads + incoming
        do_ref[:, at] = simplex_back(shares, grads).astype(BF16)
        pre_ref[...] = nn(dyn_ref[...], do_ref[:, at])
        mish_backward(pre_ref, here, hat2_ref, slope2_ref, scale_ref, 1, at, sums_ref, 2, step == steps - 1, d2_ref)
        pre_ref[...] = nn(w2_ref[...], d2_ref[:, at])
        mish_backward(pre_ref, here, hat1_ref, slope1_ref, scale_ref, 0, at, sums_ref, 0, step == steps - 1, d1_ref)
        incoming = nn(w1_ref[0:latent, :], d1_ref[:, at]) + dx_ref[0:latent, at]
        side = side + nn(tail_ref[...], d1_ref[:, at]) + dx_ref[latent:, at]
        incoming = incoming.astype(BF16).astype(F32)
        pending.append(step)
        if len(pending) == 2 or step == order[-1]:
            low, high = min(pending), max(pending) + 1
            add_terms(slice(low * LANES, high * LANES), high == order[0] + 1, low == order[-1])
            pending = []

    first_ref[...] = incoming.astype(BF16)
    side_ref[...] = side
    loss_ref[...] = loss


def ending_kernel(
    slots, tasks, task_width, acted, observed, after,
    place_ref, low_ref, first_ref, side_ref, loss_ref, soft_ref, ein_ref, eh_ref, ehat_ref, eslope_ref, escale_ref,
    ids_ref, e1_ref, eg_ref, e2_ref, *rest,
):
    out_refs, rest = rest[after : after + 4], rest[after + 4 :]
    erows_ref, espread_ref, e1p_ref, epre_ref, esums_ref, ed_ref, egrad_ref = rest
    mine = own_lanes(place_ref)
    here = slice(0, LANES)
    latent = first_ref.shape[0]
    spread_columns(eg_ref[...], eg_ref[...], erows_ref, espread_ref)
    e1p_ref[...] = padded_rows(e1_ref[...], e1p_ref.shape[0])
    d_enc = simplex_back(soft_ref[:, 0:LANES], first_ref[...].astype(F32)).astype(BF16)
    epre_ref[...] = nn(e2_ref[...], d_enc)
    mish_backward(epre_ref, here, ehat_ref, eslope_ref, escale_ref, 0, here, esums_ref, 0, True, ed_ref)
    side_enc = nn(e1p_ref[...], ed_ref[...])
    enc_width = epre_ref.shape[0]
    half = GROUP // 2
    groups = enc_width // half
    kept = egrad_ref.shape[2]
    enc_second = nt(eh_ref[...], d_enc)
    egrad_ref[:, 0:half, :] = enc_second[:, 0:kept].reshape(groups, half, kept)
    egrad_ref[:, half:, 0 : latent - kept] = enc_second[:, kept:].reshape(groups, half, latent - kept)
    enc_first = nt(ed_ref[...], ein_ref[...])
    egrad_ref[:, half:, latent - kept : kept - LANES] = enc_first[:, 0:LANES].reshape(groups, half, LANES)
    second_lanes = with_vectors(enc_first[:, LANES : 2 * LANES], vector_sums(esums_ref, espread_ref, 1), LANES - 2)
    egrad_ref[:, half:, kept - LANES :] = second_lanes.reshape(groups, half, LANES)

    kinds = lax.broadcasted_iota(jnp.int32, (tasks, LANES), 0)
    onehot = (kinds == ids_ref[:, mine]).astype(F32)
    over_lanes = (((1,), (1,)), ((), ()))
    highest = lax.Precision.HIGHEST
    side_terms = lax.dot_general(onehot, side_ref[...], over_lanes, precision=highest, preferred_element_type=F32)
    enc_terms = lax.dot_general(onehot, side_enc, over_lanes, precision=highest, preferred_element_type=F32)
    table = pltpu.roll(side_terms, LANES - acted, 1)
    table = table + pltpu.roll(enc_terms, enc_terms.shape[1] - observed, 1)[:, 0:LANES]
    lane = lax.broadcasted_iota(jnp.int32, table.shape, 1)
    table = jnp.where(lane < task_width, table, 0.0)
    table = jnp.where((lane == LANES - 1) & (kinds == 0), jnp.sum(loss_ref[...], axis=1, keepdims=True), table)
    table_rows = [table[start : start + GROUP] for start in range(0, tasks, GROUP)]
    table_block = jnp.concatenate(table_rows, axis=1).astype(BF16)
    count = low_ref.shape[1] // LANES
    units = (count + kept // LANES) // 2
    for half_no in range(2):
        for relative, (which, slot) in enumerate(slots[half_no]):
            dest = place_ref[0] ^ relative
            start = pl.multiple_of(dest * GROUP, GROUP)
            out_ref = out_refs[2 * half_no + which]
            block = egrad_ref[dest].astype(BF16) if half_no else None
            for unit in range(units):
                column = half_no * units + unit
                if column < count:
                    piece = low_ref[pl.ds(start, GROUP), column * LANES : (column + 1) * LANES]
                else:
                    piece = block[:, (column - count) * LANES : (column - count + 1) * LANES]
                out_ref[slot * units + unit] = piece
    last = len(slots[0]) // 2 * units
    for unit in range(tasks // GROUP):
        for out_ref in out_refs[0:2]:
            out_ref[last + unit] = table_block[:, unit * LANES : (unit + 1) * LANES]


def final_kernel(tasks, task_width, enc_in, bins, net_in, *refs):
    outs = refs[-12:]
    (loss_ref, table_ref, e1_ref, eg_ref, es_ref, e2_ref, first_ref, second_ref, gain_ref, shift_ref, dyn_ref, head_ref) = outs
    refs = refs[:-12]
    tail_refs, refs = refs[:2], refs[2:]
    latent = second_ref.shape[2]
    first_end = latent + LANES
    second_end = first_end + latent

    def put_net(net, value):
        first_ref[net] = value[:, 0:net_in]
        second_ref[net] = value[:, first_end:second_end]
        turned = jnp.transpose(value[:, latent:first_end])
        for layer in range(2):
            row = net_in - latent + 2 * layer
            gain_ref[net, layer : layer + 1, :] = turned[row : row + 1, :]
            shift_ref[net, layer : layer + 1, :] = turned[row + 1 : row + 2, :]

    sums = functools.reduce(jnp.add, [ref[...].astype(F32) for ref in tail_refs])
    units = sums.shape[0] - tasks // GROUP
    tail = jnp.concatenate([sums[unit] for unit in range(units)], axis=1)
    put_net(0, tail)
    dyn_ref[...] = tail[:, second_end : second_end + latent]
    enc = tail[:, second_end + latent :]
    half = GROUP // 2
    kept = enc.shape[1]
    e2_ref[:, 0:kept] = 0.3 * enc[0:half, :]
    e2_ref[:, kept:] = 0.3 * enc[half:, 0 : latent - kept]
    e1_ref[...] = 0.3 * enc[half:, latent - kept : latent - kept + enc_in]
    turned = 0.3 * jnp.transpose(enc[half:, kept - LANES :])
    eg_ref[...] = turned[LANES - 2 : LANES - 1, :]
    es_ref[...] = turned[LANES - 1 : LANES, :]
    loss_ref[...] = sums[units, 0:1, LANES - 1 : LANES]
    for place in range(tasks // GROUP):
        table_ref[place * GROUP : (place + 1) * GROUP, :] = sums[units + place, :, 0:task_width]
    net = 1
    def put_head(value):
        put_net(net, value)
        head_ref[net - 1] = value[:, second_end : second_end + bins]

    one_ref, other_ref, last_one_ref, last_other_ref = refs
    for one in range(one_ref.shape[1]):
        put_head(one_ref[0, one].astype(F32) + other_ref[0, one].astype(F32))
        net += 1
    sums = last_one_ref[...].astype(F32) + last_other_ref[...].astype(F32)
    units = (second_end + LANES) // LANES
    for start in range(0, sums.shape[0], units):
        put_head(jnp.concatenate([sums[start + unit] for unit in range(units)], axis=1))
        net += 1


def swap(value, axis, distance):
    count = lax.axis_size(axis)
    return lax.ppermute(value, axis, [(place, place ^ distance) for place in range(count)])


def exchange(parts, axis, scale):
    total = parts[0].astype(F32)
    for distance in range(1, len(parts)):
        total = total + swap(parts[distance], axis, distance * scale).astype(F32)
    return total


def scatter_plain(packed, chips, sections):
    held = packed.reshape((sections, chips, CORES) + packed.shape[1:])
    batch_no = lax.axis_index("batch")
    places = (
        ("batch", 1, CORES, 2, batch_no % CORES),
        ("batch", CORES, chips, 1, batch_no // CORES),
        ("section", 1, sections, 0, lax.axis_index("section")),
    )
    for axis, scale, count, dim, mine in places:
        parts = [lax.dynamic_index_in_dim(held, mine ^ other, dim, keepdims=False) for other in range(count)]
        held = exchange(parts, axis, scale)
        held = held.astype(BF16) if dim else held
    return held


def on_device(
    observations,
    actions,
    targets,
    task_ids,
    horizons,
    reward_bins,
    value_bins,
    task_table,
    enc_first,
    enc_gain,
    enc_shift,
    enc_second,
    net_first,
    net_second,
    net_gain,
    net_shift,
    dyn_out,
    head_out,
):
    sections = lax.axis_size("section")
    batches = lax.axis_size("batch")
    section_no = lax.axis_index("section")
    chips = batches // CORES
    devices = sections * batches
    steps, rows_all, acted = actions.shape
    observed = observations.shape[1]
    rows = rows_all // sections
    latent = dyn_out.shape[1]
    hidden = dyn_out.shape[0]
    tasks, task_width = task_table.shape
    heads, _, bins = head_out.shape
    nets, net_in, _ = net_first.shape
    enc_in, enc_width = enc_first.shape
    wide = steps * LANES
    scale = 1.0 / (rows_all * batches * steps)
    groups = hidden // GROUP
    in_place = hidden // devices == GROUP
    start = section_no * rows
    block_no = start // LANES
    first_lane = start - block_no * LANES
    me = section_no * batches + lax.axis_index("batch") if in_place else jnp.int32(0)
    place = jnp.stack([me, block_no, first_lane, first_lane + rows]).astype(jnp.int32)
    bits = [("batch", 1 << bit) for bit in range(batches.bit_length() - 1)]
    bits += [("section", 1 << bit) for bit in range(sections.bit_length() - 1)]

    def slots_of(order):
        if not in_place:
            return tuple((relative // (groups // 2), relative % (groups // 2)) for relative in range(groups))
        found = []
        for relative in range(groups):
            slot = 0
            for bit in order:
                slot = 2 * slot + (relative >> bit & 1)
            found.append((slot // (groups // 2), slot % (groups // 2)))
        return tuple(found)

    plain = tuple(range(len(bits)))
    y_first = (0, 2, 1) + tuple(range(3, len(bits))) if in_place else plain
    half_slots = groups // 2
    shape_of = jax.ShapeDtypeStruct
    smem = pl.BlockSpec(memory_space=pltpu.SMEM)
    local = pl.BlockSpec(memory_space=pltpu.VMEM)
    far = pl.BlockSpec(memory_space=pltpu.HBM)
    anywhere = pl.BlockSpec(memory_space=pl.ANY)
    first_far, second_far, dyn_far, targets_far = [
        pltpu.with_memory_space_constraint(array, pltpu.HBM) for array in (net_first, net_second, dyn_out, targets)
    ]
    vmem = pltpu.VMEM
    dmas = pltpu.SemaphoreType.DMA

    def params(mebibytes):
        return pltpu.CompilerParams(vmem_limit_bytes=mebibytes * 1024 * 1024)

    def cost(flops, moved):
        return pl.CostEstimate(flops=flops, bytes_accessed=moved, transcendentals=0)

    ids_row = task_ids.reshape(1, rows_all)
    horizon_row = horizons.reshape(1, rows_all)
    eg_row = enc_gain.reshape(1, enc_width)
    es_row = enc_shift.reshape(1, enc_width)
    head_turned = head_out.transpose(0, 2, 1)
    low = lambda lanes: shape_of((hidden, lanes), BF16)
    forward_shapes = (
        shape_of((latent + LANES, wide), BF16),
        shape_of((latent, wide + LANES), F32),
        low(wide), low(wide), low(wide), low(wide), low(wide), low(wide),
        shape_of((8, wide), F32),
        shape_of((2 * LANES, LANES), BF16),
        shape_of((enc_width, LANES), BF16),
        shape_of((enc_width, LANES), BF16),
        shape_of((enc_width, LANES), BF16),
        shape_of((8, LANES), F32),
        shape_of((net_in, hidden), BF16),
        shape_of((hidden, hidden), BF16),
        shape_of((hidden, latent), BF16),
        shape_of((wide, latent + LANES), BF16),
    )

    weight_shapes = (shape_of((net_in, hidden), BF16), shape_of((hidden, hidden), BF16))

    early = [
        pltpu.with_memory_space_constraint(array, pltpu.HBM)
        for array in (
            observations.T, actions.transpose(0, 2, 1), ids_row, task_table, enc_first, eg_row, es_row, enc_second,
            net_gain, net_shift,
        )
    ]
    made = pl.pallas_call(
        functools.partial(forward_kernel, steps),
        out_shape=forward_shapes + weight_shapes,
        in_specs=[smem] + [far] * 13,
        out_specs=[local] * (len(forward_shapes) + 2),
        scratch_shapes=[
            vmem((8, hidden), F32),
            vmem((4, hidden, LANES), F32),
            vmem((8, enc_width), F32),
            vmem((2, enc_width, LANES), F32),
            vmem((tasks, 2 * LANES), F32),
            vmem((LANES, LANES), F32),
            vmem((2 * LANES, enc_width), BF16),
            vmem((hidden, latent + LANES), BF16),
            vmem((hidden, hidden), BF16),
            vmem((latent, hidden), BF16),
            vmem((hidden, LANES), F32),
            vmem((enc_width, LANES), F32),
            *[vmem(each.shape, each.dtype) for each in early],
            dmas((5,)),
            dmas((len(early),)),
        ],
        compiler_params=params(VMEM_A),
        cost_estimate=cost(10_000_000_000, 8_000_000),
        name="forward_chain",
    )(
        place, *early, first_far, second_far, dyn_far,
    )
    saved, x_rows, weights = made[:-3], made[-3], made[-2:]
    xt = saved[0]
    head_width = latent + LANES + hidden + LANES

    def run_head(head, ahead, weights, before, after):
        all_units = head_width // LANES
        packs = [(slots_of(plain), 0, 0)]
        if in_place and head == heads - 2:
            packs = [(slots_of(plain), 0, all_units)]
        if in_place and head == heads - 1:
            packs = [(slots_of(plain), 0, all_units // 2), (slots_of(y_first), all_units // 2, all_units // 2)]
        pack_shapes = []
        for _, _, count in packs:
            shape = (half_slots * count, GROUP, LANES) if count else (half_slots, GROUP, head_width)
            pack_shapes += [shape_of(shape, BF16)] * 2
        dx_shape = shape_of((latent + LANES, wide), F32)
        out_shapes = (*pack_shapes, dx_shape, shape_of((1, LANES), F32))
        args = [place, xt, x_rows, *weights, head_turned, net_gain, net_shift, reward_bins, value_bins, horizon_row]
        specs = [smem] + [local] * 10
        aliases = {}
        if before is not None:
            aliases = {len(args): len(pack_shapes)}
            args.append(before)
            specs.append(local)
        args += after
        specs += [anywhere] * len(after)
        if ahead:
            args += [first_far, second_far]
            specs += [far, far]
            out_shapes += weight_shapes
        low_wide = vmem((hidden, wide), BF16)
        scratch = [
            vmem((8, hidden), F32),
            vmem((4, hidden, LANES), F32),
            vmem((LANES, hidden), BF16),
            vmem((hidden, LANES), BF16),
            vmem((LANES, hidden), BF16),
            vmem((hidden, wide), F32),
            vmem((LANES, wide), F32),
        ]
        scratch += [low_wide] * 6
        scratch += [vmem((8, wide), F32), vmem((4, hidden, LANES), F32)]
        scratch += [low_wide] * 3
        scratch += [vmem((LANES, wide), BF16), vmem((hidden, head_width), BF16)]
        if ahead:
            scratch.append(dmas((2,)))
        return pl.pallas_call(
            functools.partial(
                heads_kernel, steps, scale, packs, head, ahead, heads, bins, before is not None, len(after)
            ),
            out_shape=out_shapes,
            in_specs=specs,
            out_specs=[local] * len(out_shapes),
            scratch_shapes=scratch,
            input_output_aliases=aliases,
            compiler_params=params(VMEM_B),
            cost_estimate=cost(9_000_000_000, 4_000_000),
            name=f"head_{head}",
        )(*args)

    def phase(pair, bit):
        return pair[0], swap(pair[1], *bits[bit])

    def fold(members, *tokens):
        slots_now = members[0][0].shape[0] // 2
        shape = members[0][0].shape[1:]
        stacked = len(shape) == 3
        if stacked:
            shape = (len(members) * shape[0],) + shape[1:]
        elif len(members) > 1:
            shape = (len(members),) + shape
        out_shape = shape_of((slots_now,) + shape, BF16)

        def fold_kernel(*refs):
            refs = refs[len(tokens) :]
            outs = refs[-2:]
            for place in range(len(members)):
                kept_ref, came_ref = refs[2 * place], refs[2 * place + 1]
                for half in range(2):
                    part = pl.ds(half * slots_now, slots_now)
                    value = (kept_ref[part].astype(F32) + came_ref[part].astype(F32)).astype(BF16)
                    if stacked:
                        count = kept_ref.shape[1]
                        outs[half][:, place * count : (place + 1) * count] = value
                    elif len(members) > 1:
                        outs[half][:, place] = value
                    else:
                        outs[half][...] = value

        return run_fold(fold_kernel, out_shape, members, tokens)

    def fold_units(members, slots_now, common, *tokens):
        counts = [(kept.shape[0] - (0 if place else common)) // slots_now for place, (kept, _) in enumerate(members)]
        half_now = slots_now // 2
        width = sum(counts)
        out_shape = shape_of((half_now * width + common,) + members[0][0].shape[1:], BF16)

        def fold_kernel(*refs):
            refs = refs[len(tokens) :]
            outs = refs[-2:]
            before = 0
            for place, count in enumerate(counts):
                kept_ref, came_ref = refs[2 * place], refs[2 * place + 1]

                def added(start, size):
                    part = pl.ds(start, size)
                    return (kept_ref[part].astype(F32) + came_ref[part].astype(F32)).astype(BF16)

                for half in range(2):
                    if len(counts) == 1:
                        outs[half][0 : half_now * count] = added(half * half_now * count, half_now * count)
                    else:
                        for slot in range(half_now):
                            at = slot * width + before
                            outs[half][at : at + count] = added((half * half_now + slot) * count, count)
                if place == 0 and common:
                    value = added(slots_now * count, common)
                    for out in outs:
                        out[half_now * width :] = value
                before += count

        return run_fold(fold_kernel, out_shape, members, tokens)

    def run_fold(kernel, out_shape, members, tokens):
        inputs = [each for member in members for each in member]
        return pl.pallas_call(
            kernel,
            out_shape=(out_shape, out_shape),
            in_specs=[anywhere] * len(tokens) + [local] * len(inputs),
            out_specs=(local, local),
            compiler_params=params(VMEM_SUM),
            cost_estimate=cost(1_000_000, 2_000_000),
            name="fold",
        )(*tokens, *inputs)

    net_width = latent + LANES + hidden + latent
    chain_inputs = saved[:9] + saved[14:]

    def run_backward(order, losses, held, after):
        final = order[-1] == 0
        out_shapes = (
            shape_of((hidden, net_width), BF16 if final else F32),
            shape_of((latent, LANES), BF16),
            shape_of((LANES, LANES), F32),
            shape_of((1, LANES), F32),
            shape_of((4, hidden, LANES), F32),
        )
        args = [place, *chain_inputs, horizon_row, net_gain, dx, *losses, *held]
        return pl.pallas_call(
            functools.partial(backward_kernel, steps, scale, order, len(losses), len(after)),
            out_shape=out_shapes,
            in_specs=[smem] + [local] * (len(args) - 1) + [anywhere] * len(after) + [far],
            out_specs=[local] * len(out_shapes),
            scratch_shapes=[
                vmem((steps, LANES, latent), BF16),
                vmem((8, hidden), F32),
                vmem((4, hidden, LANES), F32),
                vmem((LANES, hidden), BF16),
                vmem((hidden, LANES), F32),
                vmem((hidden, wide), BF16),
                vmem((hidden, wide), BF16),
                vmem((latent, wide), BF16),
                vmem((hidden, net_width), F32),
                dmas((steps,)),
            ],
            compiler_params=params(VMEM_C),
            cost_estimate=cost(7_000_000_000, 8_000_000),
            name=f"backward_{order[0]}",
        )(*args, *after, targets_far)

    packs, loss_parts = [], []
    dx = None
    after = []
    cores, pairs = [], []
    units_all = head_width // LANES
    for head in range(heads):
        result = run_head(head, head + 1 < heads, weights, dx, after)
        sent = 4 if in_place and head == heads - 1 else 2
        dx, loss = result[sent : sent + 2]
        weights = result[sent + 2 :]
        packs.append(result[:sent])
        loss_parts.append(loss)
        after = []
        if in_place:
            if 1 <= head <= heads - 2:
                crossing = fold([cores[head - 1]], loss)
                after.append(crossing[0])
                pairs.append(phase(crossing, plain[1]))
            if head in (3, 5):
                crossing = fold(pairs[head - 3 : head - 1], loss)
                after.append(crossing[0])
                pairs[head - 3] = phase(crossing, plain[2])
            if head == heads - 1:
                fourth = fold_units([cores[head - 1]], half_slots, 0, loss)
                after.append(fourth[0])
                fourth = phase(fourth, plain[1])
                cores.append(phase(result[0:2], plain[0]))
                cores.append(phase(result[2:4], y_first[0]))
            else:
                cores.append(phase(result[0:2], plain[0]))
    half_way = steps // 2
    chain = run_backward(tuple(range(steps - 1, half_way - 1, -1)), loss_parts, [], after)
    after = []
    if in_place:
        token = chain[3]
        fifth = fold_units([cores[heads - 1]], half_slots, 0, token)
        sixth = fold_units([cores[heads]], half_slots, 0, token)
        fourth = fold_units([fourth], half_slots // 2, 0, token)
        group = fold([pairs[0], pairs[2]], token)
        after = [fifth[0], sixth[0], fourth[0], group[0]]
        fifth = phase(fifth, plain[1])
        sixth = phase(sixth, y_first[1])
        group = phase(group, plain[3])
        fourth = phase(fourth, plain[2])
    chain = run_backward(
        tuple(range(half_way - 1, -1, -1)), [chain[3]], [chain[0], chain[1], chain[2], chain[4]], after
    )
    after = []
    if in_place:
        token = chain[3]
        fifth = fold_units([fifth], half_slots // 2, 0, token)
        sixth = fold_units([sixth], half_slots // 2, 0, token)
        group = fold([group], token)
        after = [fifth[0], sixth[0], group[0], fourth[1]]
        fifth = phase(fifth, plain[2])
        sixth = phase(sixth, y_first[2])
        group = phase(group, plain[4])

    enc_lanes = latent - LANES
    units = (net_width + enc_lanes) // 2 // LANES
    common = tasks // GROUP
    one_shape = shape_of((half_slots * units + common, GROUP, LANES), BF16)
    two_shape = shape_of((half_slots * units, GROUP, LANES), BF16)
    tail_slots = (slots_of(plain), slots_of(y_first))
    ended = pl.pallas_call(
        functools.partial(ending_kernel, tail_slots, tasks, task_width, acted, observed, len(after)),
        out_shape=(one_shape, one_shape, two_shape, two_shape),
        in_specs=[smem] + [local] * 14 + [anywhere] * len(after),
        out_specs=[local] * 4,
        scratch_shapes=[
            vmem((8, enc_width), F32),
            vmem((2, enc_width, LANES), F32),
            vmem((2 * LANES, enc_width), BF16),
            vmem((enc_width, LANES), F32),
            vmem((2, enc_width, LANES), F32),
            vmem((enc_width, LANES), BF16),
            vmem((groups, GROUP, enc_lanes), F32),
        ],
        compiler_params=params(VMEM_SUM),
        cost_estimate=cost(1_000_000_000, 4_000_000),
        name="ending",
    )(place, *chain[:4], saved[1], *saved[9:14], ids_row, enc_first, eg_row, enc_second, *after)

    if in_place:
        one = phase(ended[0:2], plain[0])
        two = phase(ended[2:4], y_first[0])
        one = phase(fold_units([one], half_slots, common, ended[0]), plain[1])
        two = phase(fold_units([two], half_slots, 0, ended[0]), y_first[1])
        last = phase(fold_units([fourth, fifth, sixth], half_slots // 4, 0, ended[0]), plain[3])
        one = fold_units([one], half_slots // 2, common, last[1])
        two = fold_units([two], half_slots // 2, 0, last[1])
        last = phase(fold_units([last], half_slots // 8, 0, ended[0]), plain[4])
        one = phase(one, plain[2])
        two = phase(two, y_first[2])
        tail = phase(fold_units([one, two], half_slots // 4, common, last[1], group[1]), plain[3])
        tail = phase(fold_units([tail], half_slots // 8, common), plain[4])
        each = GROUP // 2
        out_shapes = (
            shape_of((1, 1), F32),
            shape_of((tasks, task_width), F32),
            shape_of((each, enc_in), F32),
            shape_of((1, each), F32),
            shape_of((1, each), F32),
            shape_of((each, latent), F32),
            shape_of((nets, GROUP, net_in), F32),
            shape_of((nets, GROUP, hidden), F32),
            shape_of((nets, 2, GROUP), F32),
            shape_of((nets, 2, GROUP), F32),
            shape_of((GROUP, latent), F32),
            shape_of((heads, GROUP, bins), F32),
        )
        ends = [*tail, *group, *last]
        outs = list(pl.pallas_call(
            functools.partial(final_kernel, tasks, task_width, enc_in, bins, net_in),
            out_shape=out_shapes,
            in_specs=[local] * len(ends),
            out_specs=[local] * len(out_shapes),
            compiler_params=params(VMEM_SUM),
            cost_estimate=cost(1_000_000, 4_000_000),
            name="last_sums",
        )(*ends))
        outs[0] = outs[0].reshape(())
        outs[2] = outs[2].T
        outs[3], outs[4] = outs[3].reshape(each), outs[4].reshape(each)
        outs[6] = outs[6].transpose(0, 2, 1)
        outs[7] = outs[7].transpose(0, 2, 1)
        return tuple(outs)

    def scattered(keep, send):
        mine = hidden // devices
        packed = jnp.concatenate([keep, send], axis=0)
        middle = packed.shape[1:-2]
        packed = packed.reshape((groups,) + middle + (GROUP // mine, mine, packed.shape[-1]))
        packed = jnp.moveaxis(packed, -3, 1).reshape((devices,) + middle + (mine, packed.shape[-1]))
        return scatter_plain(packed, chips, sections)

    head_sum = jnp.stack([scattered(*pack) for pack in packs], axis=0)
    enc_each = enc_width // devices
    def by_rows(place):
        parts = [each[: half_slots * units].reshape(half_slots, units, GROUP, LANES) for each in (ended[place], ended[2 + place])]
        joined = jnp.concatenate(parts, axis=1).transpose(0, 2, 1, 3)
        return joined.reshape(half_slots, GROUP, 2 * units * LANES)

    keep, send = by_rows(0), by_rows(1)
    table_sum = lax.psum(ended[0][half_slots * units :].astype(F32), ("section", "batch"))
    table_sum = table_sum.transpose(1, 0, 2).reshape(GROUP, common * LANES)
    net_sum = scattered(keep[:, :, 0:net_width], send[:, :, 0:net_width])
    enc_all = jnp.concatenate([keep, send], axis=0)[:, :, net_width:]
    enc_all = enc_all.reshape(groups, 2, enc_width // groups, enc_lanes)
    enc_all = enc_all.transpose(0, 2, 1, 3).reshape(devices, enc_each, 2, enc_lanes)
    enc_sum = scatter_plain(enc_all, chips, sections)
    enc_low, enc_high = enc_sum[:, 0], enc_sum[:, 1]
    s_enc_second = jnp.concatenate([enc_low, enc_high[:, 0 : latent - enc_lanes]], axis=1)
    enc_rows = enc_high[:, latent - enc_lanes :]
    first_end = latent + LANES
    net_row = jnp.concatenate([net_sum[:, 0 : first_end + hidden], jnp.zeros_like(net_sum[:, 0:LANES])], axis=1)
    sums = jnp.concatenate([net_row[None], head_sum], axis=0)
    vectors = sums[:, :, net_in : net_in + 4].transpose(0, 2, 1)
    table = table_sum.reshape(GROUP, tasks // GROUP, LANES).transpose(1, 0, 2).reshape(tasks, LANES)
    return (
        table[0, LANES - 1],
        table[:, 0:task_width],
        0.3 * enc_rows[:, 0:enc_in].T,
        0.3 * enc_rows[:, 2 * LANES - 2],
        0.3 * enc_rows[:, 2 * LANES - 1],
        0.3 * s_enc_second,
        sums[:, :, 0:net_in].transpose(0, 2, 1),
        sums[:, :, first_end : first_end + hidden].transpose(0, 2, 1),
        vectors[:, 0::2],
        vectors[:, 1::2],
        net_sum[:, first_end + hidden :],
        head_sum[:, :, first_end + hidden : first_end + hidden + bins],
    )


def solution(mesh):
    both = ("section", "batch")
    return jax.shard_map(
        on_device,
        mesh=mesh,
        in_specs=(
            P("batch", None),
            P(None, "batch", None),
            P(None, "batch", None),
            P("batch"),
            P("batch"),
            P(None, "batch"),
            P(None, "batch"),
        )
        + (P(),) * 11,
        out_specs=(
            P(),
            P(),
            P(None, both),
            P(both),
            P(both),
            P(both, None),
            P(None, None, both),
            P(None, None, both),
            P(None, None, both),
            P(None, None, both),
            P(both, None),
            P(None, both, None),
        ),
        check_vma=False,
    )
```

```python
import functools

import jax
import jax.numpy as jnp
from jax import lax
from jax.experimental import pallas as pl
from jax.experimental.pallas import tpu as pltpu
from jax.sharding import PartitionSpec as P

CORES = 2
LANES = 128
GROUP = 16
BF16 = jnp.bfloat16
F32 = jnp.float32
VMEM_A = 18
VMEM_B = 20
VMEM_SUM = 6
VMEM_C = 20


def nn(left, right):
    return lax.dot_general(left, right, (((1,), (0,)), ((), ())), preferred_element_type=F32)


def nt(left, right):
    return lax.dot_general(left, right, (((1,), (1,)), ((), ())), preferred_element_type=F32)


def tn(left, right):
    return lax.dot_general(left, right, (((0,), (0,)), ((), ())), preferred_element_type=F32)


def column_sum(value):
    grouped = value.reshape(value.shape[0] // 8, 8, value.shape[1])
    return jnp.sum(jnp.sum(grouped, axis=0), axis=0, keepdims=True)


def slabs(features, size=64):
    return [slice(start, start + size) for start in range(0, features, size)]


def lanes_of(step):
    return slice(step * LANES, (step + 1) * LANES)


def spread_columns(gain_rows, shift_rows, rows_ref, spread_ref):
    count = gain_rows.shape[0]
    rows_ref[...] = jnp.zeros_like(rows_ref)
    rows_ref[0:count, :] = gain_rows
    rows_ref[count : 2 * count, :] = shift_rows
    turned = jnp.transpose(rows_ref[...])
    for place in range(2 * count):
        spread_ref[place] = jnp.broadcast_to(turned[:, place : place + 1], spread_ref.shape[1:])


def mish_forward(pre_ref, pre_at, gain_ref, shift_ref, hid_ref, hat_ref, slope_ref, scale_ref, scale_row, at):
    features = pre_ref.shape[0]
    row_mean = column_sum(pre_ref[:, pre_at]) * (1.0 / features)
    centred = pre_ref[:, pre_at] - row_mean
    spread = column_sum(centred * centred) * (1.0 / features)
    scale = lax.rsqrt(spread + 1e-05)
    scale_ref[scale_row : scale_row + 1, at] = scale
    for part in slabs(features):
        hat = (pre_ref[part, pre_at] - row_mean) * scale
        normed = hat * gain_ref[part, :] + shift_ref[part, :]
        power = jnp.exp(normed)
        top = power * (power + 2.0)
        inverse = pl.reciprocal(top + 2.0, approx=True)
        ratio = top * inverse
        hid_ref[part, at] = (normed * ratio).astype(BF16)
        tilt = power * inverse
        slope = ratio + normed * (4.0 * (tilt * (tilt + inverse)))
        slope_ref[part, at] = (slope * gain_ref[part, :]).astype(BF16)
        hat_ref[part, at] = hat.astype(BF16)


def mish_backward(grad_ref, grad_at, hat_ref, slope_ref, scale_ref, scale_row, at, sums_ref, sums_at, first, out_ref):
    features = grad_ref.shape[0]
    total_one = jnp.zeros((8, LANES), F32)
    total_two = jnp.zeros((8, LANES), F32)
    for part in slabs(features):
        term = grad_ref[part, grad_at] * slope_ref[part, at].astype(F32)
        grad_ref[part, grad_at] = term
        crossed = term * hat_ref[part, at].astype(F32)
        groups = (term.shape[0] // 8, 8, LANES)
        total_one = total_one + jnp.sum(term.reshape(groups), axis=0)
        total_two = total_two + jnp.sum(crossed.reshape(groups), axis=0)
        if first:
            sums_ref[sums_at, part, :] = term
            sums_ref[sums_at + 1, part, :] = crossed
        else:
            sums_ref[sums_at, part, :] += term
            sums_ref[sums_at + 1, part, :] += crossed
    mean_one = jnp.sum(total_one, axis=0, keepdims=True) * (1.0 / features)
    mean_two = jnp.sum(total_two, axis=0, keepdims=True) * (1.0 / features)
    scale = scale_ref[scale_row : scale_row + 1, at]
    for part in slabs(features):
        rest = grad_ref[part, grad_at] - mean_one - hat_ref[part, at].astype(F32) * mean_two
        out_ref[part, at] = (rest * scale).astype(BF16)


def mish_forward_low(pre_ref, gain_ref, shift_ref, hid_ref, hat_ref, slope_ref, scale_ref, scale_row, at):
    features = pre_ref.shape[0]
    row_mean = column_sum(pre_ref[:, at]) * (1.0 / features)
    centred = pre_ref[:, at] - row_mean
    spread = column_sum(centred * centred) * (1.0 / features)
    scale = lax.rsqrt(spread + 1e-05)
    scale_ref[scale_row : scale_row + 1, at] = scale
    for part in slabs(features):
        hat = (pre_ref[part, at] - row_mean) * scale
        normed = (hat * gain_ref[part, :] + shift_ref[part, :]).astype(BF16)
        hat_ref[part, at] = hat.astype(BF16)
        power = jnp.exp(normed)
        top = power * (power + 2.0)
        inverse = pl.reciprocal(top + 2.0, approx=True)
        ratio = top * inverse
        hid_ref[part, at] = normed * ratio
        tilt = power * inverse
        slope = ratio + (4.0 * normed) * (tilt * (tilt + inverse))
        slope_ref[part, at] = slope * gain_ref[part, :].astype(BF16)


def mish_backward_low(grad_ref, hat_ref, slope_ref, scale_ref, scale_row, steps, sums_ref, sums_at, out_ref):
    features = grad_ref.shape[0]
    rows = []
    for step in range(steps):
        at = lanes_of(step)
        total_one = jnp.zeros((16, LANES), F32)
        total_two = jnp.zeros((16, LANES), F32)
        for part in slabs(features):
            term = grad_ref[part, at] * slope_ref[part, at]
            crossed = term * hat_ref[part, at]
            grad_ref[part, at] = term
            groups = (term.shape[0] // 16, 16, LANES)
            term = term.reshape(groups)
            crossed = crossed.reshape(groups)
            total_one = total_one + functools.reduce(jnp.add, [term[k] for k in range(groups[0])]).astype(F32)
            total_two = total_two + functools.reduce(jnp.add, [crossed[k] for k in range(groups[0])]).astype(F32)
        scale = scale_ref[scale_row : scale_row + 1, at]
        mean_one = jnp.sum(total_one, axis=0, keepdims=True) * (1.0 / features)
        mean_two = jnp.sum(total_two, axis=0, keepdims=True) * (1.0 / features)
        rows.append((mean_one.astype(BF16), mean_two.astype(BF16), scale.astype(BF16)))
    for part in slabs(features):
        sum_one, sum_two = None, None
        for step, (mean_one, mean_two, scale) in enumerate(rows):
            at = lanes_of(step)
            term = grad_ref[part, at]
            hat = hat_ref[part, at]
            out_ref[part, at] = (term - mean_one - hat * mean_two) * scale
            crossed = term * hat
            sum_one = term if sum_one is None else sum_one + term
            sum_two = crossed if sum_two is None else sum_two + crossed
        sums_ref[sums_at, part, :] = sum_one.astype(F32)
        sums_ref[sums_at + 1, part, :] = sum_two.astype(F32)


def simplex(values):
    grouped = values.reshape(values.shape[0] // 8, 8, values.shape[1])
    powers = jnp.exp(grouped - jnp.max(grouped, axis=1, keepdims=True))
    shares = powers / jnp.sum(powers, axis=1, keepdims=True)
    return shares.reshape(values.shape)


def simplex_back(shares, grads):
    grouped = (shares.shape[0] // 8, 8, shares.shape[1])
    crossed = jnp.sum((shares * grads).reshape(grouped), axis=1, keepdims=True)
    return (shares.reshape(grouped) * (grads.reshape(grouped) - crossed)).reshape(shares.shape)


def row_weight(step, steps, scale, horizon_row, place_ref):
    lane = lax.broadcasted_iota(jnp.int32, (1, LANES), 1)
    mine = (lane >= place_ref[2]) & (lane < place_ref[3]) & (horizon_row > step)
    return jnp.where(mine, F32(scale * 0.5 ** (step / (steps - 1))), 0.0)


def padded_rows(value, rows):
    zeros = jnp.zeros((rows - value.shape[0], value.shape[1]), F32)
    return jnp.concatenate([value.astype(F32), zeros], axis=0).astype(BF16)


def transpose_into(out_ref, source_ref, rows):
    for start in range(0, rows, LANES):
        out_ref[:, start : start + LANES] = jnp.transpose(source_ref[start : start + LANES, :])


def vector_sums(sums_ref, gains_ref, layers):
    vectors = []
    for layer in range(layers):
        inverse = 1.0 / gains_ref[layer]
        vectors.append(jnp.sum(sums_ref[2 * layer + 1] * inverse, axis=1, keepdims=True))
        vectors.append(jnp.sum(sums_ref[2 * layer] * inverse, axis=1, keepdims=True))
    return vectors


def own_lanes(place_ref):
    return pl.ds(pl.multiple_of(place_ref[1] * LANES, LANES), LANES)


def load_all(copies):
    made = [pltpu.make_async_copy(*each) for each in copies]
    for each in made:
        each.start()
    return made


def with_vectors(value, vectors, first_lane):
    lane = lax.broadcasted_iota(jnp.int32, value.shape, 1)
    for place, vector in enumerate(vectors):
        value = jnp.where(lane == first_lane + place, vector, value)
    return value


def forward_kernel(
    steps,
    place_ref, obs_hbm, act_hbm, ids_hbm, table_hbm, e1_hbm, eg_hbm, es_hbm, e2_hbm, g_hbm, s_hbm,
    w1_hbm, w2_hbm, dyn_hbm,
    xt_ref, soft_ref, h1_ref, hat1_ref, slope1_ref, h2_ref, hat2_ref, slope2_ref, scale_ref,
    ein_ref, eh_ref, ehat_ref, eslope_ref, escale_ref,
    w1_ref, w2_ref, dyn_ref, x_ref, next1_ref, next2_ref,
    rows_ref, spread_ref, erows_ref, espread_ref, wide_ref, tall_ref, e1p_ref, w1t_ref, w2t_ref, dynt_ref, pre_ref, epre_ref,
    obs_ref, act_ref, ids_ref, table_ref, e1_ref, eg_ref, es_ref, e2_ref, g_ref, s_ref,
    sems, early_sems,
):
    early = load_all([
        (table_hbm, table_ref, early_sems.at[0]),
        (ids_hbm, ids_ref, early_sems.at[1]),
        (obs_hbm, obs_ref, early_sems.at[2]),
        (e1_hbm, e1_ref, early_sems.at[3]),
        (eg_hbm, eg_ref, early_sems.at[4]),
        (es_hbm, es_ref, early_sems.at[5]),
        (e2_hbm, e2_ref, early_sems.at[6]),
        (act_hbm, act_ref, early_sems.at[7]),
        (g_hbm, g_ref, early_sems.at[8]),
        (s_hbm, s_ref, early_sems.at[9]),
    ])
    first, second, third, fourth, fifth = load_all([
        (w1_hbm.at[0], w1_ref, sems.at[0]),
        (w2_hbm.at[0], w2_ref, sems.at[1]),
        (dyn_hbm, dyn_ref, sems.at[2]),
        (w1_hbm.at[1], next1_ref, sems.at[3]),
        (w2_hbm.at[1], next2_ref, sems.at[4]),
    ])
    latent = dyn_ref.shape[1]
    tasks, task_width = table_ref.shape
    observed = obs_ref.shape[0]
    acted = act_ref.shape[1]
    mine = own_lanes(place_ref)
    for each in early:
        each.wait()
    spread_columns(eg_ref[...], es_ref[...], erows_ref, espread_ref)
    kinds = lax.broadcasted_iota(jnp.int32, (tasks, LANES), 0)
    onehot = (kinds == ids_ref[:, mine]).astype(F32).astype(BF16)
    wide_ref[...] = jnp.zeros_like(wide_ref)
    wide_ref[:, 0:task_width] = table_ref[...].astype(F32)
    table_tail = pltpu.roll(wide_ref[:, 0:LANES], acted, 1).astype(BF16)
    table_enc = pltpu.roll(wide_ref[...], observed, 1).astype(BF16)
    aux = tn(table_tail, onehot)
    tall_ref[...] = jnp.zeros_like(tall_ref)
    tall_ref[0:observed, :] = obs_ref[:, mine].astype(F32)
    ein = tn(table_enc, onehot)
    ein_ref[0:LANES, :] = (ein[0:LANES] + tall_ref[...]).astype(BF16)
    ein_ref[LANES:, :] = ein[LANES:].astype(BF16)
    e1p_ref[...] = padded_rows(e1_ref[...], e1p_ref.shape[0])
    epre_ref[...] = tn(e1p_ref[...], ein_ref[...])
    here = slice(0, LANES)
    mish_forward(epre_ref, here, espread_ref.at[0], espread_ref.at[1], eh_ref, ehat_ref, eslope_ref, escale_ref, 0, here)
    shares = simplex(tn(e2_ref[...], eh_ref[...]))
    soft_ref[:, 0:LANES] = shares
    xt_ref[0:latent, 0:LANES] = shares.astype(BF16)
    spread_columns(g_ref[0], s_ref[0], rows_ref, spread_ref)
    for step in range(steps):
        tall_ref[...] = jnp.zeros_like(tall_ref)
        tall_ref[0:acted, :] = act_ref[step, :, mine].astype(F32)
        xt_ref[latent:, lanes_of(step)] = (aux + tall_ref[...]).astype(BF16)
    first.wait()
    transpose_into(w1t_ref, w1_ref, latent)
    w1t_ref[:, latent:] = jnp.transpose(padded_rows(w1_ref[latent:, :], LANES))
    second.wait()
    transpose_into(w2t_ref, w2_ref, latent)
    third.wait()
    transpose_into(dynt_ref, dyn_ref, latent)
    for step in range(steps):
        at = lanes_of(step)
        pre_ref[...] = nn(w1t_ref[...], xt_ref[:, at])
        mish_forward(pre_ref, here, spread_ref.at[0], spread_ref.at[2], h1_ref, hat1_ref, slope1_ref, scale_ref, 0, at)
        pre_ref[...] = nn(w2t_ref[...], h1_ref[:, at])
        mish_forward(pre_ref, here, spread_ref.at[1], spread_ref.at[3], h2_ref, hat2_ref, slope2_ref, scale_ref, 1, at)
        shares = simplex(nn(dynt_ref[...], h2_ref[:, at]))
        soft_ref[:, lanes_of(step + 1)] = shares
        if step + 1 < steps:
            xt_ref[0:latent, lanes_of(step + 1)] = shares.astype(BF16)
    for step in range(steps):
        for start in range(0, latent + LANES, LANES):
            x_ref[lanes_of(step), start : start + LANES] = jnp.transpose(xt_ref[start : start + LANES, lanes_of(step)])
    fourth.wait()
    fifth.wait()


def heads_kernel(steps, scale, packs, head, ahead, heads, bins, chained, after, *refs):
    refs = list(refs)
    place_ref, xt_ref, x_ref, w1_ref, w2_ref, ho_ref, g_ref, s_ref, rb_ref, vb_ref, hz_ref = refs[:11]
    refs = refs[11:]
    before_ref = refs.pop(0) if chained else None
    refs = refs[after:]
    w1_hbm, w2_hbm = refs[:2] if ahead else (None, None)
    refs = refs[2:] if ahead else refs
    pack_refs, refs = refs[: 2 * len(packs)], refs[2 * len(packs) :]
    dx_ref, loss_ref = refs[:2]
    refs = refs[2:]
    copies = []
    if ahead:
        next1_ref, next2_ref, sems = refs[0], refs[1], refs[-1]
        refs = refs[2:-1]
        copies = load_all([
            (w1_hbm.at[head + 2], next1_ref, sems.at[0]),
            (w2_hbm.at[head + 2], next2_ref, sems.at[1]),
        ])
    (rows_ref, spread_ref, tail_ref, hop_ref, hot_ref, pre_ref, lg_ref, h1_ref, hat1_ref, slope1_ref,
     h2_ref, hat2_ref, slope2_ref, scale_ref, sums_ref, dh_ref, d2_ref, d1_ref, dl_ref, grad_ref) = refs
    latent = w2_ref.shape[0]
    tail_rows = w1_ref.shape[0] - latent
    mine = own_lanes(place_ref)
    horizon_row = hz_ref[:, mine]
    bin_ids = lax.broadcasted_iota(jnp.int32, (LANES, LANES), 0)
    first_end = latent + LANES
    losses = []
    spread_columns(g_ref[head + 1], s_ref[head + 1], rows_ref, spread_ref)
    tail_ref[...] = padded_rows(w1_ref[latent:, :], LANES)
    hot_ref[...] = padded_rows(ho_ref[head], LANES)
    hop_ref[...] = jnp.transpose(hot_ref[...])
    gain1, gain2, shift1, shift2 = [spread_ref.at[place] for place in range(4)]
    pre_ref[...] = tn(w1_ref[0:latent, :], xt_ref[0:latent, :]) + tn(tail_ref[...], xt_ref[latent:, :])
    for step in range(steps):
        mish_forward_low(pre_ref, gain1, shift1, h1_ref, hat1_ref, slope1_ref, scale_ref, 0, lanes_of(step))
    pre_ref[...] = tn(w2_ref[...], h1_ref[...])
    for step in range(steps):
        mish_forward_low(pre_ref, gain2, shift2, h2_ref, hat2_ref, slope2_ref, scale_ref, 1, lanes_of(step))
    lg_ref[...] = nn(hot_ref[...], h2_ref[...])
    share = 0.1 if head == 0 else 0.1 / (heads - 1)
    bins_ref = rb_ref if head == 0 else vb_ref
    for step in range(steps):
        at = lanes_of(step)
        logits = jnp.where(bin_ids < bins, lg_ref[:, at], F32(-1e30))
        chosen = bin_ids == bins_ref[step : step + 1, mine]
        top = jnp.max(logits, axis=0, keepdims=True)
        powers = jnp.exp(logits - top)
        total = column_sum(powers)
        picked = column_sum(jnp.where(chosen, logits, 0.0))
        weight = row_weight(step, steps, scale * share, horizon_row, place_ref)
        losses.append(weight * (jnp.log(total) + top - picked))
        dl_ref[:, at] = (powers * (weight / total) - jnp.where(chosen, weight, 0.0)).astype(BF16)
    dh_ref[...] = nn(hop_ref[...], dl_ref[...]).astype(BF16)
    grad_ref[:, first_end + latent :] = nt(h2_ref[...], dl_ref[...]).astype(BF16)
    mish_backward_low(dh_ref, hat2_ref, slope2_ref, scale_ref, 1, steps, sums_ref, 2, d2_ref)
    dh_ref[...] = nn(w2_ref[...], d2_ref[...]).astype(BF16)
    grad_ref[:, first_end : first_end + latent] = nt(d2_ref[...], h1_ref[...]).astype(BF16)
    mish_backward_low(dh_ref, hat1_ref, slope1_ref, scale_ref, 0, steps, sums_ref, 0, d1_ref)
    low_part = nn(w1_ref[0:latent, :], d1_ref[...])
    side_part = nn(tail_ref[...], d1_ref[...])
    if not chained:
        dx_ref[0:latent, :] = low_part
        dx_ref[latent:, :] = side_part
    else:
        dx_ref[0:latent, :] = before_ref[0:latent, :] + low_part
        dx_ref[latent:, :] = before_ref[latent:, :] + side_part
    grad_ref[:, 0:latent] = nn(d1_ref[...], x_ref[:, 0:latent]).astype(BF16)
    side_terms = nn(d1_ref[...], x_ref[:, latent:])
    side_terms = with_vectors(side_terms, vector_sums(sums_ref, spread_ref, 2), tail_rows)
    grad_ref[:, latent:first_end] = side_terms.astype(BF16)
    for place, (slots, first, units) in enumerate(packs):
        for relative, (which, slot) in enumerate(slots):
            start = pl.multiple_of((place_ref[0] ^ relative) * GROUP, GROUP)
            out_ref = pack_refs[2 * place + which]
            if not units:
                out_ref[slot] = grad_ref[pl.ds(start, GROUP), :]
                continue
            block = grad_ref[pl.ds(start, GROUP), first * LANES : (first + units) * LANES]
            for unit in range(units):
                out_ref[slot * units + unit] = block[:, unit * LANES : (unit + 1) * LANES]
    loss_ref[...] = functools.reduce(jnp.add, losses)
    for each in copies:
        each.wait()


def backward_kernel(
    steps, scale, order, losses, after,
    place_ref, xt_ref, soft_ref, h1_ref, hat1_ref, slope1_ref, h2_ref, hat2_ref, slope2_ref, scale_ref,
    w1_ref, w2_ref, dyn_ref, hz_ref, g_ref, dx_ref, *rest,
):
    initial = order[0] == steps - 1
    final = order[-1] == 0
    loss_refs, rest = rest[:losses], rest[losses:]
    held_refs, rest = ((), rest) if initial else (rest[:4], rest[4:])
    (tgt_hbm, low_ref, first_ref, side_ref, loss_ref, sums_ref, tgt_ref, rows_ref, spread_ref, tail_ref, pre_ref,
     d1_ref, d2_ref, do_ref, grad_ref, sems) = rest[after:]
    mine = own_lanes(place_ref)
    loads = dict(zip(order, load_all([(tgt_hbm.at[step, mine, :], tgt_ref.at[step], sems.at[step]) for step in order])))
    latent = dyn_ref.shape[1]
    here = slice(0, LANES)
    horizon_row = hz_ref[:, mine]
    spread_columns(g_ref[0], g_ref[0], rows_ref, spread_ref)
    tail_rows = w1_ref.shape[0] - latent
    tail_ref[...] = padded_rows(w1_ref[latent:, :], LANES)
    first_end = latent + LANES
    second_end = first_end + latent
    if initial:
        loss = functools.reduce(jnp.add, [each[...] for each in loss_refs])
        side = jnp.zeros((LANES, LANES), F32)
        incoming = None
    else:
        before_ref, given_ref, given_side_ref, given_sums_ref = held_refs
        loss = loss_refs[0][...]
        side = given_side_ref[...]
        incoming = given_ref[...].astype(F32)
        sums_ref[...] = given_sums_ref[...]
    pending = []

    def add_terms(at, fresh, last):
        terms = (
            (slice(0, first_end), nt(d1_ref[:, at], xt_ref[:, at])),
            (slice(first_end, second_end), nt(d2_ref[:, at], h1_ref[:, at])),
            (slice(second_end, second_end + latent), nt(h2_ref[:, at], do_ref[:, at])),
        )
        for lanes, term in terms:
            if not fresh:
                term = term + grad_ref[:, lanes]
            elif not initial:
                term = term + before_ref[:, lanes]
            out_ref = low_ref if last else grad_ref
            if last and final and lanes.start == 0:
                out_ref[:, 0:latent] = term[:, 0:latent].astype(out_ref.dtype)
                vectors = vector_sums(sums_ref, spread_ref, 2)
                out_ref[:, latent:first_end] = with_vectors(term[:, latent:], vectors, tail_rows).astype(out_ref.dtype)
            else:
                out_ref[:, lanes] = term.astype(out_ref.dtype)

    for step in order:
        at = lanes_of(step)
        weight = row_weight(step, steps, scale, horizon_row, place_ref)
        shares = soft_ref[:, lanes_of(step + 1)]
        loads[step].wait()
        residue = shares - jnp.transpose(tgt_ref[step].astype(F32))
        loss = loss + (20.0 / latent) * weight * column_sum(residue * residue)
        grads = residue * ((40.0 / latent) * weight)
        if incoming is not None:
            grads = grads + incoming
        do_ref[:, at] = simplex_back(shares, grads).astype(BF16)
        pre_ref[...] = nn(dyn_ref[...], do_ref[:, at])
        mish_backward(pre_ref, here, hat2_ref, slope2_ref, scale_ref, 1, at, sums_ref, 2, step == steps - 1, d2_ref)
        pre_ref[...] = nn(w2_ref[...], d2_ref[:, at])
        mish_backward(pre_ref, here, hat1_ref, slope1_ref, scale_ref, 0, at, sums_ref, 0, step == steps - 1, d1_ref)
        incoming = nn(w1_ref[0:latent, :], d1_ref[:, at]) + dx_ref[0:latent, at]
        side = side + nn(tail_ref[...], d1_ref[:, at]) + dx_ref[latent:, at]
        incoming = incoming.astype(BF16).astype(F32)
        pending.append(step)
        if len(pending) == 2 or step == order[-1]:
            low, high = min(pending), max(pending) + 1
            add_terms(slice(low * LANES, high * LANES), high == order[0] + 1, low == order[-1])
            pending = []

    first_ref[...] = incoming.astype(BF16)
    side_ref[...] = side
    loss_ref[...] = loss


def ending_kernel(
    slots, tasks, task_width, acted, observed, after,
    place_ref, low_ref, first_ref, side_ref, loss_ref, soft_ref, ein_ref, eh_ref, ehat_ref, eslope_ref, escale_ref,
    ids_ref, e1_ref, eg_ref, e2_ref, *rest,
):
    out_refs, rest = rest[after : after + 4], rest[after + 4 :]
    erows_ref, espread_ref, e1p_ref, epre_ref, esums_ref, ed_ref, egrad_ref = rest
    mine = own_lanes(place_ref)
    here = slice(0, LANES)
    latent = first_ref.shape[0]
    spread_columns(eg_ref[...], eg_ref[...], erows_ref, espread_ref)
    e1p_ref[...] = padded_rows(e1_ref[...], e1p_ref.shape[0])
    d_enc = simplex_back(soft_ref[:, 0:LANES], first_ref[...].astype(F32)).astype(BF16)
    epre_ref[...] = nn(e2_ref[...], d_enc)
    mish_backward(epre_ref, here, ehat_ref, eslope_ref, escale_ref, 0, here, esums_ref, 0, True, ed_ref)
    side_enc = nn(e1p_ref[...], ed_ref[...])
    enc_width = epre_ref.shape[0]
    half = GROUP // 2
    groups = enc_width // half
    kept = egrad_ref.shape[2]
    enc_second = nt(eh_ref[...], d_enc)
    egrad_ref[:, 0:half, :] = enc_second[:, 0:kept].reshape(groups, half, kept)
    egrad_ref[:, half:, 0 : latent - kept] = enc_second[:, kept:].reshape(groups, half, latent - kept)
    enc_first = nt(ed_ref[...], ein_ref[...])
    egrad_ref[:, half:, latent - kept : kept - LANES] = enc_first[:, 0:LANES].reshape(groups, half, LANES)
    second_lanes = with_vectors(enc_first[:, LANES : 2 * LANES], vector_sums(esums_ref, espread_ref, 1), LANES - 2)
    egrad_ref[:, half:, kept - LANES :] = second_lanes.reshape(groups, half, LANES)

    kinds = lax.broadcasted_iota(jnp.int32, (tasks, LANES), 0)
    onehot = (kinds == ids_ref[:, mine]).astype(F32)
    over_lanes = (((1,), (1,)), ((), ()))
    highest = lax.Precision.HIGHEST
    side_terms = lax.dot_general(onehot, side_ref[...], over_lanes, precision=highest, preferred_element_type=F32)
    enc_terms = lax.dot_general(onehot, side_enc, over_lanes, precision=highest, preferred_element_type=F32)
    table = pltpu.roll(side_terms, LANES - acted, 1)
    table = table + pltpu.roll(enc_terms, enc_terms.shape[1] - observed, 1)[:, 0:LANES]
    lane = lax.broadcasted_iota(jnp.int32, table.shape, 1)
    table = jnp.where(lane < task_width, table, 0.0)
    table = jnp.where((lane == LANES - 1) & (kinds == 0), jnp.sum(loss_ref[...], axis=1, keepdims=True), table)
    table_rows = [table[start : start + GROUP] for start in range(0, tasks, GROUP)]
    table_block = jnp.concatenate(table_rows, axis=1).astype(BF16)
    count = low_ref.shape[1] // LANES
    units = (count + kept // LANES) // 2
    for half_no in range(2):
        for relative, (which, slot) in enumerate(slots[half_no]):
            dest = place_ref[0] ^ relative
            start = pl.multiple_of(dest * GROUP, GROUP)
            out_ref = out_refs[2 * half_no + which]
            ending = count if half_no else units
            block = low_ref[pl.ds(start, GROUP), half_no * units * LANES : ending * LANES]
            if half_no:
                block = jnp.concatenate([block, egrad_ref[dest].astype(BF16)], axis=1)
            for unit in range(units):
                out_ref[slot * units + unit] = block[:, unit * LANES : (unit + 1) * LANES]
    last = len(slots[0]) // 2 * units
    for unit in range(tasks // GROUP):
        for out_ref in out_refs[0:2]:
            out_ref[last + unit] = table_block[:, unit * LANES : (unit + 1) * LANES]


def final_kernel(tasks, task_width, enc_in, bins, net_in, *refs):
    outs = refs[-12:]
    (loss_ref, table_ref, e1_ref, eg_ref, es_ref, e2_ref, first_ref, second_ref, gain_ref, shift_ref, dyn_ref, head_ref) = outs
    refs = refs[:-12]
    tail_refs, refs = refs[:2], refs[2:]
    latent = second_ref.shape[2]
    first_end = latent + LANES
    second_end = first_end + latent

    def put_net(net, value):
        first_ref[net] = value[:, 0:net_in]
        second_ref[net] = value[:, first_end:second_end]
        turned = jnp.transpose(value[:, latent:first_end])
        for layer in range(2):
            row = net_in - latent + 2 * layer
            gain_ref[net, layer : layer + 1, :] = turned[row : row + 1, :]
            shift_ref[net, layer : layer + 1, :] = turned[row + 1 : row + 2, :]

    sums = functools.reduce(jnp.add, [ref[...].astype(F32) for ref in tail_refs])
    units = sums.shape[0] - tasks // GROUP
    tail = jnp.concatenate([sums[unit] for unit in range(units)], axis=1)
    put_net(0, tail)
    dyn_ref[...] = tail[:, second_end : second_end + latent]
    enc = tail[:, second_end + latent :]
    half = GROUP // 2
    kept = enc.shape[1]
    e2_ref[:, 0:kept] = 0.3 * enc[0:half, :]
    e2_ref[:, kept:] = 0.3 * enc[half:, 0 : latent - kept]
    e1_ref[...] = 0.3 * enc[half:, latent - kept : latent - kept + enc_in]
    turned = 0.3 * jnp.transpose(enc[half:, kept - LANES :])
    eg_ref[...] = turned[LANES - 2 : LANES - 1, :]
    es_ref[...] = turned[LANES - 1 : LANES, :]
    loss_ref[...] = sums[units, 0:1, LANES - 1 : LANES]
    for place in range(tasks // GROUP):
        table_ref[place * GROUP : (place + 1) * GROUP, :] = sums[units + place, :, 0:task_width]
    net = 1
    def put_head(value):
        put_net(net, value)
        head_ref[net - 1] = value[:, second_end : second_end + bins]

    one_ref, other_ref, last_one_ref, last_other_ref = refs
    for one in range(one_ref.shape[1]):
        put_head(one_ref[0, one].astype(F32) + other_ref[0, one].astype(F32))
        net += 1
    sums = last_one_ref[...].astype(F32) + last_other_ref[...].astype(F32)
    units = (second_end + LANES) // LANES
    for start in range(0, sums.shape[0], units):
        put_head(jnp.concatenate([sums[start + unit] for unit in range(units)], axis=1))
        net += 1


def swap(value, axis, distance):
    count = lax.axis_size(axis)
    return lax.ppermute(value, axis, [(place, place ^ distance) for place in range(count)])


def exchange(parts, axis, scale):
    total = parts[0].astype(F32)
    for distance in range(1, len(parts)):
        total = total + swap(parts[distance], axis, distance * scale).astype(F32)
    return total


def scatter_plain(packed, chips, sections):
    held = packed.reshape((sections, chips, CORES) + packed.shape[1:])
    batch_no = lax.axis_index("batch")
    places = (
        ("batch", 1, CORES, 2, batch_no % CORES),
        ("batch", CORES, chips, 1, batch_no // CORES),
        ("section", 1, sections, 0, lax.axis_index("section")),
    )
    for axis, scale, count, dim, mine in places:
        parts = [lax.dynamic_index_in_dim(held, mine ^ other, dim, keepdims=False) for other in range(count)]
        held = exchange(parts, axis, scale)
        held = held.astype(BF16) if dim else held
    return held


def on_device(
    observations,
    actions,
    targets,
    task_ids,
    horizons,
    reward_bins,
    value_bins,
    task_table,
    enc_first,
    enc_gain,
    enc_shift,
    enc_second,
    net_first,
    net_second,
    net_gain,
    net_shift,
    dyn_out,
    head_out,
):
    sections = lax.axis_size("section")
    batches = lax.axis_size("batch")
    section_no = lax.axis_index("section")
    chips = batches // CORES
    devices = sections * batches
    steps, rows_all, acted = actions.shape
    observed = observations.shape[1]
    rows = rows_all // sections
    latent = dyn_out.shape[1]
    hidden = dyn_out.shape[0]
    tasks, task_width = task_table.shape
    heads, _, bins = head_out.shape
    nets, net_in, _ = net_first.shape
    enc_in, enc_width = enc_first.shape
    wide = steps * LANES
    scale = 1.0 / (rows_all * batches * steps)
    groups = hidden // GROUP
    in_place = hidden // devices == GROUP
    start = section_no * rows
    block_no = start // LANES
    first_lane = start - block_no * LANES
    me = section_no * batches + lax.axis_index("batch") if in_place else jnp.int32(0)
    place = jnp.stack([me, block_no, first_lane, first_lane + rows]).astype(jnp.int32)
    bits = [("batch", 1 << bit) for bit in range(batches.bit_length() - 1)]
    bits += [("section", 1 << bit) for bit in range(sections.bit_length() - 1)]

    def slots_of(order):
        if not in_place:
            return tuple((relative // (groups // 2), relative % (groups // 2)) for relative in range(groups))
        found = []
        for relative in range(groups):
            slot = 0
            for bit in order:
                slot = 2 * slot + (relative >> bit & 1)
            found.append((slot // (groups // 2), slot % (groups // 2)))
        return tuple(found)

    plain = tuple(range(len(bits)))
    y_first = (0, 2, 1) + tuple(range(3, len(bits))) if in_place else plain
    half_slots = groups // 2
    shape_of = jax.ShapeDtypeStruct
    smem = pl.BlockSpec(memory_space=pltpu.SMEM)
    local = pl.BlockSpec(memory_space=pltpu.VMEM)
    far = pl.BlockSpec(memory_space=pltpu.HBM)
    anywhere = pl.BlockSpec(memory_space=pl.ANY)
    first_far, second_far, dyn_far, targets_far = [
        pltpu.with_memory_space_constraint(array, pltpu.HBM) for array in (net_first, net_second, dyn_out, targets)
    ]
    vmem = pltpu.VMEM
    dmas = pltpu.SemaphoreType.DMA

    def params(mebibytes):
        return pltpu.CompilerParams(vmem_limit_bytes=mebibytes * 1024 * 1024)

    def cost(flops, moved):
        return pl.CostEstimate(flops=flops, bytes_accessed=moved, transcendentals=0)

    ids_row = task_ids.reshape(1, rows_all)
    horizon_row = horizons.reshape(1, rows_all)
    eg_row = enc_gain.reshape(1, enc_width)
    es_row = enc_shift.reshape(1, enc_width)
    head_turned = head_out.transpose(0, 2, 1)
    low = lambda lanes: shape_of((hidden, lanes), BF16)
    forward_shapes = (
        shape_of((latent + LANES, wide), BF16),
        shape_of((latent, wide + LANES), F32),
        low(wide), low(wide), low(wide), low(wide), low(wide), low(wide),
        shape_of((8, wide), F32),
        shape_of((2 * LANES, LANES), BF16),
        shape_of((enc_width, LANES), BF16),
        shape_of((enc_width, LANES), BF16),
        shape_of((enc_width, LANES), BF16),
        shape_of((8, LANES), F32),
        shape_of((net_in, hidden), BF16),
        shape_of((hidden, hidden), BF16),
        shape_of((hidden, latent), BF16),
        shape_of((wide, latent + LANES), BF16),
    )

    weight_shapes = (shape_of((net_in, hidden), BF16), shape_of((hidden, hidden), BF16))

    early = [
        pltpu.with_memory_space_constraint(array, pltpu.HBM)
        for array in (
            observations.T, actions.transpose(0, 2, 1), ids_row, task_table, enc_first, eg_row, es_row, enc_second,
            net_gain, net_shift,
        )
    ]
    made = pl.pallas_call(
        functools.partial(forward_kernel, steps),
        out_shape=forward_shapes + weight_shapes,
        in_specs=[smem] + [far] * 13,
        out_specs=[local] * (len(forward_shapes) + 2),
        scratch_shapes=[
            vmem((8, hidden), F32),
            vmem((4, hidden, LANES), F32),
            vmem((8, enc_width), F32),
            vmem((2, enc_width, LANES), F32),
            vmem((tasks, 2 * LANES), F32),
            vmem((LANES, LANES), F32),
            vmem((2 * LANES, enc_width), BF16),
            vmem((hidden, latent + LANES), BF16),
            vmem((hidden, hidden), BF16),
            vmem((latent, hidden), BF16),
            vmem((hidden, LANES), F32),
            vmem((enc_width, LANES), F32),
            *[vmem(each.shape, each.dtype) for each in early],
            dmas((5,)),
            dmas((len(early),)),
        ],
        compiler_params=params(VMEM_A),
        cost_estimate=cost(10_000_000_000, 8_000_000),
        name="forward_chain",
    )(
        place, *early, first_far, second_far, dyn_far,
    )
    saved, x_rows, weights = made[:-3], made[-3], made[-2:]
    xt = saved[0]
    head_width = latent + LANES + hidden + LANES

    def run_head(head, ahead, weights, before, after):
        all_units = head_width // LANES
        packs = [(slots_of(plain), 0, 0)]
        if in_place and head == heads - 2:
            packs = [(slots_of(plain), 0, all_units)]
        if in_place and head == heads - 1:
            packs = [(slots_of(plain), 0, all_units // 2), (slots_of(y_first), all_units // 2, all_units // 2)]
        pack_shapes = []
        for _, _, count in packs:
            shape = (half_slots * count, GROUP, LANES) if count else (half_slots, GROUP, head_width)
            pack_shapes += [shape_of(shape, BF16)] * 2
        dx_shape = shape_of((latent + LANES, wide), F32)
        out_shapes = (*pack_shapes, dx_shape, shape_of((1, LANES), F32))
        args = [place, xt, x_rows, *weights, head_turned, net_gain, net_shift, reward_bins, value_bins, horizon_row]
        specs = [smem] + [local] * 10
        aliases = {}
        if before is not None:
            aliases = {len(args): len(pack_shapes)}
            args.append(before)
            specs.append(local)
        args += after
        specs += [anywhere] * len(after)
        if ahead:
            args += [first_far, second_far]
            specs += [far, far]
            out_shapes += weight_shapes
        low_wide = vmem((hidden, wide), BF16)
        scratch = [
            vmem((8, hidden), F32),
            vmem((4, hidden, LANES), F32),
            vmem((LANES, hidden), BF16),
            vmem((hidden, LANES), BF16),
            vmem((LANES, hidden), BF16),
            vmem((hidden, wide), F32),
            vmem((LANES, wide), F32),
        ]
        scratch += [low_wide] * 6
        scratch += [vmem((8, wide), F32), vmem((4, hidden, LANES), F32)]
        scratch += [low_wide] * 3
        scratch += [vmem((LANES, wide), BF16), vmem((hidden, head_width), BF16)]
        if ahead:
            scratch.append(dmas((2,)))
        return pl.pallas_call(
            functools.partial(
                heads_kernel, steps, scale, packs, head, ahead, heads, bins, before is not None, len(after)
            ),
            out_shape=out_shapes,
            in_specs=specs,
            out_specs=[local] * len(out_shapes),
            scratch_shapes=scratch,
            input_output_aliases=aliases,
            compiler_params=params(VMEM_B),
            cost_estimate=cost(9_000_000_000, 4_000_000),
            name=f"head_{head}",
        )(*args)

    def phase(pair, bit):
        return pair[0], swap(pair[1], *bits[bit])

    def fold(members, *tokens):
        slots_now = members[0][0].shape[0] // 2
        shape = members[0][0].shape[1:]
        stacked = len(shape) == 3
        if stacked:
            shape = (len(members) * shape[0],) + shape[1:]
        elif len(members) > 1:
            shape = (len(members),) + shape
        out_shape = shape_of((slots_now,) + shape, BF16)

        def fold_kernel(*refs):
            refs = refs[len(tokens) :]
            outs = refs[-2:]
            for place in range(len(members)):
                kept_ref, came_ref = refs[2 * place], refs[2 * place + 1]
                for half in range(2):
                    part = pl.ds(half * slots_now, slots_now)
                    value = (kept_ref[part].astype(F32) + came_ref[part].astype(F32)).astype(BF16)
                    if stacked:
                        count = kept_ref.shape[1]
                        outs[half][:, place * count : (place + 1) * count] = value
                    elif len(members) > 1:
                        outs[half][:, place] = value
                    else:
                        outs[half][...] = value

        return run_fold(fold_kernel, out_shape, members, tokens)

    def fold_units(members, slots_now, common, *tokens):
        counts = [(kept.shape[0] - (0 if place else common)) // slots_now for place, (kept, _) in enumerate(members)]
        half_now = slots_now // 2
        width = sum(counts)
        out_shape = shape_of((half_now * width + common,) + members[0][0].shape[1:], BF16)

        def fold_kernel(*refs):
            refs = refs[len(tokens) :]
            outs = refs[-2:]
            before = 0
            for place, count in enumerate(counts):
                kept_ref, came_ref = refs[2 * place], refs[2 * place + 1]

                def added(start, size):
                    part = pl.ds(start, size)
                    return (kept_ref[part].astype(F32) + came_ref[part].astype(F32)).astype(BF16)

                for half in range(2):
                    if len(counts) == 1:
                        outs[half][0 : half_now * count] = added(half * half_now * count, half_now * count)
                    else:
                        for slot in range(half_now):
                            at = slot * width + before
                            outs[half][at : at + count] = added((half * half_now + slot) * count, count)
                if place == 0 and common:
                    value = added(slots_now * count, common)
                    for out in outs:
                        out[half_now * width :] = value
                before += count

        return run_fold(fold_kernel, out_shape, members, tokens)

    def run_fold(kernel, out_shape, members, tokens):
        inputs = [each for member in members for each in member]
        return pl.pallas_call(
            kernel,
            out_shape=(out_shape, out_shape),
            in_specs=[anywhere] * len(tokens) + [local] * len(inputs),
            out_specs=(local, local),
            compiler_params=params(VMEM_SUM),
            cost_estimate=cost(1_000_000, 2_000_000),
            name="fold",
        )(*tokens, *inputs)

    net_width = latent + LANES + hidden + latent
    chain_inputs = saved[:9] + saved[14:]

    def run_backward(order, losses, held, after):
        final = order[-1] == 0
        out_shapes = (
            shape_of((hidden, net_width), BF16 if final else F32),
            shape_of((latent, LANES), BF16),
            shape_of((LANES, LANES), F32),
            shape_of((1, LANES), F32),
            shape_of((4, hidden, LANES), F32),
        )
        args = [place, *chain_inputs, horizon_row, net_gain, dx, *losses, *held]
        return pl.pallas_call(
            functools.partial(backward_kernel, steps, scale, order, len(losses), len(after)),
            out_shape=out_shapes,
            in_specs=[smem] + [local] * (len(args) - 1) + [anywhere] * len(after) + [far],
            out_specs=[local] * len(out_shapes),
            scratch_shapes=[
                vmem((steps, LANES, latent), BF16),
                vmem((8, hidden), F32),
                vmem((4, hidden, LANES), F32),
                vmem((LANES, hidden), BF16),
                vmem((hidden, LANES), F32),
                vmem((hidden, wide), BF16),
                vmem((hidden, wide), BF16),
                vmem((latent, wide), BF16),
                vmem((hidden, net_width), F32),
                dmas((steps,)),
            ],
            compiler_params=params(VMEM_C),
            cost_estimate=cost(7_000_000_000, 8_000_000),
            name=f"backward_{order[0]}",
        )(*args, *after, targets_far)

    packs, loss_parts = [], []
    dx = None
    after = []
    cores, pairs = [], []
    units_all = head_width // LANES
    for head in range(heads):
        result = run_head(head, head + 1 < heads, weights, dx, after)
        sent = 4 if in_place and head == heads - 1 else 2
        dx, loss = result[sent : sent + 2]
        weights = result[sent + 2 :]
        packs.append(result[:sent])
        loss_parts.append(loss)
        after = []
        if in_place:
            if 1 <= head <= heads - 2:
                crossing = fold([cores[head - 1]], loss)
                after.append(crossing[0])
                pairs.append(phase(crossing, plain[1]))
            if head in (3, 5):
                crossing = fold(pairs[head - 3 : head - 1], loss)
                after.append(crossing[0])
                pairs[head - 3] = phase(crossing, plain[2])
            if head == heads - 1:
                fourth = fold_units([cores[head - 1]], half_slots, 0, loss)
                after.append(fourth[0])
                fourth = phase(fourth, plain[1])
                cores.append(phase(result[0:2], plain[0]))
                cores.append(phase(result[2:4], y_first[0]))
            else:
                cores.append(phase(result[0:2], plain[0]))
    half_way = steps // 2
    chain = run_backward(tuple(range(steps - 1, half_way - 1, -1)), loss_parts, [], after)
    after = []
    if in_place:
        token = chain[3]
        fifth = fold_units([cores[heads - 1]], half_slots, 0, token)
        sixth = fold_units([cores[heads]], half_slots, 0, token)
        fourth = fold_units([fourth], half_slots // 2, 0, token)
        group = fold([pairs[0], pairs[2]], token)
        after = [fifth[0], sixth[0], fourth[0], group[0]]
        fifth = phase(fifth, plain[1])
        sixth = phase(sixth, y_first[1])
        group = phase(group, plain[3])
        fourth = phase(fourth, plain[2])
    chain = run_backward(
        tuple(range(half_way - 1, -1, -1)), [chain[3]], [chain[0], chain[1], chain[2], chain[4]], after
    )
    after = []
    if in_place:
        token = chain[3]
        fifth = fold_units([fifth], half_slots // 2, 0, token)
        sixth = fold_units([sixth], half_slots // 2, 0, token)
        group = fold([group], token)
        after = [fifth[0], sixth[0], group[0], fourth[1]]
        fifth = phase(fifth, plain[2])
        sixth = phase(sixth, y_first[2])
        group = phase(group, plain[4])

    enc_lanes = latent - LANES
    units = (net_width + enc_lanes) // 2 // LANES
    common = tasks // GROUP
    one_shape = shape_of((half_slots * units + common, GROUP, LANES), BF16)
    two_shape = shape_of((half_slots * units, GROUP, LANES), BF16)
    tail_slots = (slots_of(plain), slots_of(y_first))
    ended = pl.pallas_call(
        functools.partial(ending_kernel, tail_slots, tasks, task_width, acted, observed, len(after)),
        out_shape=(one_shape, one_shape, two_shape, two_shape),
        in_specs=[smem] + [local] * 14 + [anywhere] * len(after),
        out_specs=[local] * 4,
        scratch_shapes=[
            vmem((8, enc_width), F32),
            vmem((2, enc_width, LANES), F32),
            vmem((2 * LANES, enc_width), BF16),
            vmem((enc_width, LANES), F32),
            vmem((2, enc_width, LANES), F32),
            vmem((enc_width, LANES), BF16),
            vmem((groups, GROUP, enc_lanes), F32),
        ],
        compiler_params=params(VMEM_SUM),
        cost_estimate=cost(1_000_000_000, 4_000_000),
        name="ending",
    )(place, *chain[:4], saved[1], *saved[9:14], ids_row, enc_first, eg_row, enc_second, *after)

    if in_place:
        one = phase(ended[0:2], plain[0])
        two = phase(ended[2:4], y_first[0])
        one = phase(fold_units([one], half_slots, common, fifth[1], sixth[1]), plain[1])
        two = phase(fold_units([two], half_slots, 0, fifth[1], sixth[1]), y_first[1])
        last = phase(fold_units([fourth, fifth, sixth], half_slots // 4, 0, ended[0]), plain[3])
        one = fold_units([one], half_slots // 2, common, last[1], group[1])
        two = fold_units([two], half_slots // 2, 0, last[1], group[1])
        last = phase(fold_units([last], half_slots // 8, 0, ended[0]), plain[4])
        one = phase(one, plain[2])
        two = phase(two, y_first[2])
        tail = phase(fold_units([one, two], half_slots // 4, common, last[1]), plain[3])
        tail = phase(fold_units([tail], half_slots // 8, common), plain[4])
        each = GROUP // 2
        out_shapes = (
            shape_of((1, 1), F32),
            shape_of((tasks, task_width), F32),
            shape_of((each, enc_in), F32),
            shape_of((1, each), F32),
            shape_of((1, each), F32),
            shape_of((each, latent), F32),
            shape_of((nets, GROUP, net_in), F32),
            shape_of((nets, GROUP, hidden), F32),
            shape_of((nets, 2, GROUP), F32),
            shape_of((nets, 2, GROUP), F32),
            shape_of((GROUP, latent), F32),
            shape_of((heads, GROUP, bins), F32),
        )
        ends = [*tail, *group, *last]
        outs = list(pl.pallas_call(
            functools.partial(final_kernel, tasks, task_width, enc_in, bins, net_in),
            out_shape=out_shapes,
            in_specs=[local] * len(ends),
            out_specs=[local] * len(out_shapes),
            compiler_params=params(VMEM_SUM),
            cost_estimate=cost(1_000_000, 4_000_000),
            name="last_sums",
        )(*ends))
        outs[0] = outs[0].reshape(())
        outs[2] = outs[2].T
        outs[3], outs[4] = outs[3].reshape(each), outs[4].reshape(each)
        outs[6] = outs[6].transpose(0, 2, 1)
        outs[7] = outs[7].transpose(0, 2, 1)
        return tuple(outs)

    def scattered(keep, send):
        mine = hidden // devices
        packed = jnp.concatenate([keep, send], axis=0)
        middle = packed.shape[1:-2]
        packed = packed.reshape((groups,) + middle + (GROUP // mine, mine, packed.shape[-1]))
        packed = jnp.moveaxis(packed, -3, 1).reshape((devices,) + middle + (mine, packed.shape[-1]))
        return scatter_plain(packed, chips, sections)

    head_sum = jnp.stack([scattered(*pack) for pack in packs], axis=0)
    enc_each = enc_width // devices
    def by_rows(place):
        parts = [each[: half_slots * units].reshape(half_slots, units, GROUP, LANES) for each in (ended[place], ended[2 + place])]
        joined = jnp.concatenate(parts, axis=1).transpose(0, 2, 1, 3)
        return joined.reshape(half_slots, GROUP, 2 * units * LANES)

    keep, send = by_rows(0), by_rows(1)
    table_sum = lax.psum(ended[0][half_slots * units :].astype(F32), ("section", "batch"))
    table_sum = table_sum.transpose(1, 0, 2).reshape(GROUP, common * LANES)
    net_sum = scattered(keep[:, :, 0:net_width], send[:, :, 0:net_width])
    enc_all = jnp.concatenate([keep, send], axis=0)[:, :, net_width:]
    enc_all = enc_all.reshape(groups, 2, enc_width // groups, enc_lanes)
    enc_all = enc_all.transpose(0, 2, 1, 3).reshape(devices, enc_each, 2, enc_lanes)
    enc_sum = scatter_plain(enc_all, chips, sections)
    enc_low, enc_high = enc_sum[:, 0], enc_sum[:, 1]
    s_enc_second = jnp.concatenate([enc_low, enc_high[:, 0 : latent - enc_lanes]], axis=1)
    enc_rows = enc_high[:, latent - enc_lanes :]
    first_end = latent + LANES
    net_row = jnp.concatenate([net_sum[:, 0 : first_end + hidden], jnp.zeros_like(net_sum[:, 0:LANES])], axis=1)
    sums = jnp.concatenate([net_row[None], head_sum], axis=0)
    vectors = sums[:, :, net_in : net_in + 4].transpose(0, 2, 1)
    table = table_sum.reshape(GROUP, tasks // GROUP, LANES).transpose(1, 0, 2).reshape(tasks, LANES)
    return (
        table[0, LANES - 1],
        table[:, 0:task_width],
        0.3 * enc_rows[:, 0:enc_in].T,
        0.3 * enc_rows[:, 2 * LANES - 2],
        0.3 * enc_rows[:, 2 * LANES - 1],
        0.3 * s_enc_second,
        sums[:, :, 0:net_in].transpose(0, 2, 1),
        sums[:, :, first_end : first_end + hidden].transpose(0, 2, 1),
        vectors[:, 0::2],
        vectors[:, 1::2],
        net_sum[:, first_end + hidden :],
        head_sum[:, :, first_end + hidden : first_end + hidden + bins],
    )


def solution(mesh):
    both = ("section", "batch")
    return jax.shard_map(
        on_device,
        mesh=mesh,
        in_specs=(
            P("batch", None),
            P(None, "batch", None),
            P(None, "batch", None),
            P("batch"),
            P("batch"),
            P(None, "batch"),
            P(None, "batch"),
        )
        + (P(),) * 11,
        out_specs=(
            P(),
            P(),
            P(None, both),
            P(both),
            P(both),
            P(both, None),
            P(None, None, both),
            P(None, None, both),
            P(None, None, both),
            P(None, None, both),
            P(both, None),
            P(None, both, None),
        ),
        check_vma=False,
    )
```

```python
import functools

import jax
import jax.numpy as jnp
from jax import lax
from jax.experimental import pallas as pl
from jax.experimental.pallas import tpu as pltpu
from jax.sharding import PartitionSpec as P

CORES = 2
LANES = 128
GROUP = 16
BF16 = jnp.bfloat16
F32 = jnp.float32
VMEM_A = 18
VMEM_B = 20
VMEM_SUM = 6
VMEM_C = 20


def nn(left, right):
    return lax.dot_general(left, right, (((1,), (0,)), ((), ())), preferred_element_type=F32)


def nt(left, right):
    return lax.dot_general(left, right, (((1,), (1,)), ((), ())), preferred_element_type=F32)


def tn(left, right):
    return lax.dot_general(left, right, (((0,), (0,)), ((), ())), preferred_element_type=F32)


def column_sum(value):
    grouped = value.reshape(value.shape[0] // 8, 8, value.shape[1])
    return jnp.sum(jnp.sum(grouped, axis=0), axis=0, keepdims=True)


def slabs(features, size=64):
    return [slice(start, start + size) for start in range(0, features, size)]


def lanes_of(step):
    return slice(step * LANES, (step + 1) * LANES)


def spread_columns(gain_rows, shift_rows, rows_ref, spread_ref):
    count = gain_rows.shape[0]
    rows_ref[...] = jnp.zeros_like(rows_ref)
    rows_ref[0:count, :] = gain_rows
    rows_ref[count : 2 * count, :] = shift_rows
    turned = jnp.transpose(rows_ref[...])
    for place in range(2 * count):
        spread_ref[place] = jnp.broadcast_to(turned[:, place : place + 1], spread_ref.shape[1:])


def mish_forward(pre_ref, pre_at, gain_ref, shift_ref, hid_ref, hat_ref, slope_ref, scale_ref, scale_row, at):
    features = pre_ref.shape[0]
    row_mean = column_sum(pre_ref[:, pre_at]) * (1.0 / features)
    centred = pre_ref[:, pre_at] - row_mean
    spread = column_sum(centred * centred) * (1.0 / features)
    scale = lax.rsqrt(spread + 1e-05)
    scale_ref[scale_row : scale_row + 1, at] = scale
    for part in slabs(features):
        hat = (pre_ref[part, pre_at] - row_mean) * scale
        normed = hat * gain_ref[part, :] + shift_ref[part, :]
        power = jnp.exp(normed)
        top = power * (power + 2.0)
        inverse = pl.reciprocal(top + 2.0, approx=True)
        ratio = top * inverse
        hid_ref[part, at] = (normed * ratio).astype(BF16)
        tilt = power * inverse
        slope = ratio + normed * (4.0 * (tilt * (tilt + inverse)))
        slope_ref[part, at] = (slope * gain_ref[part, :]).astype(BF16)
        hat_ref[part, at] = hat.astype(BF16)


def mish_backward(grad_ref, grad_at, hat_ref, slope_ref, scale_ref, scale_row, at, sums_ref, sums_at, first, out_ref):
    features = grad_ref.shape[0]
    total_one = jnp.zeros((8, LANES), F32)
    total_two = jnp.zeros((8, LANES), F32)
    for part in slabs(features):
        term = grad_ref[part, grad_at] * slope_ref[part, at].astype(F32)
        grad_ref[part, grad_at] = term
        crossed = term * hat_ref[part, at].astype(F32)
        groups = (term.shape[0] // 8, 8, LANES)
        total_one = total_one + jnp.sum(term.reshape(groups), axis=0)
        total_two = total_two + jnp.sum(crossed.reshape(groups), axis=0)
        if first:
            sums_ref[sums_at, part, :] = term
            sums_ref[sums_at + 1, part, :] = crossed
        else:
            sums_ref[sums_at, part, :] += term
            sums_ref[sums_at + 1, part, :] += crossed
    mean_one = jnp.sum(total_one, axis=0, keepdims=True) * (1.0 / features)
    mean_two = jnp.sum(total_two, axis=0, keepdims=True) * (1.0 / features)
    scale = scale_ref[scale_row : scale_row + 1, at]
    for part in slabs(features):
        rest = grad_ref[part, grad_at] - mean_one - hat_ref[part, at].astype(F32) * mean_two
        out_ref[part, at] = (rest * scale).astype(BF16)


def mish_forward_low(pre_ref, gain_ref, shift_ref, hid_ref, hat_ref, slope_ref, scale_ref, scale_row, at):
    features = pre_ref.shape[0]
    row_mean = column_sum(pre_ref[:, at]) * (1.0 / features)
    centred = pre_ref[:, at] - row_mean
    spread = column_sum(centred * centred) * (1.0 / features)
    scale = lax.rsqrt(spread + 1e-05)
    scale_ref[scale_row : scale_row + 1, at] = scale
    for part in slabs(features):
        hat = (pre_ref[part, at] - row_mean) * scale
        normed = (hat * gain_ref[part, :] + shift_ref[part, :]).astype(BF16)
        hat_ref[part, at] = hat.astype(BF16)
        power = jnp.exp(normed)
        top = power * (power + 2.0)
        inverse = pl.reciprocal(top + 2.0, approx=True)
        ratio = top * inverse
        hid_ref[part, at] = normed * ratio
        tilt = power * inverse
        slope = ratio + (4.0 * normed) * (tilt * (tilt + inverse))
        slope_ref[part, at] = slope * gain_ref[part, :].astype(BF16)


def mish_backward_low(grad_ref, hat_ref, slope_ref, scale_ref, scale_row, steps, sums_ref, sums_at, out_ref):
    features = grad_ref.shape[0]
    rows = []
    for step in range(steps):
        at = lanes_of(step)
        total_one = jnp.zeros((16, LANES), F32)
        total_two = jnp.zeros((16, LANES), F32)
        for part in slabs(features):
            term = grad_ref[part, at] * slope_ref[part, at]
            crossed = term * hat_ref[part, at]
            grad_ref[part, at] = term
            groups = (term.shape[0] // 16, 16, LANES)
            term = term.reshape(groups)
            crossed = crossed.reshape(groups)
            total_one = total_one + functools.reduce(jnp.add, [term[k] for k in range(groups[0])]).astype(F32)
            total_two = total_two + functools.reduce(jnp.add, [crossed[k] for k in range(groups[0])]).astype(F32)
        scale = scale_ref[scale_row : scale_row + 1, at]
        mean_one = jnp.sum(total_one, axis=0, keepdims=True) * (1.0 / features)
        mean_two = jnp.sum(total_two, axis=0, keepdims=True) * (1.0 / features)
        rows.append((mean_one.astype(BF16), mean_two.astype(BF16), scale.astype(BF16)))
    for part in slabs(features):
        sum_one, sum_two = None, None
        for step, (mean_one, mean_two, scale) in enumerate(rows):
            at = lanes_of(step)
            term = grad_ref[part, at]
            hat = hat_ref[part, at]
            out_ref[part, at] = (term - mean_one - hat * mean_two) * scale
            crossed = term * hat
            sum_one = term if sum_one is None else sum_one + term
            sum_two = crossed if sum_two is None else sum_two + crossed
        sums_ref[sums_at, part, :] = sum_one.astype(F32)
        sums_ref[sums_at + 1, part, :] = sum_two.astype(F32)


def simplex(values):
    grouped = values.reshape(values.shape[0] // 8, 8, values.shape[1])
    powers = jnp.exp(grouped - jnp.max(grouped, axis=1, keepdims=True))
    shares = powers / jnp.sum(powers, axis=1, keepdims=True)
    return shares.reshape(values.shape)


def simplex_back(shares, grads):
    grouped = (shares.shape[0] // 8, 8, shares.shape[1])
    crossed = jnp.sum((shares * grads).reshape(grouped), axis=1, keepdims=True)
    return (shares.reshape(grouped) * (grads.reshape(grouped) - crossed)).reshape(shares.shape)


def row_weight(step, steps, scale, horizon_row, place_ref):
    lane = lax.broadcasted_iota(jnp.int32, (1, LANES), 1)
    mine = (lane >= place_ref[2]) & (lane < place_ref[3]) & (horizon_row > step)
    return jnp.where(mine, F32(scale * 0.5 ** (step / (steps - 1))), 0.0)


def padded_rows(value, rows):
    zeros = jnp.zeros((rows - value.shape[0], value.shape[1]), F32)
    return jnp.concatenate([value.astype(F32), zeros], axis=0).astype(BF16)


def transpose_into(out_ref, source_ref, rows):
    for start in range(0, rows, LANES):
        out_ref[:, start : start + LANES] = jnp.transpose(source_ref[start : start + LANES, :])


def vector_sums(sums_ref, gains_ref, layers):
    vectors = []
    for layer in range(layers):
        inverse = 1.0 / gains_ref[layer]
        vectors.append(jnp.sum(sums_ref[2 * layer + 1] * inverse, axis=1, keepdims=True))
        vectors.append(jnp.sum(sums_ref[2 * layer] * inverse, axis=1, keepdims=True))
    return vectors


def own_lanes(place_ref):
    return pl.ds(pl.multiple_of(place_ref[1] * LANES, LANES), LANES)


def load_all(copies):
    made = [pltpu.make_async_copy(*each) for each in copies]
    for each in made:
        each.start()
    return made


def with_vectors(value, vectors, first_lane):
    lane = lax.broadcasted_iota(jnp.int32, value.shape, 1)
    for place, vector in enumerate(vectors):
        value = jnp.where(lane == first_lane + place, vector, value)
    return value


def forward_kernel(
    steps,
    place_ref, obs_hbm, act_hbm, ids_hbm, table_hbm, e1_hbm, eg_hbm, es_hbm, e2_hbm, g_hbm, s_hbm,
    w1_hbm, w2_hbm, dyn_hbm,
    xt_ref, soft_ref, h1_ref, hat1_ref, slope1_ref, h2_ref, hat2_ref, slope2_ref, scale_ref,
    ein_ref, eh_ref, ehat_ref, eslope_ref, escale_ref,
    w1_ref, w2_ref, dyn_ref, x_ref, next1_ref, next2_ref,
    rows_ref, spread_ref, erows_ref, espread_ref, wide_ref, tall_ref, e1p_ref, w1t_ref, w2t_ref, dynt_ref, pre_ref, epre_ref,
    obs_ref, act_ref, ids_ref, table_ref, e1_ref, eg_ref, es_ref, e2_ref, g_ref, s_ref,
    sems, early_sems,
):
    early = load_all([
        (table_hbm, table_ref, early_sems.at[0]),
        (ids_hbm, ids_ref, early_sems.at[1]),
        (obs_hbm, obs_ref, early_sems.at[2]),
        (e1_hbm, e1_ref, early_sems.at[3]),
        (eg_hbm, eg_ref, early_sems.at[4]),
        (es_hbm, es_ref, early_sems.at[5]),
        (e2_hbm, e2_ref, early_sems.at[6]),
        (act_hbm, act_ref, early_sems.at[7]),
        (g_hbm, g_ref, early_sems.at[8]),
        (s_hbm, s_ref, early_sems.at[9]),
    ])
    first, second, third, fourth, fifth = load_all([
        (w1_hbm.at[0], w1_ref, sems.at[0]),
        (w2_hbm.at[0], w2_ref, sems.at[1]),
        (dyn_hbm, dyn_ref, sems.at[2]),
        (w1_hbm.at[1], next1_ref, sems.at[3]),
        (w2_hbm.at[1], next2_ref, sems.at[4]),
    ])
    latent = dyn_ref.shape[1]
    tasks, task_width = table_ref.shape
    observed = obs_ref.shape[0]
    acted = act_ref.shape[1]
    mine = own_lanes(place_ref)
    for each in early:
        each.wait()
    spread_columns(eg_ref[...], es_ref[...], erows_ref, espread_ref)
    kinds = lax.broadcasted_iota(jnp.int32, (tasks, LANES), 0)
    onehot = (kinds == ids_ref[:, mine]).astype(F32).astype(BF16)
    wide_ref[...] = jnp.zeros_like(wide_ref)
    wide_ref[:, 0:task_width] = table_ref[...].astype(F32)
    table_tail = pltpu.roll(wide_ref[:, 0:LANES], acted, 1).astype(BF16)
    table_enc = pltpu.roll(wide_ref[...], observed, 1).astype(BF16)
    aux = tn(table_tail, onehot)
    tall_ref[...] = jnp.zeros_like(tall_ref)
    tall_ref[0:observed, :] = obs_ref[:, mine].astype(F32)
    ein = tn(table_enc, onehot)
    ein_ref[0:LANES, :] = (ein[0:LANES] + tall_ref[...]).astype(BF16)
    ein_ref[LANES:, :] = ein[LANES:].astype(BF16)
    e1p_ref[...] = padded_rows(e1_ref[...], e1p_ref.shape[0])
    epre_ref[...] = tn(e1p_ref[...], ein_ref[...])
    here = slice(0, LANES)
    mish_forward(epre_ref, here, espread_ref.at[0], espread_ref.at[1], eh_ref, ehat_ref, eslope_ref, escale_ref, 0, here)
    shares = simplex(tn(e2_ref[...], eh_ref[...]))
    soft_ref[:, 0:LANES] = shares
    xt_ref[0:latent, 0:LANES] = shares.astype(BF16)
    spread_columns(g_ref[0], s_ref[0], rows_ref, spread_ref)
    for step in range(steps):
        tall_ref[...] = jnp.zeros_like(tall_ref)
        tall_ref[0:acted, :] = act_ref[step, :, mine].astype(F32)
        xt_ref[latent:, lanes_of(step)] = (aux + tall_ref[...]).astype(BF16)
    first.wait()
    transpose_into(w1t_ref, w1_ref, latent)
    w1t_ref[:, latent:] = jnp.transpose(padded_rows(w1_ref[latent:, :], LANES))
    second.wait()
    transpose_into(w2t_ref, w2_ref, latent)
    third.wait()
    transpose_into(dynt_ref, dyn_ref, latent)
    for step in range(steps):
        at = lanes_of(step)
        pre_ref[...] = nn(w1t_ref[...], xt_ref[:, at])
        mish_forward(pre_ref, here, spread_ref.at[0], spread_ref.at[2], h1_ref, hat1_ref, slope1_ref, scale_ref, 0, at)
        pre_ref[...] = nn(w2t_ref[...], h1_ref[:, at])
        mish_forward(pre_ref, here, spread_ref.at[1], spread_ref.at[3], h2_ref, hat2_ref, slope2_ref, scale_ref, 1, at)
        shares = simplex(nn(dynt_ref[...], h2_ref[:, at]))
        soft_ref[:, lanes_of(step + 1)] = shares
        if step + 1 < steps:
            xt_ref[0:latent, lanes_of(step + 1)] = shares.astype(BF16)
    for step in range(steps):
        for start in range(0, latent + LANES, LANES):
            x_ref[lanes_of(step), start : start + LANES] = jnp.transpose(xt_ref[start : start + LANES, lanes_of(step)])
    fourth.wait()
    fifth.wait()


def heads_kernel(steps, scale, packs, head, ahead, heads, bins, chained, after, *refs):
    refs = list(refs)
    place_ref, xt_ref, x_ref, w1_ref, w2_ref, ho_ref, g_ref, s_ref, rb_ref, vb_ref, hz_ref = refs[:11]
    refs = refs[11:]
    before_ref = refs.pop(0) if chained else None
    refs = refs[after:]
    w1_hbm, w2_hbm = refs[:2] if ahead else (None, None)
    refs = refs[2:] if ahead else refs
    pack_refs, refs = refs[: 2 * len(packs)], refs[2 * len(packs) :]
    dx_ref, loss_ref = refs[:2]
    refs = refs[2:]
    copies = []
    if ahead:
        next1_ref, next2_ref, sems = refs[0], refs[1], refs[-1]
        refs = refs[2:-1]
        copies = load_all([
            (w1_hbm.at[head + 2], next1_ref, sems.at[0]),
            (w2_hbm.at[head + 2], next2_ref, sems.at[1]),
        ])
    (rows_ref, spread_ref, tail_ref, hop_ref, hot_ref, pre_ref, lg_ref, h1_ref, hat1_ref, slope1_ref,
     h2_ref, hat2_ref, slope2_ref, scale_ref, sums_ref, dh_ref, d2_ref, d1_ref, dl_ref, grad_ref) = refs
    latent = w2_ref.shape[0]
    tail_rows = w1_ref.shape[0] - latent
    mine = own_lanes(place_ref)
    horizon_row = hz_ref[:, mine]
    bin_ids = lax.broadcasted_iota(jnp.int32, (LANES, LANES), 0)
    first_end = latent + LANES
    losses = []
    spread_columns(g_ref[head + 1], s_ref[head + 1], rows_ref, spread_ref)
    tail_ref[...] = padded_rows(w1_ref[latent:, :], LANES)
    hot_ref[...] = padded_rows(ho_ref[head], LANES)
    hop_ref[...] = jnp.transpose(hot_ref[...])
    gain1, gain2, shift1, shift2 = [spread_ref.at[place] for place in range(4)]
    pre_ref[...] = tn(w1_ref[0:latent, :], xt_ref[0:latent, :]) + tn(tail_ref[...], xt_ref[latent:, :])
    for step in range(steps):
        mish_forward_low(pre_ref, gain1, shift1, h1_ref, hat1_ref, slope1_ref, scale_ref, 0, lanes_of(step))
    pre_ref[...] = tn(w2_ref[...], h1_ref[...])
    for step in range(steps):
        mish_forward_low(pre_ref, gain2, shift2, h2_ref, hat2_ref, slope2_ref, scale_ref, 1, lanes_of(step))
    lg_ref[...] = nn(hot_ref[...], h2_ref[...])
    share = 0.1 if head == 0 else 0.1 / (heads - 1)
    bins_ref = rb_ref if head == 0 else vb_ref
    for step in range(steps):
        at = lanes_of(step)
        logits = jnp.where(bin_ids < bins, lg_ref[:, at], F32(-1e30))
        chosen = bin_ids == bins_ref[step : step + 1, mine]
        top = jnp.max(logits, axis=0, keepdims=True)
        powers = jnp.exp(logits - top)
        total = column_sum(powers)
        picked = column_sum(jnp.where(chosen, logits, 0.0))
        weight = row_weight(step, steps, scale * share, horizon_row, place_ref)
        losses.append(weight * (jnp.log(total) + top - picked))
        dl_ref[:, at] = (powers * (weight / total) - jnp.where(chosen, weight, 0.0)).astype(BF16)
    dh_ref[...] = nn(hop_ref[...], dl_ref[...]).astype(BF16)
    grad_ref[:, first_end + latent :] = nt(h2_ref[...], dl_ref[...]).astype(BF16)
    mish_backward_low(dh_ref, hat2_ref, slope2_ref, scale_ref, 1, steps, sums_ref, 2, d2_ref)
    dh_ref[...] = nn(w2_ref[...], d2_ref[...]).astype(BF16)
    grad_ref[:, first_end : first_end + latent] = nt(d2_ref[...], h1_ref[...]).astype(BF16)
    mish_backward_low(dh_ref, hat1_ref, slope1_ref, scale_ref, 0, steps, sums_ref, 0, d1_ref)
    low_part = nn(w1_ref[0:latent, :], d1_ref[...])
    side_part = nn(tail_ref[...], d1_ref[...])
    if not chained:
        dx_ref[0:latent, :] = low_part
        dx_ref[latent:, :] = side_part
    else:
        dx_ref[0:latent, :] = before_ref[0:latent, :] + low_part
        dx_ref[latent:, :] = before_ref[latent:, :] + side_part
    grad_ref[:, 0:latent] = nn(d1_ref[...], x_ref[:, 0:latent]).astype(BF16)
    side_terms = nn(d1_ref[...], x_ref[:, latent:])
    side_terms = with_vectors(side_terms, vector_sums(sums_ref, spread_ref, 2), tail_rows)
    grad_ref[:, latent:first_end] = side_terms.astype(BF16)
    for place, (slots, first, units) in enumerate(packs):
        for relative, (which, slot) in enumerate(slots):
            start = pl.multiple_of((place_ref[0] ^ relative) * GROUP, GROUP)
            out_ref = pack_refs[2 * place + which]
            if not units:
                out_ref[slot] = grad_ref[pl.ds(start, GROUP), :]
                continue
            block = grad_ref[pl.ds(start, GROUP), first * LANES : (first + units) * LANES]
            for unit in range(units):
                out_ref[slot * units + unit] = block[:, unit * LANES : (unit + 1) * LANES]
    loss_ref[...] = functools.reduce(jnp.add, losses)
    for each in copies:
        each.wait()


def backward_kernel(
    steps, scale, order, losses, after,
    place_ref, xt_ref, soft_ref, h1_ref, hat1_ref, slope1_ref, h2_ref, hat2_ref, slope2_ref, scale_ref,
    w1_ref, w2_ref, dyn_ref, hz_ref, g_ref, dx_ref, *rest,
):
    initial = order[0] == steps - 1
    final = order[-1] == 0
    loss_refs, rest = rest[:losses], rest[losses:]
    held_refs, rest = ((), rest) if initial else (rest[:4], rest[4:])
    (tgt_hbm, low_ref, first_ref, side_ref, loss_ref, sums_ref, tgt_ref, rows_ref, spread_ref, tail_ref, pre_ref,
     d1_ref, d2_ref, do_ref, grad_ref, sems) = rest[after:]
    mine = own_lanes(place_ref)
    loads = dict(zip(order, load_all([(tgt_hbm.at[step, mine, :], tgt_ref.at[step], sems.at[step]) for step in order])))
    latent = dyn_ref.shape[1]
    here = slice(0, LANES)
    horizon_row = hz_ref[:, mine]
    spread_columns(g_ref[0], g_ref[0], rows_ref, spread_ref)
    tail_rows = w1_ref.shape[0] - latent
    tail_ref[...] = padded_rows(w1_ref[latent:, :], LANES)
    first_end = latent + LANES
    second_end = first_end + latent
    if initial:
        loss = functools.reduce(jnp.add, [each[...] for each in loss_refs])
        side = jnp.zeros((LANES, LANES), F32)
        incoming = None
    else:
        before_ref, given_ref, given_side_ref, given_sums_ref = held_refs
        loss = loss_refs[0][...]
        side = given_side_ref[...]
        incoming = given_ref[...].astype(F32)
        sums_ref[...] = given_sums_ref[...]
    pending = []

    def add_terms(at, fresh, last):
        terms = (
            (slice(0, first_end), nt(d1_ref[:, at], xt_ref[:, at])),
            (slice(first_end, second_end), nt(d2_ref[:, at], h1_ref[:, at])),
            (slice(second_end, second_end + latent), nt(h2_ref[:, at], do_ref[:, at])),
        )
        for lanes, term in terms:
            if not fresh:
                term = term + grad_ref[:, lanes]
            elif not initial:
                term = term + before_ref[:, lanes]
            out_ref = low_ref if last else grad_ref
            if last and final and lanes.start == 0:
                out_ref[:, 0:latent] = term[:, 0:latent].astype(out_ref.dtype)
                vectors = vector_sums(sums_ref, spread_ref, 2)
                out_ref[:, latent:first_end] = with_vectors(term[:, latent:], vectors, tail_rows).astype(out_ref.dtype)
            else:
                out_ref[:, lanes] = term.astype(out_ref.dtype)

    for step in order:
        at = lanes_of(step)
        weight = row_weight(step, steps, scale, horizon_row, place_ref)
        shares = soft_ref[:, lanes_of(step + 1)]
        loads[step].wait()
        residue = shares - jnp.transpose(tgt_ref[step].astype(F32))
        loss = loss + (20.0 / latent) * weight * column_sum(residue * residue)
        grads = residue * ((40.0 / latent) * weight)
        if incoming is not None:
            grads = grads + incoming
        do_ref[:, at] = simplex_back(shares, grads).astype(BF16)
        pre_ref[...] = nn(dyn_ref[...], do_ref[:, at])
        mish_backward(pre_ref, here, hat2_ref, slope2_ref, scale_ref, 1, at, sums_ref, 2, step == steps - 1, d2_ref)
        pre_ref[...] = nn(w2_ref[...], d2_ref[:, at])
        mish_backward(pre_ref, here, hat1_ref, slope1_ref, scale_ref, 0, at, sums_ref, 0, step == steps - 1, d1_ref)
        incoming = nn(w1_ref[0:latent, :], d1_ref[:, at]) + dx_ref[0:latent, at]
        side = side + nn(tail_ref[...], d1_ref[:, at]) + dx_ref[latent:, at]
        incoming = incoming.astype(BF16).astype(F32)
        pending.append(step)
        if len(pending) == 2 or step == order[-1]:
            low, high = min(pending), max(pending) + 1
            add_terms(slice(low * LANES, high * LANES), high == order[0] + 1, low == order[-1])
            pending = []

    first_ref[...] = incoming.astype(BF16)
    side_ref[...] = side
    loss_ref[...] = loss


def ending_kernel(
    slots, tasks, task_width, acted, observed, after,
    place_ref, low_ref, first_ref, side_ref, loss_ref, soft_ref, ein_ref, eh_ref, ehat_ref, eslope_ref, escale_ref,
    ids_ref, e1_ref, eg_ref, e2_ref, *rest,
):
    out_refs, rest = rest[after : after + 2], rest[after + 2 :]
    erows_ref, espread_ref, e1p_ref, epre_ref, esums_ref, ed_ref, egrad_ref = rest
    mine = own_lanes(place_ref)
    here = slice(0, LANES)
    latent = first_ref.shape[0]
    spread_columns(eg_ref[...], eg_ref[...], erows_ref, espread_ref)
    e1p_ref[...] = padded_rows(e1_ref[...], e1p_ref.shape[0])
    d_enc = simplex_back(soft_ref[:, 0:LANES], first_ref[...].astype(F32)).astype(BF16)
    epre_ref[...] = nn(e2_ref[...], d_enc)
    mish_backward(epre_ref, here, ehat_ref, eslope_ref, escale_ref, 0, here, esums_ref, 0, True, ed_ref)
    side_enc = nn(e1p_ref[...], ed_ref[...])
    enc_width = epre_ref.shape[0]
    half = GROUP // 2
    groups = enc_width // half
    kept = egrad_ref.shape[2]
    enc_second = nt(eh_ref[...], d_enc)
    egrad_ref[:, 0:half, :] = enc_second[:, 0:kept].reshape(groups, half, kept)
    egrad_ref[:, half:, 0 : latent - kept] = enc_second[:, kept:].reshape(groups, half, latent - kept)
    enc_first = nt(ed_ref[...], ein_ref[...])
    egrad_ref[:, half:, latent - kept : kept - LANES] = enc_first[:, 0:LANES].reshape(groups, half, LANES)
    second_lanes = with_vectors(enc_first[:, LANES : 2 * LANES], vector_sums(esums_ref, espread_ref, 1), LANES - 2)
    egrad_ref[:, half:, kept - LANES :] = second_lanes.reshape(groups, half, LANES)

    kinds = lax.broadcasted_iota(jnp.int32, (tasks, LANES), 0)
    onehot = (kinds == ids_ref[:, mine]).astype(F32)
    over_lanes = (((1,), (1,)), ((), ()))
    highest = lax.Precision.HIGHEST
    side_terms = lax.dot_general(onehot, side_ref[...], over_lanes, precision=highest, preferred_element_type=F32)
    enc_terms = lax.dot_general(onehot, side_enc, over_lanes, precision=highest, preferred_element_type=F32)
    table = pltpu.roll(side_terms, LANES - acted, 1)
    table = table + pltpu.roll(enc_terms, enc_terms.shape[1] - observed, 1)[:, 0:LANES]
    lane = lax.broadcasted_iota(jnp.int32, table.shape, 1)
    table = jnp.where(lane < task_width, table, 0.0)
    table = jnp.where((lane == LANES - 1) & (kinds == 0), jnp.sum(loss_ref[...], axis=1, keepdims=True), table)
    table_rows = [table[start : start + GROUP] for start in range(0, tasks, GROUP)]
    table_block = jnp.concatenate(table_rows, axis=1).astype(BF16)
    count = low_ref.shape[1] // LANES
    units = count + kept // LANES
    for relative, (which, slot) in enumerate(slots):
        dest = place_ref[0] ^ relative
        start = pl.multiple_of(dest * GROUP, GROUP)
        block = jnp.concatenate([low_ref[pl.ds(start, GROUP), :], egrad_ref[dest].astype(BF16)], axis=1)
        for unit in range(units):
            out_refs[which][slot * units + unit] = block[:, unit * LANES : (unit + 1) * LANES]
    last = len(slots) // 2 * units
    for unit in range(tasks // GROUP):
        for out_ref in out_refs:
            out_ref[last + unit] = table_block[:, unit * LANES : (unit + 1) * LANES]


def final_kernel(tasks, task_width, enc_in, bins, net_in, *refs):
    outs = refs[-12:]
    (loss_ref, table_ref, e1_ref, eg_ref, es_ref, e2_ref, first_ref, second_ref, gain_ref, shift_ref, dyn_ref, head_ref) = outs
    refs = refs[:-12]
    tail_refs, refs = refs[:4], refs[4:]
    latent = second_ref.shape[2]
    first_end = latent + LANES
    second_end = first_end + latent

    def put_net(net, value):
        first_ref[net] = value[:, 0:net_in]
        second_ref[net] = value[:, first_end:second_end]
        turned = jnp.transpose(value[:, latent:first_end])
        for layer in range(2):
            row = net_in - latent + 2 * layer
            gain_ref[net, layer : layer + 1, :] = turned[row : row + 1, :]
            shift_ref[net, layer : layer + 1, :] = turned[row + 1 : row + 2, :]

    sums = functools.reduce(jnp.add, [ref[...].astype(F32) for ref in tail_refs])
    units = sums.shape[0] - tasks // GROUP
    tail = jnp.concatenate([sums[unit] for unit in range(units)], axis=1)
    put_net(0, tail)
    dyn_ref[...] = tail[:, second_end : second_end + latent]
    enc = tail[:, second_end + latent :]
    half = GROUP // 2
    kept = enc.shape[1]
    e2_ref[:, 0:kept] = 0.3 * enc[0:half, :]
    e2_ref[:, kept:] = 0.3 * enc[half:, 0 : latent - kept]
    e1_ref[...] = 0.3 * enc[half:, latent - kept : latent - kept + enc_in]
    turned = 0.3 * jnp.transpose(enc[half:, kept - LANES :])
    eg_ref[...] = turned[LANES - 2 : LANES - 1, :]
    es_ref[...] = turned[LANES - 1 : LANES, :]
    loss_ref[...] = sums[units, 0:1, LANES - 1 : LANES]
    for place in range(tasks // GROUP):
        table_ref[place * GROUP : (place + 1) * GROUP, :] = sums[units + place, :, 0:task_width]
    net = 1
    def put_head(value):
        put_net(net, value)
        head_ref[net - 1] = value[:, second_end : second_end + bins]

    one_ref, other_ref, last_one_ref, last_other_ref = refs
    for one in range(one_ref.shape[1]):
        put_head(one_ref[0, one].astype(F32) + other_ref[0, one].astype(F32))
        net += 1
    sums = last_one_ref[...].astype(F32) + last_other_ref[...].astype(F32)
    units = (second_end + LANES) // LANES
    for start in range(0, sums.shape[0], units):
        put_head(jnp.concatenate([sums[start + unit] for unit in range(units)], axis=1))
        net += 1


def swap(value, axis, distance):
    count = lax.axis_size(axis)
    return lax.ppermute(value, axis, [(place, place ^ distance) for place in range(count)])


def exchange(parts, axis, scale):
    total = parts[0].astype(F32)
    for distance in range(1, len(parts)):
        total = total + swap(parts[distance], axis, distance * scale).astype(F32)
    return total


def scatter_plain(packed, chips, sections):
    held = packed.reshape((sections, chips, CORES) + packed.shape[1:])
    batch_no = lax.axis_index("batch")
    places = (
        ("batch", 1, CORES, 2, batch_no % CORES),
        ("batch", CORES, chips, 1, batch_no // CORES),
        ("section", 1, sections, 0, lax.axis_index("section")),
    )
    for axis, scale, count, dim, mine in places:
        parts = [lax.dynamic_index_in_dim(held, mine ^ other, dim, keepdims=False) for other in range(count)]
        held = exchange(parts, axis, scale)
        held = held.astype(BF16) if dim else held
    return held


def on_device(
    observations,
    actions,
    targets,
    task_ids,
    horizons,
    reward_bins,
    value_bins,
    task_table,
    enc_first,
    enc_gain,
    enc_shift,
    enc_second,
    net_first,
    net_second,
    net_gain,
    net_shift,
    dyn_out,
    head_out,
):
    sections = lax.axis_size("section")
    batches = lax.axis_size("batch")
    section_no = lax.axis_index("section")
    chips = batches // CORES
    devices = sections * batches
    steps, rows_all, acted = actions.shape
    observed = observations.shape[1]
    rows = rows_all // sections
    latent = dyn_out.shape[1]
    hidden = dyn_out.shape[0]
    tasks, task_width = task_table.shape
    heads, _, bins = head_out.shape
    nets, net_in, _ = net_first.shape
    enc_in, enc_width = enc_first.shape
    wide = steps * LANES
    scale = 1.0 / (rows_all * batches * steps)
    groups = hidden // GROUP
    in_place = hidden // devices == GROUP
    start = section_no * rows
    block_no = start // LANES
    first_lane = start - block_no * LANES
    me = section_no * batches + lax.axis_index("batch") if in_place else jnp.int32(0)
    place = jnp.stack([me, block_no, first_lane, first_lane + rows]).astype(jnp.int32)
    bits = [("batch", 1 << bit) for bit in range(batches.bit_length() - 1)]
    bits += [("section", 1 << bit) for bit in range(sections.bit_length() - 1)]

    def slots_of(order):
        if not in_place:
            return tuple((relative // (groups // 2), relative % (groups // 2)) for relative in range(groups))
        found = []
        for relative in range(groups):
            slot = 0
            for bit in order:
                slot = 2 * slot + (relative >> bit & 1)
            found.append((slot // (groups // 2), slot % (groups // 2)))
        return tuple(found)

    plain = tuple(range(len(bits)))
    y_first = (0, 2, 1) + tuple(range(3, len(bits))) if in_place else plain
    half_slots = groups // 2
    shape_of = jax.ShapeDtypeStruct
    smem = pl.BlockSpec(memory_space=pltpu.SMEM)
    local = pl.BlockSpec(memory_space=pltpu.VMEM)
    far = pl.BlockSpec(memory_space=pltpu.HBM)
    anywhere = pl.BlockSpec(memory_space=pl.ANY)
    first_far, second_far, dyn_far, targets_far = [
        pltpu.with_memory_space_constraint(array, pltpu.HBM) for array in (net_first, net_second, dyn_out, targets)
    ]
    vmem = pltpu.VMEM
    dmas = pltpu.SemaphoreType.DMA

    def params(mebibytes):
        return pltpu.CompilerParams(vmem_limit_bytes=mebibytes * 1024 * 1024)

    def cost(flops, moved):
        return pl.CostEstimate(flops=flops, bytes_accessed=moved, transcendentals=0)

    ids_row = task_ids.reshape(1, rows_all)
    horizon_row = horizons.reshape(1, rows_all)
    eg_row = enc_gain.reshape(1, enc_width)
    es_row = enc_shift.reshape(1, enc_width)
    head_turned = head_out.transpose(0, 2, 1)
    low = lambda lanes: shape_of((hidden, lanes), BF16)
    forward_shapes = (
        shape_of((latent + LANES, wide), BF16),
        shape_of((latent, wide + LANES), F32),
        low(wide), low(wide), low(wide), low(wide), low(wide), low(wide),
        shape_of((8, wide), F32),
        shape_of((2 * LANES, LANES), BF16),
        shape_of((enc_width, LANES), BF16),
        shape_of((enc_width, LANES), BF16),
        shape_of((enc_width, LANES), BF16),
        shape_of((8, LANES), F32),
        shape_of((net_in, hidden), BF16),
        shape_of((hidden, hidden), BF16),
        shape_of((hidden, latent), BF16),
        shape_of((wide, latent + LANES), BF16),
    )

    weight_shapes = (shape_of((net_in, hidden), BF16), shape_of((hidden, hidden), BF16))

    early = [
        pltpu.with_memory_space_constraint(array, pltpu.HBM)
        for array in (
            observations.T, actions.transpose(0, 2, 1), ids_row, task_table, enc_first, eg_row, es_row, enc_second,
            net_gain, net_shift,
        )
    ]
    made = pl.pallas_call(
        functools.partial(forward_kernel, steps),
        out_shape=forward_shapes + weight_shapes,
        in_specs=[smem] + [far] * 13,
        out_specs=[local] * (len(forward_shapes) + 2),
        scratch_shapes=[
            vmem((8, hidden), F32),
            vmem((4, hidden, LANES), F32),
            vmem((8, enc_width), F32),
            vmem((2, enc_width, LANES), F32),
            vmem((tasks, 2 * LANES), F32),
            vmem((LANES, LANES), F32),
            vmem((2 * LANES, enc_width), BF16),
            vmem((hidden, latent + LANES), BF16),
            vmem((hidden, hidden), BF16),
            vmem((latent, hidden), BF16),
            vmem((hidden, LANES), F32),
            vmem((enc_width, LANES), F32),
            *[vmem(each.shape, each.dtype) for each in early],
            dmas((5,)),
            dmas((len(early),)),
        ],
        compiler_params=params(VMEM_A),
        cost_estimate=cost(10_000_000_000, 8_000_000),
        name="forward_chain",
    )(
        place, *early, first_far, second_far, dyn_far,
    )
    saved, x_rows, weights = made[:-3], made[-3], made[-2:]
    xt = saved[0]
    head_width = latent + LANES + hidden + LANES

    def run_head(head, ahead, weights, before, after):
        all_units = head_width // LANES
        packs = [(slots_of(plain), 0, 0)]
        if in_place and head == heads - 1:
            packs = [(slots_of(plain), 0, all_units // 2), (slots_of(y_first), all_units // 2, all_units // 2)]
        pack_shapes = []
        for _, _, count in packs:
            shape = (half_slots * count, GROUP, LANES) if count else (half_slots, GROUP, head_width)
            pack_shapes += [shape_of(shape, BF16)] * 2
        dx_shape = shape_of((latent + LANES, wide), F32)
        out_shapes = (*pack_shapes, dx_shape, shape_of((1, LANES), F32))
        args = [place, xt, x_rows, *weights, head_turned, net_gain, net_shift, reward_bins, value_bins, horizon_row]
        specs = [smem] + [local] * 10
        aliases = {}
        if before is not None:
            aliases = {len(args): len(pack_shapes)}
            args.append(before)
            specs.append(local)
        args += after
        specs += [anywhere] * len(after)
        if ahead:
            args += [first_far, second_far]
            specs += [far, far]
            out_shapes += weight_shapes
        low_wide = vmem((hidden, wide), BF16)
        scratch = [
            vmem((8, hidden), F32),
            vmem((4, hidden, LANES), F32),
            vmem((LANES, hidden), BF16),
            vmem((hidden, LANES), BF16),
            vmem((LANES, hidden), BF16),
            vmem((hidden, wide), F32),
            vmem((LANES, wide), F32),
        ]
        scratch += [low_wide] * 6
        scratch += [vmem((8, wide), F32), vmem((4, hidden, LANES), F32)]
        scratch += [low_wide] * 3
        scratch += [vmem((LANES, wide), BF16), vmem((hidden, head_width), BF16)]
        if ahead:
            scratch.append(dmas((2,)))
        return pl.pallas_call(
            functools.partial(
                heads_kernel, steps, scale, packs, head, ahead, heads, bins, before is not None, len(after)
            ),
            out_shape=out_shapes,
            in_specs=specs,
            out_specs=[local] * len(out_shapes),
            scratch_shapes=scratch,
            input_output_aliases=aliases,
            compiler_params=params(VMEM_B),
            cost_estimate=cost(9_000_000_000, 4_000_000),
            name=f"head_{head}",
        )(*args)

    def phase(pair, bit):
        return pair[0], swap(pair[1], *bits[bit])

    def fold(members, *tokens):
        slots_now = members[0][0].shape[0] // 2
        shape = members[0][0].shape[1:]
        stacked = len(shape) == 3
        if stacked:
            shape = (len(members) * shape[0],) + shape[1:]
        elif len(members) > 1:
            shape = (len(members),) + shape
        out_shape = shape_of((slots_now,) + shape, BF16)

        def fold_kernel(*refs):
            refs = refs[len(tokens) :]
            outs = refs[-2:]
            for place in range(len(members)):
                kept_ref, came_ref = refs[2 * place], refs[2 * place + 1]
                for half in range(2):
                    part = pl.ds(half * slots_now, slots_now)
                    value = (kept_ref[part].astype(F32) + came_ref[part].astype(F32)).astype(BF16)
                    if stacked:
                        count = kept_ref.shape[1]
                        outs[half][:, place * count : (place + 1) * count] = value
                    elif len(members) > 1:
                        outs[half][:, place] = value
                    else:
                        outs[half][...] = value

        return run_fold(fold_kernel, out_shape, members, tokens)

    def fold_units(members, slots_now, common, *tokens):
        counts = [
            kept.shape[2] // LANES if kept.shape[2] > LANES else (kept.shape[0] - (0 if place else common)) // slots_now
            for place, (kept, _) in enumerate(members)
        ]
        half_now = slots_now // 2
        width = sum(counts)
        out_shape = shape_of((half_now * width + common, GROUP, LANES), BF16)

        def fold_kernel(*refs):
            refs = refs[len(tokens) :]
            outs = refs[-2:]
            before = 0
            for place, count in enumerate(counts):
                kept_ref, came_ref = refs[2 * place], refs[2 * place + 1]

                def added(start, size):
                    part = pl.ds(start, size)
                    return (kept_ref[part].astype(F32) + came_ref[part].astype(F32)).astype(BF16)

                for half in range(2):
                    if kept_ref.shape[2] > LANES:
                        for slot in range(half_now):
                            block = added(half * half_now + slot, 1)[0]
                            for unit in range(count):
                                piece = block[:, unit * LANES : (unit + 1) * LANES]
                                outs[half][slot * width + before + unit] = piece
                    elif len(counts) == 1:
                        outs[half][0 : half_now * count] = added(half * half_now * count, half_now * count)
                    else:
                        for slot in range(half_now):
                            at = slot * width + before
                            outs[half][at : at + count] = added((half * half_now + slot) * count, count)
                if place == 0 and common:
                    value = added(slots_now * count, common)
                    for out in outs:
                        out[half_now * width :] = value
                before += count

        return run_fold(fold_kernel, out_shape, members, tokens)

    def fold_direct(parts, slots_now, common, *tokens):
        quarter = (parts[0].shape[0] - common) // 4
        out_shape = shape_of((quarter + common, GROUP, LANES), BF16)

        def fold_kernel(*refs):
            refs = refs[len(tokens) :]
            outs = refs[-4:]

            def added(start, size):
                each = [ref[pl.ds(start, size)].astype(F32) for ref in refs[: len(parts)]]
                return functools.reduce(jnp.add, each).astype(BF16)

            shared = added(4 * quarter, common)
            for place, out in enumerate(outs):
                out[0:quarter] = added(place * quarter, quarter)
                out[quarter:] = shared

        return pl.pallas_call(
            fold_kernel,
            out_shape=(out_shape,) * 4,
            in_specs=[anywhere] * len(tokens) + [local] * len(parts),
            out_specs=(local,) * 4,
            compiler_params=params(VMEM_SUM),
            cost_estimate=cost(1_000_000, 2_000_000),
            name="fold_direct",
        )(*tokens, *parts)

    def direct(pieces, axis, high, low):
        distances = (0, low, high, high + low)
        came = [swap(pieces[place], axis, distances[place]) for place in (3, 2, 1)]
        return [pieces[0], *came]

    def run_fold(kernel, out_shape, members, tokens):
        inputs = [each for member in members for each in member]
        return pl.pallas_call(
            kernel,
            out_shape=(out_shape, out_shape),
            in_specs=[anywhere] * len(tokens) + [local] * len(inputs),
            out_specs=(local, local),
            compiler_params=params(VMEM_SUM),
            cost_estimate=cost(1_000_000, 2_000_000),
            name="fold",
        )(*tokens, *inputs)

    net_width = latent + LANES + hidden + latent
    chain_inputs = saved[:9] + saved[14:]

    def run_backward(order, losses, held, after):
        final = order[-1] == 0
        out_shapes = (
            shape_of((hidden, net_width), BF16 if final else F32),
            shape_of((latent, LANES), BF16),
            shape_of((LANES, LANES), F32),
            shape_of((1, LANES), F32),
            shape_of((4, hidden, LANES), F32),
        )
        args = [place, *chain_inputs, horizon_row, net_gain, dx, *losses, *held]
        return pl.pallas_call(
            functools.partial(backward_kernel, steps, scale, order, len(losses), len(after)),
            out_shape=out_shapes,
            in_specs=[smem] + [local] * (len(args) - 1) + [anywhere] * len(after) + [far],
            out_specs=[local] * len(out_shapes),
            scratch_shapes=[
                vmem((steps, LANES, latent), BF16),
                vmem((8, hidden), F32),
                vmem((4, hidden, LANES), F32),
                vmem((LANES, hidden), BF16),
                vmem((hidden, LANES), F32),
                vmem((hidden, wide), BF16),
                vmem((hidden, wide), BF16),
                vmem((latent, wide), BF16),
                vmem((hidden, net_width), F32),
                dmas((steps,)),
            ],
            compiler_params=params(VMEM_C),
            cost_estimate=cost(7_000_000_000, 8_000_000),
            name=f"backward_{order[0]}",
        )(*args, *after, targets_far)

    packs, loss_parts = [], []
    dx = None
    after = []
    cores, pairs = [], []
    units_all = head_width // LANES
    for head in range(heads):
        result = run_head(head, head + 1 < heads, weights, dx, after)
        sent = 4 if in_place and head == heads - 1 else 2
        dx, loss = result[sent : sent + 2]
        weights = result[sent + 2 :]
        packs.append(result[:sent])
        loss_parts.append(loss)
        after = []
        if in_place:
            if 1 <= head <= heads - 2:
                crossing = fold([cores[head - 1]], loss)
                after.append(crossing[0])
                pairs.append(phase(crossing, plain[1]))
            if head in (3, 5):
                crossing = fold(pairs[head - 3 : head - 1], loss)
                after.append(crossing[0])
                pairs[head - 3] = phase(crossing, plain[2])
            if head == heads - 1:
                fourth = fold([cores[head - 1]], loss)
                after.append(fourth[0])
                fourth = phase(fourth, plain[1])
                cores.append(phase(result[0:2], plain[0]))
                cores.append(phase(result[2:4], y_first[0]))
            else:
                cores.append(phase(result[0:2], plain[0]))
    half_way = steps // 2
    chain = run_backward(tuple(range(steps - 1, half_way - 1, -1)), loss_parts, [], after)
    after = []
    if in_place:
        token = chain[3]
        fifth = fold_units([cores[heads - 1]], half_slots, 0, token)
        sixth = fold_units([cores[heads]], half_slots, 0, token)
        fourth = fold([fourth], token)
        group = fold([pairs[0], pairs[2]], token)
        after = [fifth[0], sixth[0], fourth[0], group[0]]
        fifth = phase(fifth, plain[1])
        sixth = phase(sixth, y_first[1])
        group = phase(group, plain[3])
        fourth = phase(fourth, plain[2])
    chain = run_backward(
        tuple(range(half_way - 1, -1, -1)), [chain[3]], [chain[0], chain[1], chain[2], chain[4]], after
    )
    after = []
    if in_place:
        token = chain[3]
        fifth = fold_units([fifth], half_slots // 2, 0, token)
        sixth = fold_units([sixth], half_slots // 2, 0, token)
        group = fold([group], token)
        after = [fifth[0], sixth[0], group[0], fourth[1]]
        fifth = phase(fifth, plain[2])
        sixth = phase(sixth, y_first[2])
        group = phase(group, plain[4])

    enc_lanes = latent - LANES
    units = (net_width + enc_lanes) // LANES
    common = tasks // GROUP
    tail_shape = shape_of((half_slots * units + common, GROUP, LANES), BF16)
    ended = pl.pallas_call(
        functools.partial(ending_kernel, slots_of(plain), tasks, task_width, acted, observed, len(after)),
        out_shape=(tail_shape, tail_shape),
        in_specs=[smem] + [local] * 14 + [anywhere] * len(after),
        out_specs=[local] * 2,
        scratch_shapes=[
            vmem((8, enc_width), F32),
            vmem((2, enc_width, LANES), F32),
            vmem((2 * LANES, enc_width), BF16),
            vmem((enc_width, LANES), F32),
            vmem((2, enc_width, LANES), F32),
            vmem((enc_width, LANES), BF16),
            vmem((groups, GROUP, enc_lanes), F32),
        ],
        compiler_params=params(VMEM_SUM),
        cost_estimate=cost(1_000_000_000, 4_000_000),
        name="ending",
    )(place, *chain[:4], saved[1], *saved[9:14], ids_row, enc_first, eg_row, enc_second, *after)

    if in_place:
        tail = phase(ended, plain[0])
        pieces = fold_direct(tail, half_slots, common, fifth[1], sixth[1])
        tail = direct(pieces, "batch", CORES, 2 * CORES)
        last = phase(fold_units([fourth, fifth, sixth], half_slots // 4, 0, ended[0]), plain[3])
        last = phase(fold_units([last], half_slots // 8, 0, ended[0]), plain[4])
        pieces = fold_direct(tail, half_slots // 4, common, last[1], group[1])
        tail = direct(pieces, "section", 1, 2)
        each = GROUP // 2
        out_shapes = (
            shape_of((1, 1), F32),
            shape_of((tasks, task_width), F32),
            shape_of((each, enc_in), F32),
            shape_of((1, each), F32),
            shape_of((1, each), F32),
            shape_of((each, latent), F32),
            shape_of((nets, GROUP, net_in), F32),
            shape_of((nets, GROUP, hidden), F32),
            shape_of((nets, 2, GROUP), F32),
            shape_of((nets, 2, GROUP), F32),
            shape_of((GROUP, latent), F32),
            shape_of((heads, GROUP, bins), F32),
        )
        ends = [*tail, *group, *last]
        outs = list(pl.pallas_call(
            functools.partial(final_kernel, tasks, task_width, enc_in, bins, net_in),
            out_shape=out_shapes,
            in_specs=[local] * len(ends),
            out_specs=[local] * len(out_shapes),
            compiler_params=params(VMEM_SUM),
            cost_estimate=cost(1_000_000, 4_000_000),
            name="last_sums",
        )(*ends))
        outs[0] = outs[0].reshape(())
        outs[2] = outs[2].T
        outs[3], outs[4] = outs[3].reshape(each), outs[4].reshape(each)
        outs[6] = outs[6].transpose(0, 2, 1)
        outs[7] = outs[7].transpose(0, 2, 1)
        return tuple(outs)

    def scattered(keep, send):
        mine = hidden // devices
        packed = jnp.concatenate([keep, send], axis=0)
        middle = packed.shape[1:-2]
        packed = packed.reshape((groups,) + middle + (GROUP // mine, mine, packed.shape[-1]))
        packed = jnp.moveaxis(packed, -3, 1).reshape((devices,) + middle + (mine, packed.shape[-1]))
        return scatter_plain(packed, chips, sections)

    head_sum = jnp.stack([scattered(*pack) for pack in packs], axis=0)
    enc_each = enc_width // devices
    def by_rows(array):
        joined = array[: half_slots * units].reshape(half_slots, units, GROUP, LANES).transpose(0, 2, 1, 3)
        return joined.reshape(half_slots, GROUP, units * LANES)

    keep, send = by_rows(ended[0]), by_rows(ended[1])
    table_sum = lax.psum(ended[0][half_slots * units :].astype(F32), ("section", "batch"))
    table_sum = table_sum.transpose(1, 0, 2).reshape(GROUP, common * LANES)
    net_sum = scattered(keep[:, :, 0:net_width], send[:, :, 0:net_width])
    enc_all = jnp.concatenate([keep, send], axis=0)[:, :, net_width:]
    enc_all = enc_all.reshape(groups, 2, enc_width // groups, enc_lanes)
    enc_all = enc_all.transpose(0, 2, 1, 3).reshape(devices, enc_each, 2, enc_lanes)
    enc_sum = scatter_plain(enc_all, chips, sections)
    enc_low, enc_high = enc_sum[:, 0], enc_sum[:, 1]
    s_enc_second = jnp.concatenate([enc_low, enc_high[:, 0 : latent - enc_lanes]], axis=1)
    enc_rows = enc_high[:, latent - enc_lanes :]
    first_end = latent + LANES
    net_row = jnp.concatenate([net_sum[:, 0 : first_end + hidden], jnp.zeros_like(net_sum[:, 0:LANES])], axis=1)
    sums = jnp.concatenate([net_row[None], head_sum], axis=0)
    vectors = sums[:, :, net_in : net_in + 4].transpose(0, 2, 1)
    table = table_sum.reshape(GROUP, tasks // GROUP, LANES).transpose(1, 0, 2).reshape(tasks, LANES)
    return (
        table[0, LANES - 1],
        table[:, 0:task_width],
        0.3 * enc_rows[:, 0:enc_in].T,
        0.3 * enc_rows[:, 2 * LANES - 2],
        0.3 * enc_rows[:, 2 * LANES - 1],
        0.3 * s_enc_second,
        sums[:, :, 0:net_in].transpose(0, 2, 1),
        sums[:, :, first_end : first_end + hidden].transpose(0, 2, 1),
        vectors[:, 0::2],
        vectors[:, 1::2],
        net_sum[:, first_end + hidden :],
        head_sum[:, :, first_end + hidden : first_end + hidden + bins],
    )


def solution(mesh):
    both = ("section", "batch")
    return jax.shard_map(
        on_device,
        mesh=mesh,
        in_specs=(
            P("batch", None),
            P(None, "batch", None),
            P(None, "batch", None),
            P("batch"),
            P("batch"),
            P(None, "batch"),
            P(None, "batch"),
        )
        + (P(),) * 11,
        out_specs=(
            P(),
            P(),
            P(None, both),
            P(both),
            P(both),
            P(both, None),
            P(None, None, both),
            P(None, None, both),
            P(None, None, both),
            P(None, None, both),
            P(both, None),
            P(None, both, None),
        ),
        check_vma=False,
    )
```

```python
import functools

import jax
import jax.numpy as jnp
from jax import lax
from jax.experimental import pallas as pl
from jax.experimental.pallas import tpu as pltpu
from jax.sharding import PartitionSpec as P

CORES = 2
LANES = 128
GROUP = 16
BF16 = jnp.bfloat16
F32 = jnp.float32
VMEM_A = 18
VMEM_B = 20
VMEM_SUM = 6
VMEM_C = 20


def nn(left, right):
    return lax.dot_general(left, right, (((1,), (0,)), ((), ())), preferred_element_type=F32)


def nt(left, right):
    return lax.dot_general(left, right, (((1,), (1,)), ((), ())), preferred_element_type=F32)


def tn(left, right):
    return lax.dot_general(left, right, (((0,), (0,)), ((), ())), preferred_element_type=F32)


def column_sum(value):
    grouped = value.reshape(value.shape[0] // 8, 8, value.shape[1])
    return jnp.sum(jnp.sum(grouped, axis=0), axis=0, keepdims=True)


def slabs(features, size=64):
    return [slice(start, start + size) for start in range(0, features, size)]


def lanes_of(step):
    return slice(step * LANES, (step + 1) * LANES)


def spread_columns(gain_rows, shift_rows, rows_ref, spread_ref):
    count = gain_rows.shape[0]
    rows_ref[...] = jnp.zeros_like(rows_ref)
    rows_ref[0:count, :] = gain_rows
    rows_ref[count : 2 * count, :] = shift_rows
    turned = jnp.transpose(rows_ref[...])
    for place in range(2 * count):
        spread_ref[place] = jnp.broadcast_to(turned[:, place : place + 1], spread_ref.shape[1:])


def mish_forward(pre_ref, pre_at, gain_ref, shift_ref, hid_ref, hat_ref, slope_ref, scale_ref, scale_row, at):
    features = pre_ref.shape[0]
    row_mean = column_sum(pre_ref[:, pre_at]) * (1.0 / features)
    centred = pre_ref[:, pre_at] - row_mean
    spread = column_sum(centred * centred) * (1.0 / features)
    scale = lax.rsqrt(spread + 1e-05)
    scale_ref[scale_row : scale_row + 1, at] = scale
    for part in slabs(features):
        hat = (pre_ref[part, pre_at] - row_mean) * scale
        normed = hat * gain_ref[part, :] + shift_ref[part, :]
        power = jnp.exp(normed)
        top = power * (power + 2.0)
        inverse = pl.reciprocal(top + 2.0, approx=True)
        ratio = top * inverse
        hid_ref[part, at] = (normed * ratio).astype(BF16)
        tilt = power * inverse
        slope = ratio + normed * (4.0 * (tilt * (tilt + inverse)))
        slope_ref[part, at] = (slope * gain_ref[part, :]).astype(BF16)
        hat_ref[part, at] = hat.astype(BF16)


def mish_backward(grad_ref, grad_at, hat_ref, slope_ref, scale_ref, scale_row, at, sums_ref, sums_at, first, out_ref):
    features = grad_ref.shape[0]
    total_one = jnp.zeros((8, LANES), F32)
    total_two = jnp.zeros((8, LANES), F32)
    for part in slabs(features):
        term = grad_ref[part, grad_at] * slope_ref[part, at].astype(F32)
        grad_ref[part, grad_at] = term
        crossed = term * hat_ref[part, at].astype(F32)
        groups = (term.shape[0] // 8, 8, LANES)
        total_one = total_one + jnp.sum(term.reshape(groups), axis=0)
        total_two = total_two + jnp.sum(crossed.reshape(groups), axis=0)
        if first:
            sums_ref[sums_at, part, :] = term
            sums_ref[sums_at + 1, part, :] = crossed
        else:
            sums_ref[sums_at, part, :] += term
            sums_ref[sums_at + 1, part, :] += crossed
    mean_one = jnp.sum(total_one, axis=0, keepdims=True) * (1.0 / features)
    mean_two = jnp.sum(total_two, axis=0, keepdims=True) * (1.0 / features)
    scale = scale_ref[scale_row : scale_row + 1, at]
    for part in slabs(features):
        rest = grad_ref[part, grad_at] - mean_one - hat_ref[part, at].astype(F32) * mean_two
        out_ref[part, at] = (rest * scale).astype(BF16)


def mish_forward_low(pre_ref, gain_ref, shift_ref, hid_ref, hat_ref, slope_ref, scale_ref, scale_row, at):
    features = pre_ref.shape[0]
    row_mean = column_sum(pre_ref[:, at]) * (1.0 / features)
    centred = pre_ref[:, at] - row_mean
    spread = column_sum(centred * centred) * (1.0 / features)
    scale = lax.rsqrt(spread + 1e-05)
    scale_ref[scale_row : scale_row + 1, at] = scale
    for part in slabs(features):
        hat = (pre_ref[part, at] - row_mean) * scale
        normed = (hat * gain_ref[part, :] + shift_ref[part, :]).astype(BF16)
        hat_ref[part, at] = hat.astype(BF16)
        power = jnp.exp(normed)
        top = power * (power + 2.0)
        inverse = pl.reciprocal(top + 2.0, approx=True)
        ratio = top * inverse
        hid_ref[part, at] = normed * ratio
        tilt = power * inverse
        slope = ratio + (4.0 * normed) * (tilt * (tilt + inverse))
        slope_ref[part, at] = slope * gain_ref[part, :].astype(BF16)


def mish_backward_low(grad_ref, hat_ref, slope_ref, scale_ref, scale_row, steps, sums_ref, sums_at, out_ref):
    features = grad_ref.shape[0]
    rows = []
    for step in range(steps):
        at = lanes_of(step)
        total_one = jnp.zeros((16, LANES), F32)
        total_two = jnp.zeros((16, LANES), F32)
        for part in slabs(features):
            term = grad_ref[part, at] * slope_ref[part, at]
            crossed = term * hat_ref[part, at]
            grad_ref[part, at] = term
            groups = (term.shape[0] // 16, 16, LANES)
            term = term.reshape(groups)
            crossed = crossed.reshape(groups)
            total_one = total_one + functools.reduce(jnp.add, [term[k] for k in range(groups[0])]).astype(F32)
            total_two = total_two + functools.reduce(jnp.add, [crossed[k] for k in range(groups[0])]).astype(F32)
        scale = scale_ref[scale_row : scale_row + 1, at]
        mean_one = jnp.sum(total_one, axis=0, keepdims=True) * (1.0 / features)
        mean_two = jnp.sum(total_two, axis=0, keepdims=True) * (1.0 / features)
        rows.append((mean_one.astype(BF16), mean_two.astype(BF16), scale.astype(BF16)))
    for part in slabs(features):
        sum_one, sum_two = None, None
        for step, (mean_one, mean_two, scale) in enumerate(rows):
            at = lanes_of(step)
            term = grad_ref[part, at]
            hat = hat_ref[part, at]
            out_ref[part, at] = (term - mean_one - hat * mean_two) * scale
            crossed = term * hat
            sum_one = term if sum_one is None else sum_one + term
            sum_two = crossed if sum_two is None else sum_two + crossed
        sums_ref[sums_at, part, :] = sum_one.astype(F32)
        sums_ref[sums_at + 1, part, :] = sum_two.astype(F32)


def simplex(values):
    grouped = values.reshape(values.shape[0] // 8, 8, values.shape[1])
    powers = jnp.exp(grouped - jnp.max(grouped, axis=1, keepdims=True))
    shares = powers / jnp.sum(powers, axis=1, keepdims=True)
    return shares.reshape(values.shape)


def simplex_back(shares, grads):
    grouped = (shares.shape[0] // 8, 8, shares.shape[1])
    crossed = jnp.sum((shares * grads).reshape(grouped), axis=1, keepdims=True)
    return (shares.reshape(grouped) * (grads.reshape(grouped) - crossed)).reshape(shares.shape)


def row_weight(step, steps, scale, horizon_row, place_ref):
    lane = lax.broadcasted_iota(jnp.int32, (1, LANES), 1)
    mine = (lane >= place_ref[2]) & (lane < place_ref[3]) & (horizon_row > step)
    return jnp.where(mine, F32(scale * 0.5 ** (step / (steps - 1))), 0.0)


def padded_rows(value, rows):
    zeros = jnp.zeros((rows - value.shape[0], value.shape[1]), F32)
    return jnp.concatenate([value.astype(F32), zeros], axis=0).astype(BF16)


def transpose_into(out_ref, source_ref, rows):
    for start in range(0, rows, LANES):
        out_ref[:, start : start + LANES] = jnp.transpose(source_ref[start : start + LANES, :])


def vector_sums(sums_ref, gains_ref, layers):
    vectors = []
    for layer in range(layers):
        inverse = 1.0 / gains_ref[layer]
        vectors.append(jnp.sum(sums_ref[2 * layer + 1] * inverse, axis=1, keepdims=True))
        vectors.append(jnp.sum(sums_ref[2 * layer] * inverse, axis=1, keepdims=True))
    return vectors


def own_lanes(place_ref):
    return pl.ds(pl.multiple_of(place_ref[1] * LANES, LANES), LANES)


def load_all(copies):
    made = [pltpu.make_async_copy(*each) for each in copies]
    for each in made:
        each.start()
    return made


def with_vectors(value, vectors, first_lane):
    lane = lax.broadcasted_iota(jnp.int32, value.shape, 1)
    for place, vector in enumerate(vectors):
        value = jnp.where(lane == first_lane + place, vector, value)
    return value


def forward_kernel(
    steps,
    place_ref, obs_hbm, act_hbm, ids_hbm, table_hbm, e1_hbm, eg_hbm, es_hbm, e2_hbm, g_hbm, s_hbm,
    w1_hbm, w2_hbm, dyn_hbm,
    xt_ref, soft_ref, h1_ref, hat1_ref, slope1_ref, h2_ref, hat2_ref, slope2_ref, scale_ref,
    ein_ref, eh_ref, ehat_ref, eslope_ref, escale_ref,
    w1_ref, w2_ref, dyn_ref, x_ref, next1_ref, next2_ref,
    rows_ref, spread_ref, erows_ref, espread_ref, wide_ref, tall_ref, e1p_ref, w1t_ref, w2t_ref, dynt_ref, pre_ref, epre_ref,
    obs_ref, act_ref, ids_ref, table_ref, e1_ref, eg_ref, es_ref, e2_ref, g_ref, s_ref,
    sems, early_sems,
):
    early = load_all([
        (table_hbm, table_ref, early_sems.at[0]),
        (ids_hbm, ids_ref, early_sems.at[1]),
        (obs_hbm, obs_ref, early_sems.at[2]),
        (e1_hbm, e1_ref, early_sems.at[3]),
        (eg_hbm, eg_ref, early_sems.at[4]),
        (es_hbm, es_ref, early_sems.at[5]),
        (e2_hbm, e2_ref, early_sems.at[6]),
        (act_hbm, act_ref, early_sems.at[7]),
        (g_hbm, g_ref, early_sems.at[8]),
        (s_hbm, s_ref, early_sems.at[9]),
    ])
    first, second, third, fourth, fifth = load_all([
        (w1_hbm.at[0], w1_ref, sems.at[0]),
        (w2_hbm.at[0], w2_ref, sems.at[1]),
        (dyn_hbm, dyn_ref, sems.at[2]),
        (w1_hbm.at[1], next1_ref, sems.at[3]),
        (w2_hbm.at[1], next2_ref, sems.at[4]),
    ])
    latent = dyn_ref.shape[1]
    tasks, task_width = table_ref.shape
    observed = obs_ref.shape[0]
    acted = act_ref.shape[1]
    mine = own_lanes(place_ref)
    for each in early:
        each.wait()
    spread_columns(eg_ref[...], es_ref[...], erows_ref, espread_ref)
    kinds = lax.broadcasted_iota(jnp.int32, (tasks, LANES), 0)
    onehot = (kinds == ids_ref[:, mine]).astype(F32).astype(BF16)
    wide_ref[...] = jnp.zeros_like(wide_ref)
    wide_ref[:, 0:task_width] = table_ref[...].astype(F32)
    table_tail = pltpu.roll(wide_ref[:, 0:LANES], acted, 1).astype(BF16)
    table_enc = pltpu.roll(wide_ref[...], observed, 1).astype(BF16)
    aux = tn(table_tail, onehot)
    tall_ref[...] = jnp.zeros_like(tall_ref)
    tall_ref[0:observed, :] = obs_ref[:, mine].astype(F32)
    ein = tn(table_enc, onehot)
    ein_ref[0:LANES, :] = (ein[0:LANES] + tall_ref[...]).astype(BF16)
    ein_ref[LANES:, :] = ein[LANES:].astype(BF16)
    e1p_ref[...] = padded_rows(e1_ref[...], e1p_ref.shape[0])
    epre_ref[...] = tn(e1p_ref[...], ein_ref[...])
    here = slice(0, LANES)
    mish_forward(epre_ref, here, espread_ref.at[0], espread_ref.at[1], eh_ref, ehat_ref, eslope_ref, escale_ref, 0, here)
    shares = simplex(tn(e2_ref[...], eh_ref[...]))
    soft_ref[:, 0:LANES] = shares
    xt_ref[0:latent, 0:LANES] = shares.astype(BF16)
    spread_columns(g_ref[0], s_ref[0], rows_ref, spread_ref)
    for step in range(steps):
        tall_ref[...] = jnp.zeros_like(tall_ref)
        tall_ref[0:acted, :] = act_ref[step, :, mine].astype(F32)
        xt_ref[latent:, lanes_of(step)] = (aux + tall_ref[...]).astype(BF16)
    first.wait()
    transpose_into(w1t_ref, w1_ref, latent)
    w1t_ref[:, latent:] = jnp.transpose(padded_rows(w1_ref[latent:, :], LANES))
    second.wait()
    transpose_into(w2t_ref, w2_ref, latent)
    third.wait()
    transpose_into(dynt_ref, dyn_ref, latent)
    for step in range(steps):
        at = lanes_of(step)
        pre_ref[...] = nn(w1t_ref[...], xt_ref[:, at])
        mish_forward(pre_ref, here, spread_ref.at[0], spread_ref.at[2], h1_ref, hat1_ref, slope1_ref, scale_ref, 0, at)
        pre_ref[...] = nn(w2t_ref[...], h1_ref[:, at])
        mish_forward(pre_ref, here, spread_ref.at[1], spread_ref.at[3], h2_ref, hat2_ref, slope2_ref, scale_ref, 1, at)
        shares = simplex(nn(dynt_ref[...], h2_ref[:, at]))
        soft_ref[:, lanes_of(step + 1)] = shares
        if step + 1 < steps:
            xt_ref[0:latent, lanes_of(step + 1)] = shares.astype(BF16)
    for step in range(steps):
        for start in range(0, latent + LANES, LANES):
            x_ref[lanes_of(step), start : start + LANES] = jnp.transpose(xt_ref[start : start + LANES, lanes_of(step)])
    fourth.wait()
    fifth.wait()


def heads_kernel(steps, scale, slots, head, ahead, heads, bins, chained, after, *refs):
    refs = list(refs)
    place_ref, xt_ref, x_ref, w1_ref, w2_ref, ho_ref, g_ref, s_ref, rb_ref, vb_ref, hz_ref = refs[:11]
    refs = refs[11:]
    before_ref = refs.pop(0) if chained else None
    refs = refs[after:]
    w1_hbm, w2_hbm = refs[:2] if ahead else (None, None)
    refs = refs[2:] if ahead else refs
    pack_refs, refs = refs[:2], refs[2:]
    dx_ref, loss_ref = refs[:2]
    refs = refs[2:]
    copies = []
    if ahead:
        next1_ref, next2_ref, sems = refs[0], refs[1], refs[-1]
        refs = refs[2:-1]
        copies = load_all([
            (w1_hbm.at[head + 2], next1_ref, sems.at[0]),
            (w2_hbm.at[head + 2], next2_ref, sems.at[1]),
        ])
    (rows_ref, spread_ref, tail_ref, hop_ref, hot_ref, pre_ref, lg_ref, h1_ref, hat1_ref, slope1_ref,
     h2_ref, hat2_ref, slope2_ref, scale_ref, sums_ref, dh_ref, d2_ref, d1_ref, dl_ref, grad_ref) = refs
    latent = w2_ref.shape[0]
    tail_rows = w1_ref.shape[0] - latent
    mine = own_lanes(place_ref)
    horizon_row = hz_ref[:, mine]
    bin_ids = lax.broadcasted_iota(jnp.int32, (LANES, LANES), 0)
    first_end = latent + LANES
    losses = []
    spread_columns(g_ref[head + 1], s_ref[head + 1], rows_ref, spread_ref)
    tail_ref[...] = padded_rows(w1_ref[latent:, :], LANES)
    hot_ref[...] = padded_rows(ho_ref[head], LANES)
    hop_ref[...] = jnp.transpose(hot_ref[...])
    gain1, gain2, shift1, shift2 = [spread_ref.at[place] for place in range(4)]
    pre_ref[...] = tn(w1_ref[0:latent, :], xt_ref[0:latent, :]) + tn(tail_ref[...], xt_ref[latent:, :])
    for step in range(steps):
        mish_forward_low(pre_ref, gain1, shift1, h1_ref, hat1_ref, slope1_ref, scale_ref, 0, lanes_of(step))
    pre_ref[...] = tn(w2_ref[...], h1_ref[...])
    for step in range(steps):
        mish_forward_low(pre_ref, gain2, shift2, h2_ref, hat2_ref, slope2_ref, scale_ref, 1, lanes_of(step))
    lg_ref[...] = nn(hot_ref[...], h2_ref[...])
    share = 0.1 if head == 0 else 0.1 / (heads - 1)
    bins_ref = rb_ref if head == 0 else vb_ref
    for step in range(steps):
        at = lanes_of(step)
        logits = jnp.where(bin_ids < bins, lg_ref[:, at], F32(-1e30))
        chosen = bin_ids == bins_ref[step : step + 1, mine]
        top = jnp.max(logits, axis=0, keepdims=True)
        powers = jnp.exp(logits - top)
        total = column_sum(powers)
        picked = column_sum(jnp.where(chosen, logits, 0.0))
        weight = row_weight(step, steps, scale * share, horizon_row, place_ref)
        losses.append(weight * (jnp.log(total) + top - picked))
        dl_ref[:, at] = (powers * (weight / total) - jnp.where(chosen, weight, 0.0)).astype(BF16)
    dh_ref[...] = nn(hop_ref[...], dl_ref[...]).astype(BF16)
    grad_ref[:, first_end + latent :] = nt(h2_ref[...], dl_ref[...]).astype(BF16)
    mish_backward_low(dh_ref, hat2_ref, slope2_ref, scale_ref, 1, steps, sums_ref, 2, d2_ref)
    dh_ref[...] = nn(w2_ref[...], d2_ref[...]).astype(BF16)
    grad_ref[:, first_end : first_end + latent] = nt(d2_ref[...], h1_ref[...]).astype(BF16)
    mish_backward_low(dh_ref, hat1_ref, slope1_ref, scale_ref, 0, steps, sums_ref, 0, d1_ref)
    low_part = nn(w1_ref[0:latent, :], d1_ref[...])
    side_part = nn(tail_ref[...], d1_ref[...])
    if not chained:
        dx_ref[0:latent, :] = low_part
        dx_ref[latent:, :] = side_part
    else:
        dx_ref[0:latent, :] = before_ref[0:latent, :] + low_part
        dx_ref[latent:, :] = before_ref[latent:, :] + side_part
    grad_ref[:, 0:latent] = nn(d1_ref[...], x_ref[:, 0:latent]).astype(BF16)
    side_terms = nn(d1_ref[...], x_ref[:, latent:])
    side_terms = with_vectors(side_terms, vector_sums(sums_ref, spread_ref, 2), tail_rows)
    grad_ref[:, latent:first_end] = side_terms.astype(BF16)
    for relative, (which, slot) in enumerate(slots):
        start = pl.multiple_of((place_ref[0] ^ relative) * GROUP, GROUP)
        pack_refs[which][slot] = grad_ref[pl.ds(start, GROUP), :]
    loss_ref[...] = functools.reduce(jnp.add, losses)
    for each in copies:
        each.wait()


def backward_kernel(
    steps, scale, order, losses, after,
    place_ref, xt_ref, soft_ref, h1_ref, hat1_ref, slope1_ref, h2_ref, hat2_ref, slope2_ref, scale_ref,
    w1_ref, w2_ref, dyn_ref, hz_ref, g_ref, dx_ref, *rest,
):
    initial = order[0] == steps - 1
    final = order[-1] == 0
    loss_refs, rest = rest[:losses], rest[losses:]
    held_refs, rest = ((), rest) if initial else (rest[:4], rest[4:])
    (tgt_hbm, low_ref, first_ref, side_ref, loss_ref, sums_ref, tgt_ref, rows_ref, spread_ref, tail_ref, pre_ref,
     d1_ref, d2_ref, do_ref, grad_ref, sems) = rest[after:]
    mine = own_lanes(place_ref)
    loads = dict(zip(order, load_all([(tgt_hbm.at[step, mine, :], tgt_ref.at[step], sems.at[step]) for step in order])))
    latent = dyn_ref.shape[1]
    here = slice(0, LANES)
    horizon_row = hz_ref[:, mine]
    spread_columns(g_ref[0], g_ref[0], rows_ref, spread_ref)
    tail_rows = w1_ref.shape[0] - latent
    tail_ref[...] = padded_rows(w1_ref[latent:, :], LANES)
    first_end = latent + LANES
    second_end = first_end + latent
    if initial:
        loss = functools.reduce(jnp.add, [each[...] for each in loss_refs])
        side = jnp.zeros((LANES, LANES), F32)
        incoming = None
    else:
        before_ref, given_ref, given_side_ref, given_sums_ref = held_refs
        loss = loss_refs[0][...]
        side = given_side_ref[...]
        incoming = given_ref[...].astype(F32)
        sums_ref[...] = given_sums_ref[...]
    pending = []

    def add_terms(at, fresh, last):
        terms = (
            (slice(0, first_end), nt(d1_ref[:, at], xt_ref[:, at])),
            (slice(first_end, second_end), nt(d2_ref[:, at], h1_ref[:, at])),
            (slice(second_end, second_end + latent), nt(h2_ref[:, at], do_ref[:, at])),
        )
        for lanes, term in terms:
            if not fresh:
                term = term + grad_ref[:, lanes]
            elif not initial:
                term = term + before_ref[:, lanes]
            out_ref = low_ref if last else grad_ref
            if last and final and lanes.start == 0:
                out_ref[:, 0:latent] = term[:, 0:latent].astype(out_ref.dtype)
                vectors = vector_sums(sums_ref, spread_ref, 2)
                out_ref[:, latent:first_end] = with_vectors(term[:, latent:], vectors, tail_rows).astype(out_ref.dtype)
            else:
                out_ref[:, lanes] = term.astype(out_ref.dtype)

    for step in order:
        at = lanes_of(step)
        weight = row_weight(step, steps, scale, horizon_row, place_ref)
        shares = soft_ref[:, lanes_of(step + 1)]
        loads[step].wait()
        residue = shares - jnp.transpose(tgt_ref[step].astype(F32))
        loss = loss + (20.0 / latent) * weight * column_sum(residue * residue)
        grads = residue * ((40.0 / latent) * weight)
        if incoming is not None:
            grads = grads + incoming
        do_ref[:, at] = simplex_back(shares, grads).astype(BF16)
        pre_ref[...] = nn(dyn_ref[...], do_ref[:, at])
        mish_backward(pre_ref, here, hat2_ref, slope2_ref, scale_ref, 1, at, sums_ref, 2, step == steps - 1, d2_ref)
        pre_ref[...] = nn(w2_ref[...], d2_ref[:, at])
        mish_backward(pre_ref, here, hat1_ref, slope1_ref, scale_ref, 0, at, sums_ref, 0, step == steps - 1, d1_ref)
        incoming = nn(w1_ref[0:latent, :], d1_ref[:, at]) + dx_ref[0:latent, at]
        side = side + nn(tail_ref[...], d1_ref[:, at]) + dx_ref[latent:, at]
        incoming = incoming.astype(BF16).astype(F32)
        pending.append(step)
        if len(pending) == 2 or step == order[-1]:
            low, high = min(pending), max(pending) + 1
            add_terms(slice(low * LANES, high * LANES), high == order[0] + 1, low == order[-1])
            pending = []

    first_ref[...] = incoming.astype(BF16)
    side_ref[...] = side
    loss_ref[...] = loss


def ending_kernel(
    slots, tasks, task_width, acted, observed, after,
    place_ref, low_ref, first_ref, side_ref, loss_ref, soft_ref, ein_ref, eh_ref, ehat_ref, eslope_ref, escale_ref,
    ids_ref, e1_ref, eg_ref, e2_ref, *rest,
):
    out_refs, rest = rest[after : after + 2], rest[after + 2 :]
    erows_ref, espread_ref, e1p_ref, epre_ref, esums_ref, ed_ref, egrad_ref = rest
    mine = own_lanes(place_ref)
    here = slice(0, LANES)
    latent = first_ref.shape[0]
    spread_columns(eg_ref[...], eg_ref[...], erows_ref, espread_ref)
    e1p_ref[...] = padded_rows(e1_ref[...], e1p_ref.shape[0])
    d_enc = simplex_back(soft_ref[:, 0:LANES], first_ref[...].astype(F32)).astype(BF16)
    epre_ref[...] = nn(e2_ref[...], d_enc)
    mish_backward(epre_ref, here, ehat_ref, eslope_ref, escale_ref, 0, here, esums_ref, 0, True, ed_ref)
    side_enc = nn(e1p_ref[...], ed_ref[...])
    enc_width = epre_ref.shape[0]
    half = GROUP // 2
    groups = enc_width // half
    kept = egrad_ref.shape[2]
    enc_second = nt(eh_ref[...], d_enc)
    egrad_ref[:, 0:half, :] = enc_second[:, 0:kept].reshape(groups, half, kept)
    egrad_ref[:, half:, 0 : latent - kept] = enc_second[:, kept:].reshape(groups, half, latent - kept)
    enc_first = nt(ed_ref[...], ein_ref[...])
    egrad_ref[:, half:, latent - kept : kept - LANES] = enc_first[:, 0:LANES].reshape(groups, half, LANES)
    second_lanes = with_vectors(enc_first[:, LANES : 2 * LANES], vector_sums(esums_ref, espread_ref, 1), LANES - 2)
    egrad_ref[:, half:, kept - LANES :] = second_lanes.reshape(groups, half, LANES)

    kinds = lax.broadcasted_iota(jnp.int32, (tasks, LANES), 0)
    onehot = (kinds == ids_ref[:, mine]).astype(F32)
    over_lanes = (((1,), (1,)), ((), ()))
    highest = lax.Precision.HIGHEST
    side_terms = lax.dot_general(onehot, side_ref[...], over_lanes, precision=highest, preferred_element_type=F32)
    enc_terms = lax.dot_general(onehot, side_enc, over_lanes, precision=highest, preferred_element_type=F32)
    table = pltpu.roll(side_terms, LANES - acted, 1)
    table = table + pltpu.roll(enc_terms, enc_terms.shape[1] - observed, 1)[:, 0:LANES]
    lane = lax.broadcasted_iota(jnp.int32, table.shape, 1)
    table = jnp.where(lane < task_width, table, 0.0)
    table = jnp.where((lane == LANES - 1) & (kinds == 0), jnp.sum(loss_ref[...], axis=1, keepdims=True), table)
    table_rows = [table[start : start + GROUP] for start in range(0, tasks, GROUP)]
    table_block = jnp.concatenate(table_rows, axis=1).astype(BF16)
    count = low_ref.shape[1] // LANES
    units = count + kept // LANES
    for relative, (which, slot) in enumerate(slots):
        dest = place_ref[0] ^ relative
        start = pl.multiple_of(dest * GROUP, GROUP)
        block = jnp.concatenate([low_ref[pl.ds(start, GROUP), :], egrad_ref[dest].astype(BF16)], axis=1)
        for unit in range(units):
            out_refs[which][slot * units + unit] = block[:, unit * LANES : (unit + 1) * LANES]
    last = len(slots) // 2 * units
    for unit in range(tasks // GROUP):
        for out_ref in out_refs:
            out_ref[last + unit] = table_block[:, unit * LANES : (unit + 1) * LANES]


def final_kernel(tasks, task_width, enc_in, bins, net_in, *refs):
    outs = refs[-12:]
    (loss_ref, table_ref, e1_ref, eg_ref, es_ref, e2_ref, first_ref, second_ref, gain_ref, shift_ref, dyn_ref, head_ref) = outs
    refs = refs[:-12]
    tail_refs, refs = refs[:4], refs[4:]
    latent = second_ref.shape[2]
    first_end = latent + LANES
    second_end = first_end + latent

    def put_net(net, value):
        first_ref[net] = value[:, 0:net_in]
        second_ref[net] = value[:, first_end:second_end]
        turned = jnp.transpose(value[:, latent:first_end])
        for layer in range(2):
            row = net_in - latent + 2 * layer
            gain_ref[net, layer : layer + 1, :] = turned[row : row + 1, :]
            shift_ref[net, layer : layer + 1, :] = turned[row + 1 : row + 2, :]

    sums = functools.reduce(jnp.add, [ref[...].astype(F32) for ref in tail_refs])
    units = sums.shape[0] - tasks // GROUP
    tail = jnp.concatenate([sums[unit] for unit in range(units)], axis=1)
    put_net(0, tail)
    dyn_ref[...] = tail[:, second_end : second_end + latent]
    enc = tail[:, second_end + latent :]
    half = GROUP // 2
    kept = enc.shape[1]
    e2_ref[:, 0:kept] = 0.3 * enc[0:half, :]
    e2_ref[:, kept:] = 0.3 * enc[half:, 0 : latent - kept]
    e1_ref[...] = 0.3 * enc[half:, latent - kept : latent - kept + enc_in]
    turned = 0.3 * jnp.transpose(enc[half:, kept - LANES :])
    eg_ref[...] = turned[LANES - 2 : LANES - 1, :]
    es_ref[...] = turned[LANES - 1 : LANES, :]
    loss_ref[...] = sums[units, 0:1, LANES - 1 : LANES]
    for place in range(tasks // GROUP):
        table_ref[place * GROUP : (place + 1) * GROUP, :] = sums[units + place, :, 0:task_width]
    net = 1
    for one_ref, other_ref in zip(refs[0::2], refs[1::2]):
        for one in range(one_ref.shape[1]):
            value = one_ref[0, one].astype(F32) + other_ref[0, one].astype(F32)
            put_net(net, value)
            head_ref[net - 1] = value[:, second_end : second_end + bins]
            net += 1


def swap(value, axis, distance):
    count = lax.axis_size(axis)
    return lax.ppermute(value, axis, [(place, place ^ distance) for place in range(count)])


def exchange(parts, axis, scale):
    total = parts[0].astype(F32)
    for distance in range(1, len(parts)):
        total = total + swap(parts[distance], axis, distance * scale).astype(F32)
    return total


def scatter_plain(packed, chips, sections):
    held = packed.reshape((sections, chips, CORES) + packed.shape[1:])
    batch_no = lax.axis_index("batch")
    places = (
        ("batch", 1, CORES, 2, batch_no % CORES),
        ("batch", CORES, chips, 1, batch_no // CORES),
        ("section", 1, sections, 0, lax.axis_index("section")),
    )
    for axis, scale, count, dim, mine in places:
        parts = [lax.dynamic_index_in_dim(held, mine ^ other, dim, keepdims=False) for other in range(count)]
        held = exchange(parts, axis, scale)
        held = held.astype(BF16) if dim else held
    return held


def on_device(
    observations,
    actions,
    targets,
    task_ids,
    horizons,
    reward_bins,
    value_bins,
    task_table,
    enc_first,
    enc_gain,
    enc_shift,
    enc_second,
    net_first,
    net_second,
    net_gain,
    net_shift,
    dyn_out,
    head_out,
):
    sections = lax.axis_size("section")
    batches = lax.axis_size("batch")
    section_no = lax.axis_index("section")
    chips = batches // CORES
    devices = sections * batches
    steps, rows_all, acted = actions.shape
    observed = observations.shape[1]
    rows = rows_all // sections
    latent = dyn_out.shape[1]
    hidden = dyn_out.shape[0]
    tasks, task_width = task_table.shape
    heads, _, bins = head_out.shape
    nets, net_in, _ = net_first.shape
    enc_in, enc_width = enc_first.shape
    wide = steps * LANES
    scale = 1.0 / (rows_all * batches * steps)
    groups = hidden // GROUP
    in_place = hidden // devices == GROUP
    start = section_no * rows
    block_no = start // LANES
    first_lane = start - block_no * LANES
    me = section_no * batches + lax.axis_index("batch") if in_place else jnp.int32(0)
    place = jnp.stack([me, block_no, first_lane, first_lane + rows]).astype(jnp.int32)
    bits = [("batch", 1 << bit) for bit in range(batches.bit_length() - 1)]
    bits += [("section", 1 << bit) for bit in range(sections.bit_length() - 1)]

    def slots_of(order):
        if not in_place:
            return tuple((relative // (groups // 2), relative % (groups // 2)) for relative in range(groups))
        found = []
        for relative in range(groups):
            slot = 0
            for bit in order:
                slot = 2 * slot + (relative >> bit & 1)
            found.append((slot // (groups // 2), slot % (groups // 2)))
        return tuple(found)

    plain = tuple(range(len(bits)))
    half_slots = groups // 2
    shape_of = jax.ShapeDtypeStruct
    smem = pl.BlockSpec(memory_space=pltpu.SMEM)
    local = pl.BlockSpec(memory_space=pltpu.VMEM)
    far = pl.BlockSpec(memory_space=pltpu.HBM)
    anywhere = pl.BlockSpec(memory_space=pl.ANY)
    first_far, second_far, dyn_far, targets_far = [
        pltpu.with_memory_space_constraint(array, pltpu.HBM) for array in (net_first, net_second, dyn_out, targets)
    ]
    vmem = pltpu.VMEM
    dmas = pltpu.SemaphoreType.DMA

    def params(mebibytes):
        return pltpu.CompilerParams(vmem_limit_bytes=mebibytes * 1024 * 1024)

    def cost(flops, moved):
        return pl.CostEstimate(flops=flops, bytes_accessed=moved, transcendentals=0)

    ids_row = task_ids.reshape(1, rows_all)
    horizon_row = horizons.reshape(1, rows_all)
    eg_row = enc_gain.reshape(1, enc_width)
    es_row = enc_shift.reshape(1, enc_width)
    head_turned = head_out.transpose(0, 2, 1)
    low = lambda lanes: shape_of((hidden, lanes), BF16)
    forward_shapes = (
        shape_of((latent + LANES, wide), BF16),
        shape_of((latent, wide + LANES), F32),
        low(wide), low(wide), low(wide), low(wide), low(wide), low(wide),
        shape_of((8, wide), F32),
        shape_of((2 * LANES, LANES), BF16),
        shape_of((enc_width, LANES), BF16),
        shape_of((enc_width, LANES), BF16),
        shape_of((enc_width, LANES), BF16),
        shape_of((8, LANES), F32),
        shape_of((net_in, hidden), BF16),
        shape_of((hidden, hidden), BF16),
        shape_of((hidden, latent), BF16),
        shape_of((wide, latent + LANES), BF16),
    )

    weight_shapes = (shape_of((net_in, hidden), BF16), shape_of((hidden, hidden), BF16))

    early = [
        pltpu.with_memory_space_constraint(array, pltpu.HBM)
        for array in (
            observations.T, actions.transpose(0, 2, 1), ids_row, task_table, enc_first, eg_row, es_row, enc_second,
            net_gain, net_shift,
        )
    ]
    made = pl.pallas_call(
        functools.partial(forward_kernel, steps),
        out_shape=forward_shapes + weight_shapes,
        in_specs=[smem] + [far] * 13,
        out_specs=[local] * (len(forward_shapes) + 2),
        scratch_shapes=[
            vmem((8, hidden), F32),
            vmem((4, hidden, LANES), F32),
            vmem((8, enc_width), F32),
            vmem((2, enc_width, LANES), F32),
            vmem((tasks, 2 * LANES), F32),
            vmem((LANES, LANES), F32),
            vmem((2 * LANES, enc_width), BF16),
            vmem((hidden, latent + LANES), BF16),
            vmem((hidden, hidden), BF16),
            vmem((latent, hidden), BF16),
            vmem((hidden, LANES), F32),
            vmem((enc_width, LANES), F32),
            *[vmem(each.shape, each.dtype) for each in early],
            dmas((5,)),
            dmas((len(early),)),
        ],
        compiler_params=params(VMEM_A),
        cost_estimate=cost(10_000_000_000, 8_000_000),
        name="forward_chain",
    )(
        place, *early, first_far, second_far, dyn_far,
    )
    saved, x_rows, weights = made[:-3], made[-3], made[-2:]
    xt = saved[0]
    head_width = latent + LANES + hidden + LANES

    def run_head(head, ahead, weights, before, after):
        pack_shapes = [shape_of((half_slots, GROUP, head_width), BF16)] * 2
        dx_shape = shape_of((latent + LANES, wide), F32)
        out_shapes = (*pack_shapes, dx_shape, shape_of((1, LANES), F32))
        args = [place, xt, x_rows, *weights, head_turned, net_gain, net_shift, reward_bins, value_bins, horizon_row]
        specs = [smem] + [local] * 10
        aliases = {}
        if before is not None:
            aliases = {len(args): len(pack_shapes)}
            args.append(before)
            specs.append(local)
        args += after
        specs += [anywhere] * len(after)
        if ahead:
            args += [first_far, second_far]
            specs += [far, far]
            out_shapes += weight_shapes
        low_wide = vmem((hidden, wide), BF16)
        scratch = [
            vmem((8, hidden), F32),
            vmem((4, hidden, LANES), F32),
            vmem((LANES, hidden), BF16),
            vmem((hidden, LANES), BF16),
            vmem((LANES, hidden), BF16),
            vmem((hidden, wide), F32),
            vmem((LANES, wide), F32),
        ]
        scratch += [low_wide] * 6
        scratch += [vmem((8, wide), F32), vmem((4, hidden, LANES), F32)]
        scratch += [low_wide] * 3
        scratch += [vmem((LANES, wide), BF16), vmem((hidden, head_width), BF16)]
        if ahead:
            scratch.append(dmas((2,)))
        return pl.pallas_call(
            functools.partial(
                heads_kernel, steps, scale, slots_of(plain), head, ahead, heads, bins, before is not None, len(after)
            ),
            out_shape=out_shapes,
            in_specs=specs,
            out_specs=[local] * len(out_shapes),
            scratch_shapes=scratch,
            input_output_aliases=aliases,
            compiler_params=params(VMEM_B),
            cost_estimate=cost(9_000_000_000, 4_000_000),
            name=f"head_{head}",
        )(*args)

    def phase(pair, bit):
        return pair[0], swap(pair[1], *bits[bit])

    def fold(members, *tokens):
        slots_now = members[0][0].shape[0] // 2
        shape = members[0][0].shape[1:]
        stacked = len(shape) == 3
        if stacked:
            shape = (len(members) * shape[0],) + shape[1:]
        elif len(members) > 1:
            shape = (len(members),) + shape
        out_shape = shape_of((slots_now,) + shape, BF16)

        def fold_kernel(*refs):
            refs = refs[len(tokens) :]
            outs = refs[-2:]
            for place, member in enumerate(members):
                part_refs, refs = refs[: len(member)], refs[len(member) :]
                for half in range(2):
                    part = pl.ds(half * slots_now, slots_now)
                    value = functools.reduce(jnp.add, [ref[part].astype(F32) for ref in part_refs]).astype(BF16)
                    if stacked:
                        count = part_refs[0].shape[1]
                        outs[half][:, place * count : (place + 1) * count] = value
                    elif len(members) > 1:
                        outs[half][:, place] = value
                    else:
                        outs[half][...] = value

        inputs = [each for member in members for each in member]
        return pl.pallas_call(
            fold_kernel,
            out_shape=(out_shape, out_shape),
            in_specs=[anywhere] * len(tokens) + [local] * len(inputs),
            out_specs=(local, local),
            compiler_params=params(VMEM_SUM),
            cost_estimate=cost(1_000_000, 2_000_000),
            name="fold",
        )(*tokens, *inputs)

    def fold_direct(parts, common, *tokens):
        quarter = (parts[0].shape[0] - common) // 4
        out_shape = shape_of((quarter + common,) + parts[0].shape[1:], BF16)

        def fold_kernel(*refs):
            refs = refs[len(tokens) :]
            outs = refs[-4:]

            def added(start, size):
                each = [ref[pl.ds(start, size)].astype(F32) for ref in refs[: len(parts)]]
                return functools.reduce(jnp.add, each).astype(BF16)

            for place, out in enumerate(outs):
                out[0:quarter] = added(place * quarter, quarter)
            if common:
                shared = added(4 * quarter, common)
                for out in outs:
                    out[quarter:] = shared

        return pl.pallas_call(
            fold_kernel,
            out_shape=(out_shape,) * 4,
            in_specs=[anywhere] * len(tokens) + [local] * len(parts),
            out_specs=(local,) * 4,
            compiler_params=params(VMEM_SUM),
            cost_estimate=cost(1_000_000, 2_000_000),
            name="fold_direct",
        )(*tokens, *parts)

    def direct(pieces, axis, high, low):
        distances = (0, low, high, high + low)
        came = [swap(pieces[place], axis, distances[place]) for place in (3, 2, 1)]
        return [pieces[0], *came]

    net_width = latent + LANES + hidden + latent
    chain_inputs = saved[:9] + saved[14:]

    def run_backward(order, losses, held, after):
        final = order[-1] == 0
        out_shapes = (
            shape_of((hidden, net_width), BF16 if final else F32),
            shape_of((latent, LANES), BF16),
            shape_of((LANES, LANES), F32),
            shape_of((1, LANES), F32),
            shape_of((4, hidden, LANES), F32),
        )
        args = [place, *chain_inputs, horizon_row, net_gain, dx, *losses, *held]
        return pl.pallas_call(
            functools.partial(backward_kernel, steps, scale, order, len(losses), len(after)),
            out_shape=out_shapes,
            in_specs=[smem] + [local] * (len(args) - 1) + [anywhere] * len(after) + [far],
            out_specs=[local] * len(out_shapes),
            scratch_shapes=[
                vmem((steps, LANES, latent), BF16),
                vmem((8, hidden), F32),
                vmem((4, hidden, LANES), F32),
                vmem((LANES, hidden), BF16),
                vmem((hidden, LANES), F32),
                vmem((hidden, wide), BF16),
                vmem((hidden, wide), BF16),
                vmem((latent, wide), BF16),
                vmem((hidden, net_width), F32),
                dmas((steps,)),
            ],
            compiler_params=params(VMEM_C),
            cost_estimate=cost(7_000_000_000, 8_000_000),
            name=f"backward_{order[0]}",
        )(*args, *after, targets_far)

    packs, loss_parts = [], []
    dx = None
    after = []
    cores, pairs = [], []
    for head in range(heads):
        result = run_head(head, head + 1 < heads, weights, dx, after)
        dx, loss = result[2:4]
        weights = result[4:]
        packs.append(result[:2])
        loss_parts.append(loss)
        after = []
        if in_place:
            if head >= 1:
                crossing = fold([cores[head - 1]], loss)
                after.append(crossing[0])
                pairs.append(phase(crossing, plain[1]))
            if head in (3, 5):
                crossing = fold(pairs[head - 3 : head - 1], loss)
                after.append(crossing[0])
                pairs[head - 3] = phase(crossing, plain[2])
            cores.append(phase(result[0:2], plain[0]))
    half_way = steps // 2
    chain = run_backward(tuple(range(steps - 1, half_way - 1, -1)), loss_parts, [], after)
    after = []
    if in_place:
        token = chain[3]
        fifth = fold_direct(cores[heads - 1], 0, token)
        fourth = fold([pairs[heads - 2]], token)
        group = fold([pairs[0], pairs[2]], token)
        after = [fifth[0], fourth[0], group[0]]
        fifth = direct(fifth, "batch", CORES, 2 * CORES)
        group = phase(group, plain[3])
        fourth = phase(fourth, plain[2])
    chain = run_backward(
        tuple(range(half_way - 1, -1, -1)), [chain[3]], [chain[0], chain[1], chain[2], chain[4]], after
    )
    after = []
    if in_place:
        token = chain[3]
        group = fold([group], token)
        last = fold([fourth, fifth], token)
        after = [group[0], last[0]]
        group = phase(group, plain[4])
        last = phase(last, plain[3])

    enc_lanes = latent - LANES
    units = (net_width + enc_lanes) // LANES
    common = tasks // GROUP
    tail_shape = shape_of((half_slots * units + common, GROUP, LANES), BF16)
    ended = pl.pallas_call(
        functools.partial(ending_kernel, slots_of(plain), tasks, task_width, acted, observed, len(after)),
        out_shape=(tail_shape, tail_shape),
        in_specs=[smem] + [local] * 14 + [anywhere] * len(after),
        out_specs=[local] * 2,
        scratch_shapes=[
            vmem((8, enc_width), F32),
            vmem((2, enc_width, LANES), F32),
            vmem((2 * LANES, enc_width), BF16),
            vmem((enc_width, LANES), F32),
            vmem((2, enc_width, LANES), F32),
            vmem((enc_width, LANES), BF16),
            vmem((groups, GROUP, enc_lanes), F32),
        ],
        compiler_params=params(VMEM_SUM),
        cost_estimate=cost(1_000_000_000, 4_000_000),
        name="ending",
    )(place, *chain[:4], saved[1], *saved[9:14], ids_row, enc_first, eg_row, enc_second, *after)

    if in_place:
        pieces = fold_direct(phase(ended, plain[0]), common, last[1])
        tail = direct(pieces, "batch", CORES, 2 * CORES)
        last = phase(fold([last], ended[0]), plain[4])
        pieces = fold_direct(tail, common, last[1], group[1])
        tail = direct(pieces, "section", 1, 2)
        each = GROUP // 2
        out_shapes = (
            shape_of((1, 1), F32),
            shape_of((tasks, task_width), F32),
            shape_of((each, enc_in), F32),
            shape_of((1, each), F32),
            shape_of((1, each), F32),
            shape_of((each, latent), F32),
            shape_of((nets, GROUP, net_in), F32),
            shape_of((nets, GROUP, hidden), F32),
            shape_of((nets, 2, GROUP), F32),
            shape_of((nets, 2, GROUP), F32),
            shape_of((GROUP, latent), F32),
            shape_of((heads, GROUP, bins), F32),
        )
        ends = [*tail, *group, *last]
        outs = list(pl.pallas_call(
            functools.partial(final_kernel, tasks, task_width, enc_in, bins, net_in),
            out_shape=out_shapes,
            in_specs=[local] * len(ends),
            out_specs=[local] * len(out_shapes),
            compiler_params=params(VMEM_SUM),
            cost_estimate=cost(1_000_000, 4_000_000),
            name="last_sums",
        )(*ends))
        outs[0] = outs[0].reshape(())
        outs[2] = outs[2].T
        outs[3], outs[4] = outs[3].reshape(each), outs[4].reshape(each)
        outs[6] = outs[6].transpose(0, 2, 1)
        outs[7] = outs[7].transpose(0, 2, 1)
        return tuple(outs)

    def scattered(keep, send):
        mine = hidden // devices
        packed = jnp.concatenate([keep, send], axis=0)
        middle = packed.shape[1:-2]
        packed = packed.reshape((groups,) + middle + (GROUP // mine, mine, packed.shape[-1]))
        packed = jnp.moveaxis(packed, -3, 1).reshape((devices,) + middle + (mine, packed.shape[-1]))
        return scatter_plain(packed, chips, sections)

    head_sum = jnp.stack([scattered(*pack) for pack in packs], axis=0)
    enc_each = enc_width // devices
    def by_rows(array):
        joined = array[: half_slots * units].reshape(half_slots, units, GROUP, LANES).transpose(0, 2, 1, 3)
        return joined.reshape(half_slots, GROUP, units * LANES)

    keep, send = by_rows(ended[0]), by_rows(ended[1])
    table_sum = lax.psum(ended[0][half_slots * units :].astype(F32), ("section", "batch"))
    table_sum = table_sum.transpose(1, 0, 2).reshape(GROUP, common * LANES)
    net_sum = scattered(keep[:, :, 0:net_width], send[:, :, 0:net_width])
    enc_all = jnp.concatenate([keep, send], axis=0)[:, :, net_width:]
    enc_all = enc_all.reshape(groups, 2, enc_width // groups, enc_lanes)
    enc_all = enc_all.transpose(0, 2, 1, 3).reshape(devices, enc_each, 2, enc_lanes)
    enc_sum = scatter_plain(enc_all, chips, sections)
    enc_low, enc_high = enc_sum[:, 0], enc_sum[:, 1]
    s_enc_second = jnp.concatenate([enc_low, enc_high[:, 0 : latent - enc_lanes]], axis=1)
    enc_rows = enc_high[:, latent - enc_lanes :]
    first_end = latent + LANES
    net_row = jnp.concatenate([net_sum[:, 0 : first_end + hidden], jnp.zeros_like(net_sum[:, 0:LANES])], axis=1)
    sums = jnp.concatenate([net_row[None], head_sum], axis=0)
    vectors = sums[:, :, net_in : net_in + 4].transpose(0, 2, 1)
    table = table_sum.reshape(GROUP, tasks // GROUP, LANES).transpose(1, 0, 2).reshape(tasks, LANES)
    return (
        table[0, LANES - 1],
        table[:, 0:task_width],
        0.3 * enc_rows[:, 0:enc_in].T,
        0.3 * enc_rows[:, 2 * LANES - 2],
        0.3 * enc_rows[:, 2 * LANES - 1],
        0.3 * s_enc_second,
        sums[:, :, 0:net_in].transpose(0, 2, 1),
        sums[:, :, first_end : first_end + hidden].transpose(0, 2, 1),
        vectors[:, 0::2],
        vectors[:, 1::2],
        net_sum[:, first_end + hidden :],
        head_sum[:, :, first_end + hidden : first_end + hidden + bins],
    )


def solution(mesh):
    both = ("section", "batch")
    return jax.shard_map(
        on_device,
        mesh=mesh,
        in_specs=(
            P("batch", None),
            P(None, "batch", None),
            P(None, "batch", None),
            P("batch"),
            P("batch"),
            P(None, "batch"),
            P(None, "batch"),
        )
        + (P(),) * 11,
        out_specs=(
            P(),
            P(),
            P(None, both),
            P(both),
            P(both),
            P(both, None),
            P(None, None, both),
            P(None, None, both),
            P(None, None, both),
            P(None, None, both),
            P(both, None),
            P(None, both, None),
        ),
        check_vma=False,
    )
```

```python
import functools

import jax
import jax.numpy as jnp
from jax import lax
from jax.experimental import pallas as pl
from jax.experimental.pallas import tpu as pltpu
from jax.sharding import PartitionSpec as P

CORES = 2
LANES = 128
GROUP = 16
BF16 = jnp.bfloat16
F32 = jnp.float32
VMEM_A = 18
VMEM_B = 20
VMEM_SUM = 6
VMEM_C = 20


def nn(left, right):
    return lax.dot_general(left, right, (((1,), (0,)), ((), ())), preferred_element_type=F32)


def nt(left, right):
    return lax.dot_general(left, right, (((1,), (1,)), ((), ())), preferred_element_type=F32)


def tn(left, right):
    return lax.dot_general(left, right, (((0,), (0,)), ((), ())), preferred_element_type=F32)


def column_sum(value):
    grouped = value.reshape(value.shape[0] // 8, 8, value.shape[1])
    return jnp.sum(jnp.sum(grouped, axis=0), axis=0, keepdims=True)


def slabs(features, size=64):
    return [slice(start, start + size) for start in range(0, features, size)]


def lanes_of(step):
    return slice(step * LANES, (step + 1) * LANES)


def spread_columns(gain_rows, shift_rows, rows_ref, spread_ref):
    count = gain_rows.shape[0]
    rows_ref[...] = jnp.zeros_like(rows_ref)
    rows_ref[0:count, :] = gain_rows
    rows_ref[count : 2 * count, :] = shift_rows
    turned = jnp.transpose(rows_ref[...])
    for place in range(2 * count):
        spread_ref[place] = jnp.broadcast_to(turned[:, place : place + 1], spread_ref.shape[1:])


def mish_forward(pre_ref, pre_at, gain_ref, shift_ref, hid_ref, hat_ref, slope_ref, scale_ref, scale_row, at):
    features = pre_ref.shape[0]
    row_mean = column_sum(pre_ref[:, pre_at]) * (1.0 / features)
    centred = pre_ref[:, pre_at] - row_mean
    spread = column_sum(centred * centred) * (1.0 / features)
    scale = lax.rsqrt(spread + 1e-05)
    scale_ref[scale_row : scale_row + 1, at] = scale
    for part in slabs(features):
        hat = (pre_ref[part, pre_at] - row_mean) * scale
        normed = hat * gain_ref[part, :] + shift_ref[part, :]
        power = jnp.exp(normed)
        top = power * (power + 2.0)
        inverse = pl.reciprocal(top + 2.0, approx=True)
        ratio = top * inverse
        hid_ref[part, at] = (normed * ratio).astype(BF16)
        tilt = power * inverse
        slope = ratio + normed * (4.0 * (tilt * (tilt + inverse)))
        slope_ref[part, at] = (slope * gain_ref[part, :]).astype(BF16)
        hat_ref[part, at] = hat.astype(BF16)


def mish_backward(grad_ref, grad_at, hat_ref, slope_ref, scale_ref, scale_row, at, sums_ref, sums_at, first, out_ref):
    features = grad_ref.shape[0]
    total_one = jnp.zeros((8, LANES), F32)
    total_two = jnp.zeros((8, LANES), F32)
    for part in slabs(features):
        term = grad_ref[part, grad_at] * slope_ref[part, at].astype(F32)
        grad_ref[part, grad_at] = term
        crossed = term * hat_ref[part, at].astype(F32)
        groups = (term.shape[0] // 8, 8, LANES)
        total_one = total_one + jnp.sum(term.reshape(groups), axis=0)
        total_two = total_two + jnp.sum(crossed.reshape(groups), axis=0)
        if first:
            sums_ref[sums_at, part, :] = term
            sums_ref[sums_at + 1, part, :] = crossed
        else:
            sums_ref[sums_at, part, :] += term
            sums_ref[sums_at + 1, part, :] += crossed
    mean_one = jnp.sum(total_one, axis=0, keepdims=True) * (1.0 / features)
    mean_two = jnp.sum(total_two, axis=0, keepdims=True) * (1.0 / features)
    scale = scale_ref[scale_row : scale_row + 1, at]
    for part in slabs(features):
        rest = grad_ref[part, grad_at] - mean_one - hat_ref[part, at].astype(F32) * mean_two
        out_ref[part, at] = (rest * scale).astype(BF16)


def mish_forward_low(pre_ref, gain_ref, shift_ref, hid_ref, hat_ref, slope_ref, scale_ref, scale_row, at):
    features = pre_ref.shape[0]
    row_mean = column_sum(pre_ref[:, at]) * (1.0 / features)
    centred = pre_ref[:, at] - row_mean
    spread = column_sum(centred * centred) * (1.0 / features)
    scale = lax.rsqrt(spread + 1e-05)
    scale_ref[scale_row : scale_row + 1, at] = scale
    for part in slabs(features):
        hat = (pre_ref[part, at] - row_mean) * scale
        normed = (hat * gain_ref[part, :] + shift_ref[part, :]).astype(BF16)
        hat_ref[part, at] = hat.astype(BF16)
        power = jnp.exp(normed)
        top = power * (power + 2.0)
        inverse = pl.reciprocal(top + 2.0, approx=True)
        ratio = top * inverse
        hid_ref[part, at] = normed * ratio
        tilt = power * inverse
        slope = ratio + (4.0 * normed) * (tilt * (tilt + inverse))
        slope_ref[part, at] = slope * gain_ref[part, :].astype(BF16)


def mish_backward_low(grad_ref, hat_ref, slope_ref, scale_ref, scale_row, steps, sums_ref, sums_at, out_ref):
    features = grad_ref.shape[0]
    rows = []
    for step in range(steps):
        at = lanes_of(step)
        total_one = jnp.zeros((16, LANES), F32)
        total_two = jnp.zeros((16, LANES), F32)
        for part in slabs(features):
            term = grad_ref[part, at] * slope_ref[part, at]
            crossed = term * hat_ref[part, at]
            grad_ref[part, at] = term
            groups = (term.shape[0] // 16, 16, LANES)
            term = term.reshape(groups)
            crossed = crossed.reshape(groups)
            total_one = total_one + functools.reduce(jnp.add, [term[k] for k in range(groups[0])]).astype(F32)
            total_two = total_two + functools.reduce(jnp.add, [crossed[k] for k in range(groups[0])]).astype(F32)
        scale = scale_ref[scale_row : scale_row + 1, at]
        mean_one = jnp.sum(total_one, axis=0, keepdims=True) * (1.0 / features)
        mean_two = jnp.sum(total_two, axis=0, keepdims=True) * (1.0 / features)
        rows.append((mean_one.astype(BF16), mean_two.astype(BF16), scale.astype(BF16)))
    for part in slabs(features):
        sum_one, sum_two = None, None
        for step, (mean_one, mean_two, scale) in enumerate(rows):
            at = lanes_of(step)
            term = grad_ref[part, at]
            hat = hat_ref[part, at]
            out_ref[part, at] = (term - mean_one - hat * mean_two) * scale
            crossed = term * hat
            sum_one = term if sum_one is None else sum_one + term
            sum_two = crossed if sum_two is None else sum_two + crossed
        sums_ref[sums_at, part, :] = sum_one.astype(F32)
        sums_ref[sums_at + 1, part, :] = sum_two.astype(F32)


def simplex(values):
    grouped = values.reshape(values.shape[0] // 8, 8, values.shape[1])
    powers = jnp.exp(grouped - jnp.max(grouped, axis=1, keepdims=True))
    shares = powers / jnp.sum(powers, axis=1, keepdims=True)
    return shares.reshape(values.shape)


def simplex_back(shares, grads):
    grouped = (shares.shape[0] // 8, 8, shares.shape[1])
    crossed = jnp.sum((shares * grads).reshape(grouped), axis=1, keepdims=True)
    return (shares.reshape(grouped) * (grads.reshape(grouped) - crossed)).reshape(shares.shape)


def row_weight(step, steps, scale, horizon_row, place_ref):
    lane = lax.broadcasted_iota(jnp.int32, (1, LANES), 1)
    mine = (lane >= place_ref[2]) & (lane < place_ref[3]) & (horizon_row > step)
    return jnp.where(mine, F32(scale * 0.5 ** (step / (steps - 1))), 0.0)


def padded_rows(value, rows):
    zeros = jnp.zeros((rows - value.shape[0], value.shape[1]), F32)
    return jnp.concatenate([value.astype(F32), zeros], axis=0).astype(BF16)


def transpose_into(out_ref, source_ref, rows):
    for start in range(0, rows, LANES):
        out_ref[:, start : start + LANES] = jnp.transpose(source_ref[start : start + LANES, :])


def vector_sums(sums_ref, gains_ref, layers):
    vectors = []
    for layer in range(layers):
        inverse = 1.0 / gains_ref[layer]
        vectors.append(jnp.sum(sums_ref[2 * layer + 1] * inverse, axis=1, keepdims=True))
        vectors.append(jnp.sum(sums_ref[2 * layer] * inverse, axis=1, keepdims=True))
    return vectors


def own_lanes(place_ref):
    return pl.ds(pl.multiple_of(place_ref[1] * LANES, LANES), LANES)


def load_all(copies):
    made = [pltpu.make_async_copy(*each) for each in copies]
    for each in made:
        each.start()
    return made


def with_vectors(value, vectors, first_lane):
    lane = lax.broadcasted_iota(jnp.int32, value.shape, 1)
    for place, vector in enumerate(vectors):
        value = jnp.where(lane == first_lane + place, vector, value)
    return value


def forward_kernel(
    steps,
    place_ref, obs_hbm, act_hbm, ids_hbm, table_hbm, e1_hbm, eg_hbm, es_hbm, e2_hbm, g_hbm, s_hbm,
    w1_hbm, w2_hbm, dyn_hbm,
    xt_ref, soft_ref, h1_ref, hat1_ref, slope1_ref, h2_ref, hat2_ref, slope2_ref, scale_ref,
    ein_ref, eh_ref, ehat_ref, eslope_ref, escale_ref,
    w1_ref, w2_ref, dyn_ref, x_ref, next1_ref, next2_ref,
    rows_ref, spread_ref, erows_ref, espread_ref, wide_ref, tall_ref, e1p_ref, w1t_ref, w2t_ref, dynt_ref, pre_ref, epre_ref,
    obs_ref, act_ref, ids_ref, table_ref, e1_ref, eg_ref, es_ref, e2_ref, g_ref, s_ref,
    sems, early_sems,
):
    early = load_all([
        (table_hbm, table_ref, early_sems.at[0]),
        (ids_hbm, ids_ref, early_sems.at[1]),
        (obs_hbm, obs_ref, early_sems.at[2]),
        (e1_hbm, e1_ref, early_sems.at[3]),
        (eg_hbm, eg_ref, early_sems.at[4]),
        (es_hbm, es_ref, early_sems.at[5]),
        (e2_hbm, e2_ref, early_sems.at[6]),
        (act_hbm, act_ref, early_sems.at[7]),
        (g_hbm, g_ref, early_sems.at[8]),
        (s_hbm, s_ref, early_sems.at[9]),
    ])
    first, second, third, fourth, fifth = load_all([
        (w1_hbm.at[0], w1_ref, sems.at[0]),
        (w2_hbm.at[0], w2_ref, sems.at[1]),
        (dyn_hbm, dyn_ref, sems.at[2]),
        (w1_hbm.at[1], next1_ref, sems.at[3]),
        (w2_hbm.at[1], next2_ref, sems.at[4]),
    ])
    latent = dyn_ref.shape[1]
    tasks, task_width = table_ref.shape
    observed = obs_ref.shape[0]
    acted = act_ref.shape[1]
    mine = own_lanes(place_ref)
    for each in early:
        each.wait()
    spread_columns(eg_ref[...], es_ref[...], erows_ref, espread_ref)
    kinds = lax.broadcasted_iota(jnp.int32, (tasks, LANES), 0)
    onehot = (kinds == ids_ref[:, mine]).astype(F32).astype(BF16)
    wide_ref[...] = jnp.zeros_like(wide_ref)
    wide_ref[:, 0:task_width] = table_ref[...].astype(F32)
    table_tail = pltpu.roll(wide_ref[:, 0:LANES], acted, 1).astype(BF16)
    table_enc = pltpu.roll(wide_ref[...], observed, 1).astype(BF16)
    aux = tn(table_tail, onehot)
    tall_ref[...] = jnp.zeros_like(tall_ref)
    tall_ref[0:observed, :] = obs_ref[:, mine].astype(F32)
    ein = tn(table_enc, onehot)
    ein_ref[0:LANES, :] = (ein[0:LANES] + tall_ref[...]).astype(BF16)
    ein_ref[LANES:, :] = ein[LANES:].astype(BF16)
    e1p_ref[...] = padded_rows(e1_ref[...], e1p_ref.shape[0])
    epre_ref[...] = tn(e1p_ref[...], ein_ref[...])
    here = slice(0, LANES)
    mish_forward(epre_ref, here, espread_ref.at[0], espread_ref.at[1], eh_ref, ehat_ref, eslope_ref, escale_ref, 0, here)
    shares = simplex(tn(e2_ref[...], eh_ref[...]))
    soft_ref[:, 0:LANES] = shares
    xt_ref[0:latent, 0:LANES] = shares.astype(BF16)
    spread_columns(g_ref[0], s_ref[0], rows_ref, spread_ref)
    for step in range(steps):
        tall_ref[...] = jnp.zeros_like(tall_ref)
        tall_ref[0:acted, :] = act_ref[step, :, mine].astype(F32)
        xt_ref[latent:, lanes_of(step)] = (aux + tall_ref[...]).astype(BF16)
    first.wait()
    transpose_into(w1t_ref, w1_ref, latent)
    w1t_ref[:, latent:] = jnp.transpose(padded_rows(w1_ref[latent:, :], LANES))
    second.wait()
    transpose_into(w2t_ref, w2_ref, latent)
    third.wait()
    transpose_into(dynt_ref, dyn_ref, latent)
    for step in range(steps):
        at = lanes_of(step)
        pre_ref[...] = nn(w1t_ref[...], xt_ref[:, at])
        mish_forward(pre_ref, here, spread_ref.at[0], spread_ref.at[2], h1_ref, hat1_ref, slope1_ref, scale_ref, 0, at)
        pre_ref[...] = nn(w2t_ref[...], h1_ref[:, at])
        mish_forward(pre_ref, here, spread_ref.at[1], spread_ref.at[3], h2_ref, hat2_ref, slope2_ref, scale_ref, 1, at)
        shares = simplex(nn(dynt_ref[...], h2_ref[:, at]))
        soft_ref[:, lanes_of(step + 1)] = shares
        if step + 1 < steps:
            xt_ref[0:latent, lanes_of(step + 1)] = shares.astype(BF16)
    for step in range(steps):
        for start in range(0, latent + LANES, LANES):
            x_ref[lanes_of(step), start : start + LANES] = jnp.transpose(xt_ref[start : start + LANES, lanes_of(step)])
    fourth.wait()
    fifth.wait()


def heads_kernel(steps, scale, packs, head, ahead, heads, bins, chained, after, *refs):
    refs = list(refs)
    place_ref, xt_ref, x_ref, w1_ref, w2_ref, ho_ref, g_ref, s_ref, rb_ref, vb_ref, hz_ref = refs[:11]
    refs = refs[11:]
    before_ref = refs.pop(0) if chained else None
    refs = refs[after:]
    w1_hbm, w2_hbm = refs[:2] if ahead else (None, None)
    refs = refs[2:] if ahead else refs
    pack_refs, refs = refs[: 2 * len(packs)], refs[2 * len(packs) :]
    dx_ref, loss_ref = refs[:2]
    refs = refs[2:]
    copies = []
    if ahead:
        next1_ref, next2_ref, sems = refs[0], refs[1], refs[-1]
        refs = refs[2:-1]
        copies = load_all([
            (w1_hbm.at[head + 2], next1_ref, sems.at[0]),
            (w2_hbm.at[head + 2], next2_ref, sems.at[1]),
        ])
    (rows_ref, spread_ref, tail_ref, hop_ref, hot_ref, pre_ref, lg_ref, h1_ref, hat1_ref, slope1_ref,
     h2_ref, hat2_ref, slope2_ref, scale_ref, sums_ref, dh_ref, d2_ref, d1_ref, dl_ref, grad_ref) = refs
    latent = w2_ref.shape[0]
    tail_rows = w1_ref.shape[0] - latent
    mine = own_lanes(place_ref)
    horizon_row = hz_ref[:, mine]
    bin_ids = lax.broadcasted_iota(jnp.int32, (LANES, LANES), 0)
    first_end = latent + LANES
    losses = []
    spread_columns(g_ref[head + 1], s_ref[head + 1], rows_ref, spread_ref)
    tail_ref[...] = padded_rows(w1_ref[latent:, :], LANES)
    hot_ref[...] = padded_rows(ho_ref[head], LANES)
    hop_ref[...] = jnp.transpose(hot_ref[...])
    gain1, gain2, shift1, shift2 = [spread_ref.at[place] for place in range(4)]
    pre_ref[...] = tn(w1_ref[0:latent, :], xt_ref[0:latent, :]) + tn(tail_ref[...], xt_ref[latent:, :])
    for step in range(steps):
        mish_forward_low(pre_ref, gain1, shift1, h1_ref, hat1_ref, slope1_ref, scale_ref, 0, lanes_of(step))
    pre_ref[...] = tn(w2_ref[...], h1_ref[...])
    for step in range(steps):
        mish_forward_low(pre_ref, gain2, shift2, h2_ref, hat2_ref, slope2_ref, scale_ref, 1, lanes_of(step))
    lg_ref[...] = nn(hot_ref[...], h2_ref[...])
    share = 0.1 if head == 0 else 0.1 / (heads - 1)
    bins_ref = rb_ref if head == 0 else vb_ref
    for step in range(steps):
        at = lanes_of(step)
        logits = jnp.where(bin_ids < bins, lg_ref[:, at], F32(-1e30))
        chosen = bin_ids == bins_ref[step : step + 1, mine]
        top = jnp.max(logits, axis=0, keepdims=True)
        powers = jnp.exp(logits - top)
        total = column_sum(powers)
        picked = column_sum(jnp.where(chosen, logits, 0.0))
        weight = row_weight(step, steps, scale * share, horizon_row, place_ref)
        losses.append(weight * (jnp.log(total) + top - picked))
        dl_ref[:, at] = (powers * (weight / total) - jnp.where(chosen, weight, 0.0)).astype(BF16)
    dh_ref[...] = nn(hop_ref[...], dl_ref[...]).astype(BF16)
    grad_ref[:, first_end + latent :] = nt(h2_ref[...], dl_ref[...]).astype(BF16)
    mish_backward_low(dh_ref, hat2_ref, slope2_ref, scale_ref, 1, steps, sums_ref, 2, d2_ref)
    dh_ref[...] = nn(w2_ref[...], d2_ref[...]).astype(BF16)
    grad_ref[:, first_end : first_end + latent] = nt(d2_ref[...], h1_ref[...]).astype(BF16)
    mish_backward_low(dh_ref, hat1_ref, slope1_ref, scale_ref, 0, steps, sums_ref, 0, d1_ref)
    low_part = nn(w1_ref[0:latent, :], d1_ref[...])
    side_part = nn(tail_ref[...], d1_ref[...])
    if not chained:
        dx_ref[0:latent, :] = low_part
        dx_ref[latent:, :] = side_part
    else:
        dx_ref[0:latent, :] = before_ref[0:latent, :] + low_part
        dx_ref[latent:, :] = before_ref[latent:, :] + side_part
    grad_ref[:, 0:latent] = nn(d1_ref[...], x_ref[:, 0:latent]).astype(BF16)
    side_terms = nn(d1_ref[...], x_ref[:, latent:])
    side_terms = with_vectors(side_terms, vector_sums(sums_ref, spread_ref, 2), tail_rows)
    grad_ref[:, latent:first_end] = side_terms.astype(BF16)
    for place, (slots, first, units) in enumerate(packs):
        for relative, (which, slot) in enumerate(slots):
            start = pl.multiple_of((place_ref[0] ^ relative) * GROUP, GROUP)
            out_ref = pack_refs[2 * place + which]
            if not units:
                out_ref[slot] = grad_ref[pl.ds(start, GROUP), :]
                continue
            block = grad_ref[pl.ds(start, GROUP), first * LANES : (first + units) * LANES]
            for unit in range(units):
                out_ref[slot * units + unit] = block[:, unit * LANES : (unit + 1) * LANES]
    loss_ref[...] = functools.reduce(jnp.add, losses)
    for each in copies:
        each.wait()


def backward_kernel(
    steps, scale, order, losses, after,
    place_ref, xt_ref, soft_ref, h1_ref, hat1_ref, slope1_ref, h2_ref, hat2_ref, slope2_ref, scale_ref,
    w1_ref, w2_ref, dyn_ref, hz_ref, g_ref, dx_ref, *rest,
):
    initial = order[0] == steps - 1
    final = order[-1] == 0
    loss_refs, rest = rest[:losses], rest[losses:]
    held_refs, rest = ((), rest) if initial else (rest[:4], rest[4:])
    (tgt_hbm, low_ref, first_ref, side_ref, loss_ref, sums_ref, tgt_ref, rows_ref, spread_ref, tail_ref, pre_ref,
     d1_ref, d2_ref, do_ref, grad_ref, sems) = rest[after:]
    mine = own_lanes(place_ref)
    loads = dict(zip(order, load_all([(tgt_hbm.at[step, mine, :], tgt_ref.at[step], sems.at[step]) for step in order])))
    latent = dyn_ref.shape[1]
    here = slice(0, LANES)
    horizon_row = hz_ref[:, mine]
    spread_columns(g_ref[0], g_ref[0], rows_ref, spread_ref)
    tail_rows = w1_ref.shape[0] - latent
    tail_ref[...] = padded_rows(w1_ref[latent:, :], LANES)
    first_end = latent + LANES
    second_end = first_end + latent
    if initial:
        loss = functools.reduce(jnp.add, [each[...] for each in loss_refs])
        side = jnp.zeros((LANES, LANES), F32)
        incoming = None
    else:
        before_ref, given_ref, given_side_ref, given_sums_ref = held_refs
        loss = loss_refs[0][...]
        side = given_side_ref[...]
        incoming = given_ref[...].astype(F32)
        sums_ref[...] = given_sums_ref[...]
    pending = []

    def add_terms(at, fresh, last):
        terms = (
            (slice(0, first_end), nt(d1_ref[:, at], xt_ref[:, at])),
            (slice(first_end, second_end), nt(d2_ref[:, at], h1_ref[:, at])),
            (slice(second_end, second_end + latent), nt(h2_ref[:, at], do_ref[:, at])),
        )
        for lanes, term in terms:
            if not fresh:
                term = term + grad_ref[:, lanes]
            elif not initial:
                term = term + before_ref[:, lanes]
            out_ref = low_ref if last else grad_ref
            if last and final and lanes.start == 0:
                out_ref[:, 0:latent] = term[:, 0:latent].astype(out_ref.dtype)
                vectors = vector_sums(sums_ref, spread_ref, 2)
                out_ref[:, latent:first_end] = with_vectors(term[:, latent:], vectors, tail_rows).astype(out_ref.dtype)
            else:
                out_ref[:, lanes] = term.astype(out_ref.dtype)

    for step in order:
        at = lanes_of(step)
        weight = row_weight(step, steps, scale, horizon_row, place_ref)
        shares = soft_ref[:, lanes_of(step + 1)]
        loads[step].wait()
        residue = shares - jnp.transpose(tgt_ref[step].astype(F32))
        loss = loss + (20.0 / latent) * weight * column_sum(residue * residue)
        grads = residue * ((40.0 / latent) * weight)
        if incoming is not None:
            grads = grads + incoming
        do_ref[:, at] = simplex_back(shares, grads).astype(BF16)
        pre_ref[...] = nn(dyn_ref[...], do_ref[:, at])
        mish_backward(pre_ref, here, hat2_ref, slope2_ref, scale_ref, 1, at, sums_ref, 2, step == steps - 1, d2_ref)
        pre_ref[...] = nn(w2_ref[...], d2_ref[:, at])
        mish_backward(pre_ref, here, hat1_ref, slope1_ref, scale_ref, 0, at, sums_ref, 0, step == steps - 1, d1_ref)
        incoming = nn(w1_ref[0:latent, :], d1_ref[:, at]) + dx_ref[0:latent, at]
        side = side + nn(tail_ref[...], d1_ref[:, at]) + dx_ref[latent:, at]
        incoming = incoming.astype(BF16).astype(F32)
        pending.append(step)
        if len(pending) == 2 or step == order[-1]:
            low, high = min(pending), max(pending) + 1
            add_terms(slice(low * LANES, high * LANES), high == order[0] + 1, low == order[-1])
            pending = []

    first_ref[...] = incoming.astype(BF16)
    side_ref[...] = side
    loss_ref[...] = loss


def ending_kernel(
    slots, tasks, task_width, acted, observed, after,
    place_ref, low_ref, first_ref, side_ref, loss_ref, soft_ref, ein_ref, eh_ref, ehat_ref, eslope_ref, escale_ref,
    ids_ref, e1_ref, eg_ref, e2_ref, *rest,
):
    out_refs, rest = rest[after : after + 2], rest[after + 2 :]
    erows_ref, espread_ref, e1p_ref, epre_ref, esums_ref, ed_ref, egrad_ref = rest
    mine = own_lanes(place_ref)
    here = slice(0, LANES)
    latent = first_ref.shape[0]
    spread_columns(eg_ref[...], eg_ref[...], erows_ref, espread_ref)
    e1p_ref[...] = padded_rows(e1_ref[...], e1p_ref.shape[0])
    d_enc = simplex_back(soft_ref[:, 0:LANES], first_ref[...].astype(F32)).astype(BF16)
    epre_ref[...] = nn(e2_ref[...], d_enc)
    mish_backward(epre_ref, here, ehat_ref, eslope_ref, escale_ref, 0, here, esums_ref, 0, True, ed_ref)
    side_enc = nn(e1p_ref[...], ed_ref[...])
    enc_width = epre_ref.shape[0]
    half = GROUP // 2
    groups = enc_width // half
    kept = egrad_ref.shape[2]
    enc_second = nt(eh_ref[...], d_enc)
    egrad_ref[:, 0:half, :] = enc_second[:, 0:kept].reshape(groups, half, kept)
    egrad_ref[:, half:, 0 : latent - kept] = enc_second[:, kept:].reshape(groups, half, latent - kept)
    enc_first = nt(ed_ref[...], ein_ref[...])
    egrad_ref[:, half:, latent - kept : kept - LANES] = enc_first[:, 0:LANES].reshape(groups, half, LANES)
    second_lanes = with_vectors(enc_first[:, LANES : 2 * LANES], vector_sums(esums_ref, espread_ref, 1), LANES - 2)
    egrad_ref[:, half:, kept - LANES :] = second_lanes.reshape(groups, half, LANES)

    kinds = lax.broadcasted_iota(jnp.int32, (tasks, LANES), 0)
    onehot = (kinds == ids_ref[:, mine]).astype(F32)
    over_lanes = (((1,), (1,)), ((), ()))
    highest = lax.Precision.HIGHEST
    side_terms = lax.dot_general(onehot, side_ref[...], over_lanes, precision=highest, preferred_element_type=F32)
    enc_terms = lax.dot_general(onehot, side_enc, over_lanes, precision=highest, preferred_element_type=F32)
    table = pltpu.roll(side_terms, LANES - acted, 1)
    table = table + pltpu.roll(enc_terms, enc_terms.shape[1] - observed, 1)[:, 0:LANES]
    lane = lax.broadcasted_iota(jnp.int32, table.shape, 1)
    table = jnp.where(lane < task_width, table, 0.0)
    table = jnp.where((lane == LANES - 1) & (kinds == 0), jnp.sum(loss_ref[...], axis=1, keepdims=True), table)
    table_rows = [table[start : start + GROUP] for start in range(0, tasks, GROUP)]
    table_block = jnp.concatenate(table_rows, axis=1).astype(BF16)
    count = low_ref.shape[1] // LANES
    units = count + kept // LANES
    for relative, (which, slot) in enumerate(slots):
        dest = place_ref[0] ^ relative
        start = pl.multiple_of(dest * GROUP, GROUP)
        block = jnp.concatenate([low_ref[pl.ds(start, GROUP), :], egrad_ref[dest].astype(BF16)], axis=1)
        for unit in range(units):
            out_refs[which][slot * units + unit] = block[:, unit * LANES : (unit + 1) * LANES]
    last = len(slots) // 2 * units
    for unit in range(tasks // GROUP):
        for out_ref in out_refs:
            out_ref[last + unit] = table_block[:, unit * LANES : (unit + 1) * LANES]


def final_kernel(tasks, task_width, enc_in, bins, net_in, *refs):
    outs = refs[-12:]
    (loss_ref, table_ref, e1_ref, eg_ref, es_ref, e2_ref, first_ref, second_ref, gain_ref, shift_ref, dyn_ref, head_ref) = outs
    refs = refs[:-12]
    tail_refs, refs = refs[:4], refs[4:]
    latent = second_ref.shape[2]
    first_end = latent + LANES
    second_end = first_end + latent

    def put_net(net, value):
        first_ref[net] = value[:, 0:net_in]
        second_ref[net] = value[:, first_end:second_end]
        turned = jnp.transpose(value[:, latent:first_end])
        for layer in range(2):
            row = net_in - latent + 2 * layer
            gain_ref[net, layer : layer + 1, :] = turned[row : row + 1, :]
            shift_ref[net, layer : layer + 1, :] = turned[row + 1 : row + 2, :]

    sums = functools.reduce(jnp.add, [ref[...].astype(F32) for ref in tail_refs])
    units = sums.shape[0] - tasks // GROUP
    tail = jnp.concatenate([sums[unit] for unit in range(units)], axis=1)
    put_net(0, tail)
    dyn_ref[...] = tail[:, second_end : second_end + latent]
    enc = tail[:, second_end + latent :]
    half = GROUP // 2
    kept = enc.shape[1]
    e2_ref[:, 0:kept] = 0.3 * enc[0:half, :]
    e2_ref[:, kept:] = 0.3 * enc[half:, 0 : latent - kept]
    e1_ref[...] = 0.3 * enc[half:, latent - kept : latent - kept + enc_in]
    turned = 0.3 * jnp.transpose(enc[half:, kept - LANES :])
    eg_ref[...] = turned[LANES - 2 : LANES - 1, :]
    es_ref[...] = turned[LANES - 1 : LANES, :]
    loss_ref[...] = sums[units, 0:1, LANES - 1 : LANES]
    for place in range(tasks // GROUP):
        table_ref[place * GROUP : (place + 1) * GROUP, :] = sums[units + place, :, 0:task_width]
    net = 1
    def put_head(value):
        put_net(net, value)
        head_ref[net - 1] = value[:, second_end : second_end + bins]

    one_ref, other_ref, last_one_ref, last_other_ref = refs
    for one in range(one_ref.shape[1]):
        put_head(one_ref[0, one].astype(F32) + other_ref[0, one].astype(F32))
        net += 1
    sums = last_one_ref[...].astype(F32) + last_other_ref[...].astype(F32)
    units = (second_end + LANES) // LANES
    for start in range(0, sums.shape[0], units):
        put_head(jnp.concatenate([sums[start + unit] for unit in range(units)], axis=1))
        net += 1


def swap(value, axis, distance):
    count = lax.axis_size(axis)
    return lax.ppermute(value, axis, [(place, place ^ distance) for place in range(count)])


def exchange(parts, axis, scale):
    total = parts[0].astype(F32)
    for distance in range(1, len(parts)):
        total = total + swap(parts[distance], axis, distance * scale).astype(F32)
    return total


def scatter_plain(packed, chips, sections):
    held = packed.reshape((sections, chips, CORES) + packed.shape[1:])
    batch_no = lax.axis_index("batch")
    places = (
        ("batch", 1, CORES, 2, batch_no % CORES),
        ("batch", CORES, chips, 1, batch_no // CORES),
        ("section", 1, sections, 0, lax.axis_index("section")),
    )
    for axis, scale, count, dim, mine in places:
        parts = [lax.dynamic_index_in_dim(held, mine ^ other, dim, keepdims=False) for other in range(count)]
        held = exchange(parts, axis, scale)
        held = held.astype(BF16) if dim else held
    return held


def on_device(
    observations,
    actions,
    targets,
    task_ids,
    horizons,
    reward_bins,
    value_bins,
    task_table,
    enc_first,
    enc_gain,
    enc_shift,
    enc_second,
    net_first,
    net_second,
    net_gain,
    net_shift,
    dyn_out,
    head_out,
):
    sections = lax.axis_size("section")
    batches = lax.axis_size("batch")
    section_no = lax.axis_index("section")
    chips = batches // CORES
    devices = sections * batches
    steps, rows_all, acted = actions.shape
    observed = observations.shape[1]
    rows = rows_all // sections
    latent = dyn_out.shape[1]
    hidden = dyn_out.shape[0]
    tasks, task_width = task_table.shape
    heads, _, bins = head_out.shape
    nets, net_in, _ = net_first.shape
    enc_in, enc_width = enc_first.shape
    wide = steps * LANES
    scale = 1.0 / (rows_all * batches * steps)
    groups = hidden // GROUP
    in_place = hidden // devices == GROUP
    start = section_no * rows
    block_no = start // LANES
    first_lane = start - block_no * LANES
    me = section_no * batches + lax.axis_index("batch") if in_place else jnp.int32(0)
    place = jnp.stack([me, block_no, first_lane, first_lane + rows]).astype(jnp.int32)
    bits = [("batch", 1 << bit) for bit in range(batches.bit_length() - 1)]
    bits += [("section", 1 << bit) for bit in range(sections.bit_length() - 1)]

    def slots_of(order):
        if not in_place:
            return tuple((relative // (groups // 2), relative % (groups // 2)) for relative in range(groups))
        found = []
        for relative in range(groups):
            slot = 0
            for bit in order:
                slot = 2 * slot + (relative >> bit & 1)
            found.append((slot // (groups // 2), slot % (groups // 2)))
        return tuple(found)

    plain = tuple(range(len(bits)))
    y_first = (0, 2, 1) + tuple(range(3, len(bits))) if in_place else plain
    half_slots = groups // 2
    shape_of = jax.ShapeDtypeStruct
    smem = pl.BlockSpec(memory_space=pltpu.SMEM)
    local = pl.BlockSpec(memory_space=pltpu.VMEM)
    far = pl.BlockSpec(memory_space=pltpu.HBM)
    anywhere = pl.BlockSpec(memory_space=pl.ANY)
    first_far, second_far, dyn_far, targets_far = [
        pltpu.with_memory_space_constraint(array, pltpu.HBM) for array in (net_first, net_second, dyn_out, targets)
    ]
    vmem = pltpu.VMEM
    dmas = pltpu.SemaphoreType.DMA

    def params(mebibytes):
        return pltpu.CompilerParams(vmem_limit_bytes=mebibytes * 1024 * 1024)

    def cost(flops, moved):
        return pl.CostEstimate(flops=flops, bytes_accessed=moved, transcendentals=0)

    ids_row = task_ids.reshape(1, rows_all)
    horizon_row = horizons.reshape(1, rows_all)
    eg_row = enc_gain.reshape(1, enc_width)
    es_row = enc_shift.reshape(1, enc_width)
    head_turned = head_out.transpose(0, 2, 1)
    low = lambda lanes: shape_of((hidden, lanes), BF16)
    forward_shapes = (
        shape_of((latent + LANES, wide), BF16),
        shape_of((latent, wide + LANES), F32),
        low(wide), low(wide), low(wide), low(wide), low(wide), low(wide),
        shape_of((8, wide), F32),
        shape_of((2 * LANES, LANES), BF16),
        shape_of((enc_width, LANES), BF16),
        shape_of((enc_width, LANES), BF16),
        shape_of((enc_width, LANES), BF16),
        shape_of((8, LANES), F32),
        shape_of((net_in, hidden), BF16),
        shape_of((hidden, hidden), BF16),
        shape_of((hidden, latent), BF16),
        shape_of((wide, latent + LANES), BF16),
    )

    weight_shapes = (shape_of((net_in, hidden), BF16), shape_of((hidden, hidden), BF16))

    early = [
        pltpu.with_memory_space_constraint(array, pltpu.HBM)
        for array in (
            observations.T, actions.transpose(0, 2, 1), ids_row, task_table, enc_first, eg_row, es_row, enc_second,
            net_gain, net_shift,
        )
    ]
    made = pl.pallas_call(
        functools.partial(forward_kernel, steps),
        out_shape=forward_shapes + weight_shapes,
        in_specs=[smem] + [far] * 13,
        out_specs=[local] * (len(forward_shapes) + 2),
        scratch_shapes=[
            vmem((8, hidden), F32),
            vmem((4, hidden, LANES), F32),
            vmem((8, enc_width), F32),
            vmem((2, enc_width, LANES), F32),
            vmem((tasks, 2 * LANES), F32),
            vmem((LANES, LANES), F32),
            vmem((2 * LANES, enc_width), BF16),
            vmem((hidden, latent + LANES), BF16),
            vmem((hidden, hidden), BF16),
            vmem((latent, hidden), BF16),
            vmem((hidden, LANES), F32),
            vmem((enc_width, LANES), F32),
            *[vmem(each.shape, each.dtype) for each in early],
            dmas((5,)),
            dmas((len(early),)),
        ],
        compiler_params=params(VMEM_A),
        cost_estimate=cost(10_000_000_000, 8_000_000),
        name="forward_chain",
    )(
        place, *early, first_far, second_far, dyn_far,
    )
    saved, x_rows, weights = made[:-3], made[-3], made[-2:]
    xt = saved[0]
    head_width = latent + LANES + hidden + LANES

    def run_head(head, ahead, weights, before, after):
        all_units = head_width // LANES
        packs = [(slots_of(plain), 0, 0)]
        if in_place and head == heads - 1:
            packs = [(slots_of(plain), 0, all_units // 2), (slots_of(y_first), all_units // 2, all_units // 2)]
        pack_shapes = []
        for _, _, count in packs:
            shape = (half_slots * count, GROUP, LANES) if count else (half_slots, GROUP, head_width)
            pack_shapes += [shape_of(shape, BF16)] * 2
        dx_shape = shape_of((latent + LANES, wide), F32)
        out_shapes = (*pack_shapes, dx_shape, shape_of((1, LANES), F32))
        args = [place, xt, x_rows, *weights, head_turned, net_gain, net_shift, reward_bins, value_bins, horizon_row]
        specs = [smem] + [local] * 10
        aliases = {}
        if before is not None:
            aliases = {len(args): len(pack_shapes)}
            args.append(before)
            specs.append(local)
        args += after
        specs += [anywhere] * len(after)
        if ahead:
            args += [first_far, second_far]
            specs += [far, far]
            out_shapes += weight_shapes
        low_wide = vmem((hidden, wide), BF16)
        scratch = [
            vmem((8, hidden), F32),
            vmem((4, hidden, LANES), F32),
            vmem((LANES, hidden), BF16),
            vmem((hidden, LANES), BF16),
            vmem((LANES, hidden), BF16),
            vmem((hidden, wide), F32),
            vmem((LANES, wide), F32),
        ]
        scratch += [low_wide] * 6
        scratch += [vmem((8, wide), F32), vmem((4, hidden, LANES), F32)]
        scratch += [low_wide] * 3
        scratch += [vmem((LANES, wide), BF16), vmem((hidden, head_width), BF16)]
        if ahead:
            scratch.append(dmas((2,)))
        return pl.pallas_call(
            functools.partial(
                heads_kernel, steps, scale, packs, head, ahead, heads, bins, before is not None, len(after)
            ),
            out_shape=out_shapes,
            in_specs=specs,
            out_specs=[local] * len(out_shapes),
            scratch_shapes=scratch,
            input_output_aliases=aliases,
            compiler_params=params(VMEM_B),
            cost_estimate=cost(9_000_000_000, 4_000_000),
            name=f"head_{head}",
        )(*args)

    def phase(pair, bit):
        return pair[0], swap(pair[1], *bits[bit])

    def fold(members, *tokens):
        slots_now = members[0][0].shape[0] // 2
        shape = members[0][0].shape[1:]
        stacked = len(shape) == 3
        if stacked:
            shape = (len(members) * shape[0],) + shape[1:]
        elif len(members) > 1:
            shape = (len(members),) + shape
        out_shape = shape_of((slots_now,) + shape, BF16)

        def fold_kernel(*refs):
            refs = refs[len(tokens) :]
            outs = refs[-2:]
            for place in range(len(members)):
                kept_ref, came_ref = refs[2 * place], refs[2 * place + 1]
                for half in range(2):
                    part = pl.ds(half * slots_now, slots_now)
                    value = (kept_ref[part].astype(F32) + came_ref[part].astype(F32)).astype(BF16)
                    if stacked:
                        count = kept_ref.shape[1]
                        outs[half][:, place * count : (place + 1) * count] = value
                    elif len(members) > 1:
                        outs[half][:, place] = value
                    else:
                        outs[half][...] = value

        return run_fold(fold_kernel, out_shape, members, tokens)

    def fold_units(members, slots_now, common, *tokens):
        counts = [
            kept.shape[2] // LANES if kept.shape[2] > LANES else (kept.shape[0] - (0 if place else common)) // slots_now
            for place, (kept, _) in enumerate(members)
        ]
        half_now = slots_now // 2
        width = sum(counts)
        out_shape = shape_of((half_now * width + common, GROUP, LANES), BF16)

        def fold_kernel(*refs):
            refs = refs[len(tokens) :]
            outs = refs[-2:]
            before = 0
            for place, count in enumerate(counts):
                kept_ref, came_ref = refs[2 * place], refs[2 * place + 1]

                def added(start, size):
                    part = pl.ds(start, size)
                    return (kept_ref[part].astype(F32) + came_ref[part].astype(F32)).astype(BF16)

                for half in range(2):
                    if kept_ref.shape[2] > LANES:
                        for slot in range(half_now):
                            block = added(half * half_now + slot, 1)[0]
                            for unit in range(count):
                                piece = block[:, unit * LANES : (unit + 1) * LANES]
                                outs[half][slot * width + before + unit] = piece
                    elif len(counts) == 1:
                        outs[half][0 : half_now * count] = added(half * half_now * count, half_now * count)
                    else:
                        for slot in range(half_now):
                            at = slot * width + before
                            outs[half][at : at + count] = added((half * half_now + slot) * count, count)
                if place == 0 and common:
                    value = added(slots_now * count, common)
                    for out in outs:
                        out[half_now * width :] = value
                before += count

        return run_fold(fold_kernel, out_shape, members, tokens)

    def fold_direct(parts, slots_now, common, *tokens):
        quarter = (parts[0].shape[0] - common) // 4
        out_shape = shape_of((quarter + common, GROUP, LANES), BF16)

        def fold_kernel(*refs):
            refs = refs[len(tokens) :]
            outs = refs[-4:]

            def added(start, size):
                each = [ref[pl.ds(start, size)].astype(F32) for ref in refs[: len(parts)]]
                return functools.reduce(jnp.add, each).astype(BF16)

            shared = added(4 * quarter, common)
            for place, out in enumerate(outs):
                out[0:quarter] = added(place * quarter, quarter)
                out[quarter:] = shared

        return pl.pallas_call(
            fold_kernel,
            out_shape=(out_shape,) * 4,
            in_specs=[anywhere] * len(tokens) + [local] * len(parts),
            out_specs=(local,) * 4,
            compiler_params=params(VMEM_SUM),
            cost_estimate=cost(1_000_000, 2_000_000),
            name="fold_direct",
        )(*tokens, *parts)

    def direct(pieces, axis, high, low):
        distances = (0, low, high, high + low)
        came = [swap(pieces[place], axis, distances[place]) for place in (3, 2, 1)]
        return [pieces[0], *came]

    def run_fold(kernel, out_shape, members, tokens):
        inputs = [each for member in members for each in member]
        return pl.pallas_call(
            kernel,
            out_shape=(out_shape, out_shape),
            in_specs=[anywhere] * len(tokens) + [local] * len(inputs),
            out_specs=(local, local),
            compiler_params=params(VMEM_SUM),
            cost_estimate=cost(1_000_000, 2_000_000),
            name="fold",
        )(*tokens, *inputs)

    net_width = latent + LANES + hidden + latent
    chain_inputs = saved[:9] + saved[14:]

    def run_backward(order, losses, held, after):
        final = order[-1] == 0
        out_shapes = (
            shape_of((hidden, net_width), BF16 if final else F32),
            shape_of((latent, LANES), BF16),
            shape_of((LANES, LANES), F32),
            shape_of((1, LANES), F32),
            shape_of((4, hidden, LANES), F32),
        )
        args = [place, *chain_inputs, horizon_row, net_gain, dx, *losses, *held]
        return pl.pallas_call(
            functools.partial(backward_kernel, steps, scale, order, len(losses), len(after)),
            out_shape=out_shapes,
            in_specs=[smem] + [local] * (len(args) - 1) + [anywhere] * len(after) + [far],
            out_specs=[local] * len(out_shapes),
            scratch_shapes=[
                vmem((steps, LANES, latent), BF16),
                vmem((8, hidden), F32),
                vmem((4, hidden, LANES), F32),
                vmem((LANES, hidden), BF16),
                vmem((hidden, LANES), F32),
                vmem((hidden, wide), BF16),
                vmem((hidden, wide), BF16),
                vmem((latent, wide), BF16),
                vmem((hidden, net_width), F32),
                dmas((steps,)),
            ],
            compiler_params=params(VMEM_C),
            cost_estimate=cost(7_000_000_000, 8_000_000),
            name=f"backward_{order[0]}",
        )(*args, *after, targets_far)

    packs, loss_parts = [], []
    dx = None
    after = []
    cores, pairs = [], []
    units_all = head_width // LANES
    for head in range(heads):
        result = run_head(head, head + 1 < heads, weights, dx, after)
        sent = 4 if in_place and head == heads - 1 else 2
        dx, loss = result[sent : sent + 2]
        weights = result[sent + 2 :]
        packs.append(result[:sent])
        loss_parts.append(loss)
        after = []
        if in_place:
            if 1 <= head <= heads - 2:
                crossing = fold([cores[head - 1]], loss)
                after.append(crossing[0])
                pairs.append(phase(crossing, plain[1]))
            if head in (3, 5):
                crossing = fold(pairs[head - 3 : head - 1], loss)
                after.append(crossing[0])
                pairs[head - 3] = phase(crossing, plain[2])
            if head == heads - 1:
                fourth = fold([cores[head - 1]], loss)
                after.append(fourth[0])
                fourth = phase(fourth, plain[1])
                cores.append(phase(result[0:2], plain[0]))
                cores.append(phase(result[2:4], y_first[0]))
            else:
                cores.append(phase(result[0:2], plain[0]))
    half_way = steps // 2
    chain = run_backward(tuple(range(steps - 1, half_way - 1, -1)), loss_parts, [], after)
    after = []
    if in_place:
        token = chain[3]
        fifth = fold_units([cores[heads - 1]], half_slots, 0, token)
        sixth = fold_units([cores[heads]], half_slots, 0, token)
        fourth = fold([fourth], token)
        group = fold([pairs[0], pairs[2]], token)
        after = [fifth[0], sixth[0], fourth[0], group[0]]
        fifth = phase(fifth, plain[1])
        sixth = phase(sixth, y_first[1])
        group = phase(group, plain[3])
        fourth = phase(fourth, plain[2])
    chain = run_backward(
        tuple(range(half_way - 1, -1, -1)), [chain[3]], [chain[0], chain[1], chain[2], chain[4]], after
    )
    after = []
    if in_place:
        token = chain[3]
        fifth = fold_units([fifth], half_slots // 2, 0, token)
        sixth = fold_units([sixth], half_slots // 2, 0, token)
        group = fold([group], token)
        after = [fifth[0], sixth[0], group[0], fourth[1]]
        fifth = phase(fifth, plain[2])
        sixth = phase(sixth, y_first[2])
        group = phase(group, plain[4])

    enc_lanes = latent - LANES
    units = (net_width + enc_lanes) // LANES
    common = tasks // GROUP
    tail_shape = shape_of((half_slots * units + common, GROUP, LANES), BF16)
    ended = pl.pallas_call(
        functools.partial(ending_kernel, slots_of(plain), tasks, task_width, acted, observed, len(after)),
        out_shape=(tail_shape, tail_shape),
        in_specs=[smem] + [local] * 14 + [anywhere] * len(after),
        out_specs=[local] * 2,
        scratch_shapes=[
            vmem((8, enc_width), F32),
            vmem((2, enc_width, LANES), F32),
            vmem((2 * LANES, enc_width), BF16),
            vmem((enc_width, LANES), F32),
            vmem((2, enc_width, LANES), F32),
            vmem((enc_width, LANES), BF16),
            vmem((groups, GROUP, enc_lanes), F32),
        ],
        compiler_params=params(VMEM_SUM),
        cost_estimate=cost(1_000_000_000, 4_000_000),
        name="ending",
    )(place, *chain[:4], saved[1], *saved[9:14], ids_row, enc_first, eg_row, enc_second, *after)

    if in_place:
        tail = phase(ended, plain[0])
        pieces = fold_direct(tail, half_slots, common, fifth[1], sixth[1])
        tail = direct(pieces, "batch", CORES, 2 * CORES)
        last = phase(fold_units([fourth, fifth, sixth], half_slots // 4, 0, ended[0], group[1]), plain[3])
        last = phase(fold_units([last], half_slots // 8, 0, ended[0]), plain[4])
        pieces = fold_direct(tail, half_slots // 4, common, last[1], group[1])
        tail = direct(pieces, "section", 1, 2)
        each = GROUP // 2
        out_shapes = (
            shape_of((1, 1), F32),
            shape_of((tasks, task_width), F32),
            shape_of((each, enc_in), F32),
            shape_of((1, each), F32),
            shape_of((1, each), F32),
            shape_of((each, latent), F32),
            shape_of((nets, GROUP, net_in), F32),
            shape_of((nets, GROUP, hidden), F32),
            shape_of((nets, 2, GROUP), F32),
            shape_of((nets, 2, GROUP), F32),
            shape_of((GROUP, latent), F32),
            shape_of((heads, GROUP, bins), F32),
        )
        ends = [*tail, *group, *last]
        outs = list(pl.pallas_call(
            functools.partial(final_kernel, tasks, task_width, enc_in, bins, net_in),
            out_shape=out_shapes,
            in_specs=[local] * len(ends),
            out_specs=[local] * len(out_shapes),
            compiler_params=params(VMEM_SUM),
            cost_estimate=cost(1_000_000, 4_000_000),
            name="last_sums",
        )(*ends))
        outs[0] = outs[0].reshape(())
        outs[2] = outs[2].T
        outs[3], outs[4] = outs[3].reshape(each), outs[4].reshape(each)
        outs[6] = outs[6].transpose(0, 2, 1)
        outs[7] = outs[7].transpose(0, 2, 1)
        return tuple(outs)

    def scattered(keep, send):
        mine = hidden // devices
        packed = jnp.concatenate([keep, send], axis=0)
        middle = packed.shape[1:-2]
        packed = packed.reshape((groups,) + middle + (GROUP // mine, mine, packed.shape[-1]))
        packed = jnp.moveaxis(packed, -3, 1).reshape((devices,) + middle + (mine, packed.shape[-1]))
        return scatter_plain(packed, chips, sections)

    head_sum = jnp.stack([scattered(*pack) for pack in packs], axis=0)
    enc_each = enc_width // devices
    def by_rows(array):
        joined = array[: half_slots * units].reshape(half_slots, units, GROUP, LANES).transpose(0, 2, 1, 3)
        return joined.reshape(half_slots, GROUP, units * LANES)

    keep, send = by_rows(ended[0]), by_rows(ended[1])
    table_sum = lax.psum(ended[0][half_slots * units :].astype(F32), ("section", "batch"))
    table_sum = table_sum.transpose(1, 0, 2).reshape(GROUP, common * LANES)
    net_sum = scattered(keep[:, :, 0:net_width], send[:, :, 0:net_width])
    enc_all = jnp.concatenate([keep, send], axis=0)[:, :, net_width:]
    enc_all = enc_all.reshape(groups, 2, enc_width // groups, enc_lanes)
    enc_all = enc_all.transpose(0, 2, 1, 3).reshape(devices, enc_each, 2, enc_lanes)
    enc_sum = scatter_plain(enc_all, chips, sections)
    enc_low, enc_high = enc_sum[:, 0], enc_sum[:, 1]
    s_enc_second = jnp.concatenate([enc_low, enc_high[:, 0 : latent - enc_lanes]], axis=1)
    enc_rows = enc_high[:, latent - enc_lanes :]
    first_end = latent + LANES
    net_row = jnp.concatenate([net_sum[:, 0 : first_end + hidden], jnp.zeros_like(net_sum[:, 0:LANES])], axis=1)
    sums = jnp.concatenate([net_row[None], head_sum], axis=0)
    vectors = sums[:, :, net_in : net_in + 4].transpose(0, 2, 1)
    table = table_sum.reshape(GROUP, tasks // GROUP, LANES).transpose(1, 0, 2).reshape(tasks, LANES)
    return (
        table[0, LANES - 1],
        table[:, 0:task_width],
        0.3 * enc_rows[:, 0:enc_in].T,
        0.3 * enc_rows[:, 2 * LANES - 2],
        0.3 * enc_rows[:, 2 * LANES - 1],
        0.3 * s_enc_second,
        sums[:, :, 0:net_in].transpose(0, 2, 1),
        sums[:, :, first_end : first_end + hidden].transpose(0, 2, 1),
        vectors[:, 0::2],
        vectors[:, 1::2],
        net_sum[:, first_end + hidden :],
        head_sum[:, :, first_end + hidden : first_end + hidden + bins],
    )


def solution(mesh):
    both = ("section", "batch")
    return jax.shard_map(
        on_device,
        mesh=mesh,
        in_specs=(
            P("batch", None),
            P(None, "batch", None),
            P(None, "batch", None),
            P("batch"),
            P("batch"),
            P(None, "batch"),
            P(None, "batch"),
        )
        + (P(),) * 11,
        out_specs=(
            P(),
            P(),
            P(None, both),
            P(both),
            P(both),
            P(both, None),
            P(None, None, both),
            P(None, None, both),
            P(None, None, both),
            P(None, None, both),
            P(both, None),
            P(None, both, None),
        ),
        check_vma=False,
    )
```

```python
import functools

import jax
import jax.numpy as jnp
from jax import lax
from jax.experimental import pallas as pl
from jax.experimental.pallas import tpu as pltpu
from jax.sharding import PartitionSpec as P

CORES = 2
LANES = 128
GROUP = 16
BF16 = jnp.bfloat16
F32 = jnp.float32
VMEM_A = 18
VMEM_B = 20
VMEM_SUM = 6
VMEM_C = 20


def nn(left, right):
    return lax.dot_general(left, right, (((1,), (0,)), ((), ())), preferred_element_type=F32)


def nt(left, right):
    return lax.dot_general(left, right, (((1,), (1,)), ((), ())), preferred_element_type=F32)


def tn(left, right):
    return lax.dot_general(left, right, (((0,), (0,)), ((), ())), preferred_element_type=F32)


def column_sum(value):
    grouped = value.reshape(value.shape[0] // 8, 8, value.shape[1])
    return jnp.sum(jnp.sum(grouped, axis=0), axis=0, keepdims=True)


def slabs(features, size=64):
    return [slice(start, start + size) for start in range(0, features, size)]


def lanes_of(step):
    return slice(step * LANES, (step + 1) * LANES)


def spread_columns(gain_rows, shift_rows, rows_ref, spread_ref):
    count = gain_rows.shape[0]
    rows_ref[...] = jnp.zeros_like(rows_ref)
    rows_ref[0:count, :] = gain_rows
    rows_ref[count : 2 * count, :] = shift_rows
    turned = jnp.transpose(rows_ref[...])
    for place in range(2 * count):
        spread_ref[place] = jnp.broadcast_to(turned[:, place : place + 1], spread_ref.shape[1:])


def mish_forward(pre_ref, pre_at, gain_ref, shift_ref, hid_ref, hat_ref, slope_ref, scale_ref, scale_row, at):
    features = pre_ref.shape[0]
    row_mean = column_sum(pre_ref[:, pre_at]) * (1.0 / features)
    centred = pre_ref[:, pre_at] - row_mean
    spread = column_sum(centred * centred) * (1.0 / features)
    scale = lax.rsqrt(spread + 1e-05)
    scale_ref[scale_row : scale_row + 1, at] = scale
    for part in slabs(features):
        hat = (pre_ref[part, pre_at] - row_mean) * scale
        normed = hat * gain_ref[part, :] + shift_ref[part, :]
        power = jnp.exp(normed)
        top = power * (power + 2.0)
        inverse = pl.reciprocal(top + 2.0, approx=True)
        ratio = top * inverse
        hid_ref[part, at] = (normed * ratio).astype(BF16)
        tilt = power * inverse
        slope = ratio + normed * (4.0 * (tilt * (tilt + inverse)))
        slope_ref[part, at] = (slope * gain_ref[part, :]).astype(BF16)
        hat_ref[part, at] = hat.astype(BF16)


def mish_backward(grad_ref, grad_at, hat_ref, slope_ref, scale_ref, scale_row, at, sums_ref, sums_at, first, out_ref):
    features = grad_ref.shape[0]
    total_one = jnp.zeros((8, LANES), F32)
    total_two = jnp.zeros((8, LANES), F32)
    for part in slabs(features):
        term = grad_ref[part, grad_at] * slope_ref[part, at].astype(F32)
        grad_ref[part, grad_at] = term
        crossed = term * hat_ref[part, at].astype(F32)
        groups = (term.shape[0] // 8, 8, LANES)
        total_one = total_one + jnp.sum(term.reshape(groups), axis=0)
        total_two = total_two + jnp.sum(crossed.reshape(groups), axis=0)
        if first:
            sums_ref[sums_at, part, :] = term
            sums_ref[sums_at + 1, part, :] = crossed
        else:
            sums_ref[sums_at, part, :] += term
            sums_ref[sums_at + 1, part, :] += crossed
    mean_one = jnp.sum(total_one, axis=0, keepdims=True) * (1.0 / features)
    mean_two = jnp.sum(total_two, axis=0, keepdims=True) * (1.0 / features)
    scale = scale_ref[scale_row : scale_row + 1, at]
    for part in slabs(features):
        rest = grad_ref[part, grad_at] - mean_one - hat_ref[part, at].astype(F32) * mean_two
        out_ref[part, at] = (rest * scale).astype(BF16)


def mish_forward_low(pre_ref, gain_ref, shift_ref, hid_ref, hat_ref, slope_ref, scale_ref, scale_row, at):
    features = pre_ref.shape[0]
    row_mean = column_sum(pre_ref[:, at]) * (1.0 / features)
    centred = pre_ref[:, at] - row_mean
    spread = column_sum(centred * centred) * (1.0 / features)
    scale = lax.rsqrt(spread + 1e-05)
    scale_ref[scale_row : scale_row + 1, at] = scale
    for part in slabs(features):
        hat = (pre_ref[part, at] - row_mean) * scale
        normed = (hat * gain_ref[part, :] + shift_ref[part, :]).astype(BF16)
        hat_ref[part, at] = hat.astype(BF16)
        power = jnp.exp(normed)
        top = power * (power + 2.0)
        inverse = pl.reciprocal(top + 2.0, approx=True)
        ratio = top * inverse
        hid_ref[part, at] = normed * ratio
        tilt = power * inverse
        slope = ratio + (4.0 * normed) * (tilt * (tilt + inverse))
        slope_ref[part, at] = slope * gain_ref[part, :].astype(BF16)


def mish_backward_low(grad_ref, hat_ref, slope_ref, scale_ref, scale_row, steps, sums_ref, sums_at, out_ref):
    features = grad_ref.shape[0]
    rows = []
    for step in range(steps):
        at = lanes_of(step)
        total_one = jnp.zeros((16, LANES), F32)
        total_two = jnp.zeros((16, LANES), F32)
        for part in slabs(features):
            term = grad_ref[part, at] * slope_ref[part, at]
            crossed = term * hat_ref[part, at]
            grad_ref[part, at] = term
            groups = (term.shape[0] // 16, 16, LANES)
            term = term.reshape(groups)
            crossed = crossed.reshape(groups)
            total_one = total_one + functools.reduce(jnp.add, [term[k] for k in range(groups[0])]).astype(F32)
            total_two = total_two + functools.reduce(jnp.add, [crossed[k] for k in range(groups[0])]).astype(F32)
        scale = scale_ref[scale_row : scale_row + 1, at]
        mean_one = jnp.sum(total_one, axis=0, keepdims=True) * (1.0 / features)
        mean_two = jnp.sum(total_two, axis=0, keepdims=True) * (1.0 / features)
        rows.append((mean_one.astype(BF16), mean_two.astype(BF16), scale.astype(BF16)))
    for part in slabs(features):
        sum_one, sum_two = None, None
        for step, (mean_one, mean_two, scale) in enumerate(rows):
            at = lanes_of(step)
            term = grad_ref[part, at]
            hat = hat_ref[part, at]
            out_ref[part, at] = (term - mean_one - hat * mean_two) * scale
            crossed = term * hat
            sum_one = term if sum_one is None else sum_one + term
            sum_two = crossed if sum_two is None else sum_two + crossed
        sums_ref[sums_at, part, :] = sum_one.astype(F32)
        sums_ref[sums_at + 1, part, :] = sum_two.astype(F32)


def simplex(values):
    grouped = values.reshape(values.shape[0] // 8, 8, values.shape[1])
    powers = jnp.exp(grouped - jnp.max(grouped, axis=1, keepdims=True))
    shares = powers / jnp.sum(powers, axis=1, keepdims=True)
    return shares.reshape(values.shape)


def simplex_back(shares, grads):
    grouped = (shares.shape[0] // 8, 8, shares.shape[1])
    crossed = jnp.sum((shares * grads).reshape(grouped), axis=1, keepdims=True)
    return (shares.reshape(grouped) * (grads.reshape(grouped) - crossed)).reshape(shares.shape)


def row_weight(step, steps, scale, horizon_row, place_ref):
    lane = lax.broadcasted_iota(jnp.int32, (1, LANES), 1)
    mine = (lane >= place_ref[2]) & (lane < place_ref[3]) & (horizon_row > step)
    return jnp.where(mine, F32(scale * 0.5 ** (step / (steps - 1))), 0.0)


def padded_rows(value, rows):
    zeros = jnp.zeros((rows - value.shape[0], value.shape[1]), F32)
    return jnp.concatenate([value.astype(F32), zeros], axis=0).astype(BF16)


def transpose_into(out_ref, source_ref, rows):
    for start in range(0, rows, LANES):
        out_ref[:, start : start + LANES] = jnp.transpose(source_ref[start : start + LANES, :])


def vector_sums(sums_ref, gains_ref, layers):
    vectors = []
    for layer in range(layers):
        inverse = 1.0 / gains_ref[layer]
        vectors.append(jnp.sum(sums_ref[2 * layer + 1] * inverse, axis=1, keepdims=True))
        vectors.append(jnp.sum(sums_ref[2 * layer] * inverse, axis=1, keepdims=True))
    return vectors


def own_lanes(place_ref):
    return pl.ds(pl.multiple_of(place_ref[1] * LANES, LANES), LANES)


def load_all(copies):
    made = [pltpu.make_async_copy(*each) for each in copies]
    for each in made:
        each.start()
    return made


def with_vectors(value, vectors, first_lane):
    lane = lax.broadcasted_iota(jnp.int32, value.shape, 1)
    for place, vector in enumerate(vectors):
        value = jnp.where(lane == first_lane + place, vector, value)
    return value


def forward_kernel(
    steps,
    place_ref, obs_hbm, act_hbm, ids_hbm, table_hbm, e1_hbm, eg_hbm, es_hbm, e2_hbm, g_hbm, s_hbm,
    w1_hbm, w2_hbm, dyn_hbm,
    xt_ref, soft_ref, h1_ref, hat1_ref, slope1_ref, h2_ref, hat2_ref, slope2_ref, scale_ref,
    ein_ref, eh_ref, ehat_ref, eslope_ref, escale_ref,
    w1_ref, w2_ref, dyn_ref, x_ref, next1_ref, next2_ref,
    rows_ref, spread_ref, erows_ref, espread_ref, wide_ref, tall_ref, e1p_ref, w1t_ref, w2t_ref, dynt_ref, pre_ref, epre_ref,
    obs_ref, act_ref, ids_ref, table_ref, e1_ref, eg_ref, es_ref, e2_ref, g_ref, s_ref,
    sems, early_sems,
):
    early = load_all([
        (table_hbm, table_ref, early_sems.at[0]),
        (ids_hbm, ids_ref, early_sems.at[1]),
        (obs_hbm, obs_ref, early_sems.at[2]),
        (e1_hbm, e1_ref, early_sems.at[3]),
        (eg_hbm, eg_ref, early_sems.at[4]),
        (es_hbm, es_ref, early_sems.at[5]),
        (e2_hbm, e2_ref, early_sems.at[6]),
        (act_hbm, act_ref, early_sems.at[7]),
        (g_hbm, g_ref, early_sems.at[8]),
        (s_hbm, s_ref, early_sems.at[9]),
    ])
    first, second, third, fourth, fifth = load_all([
        (w1_hbm.at[0], w1_ref, sems.at[0]),
        (w2_hbm.at[0], w2_ref, sems.at[1]),
        (dyn_hbm, dyn_ref, sems.at[2]),
        (w1_hbm.at[1], next1_ref, sems.at[3]),
        (w2_hbm.at[1], next2_ref, sems.at[4]),
    ])
    latent = dyn_ref.shape[1]
    tasks, task_width = table_ref.shape
    observed = obs_ref.shape[0]
    acted = act_ref.shape[1]
    mine = own_lanes(place_ref)
    for each in early:
        each.wait()
    spread_columns(eg_ref[...], es_ref[...], erows_ref, espread_ref)
    kinds = lax.broadcasted_iota(jnp.int32, (tasks, LANES), 0)
    onehot = (kinds == ids_ref[:, mine]).astype(F32).astype(BF16)
    wide_ref[...] = jnp.zeros_like(wide_ref)
    wide_ref[:, 0:task_width] = table_ref[...].astype(F32)
    table_tail = pltpu.roll(wide_ref[:, 0:LANES], acted, 1).astype(BF16)
    table_enc = pltpu.roll(wide_ref[...], observed, 1).astype(BF16)
    aux = tn(table_tail, onehot)
    tall_ref[...] = jnp.zeros_like(tall_ref)
    tall_ref[0:observed, :] = obs_ref[:, mine].astype(F32)
    ein = tn(table_enc, onehot)
    ein_ref[0:LANES, :] = (ein[0:LANES] + tall_ref[...]).astype(BF16)
    ein_ref[LANES:, :] = ein[LANES:].astype(BF16)
    e1p_ref[...] = padded_rows(e1_ref[...], e1p_ref.shape[0])
    epre_ref[...] = tn(e1p_ref[...], ein_ref[...])
    here = slice(0, LANES)
    mish_forward(epre_ref, here, espread_ref.at[0], espread_ref.at[1], eh_ref, ehat_ref, eslope_ref, escale_ref, 0, here)
    shares = simplex(tn(e2_ref[...], eh_ref[...]))
    soft_ref[:, 0:LANES] = shares
    xt_ref[0:latent, 0:LANES] = shares.astype(BF16)
    spread_columns(g_ref[0], s_ref[0], rows_ref, spread_ref)
    for step in range(steps):
        tall_ref[...] = jnp.zeros_like(tall_ref)
        tall_ref[0:acted, :] = act_ref[step, :, mine].astype(F32)
        xt_ref[latent:, lanes_of(step)] = (aux + tall_ref[...]).astype(BF16)
    first.wait()
    transpose_into(w1t_ref, w1_ref, latent)
    w1t_ref[:, latent:] = jnp.transpose(padded_rows(w1_ref[latent:, :], LANES))
    second.wait()
    transpose_into(w2t_ref, w2_ref, latent)
    third.wait()
    transpose_into(dynt_ref, dyn_ref, latent)
    for step in range(steps):
        at = lanes_of(step)
        pre_ref[...] = nn(w1t_ref[...], xt_ref[:, at])
        mish_forward(pre_ref, here, spread_ref.at[0], spread_ref.at[2], h1_ref, hat1_ref, slope1_ref, scale_ref, 0, at)
        pre_ref[...] = nn(w2t_ref[...], h1_ref[:, at])
        mish_forward(pre_ref, here, spread_ref.at[1], spread_ref.at[3], h2_ref, hat2_ref, slope2_ref, scale_ref, 1, at)
        shares = simplex(nn(dynt_ref[...], h2_ref[:, at]))
        soft_ref[:, lanes_of(step + 1)] = shares
        if step + 1 < steps:
            xt_ref[0:latent, lanes_of(step + 1)] = shares.astype(BF16)
    for step in range(steps):
        for start in range(0, latent + LANES, LANES):
            x_ref[lanes_of(step), start : start + LANES] = jnp.transpose(xt_ref[start : start + LANES, lanes_of(step)])
    fourth.wait()
    fifth.wait()


def heads_kernel(steps, scale, packs, head, ahead, heads, bins, chained, after, *refs):
    refs = list(refs)
    place_ref, xt_ref, x_ref, w1_ref, w2_ref, ho_ref, g_ref, s_ref, rb_ref, vb_ref, hz_ref = refs[:11]
    refs = refs[11:]
    before_ref = refs.pop(0) if chained else None
    refs = refs[after:]
    w1_hbm, w2_hbm = refs[:2] if ahead else (None, None)
    refs = refs[2:] if ahead else refs
    pack_refs, refs = refs[: 2 * len(packs)], refs[2 * len(packs) :]
    dx_ref, loss_ref = refs[:2]
    refs = refs[2:]
    copies = []
    if ahead:
        next1_ref, next2_ref, sems = refs[0], refs[1], refs[-1]
        refs = refs[2:-1]
        copies = load_all([
            (w1_hbm.at[head + 2], next1_ref, sems.at[0]),
            (w2_hbm.at[head + 2], next2_ref, sems.at[1]),
        ])
    (rows_ref, spread_ref, tail_ref, hop_ref, hot_ref, pre_ref, lg_ref, h1_ref, hat1_ref, slope1_ref,
     h2_ref, hat2_ref, slope2_ref, scale_ref, sums_ref, dh_ref, d2_ref, d1_ref, dl_ref, grad_ref) = refs
    latent = w2_ref.shape[0]
    tail_rows = w1_ref.shape[0] - latent
    mine = own_lanes(place_ref)
    horizon_row = hz_ref[:, mine]
    bin_ids = lax.broadcasted_iota(jnp.int32, (LANES, LANES), 0)
    first_end = latent + LANES
    losses = []
    spread_columns(g_ref[head + 1], s_ref[head + 1], rows_ref, spread_ref)
    tail_ref[...] = padded_rows(w1_ref[latent:, :], LANES)
    hot_ref[...] = padded_rows(ho_ref[head], LANES)
    hop_ref[...] = jnp.transpose(hot_ref[...])
    gain1, gain2, shift1, shift2 = [spread_ref.at[place] for place in range(4)]
    pre_ref[...] = tn(w1_ref[0:latent, :], xt_ref[0:latent, :]) + tn(tail_ref[...], xt_ref[latent:, :])
    for step in range(steps):
        mish_forward_low(pre_ref, gain1, shift1, h1_ref, hat1_ref, slope1_ref, scale_ref, 0, lanes_of(step))
    pre_ref[...] = tn(w2_ref[...], h1_ref[...])
    for step in range(steps):
        mish_forward_low(pre_ref, gain2, shift2, h2_ref, hat2_ref, slope2_ref, scale_ref, 1, lanes_of(step))
    lg_ref[...] = nn(hot_ref[...], h2_ref[...])
    share = 0.1 if head == 0 else 0.1 / (heads - 1)
    bins_ref = rb_ref if head == 0 else vb_ref
    for step in range(steps):
        at = lanes_of(step)
        logits = jnp.where(bin_ids < bins, lg_ref[:, at], F32(-1e30))
        chosen = bin_ids == bins_ref[step : step + 1, mine]
        top = jnp.max(logits, axis=0, keepdims=True)
        powers = jnp.exp(logits - top)
        total = column_sum(powers)
        picked = column_sum(jnp.where(chosen, logits, 0.0))
        weight = row_weight(step, steps, scale * share, horizon_row, place_ref)
        losses.append(weight * (jnp.log(total) + top - picked))
        dl_ref[:, at] = (powers * (weight / total) - jnp.where(chosen, weight, 0.0)).astype(BF16)
    dh_ref[...] = nn(hop_ref[...], dl_ref[...]).astype(BF16)
    grad_ref[:, first_end + latent :] = nt(h2_ref[...], dl_ref[...]).astype(BF16)
    mish_backward_low(dh_ref, hat2_ref, slope2_ref, scale_ref, 1, steps, sums_ref, 2, d2_ref)
    dh_ref[...] = nn(w2_ref[...], d2_ref[...]).astype(BF16)
    grad_ref[:, first_end : first_end + latent] = nt(d2_ref[...], h1_ref[...]).astype(BF16)
    mish_backward_low(dh_ref, hat1_ref, slope1_ref, scale_ref, 0, steps, sums_ref, 0, d1_ref)
    low_part = nn(w1_ref[0:latent, :], d1_ref[...])
    side_part = nn(tail_ref[...], d1_ref[...])
    if not chained:
        dx_ref[0:latent, :] = low_part
        dx_ref[latent:, :] = side_part
    else:
        dx_ref[0:latent, :] = before_ref[0:latent, :] + low_part
        dx_ref[latent:, :] = before_ref[latent:, :] + side_part
    grad_ref[:, 0:latent] = nn(d1_ref[...], x_ref[:, 0:latent]).astype(BF16)
    side_terms = nn(d1_ref[...], x_ref[:, latent:])
    side_terms = with_vectors(side_terms, vector_sums(sums_ref, spread_ref, 2), tail_rows)
    grad_ref[:, latent:first_end] = side_terms.astype(BF16)
    for place, (slots, first, units) in enumerate(packs):
        for relative, (which, slot) in enumerate(slots):
            start = pl.multiple_of((place_ref[0] ^ relative) * GROUP, GROUP)
            out_ref = pack_refs[2 * place + which]
            if not units:
                out_ref[slot] = grad_ref[pl.ds(start, GROUP), :]
                continue
            block = grad_ref[pl.ds(start, GROUP), first * LANES : (first + units) * LANES]
            for unit in range(units):
                out_ref[slot * units + unit] = block[:, unit * LANES : (unit + 1) * LANES]
    loss_ref[...] = functools.reduce(jnp.add, losses)
    for each in copies:
        each.wait()


def backward_kernel(
    steps, scale, order, losses, after,
    place_ref, xt_ref, soft_ref, h1_ref, hat1_ref, slope1_ref, h2_ref, hat2_ref, slope2_ref, scale_ref,
    w1_ref, w2_ref, dyn_ref, hz_ref, g_ref, dx_ref, *rest,
):
    initial = order[0] == steps - 1
    final = order[-1] == 0
    loss_refs, rest = rest[:losses], rest[losses:]
    held_refs, rest = ((), rest) if initial else (rest[:4], rest[4:])
    (tgt_hbm, low_ref, first_ref, side_ref, loss_ref, sums_ref, tgt_ref, rows_ref, spread_ref, tail_ref, pre_ref,
     d1_ref, d2_ref, do_ref, grad_ref, sems) = rest[after:]
    mine = own_lanes(place_ref)
    loads = dict(zip(order, load_all([(tgt_hbm.at[step, mine, :], tgt_ref.at[step], sems.at[step]) for step in order])))
    latent = dyn_ref.shape[1]
    here = slice(0, LANES)
    horizon_row = hz_ref[:, mine]
    spread_columns(g_ref[0], g_ref[0], rows_ref, spread_ref)
    tail_rows = w1_ref.shape[0] - latent
    tail_ref[...] = padded_rows(w1_ref[latent:, :], LANES)
    first_end = latent + LANES
    second_end = first_end + latent
    if initial:
        loss = functools.reduce(jnp.add, [each[...] for each in loss_refs])
        side = jnp.zeros((LANES, LANES), F32)
        incoming = None
    else:
        before_ref, given_ref, given_side_ref, given_sums_ref = held_refs
        loss = loss_refs[0][...]
        side = given_side_ref[...]
        incoming = given_ref[...].astype(F32)
        sums_ref[...] = given_sums_ref[...]
    pending = []

    def add_terms(at, fresh, last):
        terms = (
            (slice(0, first_end), nt(d1_ref[:, at], xt_ref[:, at])),
            (slice(first_end, second_end), nt(d2_ref[:, at], h1_ref[:, at])),
            (slice(second_end, second_end + latent), nt(h2_ref[:, at], do_ref[:, at])),
        )
        for lanes, term in terms:
            if not fresh:
                term = term + grad_ref[:, lanes]
            elif not initial:
                term = term + before_ref[:, lanes]
            out_ref = low_ref if last else grad_ref
            if last and final and lanes.start == 0:
                out_ref[:, 0:latent] = term[:, 0:latent].astype(out_ref.dtype)
                vectors = vector_sums(sums_ref, spread_ref, 2)
                out_ref[:, latent:first_end] = with_vectors(term[:, latent:], vectors, tail_rows).astype(out_ref.dtype)
            else:
                out_ref[:, lanes] = term.astype(out_ref.dtype)

    for step in order:
        at = lanes_of(step)
        weight = row_weight(step, steps, scale, horizon_row, place_ref)
        shares = soft_ref[:, lanes_of(step + 1)]
        loads[step].wait()
        residue = shares - jnp.transpose(tgt_ref[step].astype(F32))
        loss = loss + (20.0 / latent) * weight * column_sum(residue * residue)
        grads = residue * ((40.0 / latent) * weight)
        if incoming is not None:
            grads = grads + incoming
        do_ref[:, at] = simplex_back(shares, grads).astype(BF16)
        pre_ref[...] = nn(dyn_ref[...], do_ref[:, at])
        mish_backward(pre_ref, here, hat2_ref, slope2_ref, scale_ref, 1, at, sums_ref, 2, step == steps - 1, d2_ref)
        pre_ref[...] = nn(w2_ref[...], d2_ref[:, at])
        mish_backward(pre_ref, here, hat1_ref, slope1_ref, scale_ref, 0, at, sums_ref, 0, step == steps - 1, d1_ref)
        incoming = nn(w1_ref[0:latent, :], d1_ref[:, at]) + dx_ref[0:latent, at]
        side = side + nn(tail_ref[...], d1_ref[:, at]) + dx_ref[latent:, at]
        incoming = incoming.astype(BF16).astype(F32)
        pending.append(step)
        if len(pending) == 2 or step == order[-1]:
            low, high = min(pending), max(pending) + 1
            add_terms(slice(low * LANES, high * LANES), high == order[0] + 1, low == order[-1])
            pending = []

    first_ref[...] = incoming.astype(BF16)
    side_ref[...] = side
    loss_ref[...] = loss


def ending_kernel(
    slots, tasks, task_width, acted, observed, after,
    place_ref, low_ref, first_ref, side_ref, loss_ref, soft_ref, ein_ref, eh_ref, ehat_ref, eslope_ref, escale_ref,
    ids_ref, e1_ref, eg_ref, e2_ref, *rest,
):
    out_refs, rest = rest[after : after + 2], rest[after + 2 :]
    erows_ref, espread_ref, e1p_ref, epre_ref, esums_ref, ed_ref, egrad_ref = rest
    mine = own_lanes(place_ref)
    here = slice(0, LANES)
    latent = first_ref.shape[0]
    spread_columns(eg_ref[...], eg_ref[...], erows_ref, espread_ref)
    e1p_ref[...] = padded_rows(e1_ref[...], e1p_ref.shape[0])
    d_enc = simplex_back(soft_ref[:, 0:LANES], first_ref[...].astype(F32)).astype(BF16)
    epre_ref[...] = nn(e2_ref[...], d_enc)
    mish_backward(epre_ref, here, ehat_ref, eslope_ref, escale_ref, 0, here, esums_ref, 0, True, ed_ref)
    side_enc = nn(e1p_ref[...], ed_ref[...])
    enc_width = epre_ref.shape[0]
    half = GROUP // 2
    groups = enc_width // half
    kept = egrad_ref.shape[2]
    enc_second = nt(eh_ref[...], d_enc)
    egrad_ref[:, 0:half, :] = enc_second[:, 0:kept].reshape(groups, half, kept)
    egrad_ref[:, half:, 0 : latent - kept] = enc_second[:, kept:].reshape(groups, half, latent - kept)
    enc_first = nt(ed_ref[...], ein_ref[...])
    egrad_ref[:, half:, latent - kept : kept - LANES] = enc_first[:, 0:LANES].reshape(groups, half, LANES)
    second_lanes = with_vectors(enc_first[:, LANES : 2 * LANES], vector_sums(esums_ref, espread_ref, 1), LANES - 2)
    egrad_ref[:, half:, kept - LANES :] = second_lanes.reshape(groups, half, LANES)

    kinds = lax.broadcasted_iota(jnp.int32, (tasks, LANES), 0)
    onehot = (kinds == ids_ref[:, mine]).astype(F32)
    over_lanes = (((1,), (1,)), ((), ()))
    highest = lax.Precision.HIGHEST
    side_terms = lax.dot_general(onehot, side_ref[...], over_lanes, precision=highest, preferred_element_type=F32)
    enc_terms = lax.dot_general(onehot, side_enc, over_lanes, precision=highest, preferred_element_type=F32)
    table = pltpu.roll(side_terms, LANES - acted, 1)
    table = table + pltpu.roll(enc_terms, enc_terms.shape[1] - observed, 1)[:, 0:LANES]
    lane = lax.broadcasted_iota(jnp.int32, table.shape, 1)
    table = jnp.where(lane < task_width, table, 0.0)
    table = jnp.where((lane == LANES - 1) & (kinds == 0), jnp.sum(loss_ref[...], axis=1, keepdims=True), table)
    table_rows = [table[start : start + GROUP] for start in range(0, tasks, GROUP)]
    table_block = jnp.concatenate(table_rows, axis=1).astype(BF16)
    count = low_ref.shape[1] // LANES
    units = count + kept // LANES
    for relative, (which, slot) in enumerate(slots):
        dest = place_ref[0] ^ relative
        start = pl.multiple_of(dest * GROUP, GROUP)
        block = jnp.concatenate([low_ref[pl.ds(start, GROUP), :], egrad_ref[dest].astype(BF16)], axis=1)
        for unit in range(units):
            out_refs[which][slot * units + unit] = block[:, unit * LANES : (unit + 1) * LANES]
    last = len(slots) // 2 * units
    for unit in range(tasks // GROUP):
        for out_ref in out_refs:
            out_ref[last + unit] = table_block[:, unit * LANES : (unit + 1) * LANES]


def final_kernel(tasks, task_width, enc_in, bins, net_in, *refs):
    outs = refs[-12:]
    (loss_ref, table_ref, e1_ref, eg_ref, es_ref, e2_ref, first_ref, second_ref, gain_ref, shift_ref, dyn_ref, head_ref) = outs
    refs = refs[:-12]
    tail_refs, refs = refs[:4], refs[4:]
    latent = second_ref.shape[2]
    first_end = latent + LANES
    second_end = first_end + latent

    def put_net(net, value):
        first_ref[net] = value[:, 0:net_in]
        second_ref[net] = value[:, first_end:second_end]
        turned = jnp.transpose(value[:, latent:first_end])
        for layer in range(2):
            row = net_in - latent + 2 * layer
            gain_ref[net, layer : layer + 1, :] = turned[row : row + 1, :]
            shift_ref[net, layer : layer + 1, :] = turned[row + 1 : row + 2, :]

    sums = functools.reduce(jnp.add, [ref[...].astype(F32) for ref in tail_refs])
    units = sums.shape[0] - tasks // GROUP
    tail = jnp.concatenate([sums[unit] for unit in range(units)], axis=1)
    put_net(0, tail)
    dyn_ref[...] = tail[:, second_end : second_end + latent]
    enc = tail[:, second_end + latent :]
    half = GROUP // 2
    kept = enc.shape[1]
    e2_ref[:, 0:kept] = 0.3 * enc[0:half, :]
    e2_ref[:, kept:] = 0.3 * enc[half:, 0 : latent - kept]
    e1_ref[...] = 0.3 * enc[half:, latent - kept : latent - kept + enc_in]
    turned = 0.3 * jnp.transpose(enc[half:, kept - LANES :])
    eg_ref[...] = turned[LANES - 2 : LANES - 1, :]
    es_ref[...] = turned[LANES - 1 : LANES, :]
    loss_ref[...] = sums[units, 0:1, LANES - 1 : LANES]
    for place in range(tasks // GROUP):
        table_ref[place * GROUP : (place + 1) * GROUP, :] = sums[units + place, :, 0:task_width]
    net = 1
    def put_head(value):
        put_net(net, value)
        head_ref[net - 1] = value[:, second_end : second_end + bins]

    one_ref, other_ref, last_one_ref, last_other_ref = refs
    for one in range(one_ref.shape[1]):
        put_head(one_ref[0, one].astype(F32) + other_ref[0, one].astype(F32))
        net += 1
    sums = last_one_ref[...].astype(F32) + last_other_ref[...].astype(F32)
    units = (second_end + LANES) // LANES
    for start in range(0, sums.shape[0], units):
        put_head(jnp.concatenate([sums[start + unit] for unit in range(units)], axis=1))
        net += 1


def swap(value, axis, distance):
    count = lax.axis_size(axis)
    return lax.ppermute(value, axis, [(place, place ^ distance) for place in range(count)])


def exchange(parts, axis, scale):
    total = parts[0].astype(F32)
    for distance in range(1, len(parts)):
        total = total + swap(parts[distance], axis, distance * scale).astype(F32)
    return total


def scatter_plain(packed, chips, sections):
    held = packed.reshape((sections, chips, CORES) + packed.shape[1:])
    batch_no = lax.axis_index("batch")
    places = (
        ("batch", 1, CORES, 2, batch_no % CORES),
        ("batch", CORES, chips, 1, batch_no // CORES),
        ("section", 1, sections, 0, lax.axis_index("section")),
    )
    for axis, scale, count, dim, mine in places:
        parts = [lax.dynamic_index_in_dim(held, mine ^ other, dim, keepdims=False) for other in range(count)]
        held = exchange(parts, axis, scale)
        held = held.astype(BF16) if dim else held
    return held


def on_device(
    observations,
    actions,
    targets,
    task_ids,
    horizons,
    reward_bins,
    value_bins,
    task_table,
    enc_first,
    enc_gain,
    enc_shift,
    enc_second,
    net_first,
    net_second,
    net_gain,
    net_shift,
    dyn_out,
    head_out,
):
    sections = lax.axis_size("section")
    batches = lax.axis_size("batch")
    section_no = lax.axis_index("section")
    chips = batches // CORES
    devices = sections * batches
    steps, rows_all, acted = actions.shape
    observed = observations.shape[1]
    rows = rows_all // sections
    latent = dyn_out.shape[1]
    hidden = dyn_out.shape[0]
    tasks, task_width = task_table.shape
    heads, _, bins = head_out.shape
    nets, net_in, _ = net_first.shape
    enc_in, enc_width = enc_first.shape
    wide = steps * LANES
    scale = 1.0 / (rows_all * batches * steps)
    groups = hidden // GROUP
    in_place = hidden // devices == GROUP
    start = section_no * rows
    block_no = start // LANES
    first_lane = start - block_no * LANES
    me = section_no * batches + lax.axis_index("batch") if in_place else jnp.int32(0)
    place = jnp.stack([me, block_no, first_lane, first_lane + rows]).astype(jnp.int32)
    bits = [("batch", 1 << bit) for bit in range(batches.bit_length() - 1)]
    bits += [("section", 1 << bit) for bit in range(sections.bit_length() - 1)]

    def slots_of(order):
        if not in_place:
            return tuple((relative // (groups // 2), relative % (groups // 2)) for relative in range(groups))
        found = []
        for relative in range(groups):
            slot = 0
            for bit in order:
                slot = 2 * slot + (relative >> bit & 1)
            found.append((slot // (groups // 2), slot % (groups // 2)))
        return tuple(found)

    plain = tuple(range(len(bits)))
    y_first = (0, 2, 1) + tuple(range(3, len(bits))) if in_place else plain
    half_slots = groups // 2
    shape_of = jax.ShapeDtypeStruct
    smem = pl.BlockSpec(memory_space=pltpu.SMEM)
    local = pl.BlockSpec(memory_space=pltpu.VMEM)
    far = pl.BlockSpec(memory_space=pltpu.HBM)
    anywhere = pl.BlockSpec(memory_space=pl.ANY)
    first_far, second_far, dyn_far, targets_far = [
        pltpu.with_memory_space_constraint(array, pltpu.HBM) for array in (net_first, net_second, dyn_out, targets)
    ]
    vmem = pltpu.VMEM
    dmas = pltpu.SemaphoreType.DMA

    def params(mebibytes):
        return pltpu.CompilerParams(vmem_limit_bytes=mebibytes * 1024 * 1024)

    def cost(flops, moved):
        return pl.CostEstimate(flops=flops, bytes_accessed=moved, transcendentals=0)

    ids_row = task_ids.reshape(1, rows_all)
    horizon_row = horizons.reshape(1, rows_all)
    eg_row = enc_gain.reshape(1, enc_width)
    es_row = enc_shift.reshape(1, enc_width)
    head_turned = head_out.transpose(0, 2, 1)
    low = lambda lanes: shape_of((hidden, lanes), BF16)
    forward_shapes = (
        shape_of((latent + LANES, wide), BF16),
        shape_of((latent, wide + LANES), F32),
        low(wide), low(wide), low(wide), low(wide), low(wide), low(wide),
        shape_of((8, wide), F32),
        shape_of((2 * LANES, LANES), BF16),
        shape_of((enc_width, LANES), BF16),
        shape_of((enc_width, LANES), BF16),
        shape_of((enc_width, LANES), BF16),
        shape_of((8, LANES), F32),
        shape_of((net_in, hidden), BF16),
        shape_of((hidden, hidden), BF16),
        shape_of((hidden, latent), BF16),
        shape_of((wide, latent + LANES), BF16),
    )

    weight_shapes = (shape_of((net_in, hidden), BF16), shape_of((hidden, hidden), BF16))

    early = [
        pltpu.with_memory_space_constraint(array, pltpu.HBM)
        for array in (
            observations.T, actions.transpose(0, 2, 1), ids_row, task_table, enc_first, eg_row, es_row, enc_second,
            net_gain, net_shift,
        )
    ]
    made = pl.pallas_call(
        functools.partial(forward_kernel, steps),
        out_shape=forward_shapes + weight_shapes,
        in_specs=[smem] + [far] * 13,
        out_specs=[local] * (len(forward_shapes) + 2),
        scratch_shapes=[
            vmem((8, hidden), F32),
            vmem((4, hidden, LANES), F32),
            vmem((8, enc_width), F32),
            vmem((2, enc_width, LANES), F32),
            vmem((tasks, 2 * LANES), F32),
            vmem((LANES, LANES), F32),
            vmem((2 * LANES, enc_width), BF16),
            vmem((hidden, latent + LANES), BF16),
            vmem((hidden, hidden), BF16),
            vmem((latent, hidden), BF16),
            vmem((hidden, LANES), F32),
            vmem((enc_width, LANES), F32),
            *[vmem(each.shape, each.dtype) for each in early],
            dmas((5,)),
            dmas((len(early),)),
        ],
        compiler_params=params(VMEM_A),
        cost_estimate=cost(10_000_000_000, 8_000_000),
        name="forward_chain",
    )(
        place, *early, first_far, second_far, dyn_far,
    )
    saved, x_rows, weights = made[:-3], made[-3], made[-2:]
    xt = saved[0]
    head_width = latent + LANES + hidden + LANES

    def run_head(head, ahead, weights, before, after):
        all_units = head_width // LANES
        packs = [(slots_of(plain), 0, 0)]
        if in_place and head == heads - 1:
            packs = [(slots_of(plain), 0, all_units // 2), (slots_of(y_first), all_units // 2, all_units // 2)]
        pack_shapes = []
        for _, _, count in packs:
            shape = (half_slots * count, GROUP, LANES) if count else (half_slots, GROUP, head_width)
            pack_shapes += [shape_of(shape, BF16)] * 2
        dx_shape = shape_of((latent + LANES, wide), F32)
        out_shapes = (*pack_shapes, dx_shape, shape_of((1, LANES), F32))
        args = [place, xt, x_rows, *weights, head_turned, net_gain, net_shift, reward_bins, value_bins, horizon_row]
        specs = [smem] + [local] * 10
        aliases = {}
        if before is not None:
            aliases = {len(args): len(pack_shapes)}
            args.append(before)
            specs.append(local)
        args += after
        specs += [anywhere] * len(after)
        if ahead:
            args += [first_far, second_far]
            specs += [far, far]
            out_shapes += weight_shapes
        low_wide = vmem((hidden, wide), BF16)
        scratch = [
            vmem((8, hidden), F32),
            vmem((4, hidden, LANES), F32),
            vmem((LANES, hidden), BF16),
            vmem((hidden, LANES), BF16),
            vmem((LANES, hidden), BF16),
            vmem((hidden, wide), F32),
            vmem((LANES, wide), F32),
        ]
        scratch += [low_wide] * 6
        scratch += [vmem((8, wide), F32), vmem((4, hidden, LANES), F32)]
        scratch += [low_wide] * 3
        scratch += [vmem((LANES, wide), BF16), vmem((hidden, head_width), BF16)]
        if ahead:
            scratch.append(dmas((2,)))
        return pl.pallas_call(
            functools.partial(
                heads_kernel, steps, scale, packs, head, ahead, heads, bins, before is not None, len(after)
            ),
            out_shape=out_shapes,
            in_specs=specs,
            out_specs=[local] * len(out_shapes),
            scratch_shapes=scratch,
            input_output_aliases=aliases,
            compiler_params=params(VMEM_B),
            cost_estimate=cost(9_000_000_000, 4_000_000),
            name=f"head_{head}",
        )(*args)

    def phase(pair, bit):
        return pair[0], swap(pair[1], *bits[bit])

    def fold(members, *tokens):
        slots_now = members[0][0].shape[0] // 2
        shape = members[0][0].shape[1:]
        stacked = len(shape) == 3
        if stacked:
            shape = (len(members) * shape[0],) + shape[1:]
        elif len(members) > 1:
            shape = (len(members),) + shape
        out_shape = shape_of((slots_now,) + shape, BF16)

        def fold_kernel(*refs):
            refs = refs[len(tokens) :]
            outs = refs[-2:]
            for place in range(len(members)):
                kept_ref, came_ref = refs[2 * place], refs[2 * place + 1]
                for half in range(2):
                    part = pl.ds(half * slots_now, slots_now)
                    value = (kept_ref[part].astype(F32) + came_ref[part].astype(F32)).astype(BF16)
                    if stacked:
                        count = kept_ref.shape[1]
                        outs[half][:, place * count : (place + 1) * count] = value
                    elif len(members) > 1:
                        outs[half][:, place] = value
                    else:
                        outs[half][...] = value

        return run_fold(fold_kernel, out_shape, members, tokens)

    def fold_units(members, slots_now, common, *tokens):
        counts = [
            kept.shape[2] // LANES if kept.shape[2] > LANES else (kept.shape[0] - (0 if place else common)) // slots_now
            for place, (kept, _) in enumerate(members)
        ]
        half_now = slots_now // 2
        width = sum(counts)
        out_shape = shape_of((half_now * width + common, GROUP, LANES), BF16)

        def fold_kernel(*refs):
            refs = refs[len(tokens) :]
            outs = refs[-2:]
            before = 0
            for place, count in enumerate(counts):
                kept_ref, came_ref = refs[2 * place], refs[2 * place + 1]

                def added(start, size):
                    part = pl.ds(start, size)
                    return (kept_ref[part].astype(F32) + came_ref[part].astype(F32)).astype(BF16)

                for half in range(2):
                    if kept_ref.shape[2] > LANES:
                        for slot in range(half_now):
                            block = added(half * half_now + slot, 1)[0]
                            for unit in range(count):
                                piece = block[:, unit * LANES : (unit + 1) * LANES]
                                outs[half][slot * width + before + unit] = piece
                    elif len(counts) == 1:
                        outs[half][0 : half_now * count] = added(half * half_now * count, half_now * count)
                    else:
                        for slot in range(half_now):
                            at = slot * width + before
                            outs[half][at : at + count] = added((half * half_now + slot) * count, count)
                if place == 0 and common:
                    value = added(slots_now * count, common)
                    for out in outs:
                        out[half_now * width :] = value
                before += count

        return run_fold(fold_kernel, out_shape, members, tokens)

    def fold_direct(parts, slots_now, common, *tokens):
        quarter = (parts[0].shape[0] - common) // 4
        out_shape = shape_of((quarter + common, GROUP, LANES), BF16)

        def fold_kernel(*refs):
            refs = refs[len(tokens) :]
            outs = refs[-4:]

            def added(start, size):
                each = [ref[pl.ds(start, size)].astype(F32) for ref in refs[: len(parts)]]
                return functools.reduce(jnp.add, each).astype(BF16)

            shared = added(4 * quarter, common)
            for place, out in enumerate(outs):
                out[0:quarter] = added(place * quarter, quarter)
                out[quarter:] = shared

        return pl.pallas_call(
            fold_kernel,
            out_shape=(out_shape,) * 4,
            in_specs=[anywhere] * len(tokens) + [local] * len(parts),
            out_specs=(local,) * 4,
            compiler_params=params(VMEM_SUM),
            cost_estimate=cost(1_000_000, 2_000_000),
            name="fold_direct",
        )(*tokens, *parts)

    def direct(pieces, axis, high, low):
        distances = (0, low, high, high + low)
        came = [swap(pieces[place], axis, distances[place]) for place in (3, 2, 1)]
        return [pieces[0], *came]

    def run_fold(kernel, out_shape, members, tokens):
        inputs = [each for member in members for each in member]
        return pl.pallas_call(
            kernel,
            out_shape=(out_shape, out_shape),
            in_specs=[anywhere] * len(tokens) + [local] * len(inputs),
            out_specs=(local, local),
            compiler_params=params(VMEM_SUM),
            cost_estimate=cost(1_000_000, 2_000_000),
            name="fold",
        )(*tokens, *inputs)

    net_width = latent + LANES + hidden + latent
    chain_inputs = saved[:9] + saved[14:]

    def run_backward(order, losses, held, after):
        final = order[-1] == 0
        out_shapes = (
            shape_of((hidden, net_width), BF16 if final else F32),
            shape_of((latent, LANES), BF16),
            shape_of((LANES, LANES), F32),
            shape_of((1, LANES), F32),
            shape_of((4, hidden, LANES), F32),
        )
        args = [place, *chain_inputs, horizon_row, net_gain, dx, *losses, *held]
        return pl.pallas_call(
            functools.partial(backward_kernel, steps, scale, order, len(losses), len(after)),
            out_shape=out_shapes,
            in_specs=[smem] + [local] * (len(args) - 1) + [anywhere] * len(after) + [far],
            out_specs=[local] * len(out_shapes),
            scratch_shapes=[
                vmem((steps, LANES, latent), BF16),
                vmem((8, hidden), F32),
                vmem((4, hidden, LANES), F32),
                vmem((LANES, hidden), BF16),
                vmem((hidden, LANES), F32),
                vmem((hidden, wide), BF16),
                vmem((hidden, wide), BF16),
                vmem((latent, wide), BF16),
                vmem((hidden, net_width), F32),
                dmas((steps,)),
            ],
            compiler_params=params(VMEM_C),
            cost_estimate=cost(7_000_000_000, 8_000_000),
            name=f"backward_{order[0]}",
        )(*args, *after, targets_far)

    packs, loss_parts = [], []
    dx = None
    after = []
    cores, pairs = [], []
    units_all = head_width // LANES
    for head in range(heads):
        result = run_head(head, head + 1 < heads, weights, dx, after)
        sent = 4 if in_place and head == heads - 1 else 2
        dx, loss = result[sent : sent + 2]
        weights = result[sent + 2 :]
        packs.append(result[:sent])
        loss_parts.append(loss)
        after = []
        if in_place:
            if 1 <= head <= heads - 2:
                crossing = fold([cores[head - 1]], loss)
                after.append(crossing[0])
                pairs.append(phase(crossing, plain[1]))
            if head in (3, 5):
                crossing = fold(pairs[head - 3 : head - 1], loss)
                after.append(crossing[0])
                pairs[head - 3] = phase(crossing, plain[2])
            if head == heads - 1:
                fourth = fold([cores[head - 1]], loss)
                after.append(fourth[0])
                fourth = phase(fourth, plain[1])
                cores.append(phase(result[0:2], plain[0]))
                cores.append(phase(result[2:4], y_first[0]))
            else:
                cores.append(phase(result[0:2], plain[0]))
    half_way = steps // 2
    chain = run_backward(tuple(range(steps - 1, half_way - 1, -1)), loss_parts, [], after)
    after = []
    if in_place:
        token = chain[3]
        fifth = fold_units([cores[heads - 1]], half_slots, 0, token)
        sixth = fold_units([cores[heads]], half_slots, 0, token)
        fourth = fold([fourth], token)
        group = fold([pairs[0], pairs[2]], token)
        after = [fifth[0], sixth[0], fourth[0], group[0]]
        fifth = phase(fifth, plain[1])
        sixth = phase(sixth, y_first[1])
        group = phase(group, plain[3])
        fourth = phase(fourth, plain[2])
    chain = run_backward(
        tuple(range(half_way - 1, -1, -1)), [chain[3]], [chain[0], chain[1], chain[2], chain[4]], after
    )
    after = []
    if in_place:
        token = chain[3]
        fifth = fold_units([fifth], half_slots // 2, 0, token)
        sixth = fold_units([sixth], half_slots // 2, 0, token)
        group = fold([group], token)
        after = [fifth[0], sixth[0], group[0], fourth[1]]
        fifth = phase(fifth, plain[2])
        sixth = phase(sixth, y_first[2])
        group = phase(group, plain[4])

    enc_lanes = latent - LANES
    units = (net_width + enc_lanes) // LANES
    common = tasks // GROUP
    tail_shape = shape_of((half_slots * units + common, GROUP, LANES), BF16)
    ended = pl.pallas_call(
        functools.partial(ending_kernel, slots_of(plain), tasks, task_width, acted, observed, len(after)),
        out_shape=(tail_shape, tail_shape),
        in_specs=[smem] + [local] * 14 + [anywhere] * len(after),
        out_specs=[local] * 2,
        scratch_shapes=[
            vmem((8, enc_width), F32),
            vmem((2, enc_width, LANES), F32),
            vmem((2 * LANES, enc_width), BF16),
            vmem((enc_width, LANES), F32),
            vmem((2, enc_width, LANES), F32),
            vmem((enc_width, LANES), BF16),
            vmem((groups, GROUP, enc_lanes), F32),
        ],
        compiler_params=params(VMEM_SUM),
        cost_estimate=cost(1_000_000_000, 4_000_000),
        name="ending",
    )(place, *chain[:4], saved[1], *saved[9:14], ids_row, enc_first, eg_row, enc_second, *after)

    if in_place:
        tail = phase(ended, plain[0])
        pieces = fold_direct(tail, half_slots, common, fifth[1], sixth[1])
        tail = direct(pieces, "batch", CORES, 2 * CORES)
        last = phase(fold_units([fourth, fifth, sixth], half_slots // 4, 0, ended[0]), plain[3])
        pieces = fold_direct(tail, half_slots // 4, common, last[1], group[1])
        last = phase(fold_units([last], half_slots // 8, 0, ended[0]), plain[4])
        tail = direct(pieces, "section", 1, 2)
        each = GROUP // 2
        out_shapes = (
            shape_of((1, 1), F32),
            shape_of((tasks, task_width), F32),
            shape_of((each, enc_in), F32),
            shape_of((1, each), F32),
            shape_of((1, each), F32),
            shape_of((each, latent), F32),
            shape_of((nets, GROUP, net_in), F32),
            shape_of((nets, GROUP, hidden), F32),
            shape_of((nets, 2, GROUP), F32),
            shape_of((nets, 2, GROUP), F32),
            shape_of((GROUP, latent), F32),
            shape_of((heads, GROUP, bins), F32),
        )
        ends = [*tail, *group, *last]
        outs = list(pl.pallas_call(
            functools.partial(final_kernel, tasks, task_width, enc_in, bins, net_in),
            out_shape=out_shapes,
            in_specs=[local] * len(ends),
            out_specs=[local] * len(out_shapes),
            compiler_params=params(VMEM_SUM),
            cost_estimate=cost(1_000_000, 4_000_000),
            name="last_sums",
        )(*ends))
        outs[0] = outs[0].reshape(())
        outs[2] = outs[2].T
        outs[3], outs[4] = outs[3].reshape(each), outs[4].reshape(each)
        outs[6] = outs[6].transpose(0, 2, 1)
        outs[7] = outs[7].transpose(0, 2, 1)
        return tuple(outs)

    def scattered(keep, send):
        mine = hidden // devices
        packed = jnp.concatenate([keep, send], axis=0)
        middle = packed.shape[1:-2]
        packed = packed.reshape((groups,) + middle + (GROUP // mine, mine, packed.shape[-1]))
        packed = jnp.moveaxis(packed, -3, 1).reshape((devices,) + middle + (mine, packed.shape[-1]))
        return scatter_plain(packed, chips, sections)

    head_sum = jnp.stack([scattered(*pack) for pack in packs], axis=0)
    enc_each = enc_width // devices
    def by_rows(array):
        joined = array[: half_slots * units].reshape(half_slots, units, GROUP, LANES).transpose(0, 2, 1, 3)
        return joined.reshape(half_slots, GROUP, units * LANES)

    keep, send = by_rows(ended[0]), by_rows(ended[1])
    table_sum = lax.psum(ended[0][half_slots * units :].astype(F32), ("section", "batch"))
    table_sum = table_sum.transpose(1, 0, 2).reshape(GROUP, common * LANES)
    net_sum = scattered(keep[:, :, 0:net_width], send[:, :, 0:net_width])
    enc_all = jnp.concatenate([keep, send], axis=0)[:, :, net_width:]
    enc_all = enc_all.reshape(groups, 2, enc_width // groups, enc_lanes)
    enc_all = enc_all.transpose(0, 2, 1, 3).reshape(devices, enc_each, 2, enc_lanes)
    enc_sum = scatter_plain(enc_all, chips, sections)
    enc_low, enc_high = enc_sum[:, 0], enc_sum[:, 1]
    s_enc_second = jnp.concatenate([enc_low, enc_high[:, 0 : latent - enc_lanes]], axis=1)
    enc_rows = enc_high[:, latent - enc_lanes :]
    first_end = latent + LANES
    net_row = jnp.concatenate([net_sum[:, 0 : first_end + hidden], jnp.zeros_like(net_sum[:, 0:LANES])], axis=1)
    sums = jnp.concatenate([net_row[None], head_sum], axis=0)
    vectors = sums[:, :, net_in : net_in + 4].transpose(0, 2, 1)
    table = table_sum.reshape(GROUP, tasks // GROUP, LANES).transpose(1, 0, 2).reshape(tasks, LANES)
    return (
        table[0, LANES - 1],
        table[:, 0:task_width],
        0.3 * enc_rows[:, 0:enc_in].T,
        0.3 * enc_rows[:, 2 * LANES - 2],
        0.3 * enc_rows[:, 2 * LANES - 1],
        0.3 * s_enc_second,
        sums[:, :, 0:net_in].transpose(0, 2, 1),
        sums[:, :, first_end : first_end + hidden].transpose(0, 2, 1),
        vectors[:, 0::2],
        vectors[:, 1::2],
        net_sum[:, first_end + hidden :],
        head_sum[:, :, first_end + hidden : first_end + hidden + bins],
    )


def solution(mesh):
    both = ("section", "batch")
    return jax.shard_map(
        on_device,
        mesh=mesh,
        in_specs=(
            P("batch", None),
            P(None, "batch", None),
            P(None, "batch", None),
            P("batch"),
            P("batch"),
            P(None, "batch"),
            P(None, "batch"),
        )
        + (P(),) * 11,
        out_specs=(
            P(),
            P(),
            P(None, both),
            P(both),
            P(both),
            P(both, None),
            P(None, None, both),
            P(None, None, both),
            P(None, None, both),
            P(None, None, both),
            P(both, None),
            P(None, both, None),
        ),
        check_vma=False,
    )
```
